32 devices in a mesh: row: 8 (over z, core), col: 4 (over y, x).
Axes of the slice: x: 2, y: 2, z: 4, core: 2. Of those that a mesh axis runs over, the one named last changes fastest.
Arguments:
- tokens: bfloat16 [4096, 1024], P('row', 'col')
- cotangent: bfloat16 [4096, 1024], P('row', 'col'), may hold values from -6 to 6
- deal_order: int32 [4096], replicated, may hold values from 0 to 4095, as said below
- seq_lengths: int32 [8, 4], P('row'), may hold values from 1 to 256, 512 in all within a row
- value_picks: int32 [4096, 4, 32], P('row'), may hold values from 0 to 65535
- norm1_gain: float32 [1024], P('col'), may hold values from 0.5 to 1.5
- w_qkv: float32 [1024, 3072], P('row', 'col'), may hold values from -0.1875 to 0.1875
- w_attn_out: float32 [1024, 1024], P('col', 'row'), may hold values from -3 to 3
- norm2_gain: float32 [1024], P('col'), may hold values from 0.5 to 1.5
- w_query: float32 [1024, 4096], P('row', 'col'), may hold values from -0.1875 to 0.1875
- sub_keys: float32 [8, 256, 512], P('col', 'row'), may hold values from -0.09375 to 0.09375
- value_table: float32 [65536, 1024], P('row', 'col'), may hold values from -6 to 6
- w_gate: float32 [1024, 1024], P('row', 'col'), may hold values from -0.1875 to 0.1875
- w_mem_out: float32 [1024, 1024], P('col', 'row'), may hold values from -0.75 to 0.75
Outputs:
- output: float32 [4096, 1024], P('row', 'col')
- grad_tokens: float32 [4096, 1024], P('row', 'col')
- grad_norm1_gain: float32 [1024], P(('col', 'row'))
- grad_w_qkv: float32 [1024, 3072], P('row', 'col')
- grad_w_attn_out: float32 [1024, 1024], P('col', 'row')
- grad_norm2_gain: float32 [1024], P(('col', 'row'))
- grad_w_query: float32 [1024, 4096], P('row', 'col')
- grad_sub_keys: float32 [8, 256, 512], P('col', 'row')
- grad_value_table: float32 [65536, 1024], P('row', 'col')
- grad_w_gate: float32 [1024, 1024], P('row', 'col')
- grad_w_mem_out: float32 [1024, 1024], P('col', 'row')
The draws below stay inside these ranges and needn't reach their ends.
Inputs may be any that keep to these rules, and one draw needn't show every extreme that they name: Dealt slot s holds initial token deal_order[s], each token once. Of the 512 tokens of one aligned block of initial positions, at most 128 go to any one aligned block of 512 dealt slots, and exactly 128 go to some block. `seq_lengths`: each row sums to 512. `value_picks`: row i of the memory pairs first-half sub-key i // 256 with second-half sub-key i % 256.
All inputs are finite; a program needn't handle non-finite values.
Results may differ from the reference program's by a relative error of at most 0.0095.
The reference program's roundings to bfloat16 on the way count: a program that leaves them out, or rounds other values in their place, can miss the bound.
Values may be sent and summed in bfloat16 or wider, within the bound.
A program may use at most 384 MiB of HBM per device.

```python
import math
import jax
import jax.numpy as jnp
import numpy as np
from jax import lax

D = 1024
H = 16
HD = 64
MH = 4
QD = 512
NK = 256
NV = 65536
PICKS = 32
SEQS = 4
TOK_DEV = 512
TOKENS = 4096
SEQ_MOST = 256
N_ROW = 8


def draw_tokens(key, part):
    key_main, key_cols, key_rows = jax.random.split(key, 3)
    base = jax.random.normal(key_main, (TOKENS, D), jnp.float32)
    spread = jnp.exp(jax.random.uniform(key_cols, (1, D), jnp.float32, -1.15, 1.15))
    row_scale = jnp.exp(jax.random.uniform(key_rows, (TOKENS, 1), jnp.float32, -1.15, 1.15))
    return (base * spread * row_scale).astype(jnp.bfloat16)


def arrange_blocks(key, table, groups, per_group):
    places = jnp.arange(per_group, dtype=jnp.int32)
    scores = jax.random.randint(key, (groups, per_group), 0, 1 << 16) * per_group + places[None, :]
    order = jnp.argsort(scores, axis=1).astype(jnp.int32)
    ends = jnp.cumsum(table, axis=1)
    starts = ends - table
    other = jnp.sum((places[None, :, None] >= ends[:, None, :]).astype(jnp.int32), axis=2)
    ranking = places[None, :] - jnp.take_along_axis(starts, other, axis=1)
    return (order, other, ranking)


def draw_deal_order(key, part):
    groups = N_ROW
    per_group = TOK_DEV
    share = per_group // groups
    key_a, key_b, key_src, key_dst = jax.random.split(key, 4)
    shift_a = jax.random.randint(key_a, (), 1, groups)
    shift_b = jax.random.randint(key_b, (), 1, groups - 1)
    shift_b = jnp.where(shift_b >= shift_a, shift_b + 1, shift_b)
    source = jnp.arange(groups, dtype=jnp.int32)[:, None]
    target = jnp.arange(groups, dtype=jnp.int32)[None, :]
    offset_gap = (target - source) % groups
    counts = share * (1 + (offset_gap == shift_a).astype(jnp.int32) - (offset_gap == shift_b).astype(jnp.int32))
    src_order, src_target, src_rank = arrange_blocks(key_src, counts, groups, per_group)
    dst_order, dst_source, dst_rank = arrange_blocks(key_dst, counts.T, groups, per_group)
    group_ids = jnp.arange(groups, dtype=jnp.int32)[:, None]
    key_one = ((group_ids * groups + src_target) * per_group + src_rank).reshape(-1)
    initial = (group_ids * per_group + src_order).reshape(-1)
    key_two = ((dst_source * groups + group_ids) * per_group + dst_rank).reshape(-1)
    slot_ids = (group_ids * per_group + dst_order).reshape(-1)
    first_order = jnp.argsort(key_one)
    second_order = jnp.argsort(key_two)
    return jnp.zeros((groups * per_group,), jnp.int32).at[slot_ids[second_order]].set(initial[first_order])


def touch_ends(values, key, least, high):
    extent = values.shape
    spot = [jax.random.randint(jax.random.fold_in(key, axis), (), 0, extent[axis]) for axis in range(len(extent))]
    values = values.at[tuple(spot)].set(least)
    longest = extent.index(max(extent))
    spot[longest] = (spot[longest] + 1) % extent[longest]
    return values.at[tuple(spot)].set(high)


def block_scale(own_key, extent, pieces, smallest, high):
    factor_of, own = 1.0, jax.random.fold_in(own_key, 6)
    for position, shards_of in pieces:
        steps = jnp.exp(jax.random.uniform(jax.random.fold_in(own, position), (shards_of,), jnp.float32, smallest / len(pieces), high / len(pieces)))
        factor_of = factor_of * jnp.repeat(steps, extent[position] // shards_of).reshape([-1 if axis == position else 1 for axis in range(len(extent))])
    return factor_of


def length_profile(count, total, reach, slope):
    weights = [(1 << 20) // math.isqrt(standing ** slope) + 1 for standing in range(2, count + 1)]
    surplus, given = total - reach - (count - 1), [1] * (count - 1)
    while surplus > 0:
        free = [i for i in range(count - 1) if given[i] < reach]
        mass, left = sum([weights[i] for i in free]), surplus
        for i in free:
            addition = min(reach - given[i], max(1, left * weights[i] // mass), surplus)
            given[i] = given[i] + addition
            surplus = surplus - addition
    return np.array([reach] + given)


def ragged(own_key, amount, total, limit, lean):
    if amount == 2:
        one = jax.random.randint(own_key, (), max(1, total - limit), min(limit, total - 1) + 1)
        return jnp.stack([one, total - one])
    sizes = jnp.asarray(length_profile(amount, total, limit, lean), jnp.int32)
    twos = (amount - 1) // 2
    source_of, receiver = sizes[1:1 + 2 * twos:2], sizes[2:2 + 2 * twos:2]
    room = jnp.minimum(source_of - 1, limit - receiver)
    moved = jax.random.randint(jax.random.fold_in(own_key, 1), (twos,), 0, 1 << 20) % (room + 1)
    sizes = sizes.at[1:1 + 2 * twos:2].set(source_of - moved).at[2:2 + 2 * twos:2].set(receiver + moved)
    return sizes[jax.random.permutation(jax.random.fold_in(own_key, 2), amount)]


def noise(stream_key, extent, scale, bound, cuts=(), kind=jnp.bfloat16):
    level = block_scale(stream_key, extent, cuts, -0.22, 0.18) if cuts else 1.0
    array = jax.random.normal(stream_key, extent, jnp.float32) * scale * level
    return jnp.minimum(jnp.maximum(array, -bound), bound).astype(kind)


def setup_inputs(seed: int = 0) -> dict:
    keys = jax.random.split(jax.random.key(seed), 15)
    return {
        "tokens": draw_tokens(jax.random.fold_in(keys[14], 71), 0),
        "cotangent": noise(keys[1], (TOKENS, D), 1.0, 6.0, ((0, 8), (1, 4))),
        "deal_order": draw_deal_order(jax.random.fold_in(keys[14], 71), 0),
        "seq_lengths": jax.vmap(lambda own: ragged(own, SEQS, TOK_DEV, SEQ_MOST, 2))(jax.random.split(keys[3], N_ROW)).reshape((N_ROW, SEQS)).astype(jnp.int32),
        "value_picks": touch_ends(jax.random.randint(keys[4], (TOKENS, MH, PICKS), 0, NV), jax.random.fold_in(keys[4], 1), 0, NV - 1).astype(jnp.int32),
        "norm1_gain": jnp.clip(1.0 + 0.1 * jax.random.normal(keys[5], (D,), jnp.float32), 0.5, 1.5),
        "w_qkv": noise(keys[6], (D, 3 * D), D ** -0.5, 0.1875, ((0, 8), (1, 4)), jnp.float32),
        "w_attn_out": noise(keys[7], (D, D), (max(D // 256, 1)) ** -0.5, 3.0, ((0, 4), (1, 8)), jnp.float32),
        "norm2_gain": jnp.clip(1.0 + 0.1 * jax.random.normal(keys[8], (D,), jnp.float32), 0.5, 1.5),
        "w_query": noise(keys[9], (D, 2 * MH * QD), D ** -0.5, 0.1875, ((0, 8), (1, 4)), jnp.float32),
        "sub_keys": noise(keys[10], (2 * MH, NK, QD), (8 * QD) ** -0.5, 0.09375, ((0, 4), (1, 8)), jnp.float32),
        "value_table": noise(keys[11], (NV, D), 1.0, 6.0, ((0, 8), (1, 4)), jnp.float32),
        "w_gate": noise(keys[12], (D, D), D ** -0.5, 0.1875, ((0, 8), (1, 4)), jnp.float32),
        "w_mem_out": noise(keys[13], (D, D), (max(D // 16, 1)) ** -0.5, 0.75, ((0, 4), (1, 8)), jnp.float32),
    }


EPS = 1e-05
MASKED = -1e+30
HIGH = lax.Precision.HIGHEST

@jax.custom_vjp
def low(v):
    return lax.optimization_barrier(v.astype(jnp.bfloat16)).astype(jnp.float32)

@jax.custom_vjp
def low_back(v):
    return v

def low_keep(v):
    return (low(v), None)

def low_pass(kept, grad):
    return (grad,)

def back_keep(v):
    return (v, None)

def back_low(kept, grad):
    return (low(grad),)
low.defvjp(low_keep, low_pass)
low_back.defvjp(back_keep, back_low)

def block_size(count):
    if count <= 1024:
        return count
    return math.gcd(count, 512)

def product(left, right):
    return jnp.dot(left, right, precision=HIGH, preferred_element_type=jnp.float32)

def rms_norm(values, gain):
    factor = lax.rsqrt(lax.optimization_barrier(jnp.mean(values * values, axis=-1, keepdims=True)) + EPS)
    return low(values * factor * low(gain))

def sequence_ids(lengths_row):
    ends = jnp.cumsum(lengths_row)
    places = jnp.arange(TOK_DEV, dtype=jnp.int32)
    return lax.optimization_barrier(jnp.sum((places[:, None] >= ends[None, :]).astype(jnp.int32), axis=1))

def attend_group(inputs):
    qkv_group, seq_ids = inputs
    queries = qkv_group[:, :, 0, :]
    key_rows = qkv_group[:, :, 1, :]
    value_rows = qkv_group[:, :, 2, :]
    block_len = block_size(TOK_DEV)
    places = jnp.arange(TOK_DEV, dtype=jnp.int32)

    def one_block(start_row):
        query_blk = lax.dynamic_slice_in_dim(queries, start_row, block_len)
        query_seq = lax.dynamic_slice_in_dim(seq_ids, start_row, block_len)
        query_pos = start_row + jnp.arange(block_len, dtype=jnp.int32)
        scores = jnp.einsum('qhd,khd->hqk', query_blk, key_rows, precision=HIGH)
        scores = low_back(scores * HD ** (-0.5))
        allowed = (query_seq[:, None] == seq_ids[None, :]) & (query_pos[:, None] >= places[None, :])
        scores = jnp.where(allowed[None], scores, MASKED)
        probs = jax.nn.softmax(scores, axis=-1)
        return jnp.einsum('hqk,khd->qhd', low(probs), value_rows, precision=HIGH)
    starts = jnp.arange(TOK_DEV // block_len, dtype=jnp.int32) * block_len
    mixed = lax.map(jax.checkpoint(one_block), starts)
    return mixed.reshape(TOK_DEV, H * HD)

def layer(tokens32, gain_one, w_qkv, w_attn_out, gain_two, w_query, sub_keys, value_table, w_gate, w_mem_out, deal_order, inverse, seq_ids, value_picks):
    dealt = tokens32[deal_order]
    hidden_one = rms_norm(dealt, gain_one)
    qkv = low_back(low(product(hidden_one, low(w_qkv))))
    grouped = qkv.reshape(N_ROW, TOK_DEV, H, 3, HD)
    mixed = lax.map(attend_group, (grouped, seq_ids)).reshape(TOKENS, D)
    mixed = low_back(low(mixed))
    resid = dealt + low_back(product(mixed, low(w_attn_out)))
    hidden_two = rms_norm(resid, gain_two)
    queries = low_back(low(product(hidden_two, low(w_query)))).reshape(TOKENS, 2 * MH, QD)
    sub_scores = low_back(jnp.einsum('tnq,njq->tnj', queries, low(sub_keys), precision=HIGH))
    pairs = sub_scores.reshape(TOKENS, MH, 2, NK)
    score = jnp.take_along_axis(pairs[:, :, 0, :], value_picks // NK, axis=2) + jnp.take_along_axis(pairs[:, :, 1, :], value_picks % NK, axis=2)
    weights = low(jax.nn.softmax(score, axis=-1))
    table_low = low(value_table)
    block_len = math.gcd(TOK_DEV, 512)
    block_count = TOKENS // block_len

    def lookup(inputs):
        weight_blk, pick_blk = inputs
        return jnp.einsum('tp,tpd->td', weight_blk, table_low[pick_blk], precision=HIGH)
    memory = lax.map(jax.checkpoint(lookup), (weights.reshape(block_count, block_len, MH * PICKS), value_picks.reshape(block_count, block_len, MH * PICKS)))
    memory = low_back(memory.reshape(TOKENS, D))
    gate = low_back(product(hidden_two, low(w_gate)))
    mixed_two = low(memory * jax.nn.silu(gate))
    result = resid + low_back(product(mixed_two, low(w_mem_out)))
    return result[inverse]

def reference(tokens, cotangent, deal_order, seq_lengths, value_picks, norm1_gain, w_qkv, w_attn_out, norm2_gain, w_query, sub_keys, value_table, w_gate, w_mem_out):
    inverse = jnp.zeros((TOKENS,), jnp.int32).at[deal_order].set(jnp.arange(TOKENS, dtype=jnp.int32))
    seq_ids = jax.vmap(sequence_ids)(seq_lengths)

    def forward(tokens32, gain_one, qkv_w, attn_w, gain_two, query_w, keys_w, table_w, gate_w, memout_w):
        return layer(tokens32, gain_one, qkv_w, attn_w, gain_two, query_w, keys_w, table_w, gate_w, memout_w, deal_order, inverse, seq_ids, value_picks)
    output, pull = jax.vjp(forward, tokens.astype(jnp.float32), norm1_gain, w_qkv, w_attn_out, norm2_gain, w_query, sub_keys, value_table, w_gate, w_mem_out)
    grads = pull(cotangent.astype(jnp.float32))
    return (output, grads[0], grads[1], grads[2], grads[3], grads[4], grads[5], grads[6], grads[7], grads[8], grads[9])
```

```python
import functools

import jax
import jax.numpy as jnp
from jax import lax
from jax.experimental import pallas as pl
from jax.experimental.pallas import tpu as pltpu
from jax.sharding import PartitionSpec as P

D = 1024
HD = 64
MH = 4
QD = 512
NK = 256
PICKS = 32


EPS = 1e-05
MASKED = -1e30


def pack_rows(values, positions, slot_count):
    buffer = jnp.zeros((slot_count,) + values.shape[1:], values.dtype)
    return buffer.at[positions].set(values)


def norm_forward(values, gain):
    factor = lax.rsqrt(jnp.mean(values * values, axis=1, keepdims=True) + EPS)
    return (factor, (values * factor * gain.astype(jnp.float32)).astype(jnp.bfloat16))


def norm_backward(values, factor, gain, grad_hidden):
    scaled = grad_hidden * gain.astype(jnp.float32)
    inner = jnp.sum(scaled * values, axis=1, keepdims=True)
    grad_values = factor * scaled - values * (factor * factor * factor) * inner / D
    grad_gain = jnp.sum(grad_hidden * values * factor, axis=0)
    return (grad_values, grad_gain)


def allowed_mask(seq_ids, start_row, block_len):
    places = jnp.arange(seq_ids.shape[0], dtype=jnp.int32)
    query_pos = start_row + jnp.arange(block_len, dtype=jnp.int32)
    return (seq_ids[:, None] == seq_ids[None, :]) & (query_pos[:, None] >= places[None, :])


NT_DIMS = (((1,), (1,)), ((), ()))
LANES = 128


def memory_kernel(
    groups, tok_block, iters, hi_ref, lo_ref, w_ref, dm_ref, table_ref, mem_ref, dw_ref, gt_ref, dense, gacc
):
    f32, low = jnp.float32, jnp.bfloat16
    spans = groups * NK // LANES
    pitch = spans + 8
    per_tok = tok_block // iters
    per_span = spans // iters
    step = pl.program_id(0)

    @pl.when(step == 0)
    def _():
        gacc[...] = jnp.zeros_like(gacc)

    places_lo = lax.broadcasted_iota(jnp.int32, (LANES, LANES), 0).astype(f32).astype(low)
    places_hi = lax.broadcasted_iota(jnp.int32, (spans, LANES), 0).astype(f32).astype(low)
    ones = jnp.ones((LANES, LANES), low)
    zeros = jnp.zeros((LANES, LANES), low)
    blank = jnp.zeros((spans, LANES), low)
    grads = dm_ref[...]
    grads_t = grads.T
    mem_ref[...] = jnp.zeros_like(mem_ref)
    dw_ref[...] = jnp.zeros_like(dw_ref)
    lo_int = lo_ref[...].astype(jnp.int32)
    hi_all = hi_ref[...]

    def token_pair(first):
        rights, lefts = [], []
        for token in (first, first + 1):
            lo_row = jnp.broadcast_to(lo_ref[pl.ds(token, 1), :], (LANES, LANES)).astype(low)
            hi_row = jnp.broadcast_to(hi_ref[pl.ds(token, 1), :], (spans, LANES)).astype(low)
            w_row = jnp.broadcast_to(w_ref[pl.ds(token, 1), :], (spans, LANES)).astype(low)
            rights.append(jnp.where(lo_row == places_lo, ones, zeros))
            lefts.append(jnp.where(hi_row == places_hi, w_row, blank))
        right = jnp.concatenate(rights, axis=1)
        left = jnp.concatenate(
            [
                jnp.concatenate([lefts[0], blank], axis=1),
                jnp.concatenate([blank, lefts[1]], axis=1),
            ],
            axis=0,
        )
        both = lax.dot_general(left, right, NT_DIMS, preferred_element_type=f32)
        for j in range(2):
            dense[pl.ds(pl.multiple_of((first + j) * pitch, 8), spans), :] = both[
                j * spans : (j + 1) * spans
            ]

    def build(it, _):
        rows = pl.ds(pl.multiple_of(it * per_span * LANES, LANES), per_span * LANES)
        products = lax.dot_general(
            grads, table_ref[rows, :], NT_DIMS, preferred_element_type=f32
        )
        found = dw_ref[...]
        pairs = per_tok // 2 // per_span
        for j in range(per_span):
            picked = jnp.take_along_axis(
                products[:, LANES * j : LANES * (j + 1)], lo_int, axis=1
            )
            found = jnp.where(hi_all == (it * per_span + j).astype(f32), picked, found)
            for u in range(pairs):
                token_pair(it * per_tok + (j * pairs + u) * 2)
        dw_ref[...] = found
        return 0

    lax.fori_loop(0, iters, build, 0)

    def multiply(it, _):
        rows = pl.ds(pl.multiple_of(it * per_span * LANES, LANES), per_span * LANES)
        weights = jnp.concatenate(
            [
                dense[pl.ds(it * per_span + j, tok_block, stride=pitch), :].astype(low)
                for j in range(per_span)
            ],
            axis=1,
        )
        mem_ref[...] += jnp.dot(weights, table_ref[rows, :], preferred_element_type=f32)
        gacc[:, rows] += jnp.dot(grads_t, weights, preferred_element_type=f32)
        return 0

    lax.fori_loop(0, iters, multiply, 0)

    @pl.when(step == pl.num_programs(0) - 1)
    def _():
        def turn(i, _):
            rows = pl.ds(pl.multiple_of(i * NK, NK), NK)
            gt_ref[rows, :] = gacc[:, rows].T
            return 0

        lax.fori_loop(0, groups, turn, 0)


def memory_call(hi, lo, weights, grads, table):
    tokens, picks = hi.shape
    rows, width = table.shape
    groups = rows // NK
    tok_block = 512
    spec = lambda n: pl.BlockSpec((tok_block, n), lambda i: (i, 0))
    return pl.pallas_call(
        functools.partial(memory_kernel, groups, tok_block, 4),
        grid=(tokens // tok_block,),
        in_specs=[
            spec(picks),
            spec(picks),
            spec(picks),
            spec(width),
            pl.BlockSpec((rows, width), lambda i: (0, 0)),
        ],
        out_specs=[
            spec(width),
            spec(picks),
            pl.BlockSpec((rows, width), lambda i: (0, 0), pipeline_mode=pl.Buffered(1)),
        ],
        out_shape=[
            jax.ShapeDtypeStruct((tokens, width), jnp.float32),
            jax.ShapeDtypeStruct((tokens, picks), jnp.float32),
            jax.ShapeDtypeStruct((rows, width), jnp.float32),
        ],
        scratch_shapes=[
            pltpu.VMEM((tok_block * (rows // LANES + 8), LANES), jnp.float32),
            pltpu.VMEM((width, rows), jnp.float32),
        ],
        compiler_params=pltpu.CompilerParams(vmem_limit_bytes=62 * 2**20),
    )(hi, lo, weights, grads, table)


def attention_forward(queries, key_rows, value_rows, seq_ids, score_scale):
    tok_rows = queries.shape[0]

    def one_block(start_row):
        scores = (
            jnp.einsum("qhd,khd->hqk", queries, key_rows, preferred_element_type=jnp.float32)
            * score_scale
        )
        scores = jnp.where(allowed_mask(seq_ids, start_row, tok_rows)[None], scores, MASKED)
        row_max = jnp.max(scores, axis=2, keepdims=True)
        shifted_exp = jnp.exp(scores - row_max)
        row_total = jnp.sum(shifted_exp, axis=2, keepdims=True)
        weights_low = (shifted_exp / row_total).astype(jnp.bfloat16)
        weighted = jnp.einsum(
            "hqk,khd->qhd", weights_low, value_rows, preferred_element_type=jnp.float32
        )
        return (weighted.astype(jnp.bfloat16), (row_max + jnp.log(row_total))[:, :, 0])

    starts = jnp.arange(tok_rows // tok_rows, dtype=jnp.int32) * tok_rows
    weighted, log_total = lax.map(one_block, starts)
    return (weighted.reshape(tok_rows, queries.shape[1] * queries.shape[2]), log_total)


def attention_backward(queries, key_rows, value_rows, grad_out, log_total, seq_ids, score_scale):
    tok_rows = queries.shape[0]

    def one_block(carry, inputs):
        key_grad, value_grad = carry
        start_row, log_blk = inputs
        scores = (
            jnp.einsum("qhd,khd->hqk", queries, key_rows, preferred_element_type=jnp.float32)
            * score_scale
        )
        scores = jnp.where(allowed_mask(seq_ids, start_row, tok_rows)[None], scores, MASKED)
        probs = jnp.exp(scores - log_blk[:, :, None])
        grad_prob = jnp.einsum(
            "qhd,khd->hqk", grad_out, value_rows, preferred_element_type=jnp.float32
        )
        inner = jnp.sum(probs * grad_prob, axis=2, keepdims=True)
        grad_score = (probs * (grad_prob - inner)).astype(jnp.bfloat16)
        query_grad = (
            jnp.einsum("hqk,khd->qhd", grad_score, key_rows, preferred_element_type=jnp.float32)
            * score_scale
        )
        key_grad = (
            key_grad
            + jnp.einsum("hqk,qhd->khd", grad_score, queries, preferred_element_type=jnp.float32)
            * score_scale
        )
        value_grad = value_grad + jnp.einsum(
            "hqk,qhd->khd", probs.astype(jnp.bfloat16), grad_out, preferred_element_type=jnp.float32
        )
        return ((key_grad, value_grad), query_grad)

    starts = jnp.arange(tok_rows // tok_rows, dtype=jnp.int32) * tok_rows
    zeros_like = jnp.zeros(queries.shape, jnp.float32)
    (key_grad, value_grad), query_grad = lax.scan(
        one_block, (zeros_like, zeros_like), (starts, log_total)
    )
    return (query_grad.reshape(queries.shape), key_grad, value_grad)


def per_device(
    tokens,
    cotangent,
    deal_order,
    seq_lengths,
    value_picks,
    norm1_gain,
    w_qkv,
    w_attn_out,
    norm2_gain,
    w_query,
    sub_keys,
    value_table,
    w_gate,
    w_mem_out,
):
    row_count = lax.axis_size("row")
    row_index = lax.axis_index("row")
    col_index = lax.axis_index("col")
    tok_rows = tokens.shape[0]
    col_width = tokens.shape[1]
    capacity = 2 * tok_rows // row_count
    slot_count = row_count * capacity
    all_rows = deal_order.shape[0]
    my_first = row_index * tok_rows
    my_slots = lax.dynamic_slice_in_dim(deal_order, my_first, tok_rows)
    source_dev = my_slots // tok_rows
    device_ids = jnp.arange(row_count, dtype=jnp.int32)
    from_source = (source_dev[:, None] == device_ids[None, :]).astype(jnp.int32)
    earlier = jnp.cumsum(from_source, axis=0) - from_source
    recv_pos = source_dev * capacity + jnp.sum(earlier * from_source, axis=1)
    owned = (deal_order // tok_rows == row_index).astype(jnp.int32).reshape(row_count, tok_rows)
    rank_all = (jnp.cumsum(owned, axis=1) - owned).reshape(all_rows)
    inverse = (
        jnp.zeros((all_rows,), jnp.int32).at[deal_order].set(jnp.arange(all_rows, dtype=jnp.int32))
    )
    dest_slot = lax.dynamic_slice_in_dim(inverse, my_first, tok_rows)
    send_pos = dest_slot // tok_rows * capacity + rank_all[dest_slot]
    got_tokens, got_cot = (
        lax.all_to_all(
            pack_rows(tokens, send_pos, slot_count), "row", split_axis=0, concat_axis=0, tiled=True
        ),
        lax.all_to_all(
            pack_rows(cotangent, send_pos, slot_count),
            "row",
            split_axis=0,
            concat_axis=0,
            tiled=True,
        ),
    )
    full_tokens, full_cot, gain_one, gain_two = (
        lax.all_gather(got_tokens[recv_pos], "col", axis=1, tiled=True),
        lax.all_gather(got_cot[recv_pos], "col", axis=1, tiled=True),
        lax.all_gather(norm1_gain.astype(jnp.bfloat16), "col", axis=0, tiled=True),
        lax.all_gather(norm2_gain.astype(jnp.bfloat16), "col", axis=0, tiled=True),
    )
    qkv_weight, query_weight, gate_weight, attn_weight, memout_weight, key_table = (
        lax.all_gather(w_qkv.astype(jnp.bfloat16), "row", axis=0, tiled=True),
        lax.all_gather(w_query.astype(jnp.bfloat16), "row", axis=0, tiled=True),
        lax.all_gather(w_gate.astype(jnp.bfloat16), "row", axis=0, tiled=True),
        lax.all_gather(w_attn_out.astype(jnp.bfloat16), "row", axis=1, tiled=True),
        lax.all_gather(w_mem_out.astype(jnp.bfloat16), "row", axis=1, tiled=True),
        lax.all_gather(sub_keys.astype(jnp.bfloat16), "row", axis=1, tiled=True),
    )
    own_rows = value_table.shape[0]
    picks_all = lax.all_gather(value_picks.reshape(tok_rows, MH * PICKS), "row", axis=0, tiled=True)
    picks_hi = (picks_all // LANES - row_index * (own_rows // LANES)).astype(jnp.float32)
    picks_lo = (picks_all % LANES).astype(jnp.float32)
    heads_here = col_width // HD
    halves_here = query_weight.shape[1] // QD
    score_scale = HD ** (-0.5)
    seq_ids = jnp.sum(
        (
            jnp.arange(tok_rows, dtype=jnp.int32)[:, None] >= jnp.cumsum(seq_lengths[0])[None, :]
        ).astype(jnp.int32),
        axis=1,
    )
    starts = jnp.arange(tok_rows // tok_rows, dtype=jnp.int32) * tok_rows
    dealt_x = full_tokens.astype(jnp.float32)
    factor_one, hidden_one = norm_forward(dealt_x, gain_one)
    qkv = (
        jnp.dot(hidden_one, qkv_weight, preferred_element_type=jnp.float32)
        .astype(jnp.bfloat16)
        .reshape(tok_rows, heads_here, 3, HD)
    )
    queries = qkv[:, :, 0, :]
    key_rows = qkv[:, :, 1, :]
    value_rows = qkv[:, :, 2, :]
    mixed, log_total = attention_forward(queries, key_rows, value_rows, seq_ids, score_scale)
    attn_part = jnp.dot(mixed, attn_weight, preferred_element_type=jnp.float32)
    resid = dealt_x + lax.psum(attn_part, "col")
    factor_two, hidden_two = norm_forward(resid, gain_two)
    mem_queries = (
        jnp.dot(hidden_two, query_weight, preferred_element_type=jnp.float32)
        .astype(jnp.bfloat16)
        .reshape(tok_rows, halves_here, QD)
    )
    sub_scores = jnp.einsum(
        "tnq,njq->tnj", mem_queries, key_table, preferred_element_type=jnp.float32
    )
    half_ids = col_index * halves_here + jnp.arange(halves_here, dtype=jnp.int32)
    head_ids = half_ids // 2
    my_picks = jnp.take(value_picks, head_ids, axis=1)
    sub_index = jnp.where((half_ids % 2 == 0)[None, :, None], my_picks // NK, my_picks % NK)
    key_ids = jnp.arange(NK, dtype=jnp.int32)

    def pick_partial(start_row):
        match = sub_index[..., None] == key_ids
        return jnp.sum(jnp.where(match, sub_scores[:, :, None, :], 0.0), axis=3)

    partial_value = lax.map(pick_partial, starts).reshape(tok_rows, halves_here * PICKS)
    gathered = lax.all_gather(partial_value, "col", axis=1, tiled=True)
    score = jnp.sum(gathered.reshape(tok_rows, MH, 2, PICKS), axis=2)
    pick_weights = jax.nn.softmax(score, axis=-1).reshape(tok_rows, MH * PICKS)
    pick_weights_low = pick_weights.astype(jnp.bfloat16)
    gate = jnp.dot(hidden_two, gate_weight, preferred_element_type=jnp.float32)
    sigmoid_gate = jax.nn.sigmoid(gate)
    grad_mixed_two = jnp.einsum(
        "tD,cD->tc", full_cot, memout_weight, preferred_element_type=jnp.float32
    )
    grad_memory = (grad_mixed_two * gate * sigmoid_gate).astype(jnp.bfloat16)
    sent = lax.all_gather(
        jnp.concatenate([pick_weights_low, grad_memory], axis=1), "row", axis=0, tiled=True
    )
    mem_part, dw_part, grad_table = memory_call(
        picks_hi,
        picks_lo,
        sent[:, : MH * PICKS].astype(jnp.float32),
        sent[:, MH * PICKS :],
        value_table.astype(jnp.bfloat16),
    )
    memory = lax.psum_scatter(mem_part, "row", scatter_dimension=0, tiled=True)
    grad_weight_pick = lax.psum(
        lax.psum_scatter(dw_part, "row", scatter_dimension=0, tiled=True), "col"
    )
    mixed_two = (memory * gate * sigmoid_gate).astype(jnp.bfloat16)
    memout_part = jnp.dot(mixed_two, memout_weight, preferred_element_type=jnp.float32)
    memory_out = lax.psum_scatter(
        memout_part.astype(jnp.bfloat16), "col", scatter_dimension=1, tiled=True
    ).astype(jnp.float32)
    result_block = lax.dynamic_slice_in_dim(resid, col_index * col_width, col_width, 1) + memory_out
    grad_memout_w = jnp.einsum("tc,tD->cD", mixed_two, full_cot, preferred_element_type=jnp.float32)
    grad_gate = (
        grad_mixed_two * memory * sigmoid_gate * (1.0 + gate * (1.0 - sigmoid_gate))
    ).astype(jnp.bfloat16)
    grad_gate_w = jnp.einsum("tD,tc->Dc", hidden_two, grad_gate, preferred_element_type=jnp.float32)
    weights_grouped = pick_weights.reshape(tok_rows, MH, PICKS)
    pick_grad_grouped = grad_weight_pick.reshape(tok_rows, MH, PICKS)
    grad_score = weights_grouped * (
        pick_grad_grouped - jnp.sum(weights_grouped * pick_grad_grouped, axis=2, keepdims=True)
    )
    grad_score_mine = jnp.take(grad_score, head_ids, axis=1)

    def sub_grad(start_row):
        match = sub_index[..., None] == key_ids
        return jnp.sum(jnp.where(match, grad_score_mine[..., None], 0.0), axis=2)

    grad_sub = lax.map(sub_grad, starts).reshape(tok_rows, halves_here, NK).astype(jnp.bfloat16)
    grad_queries = (
        jnp.einsum("tnj,njq->tnq", grad_sub, key_table, preferred_element_type=jnp.float32)
        .astype(jnp.bfloat16)
        .reshape(tok_rows, halves_here * QD)
    )
    grad_keys = jnp.einsum(
        "tnj,tnq->njq", grad_sub, mem_queries, preferred_element_type=jnp.float32
    )
    grad_query_w = jnp.einsum(
        "tD,tm->Dm", hidden_two, grad_queries, preferred_element_type=jnp.float32
    )
    hidden_two_part = jnp.einsum(
        "tm,Dm->tD", grad_queries, query_weight, preferred_element_type=jnp.float32
    ) + jnp.einsum("tc,Dc->tD", grad_gate, gate_weight, preferred_element_type=jnp.float32)
    grad_hidden_two = lax.psum(hidden_two_part, "col")
    grad_resid, grad_gain_two = norm_backward(resid, factor_two, gain_two, grad_hidden_two)
    grad_resid = grad_resid + full_cot.astype(jnp.float32)
    grad_attn_low = grad_resid.astype(jnp.bfloat16)
    grad_mixed = (
        jnp.einsum("tD,cD->tc", grad_attn_low, attn_weight, preferred_element_type=jnp.float32)
        .astype(jnp.bfloat16)
        .reshape(tok_rows, heads_here, HD)
    )
    grad_attn_w = jnp.einsum("tc,tD->cD", mixed, grad_attn_low, preferred_element_type=jnp.float32)
    query_grad, key_grad, value_grad = attention_backward(
        queries, key_rows, value_rows, grad_mixed, log_total, seq_ids, score_scale
    )
    grad_qkv = (
        jnp.stack((query_grad, key_grad, value_grad), axis=2)
        .astype(jnp.bfloat16)
        .reshape(tok_rows, heads_here * 3 * HD)
    )
    grad_qkv_w = jnp.einsum("tD,tm->Dm", hidden_one, grad_qkv, preferred_element_type=jnp.float32)
    hidden_one_part = jnp.einsum(
        "tm,Dm->tD", grad_qkv, qkv_weight, preferred_element_type=jnp.float32
    )
    grad_hidden_one = lax.psum(hidden_one_part, "col")
    grad_dealt, grad_gain_one = norm_backward(dealt_x, factor_one, gain_one, grad_hidden_one)
    grad_dealt = grad_dealt + grad_resid
    grad_block = lax.dynamic_slice_in_dim(grad_dealt, col_index * col_width, col_width, 1)
    gain_one_block = lax.dynamic_slice_in_dim(grad_gain_one, col_index * col_width, col_width)
    gain_two_block = lax.dynamic_slice_in_dim(grad_gain_two, col_index * col_width, col_width)
    grads = (
        lax.psum_scatter(grad_qkv_w, "row", scatter_dimension=0, tiled=True),
        lax.psum_scatter(grad_query_w, "row", scatter_dimension=0, tiled=True),
        lax.psum_scatter(grad_gate_w, "row", scatter_dimension=0, tiled=True),
        lax.psum_scatter(grad_attn_w, "row", scatter_dimension=1, tiled=True),
        lax.psum_scatter(grad_memout_w, "row", scatter_dimension=1, tiled=True),
        lax.psum_scatter(grad_keys, "row", scatter_dimension=1, tiled=True),
        lax.psum_scatter(gain_one_block, "row", scatter_dimension=0, tiled=True),
        lax.psum_scatter(gain_two_block, "row", scatter_dimension=0, tiled=True),
    )
    got_result, got_grad = (
        lax.all_to_all(
            pack_rows(result_block, recv_pos, slot_count),
            "row",
            split_axis=0,
            concat_axis=0,
            tiled=True,
        ),
        lax.all_to_all(
            pack_rows(grad_block, recv_pos, slot_count),
            "row",
            split_axis=0,
            concat_axis=0,
            tiled=True,
        ),
    )
    return (
        got_result[send_pos],
        got_grad[send_pos],
        grads[6],
        grads[0],
        grads[3],
        grads[7],
        grads[1],
        grads[5],
        grad_table,
        grads[2],
        grads[4],
    )


def solution(mesh):
    return jax.shard_map(
        per_device,
        mesh=mesh,
        in_specs=(
            P("row", "col"),
            P("row", "col"),
            P(),
            P("row", None),
            P("row", None, None),
            P("col"),
            P("row", "col"),
            P("col", "row"),
            P("col"),
            P("row", "col"),
            P("col", "row", None),
            P("row", "col"),
            P("row", "col"),
            P("col", "row"),
        ),
        out_specs=(
            P("row", "col"),
            P("row", "col"),
            P(("col", "row")),
            P("row", "col"),
            P("col", "row"),
            P(("col", "row")),
            P("row", "col"),
            P("col", "row", None),
            P("row", "col"),
            P("row", "col"),
            P("col", "row"),
        ),
        check_vma=False,
    )
```

```python
import functools

import jax
import jax.numpy as jnp
from jax import lax
from jax.experimental import pallas as pl
from jax.experimental.pallas import tpu as pltpu
from jax.sharding import PartitionSpec as P

D = 1024
HD = 64
MH = 4
QD = 512
NK = 256
PICKS = 32
LANES = 128
EPS = 1e-05
MASKED = -1e30
F32 = jnp.float32
LOW = jnp.bfloat16
MESH = pl.DeviceIdType.MESH
NT_DIMS = (((1,), (1,)), ((), ()))
VMEM_SPEC = pl.BlockSpec(memory_space=pltpu.VMEM)
VMEM_BYTES = 60 * 2**20


def flip(index, mask):
    bit = 1
    while bit <= mask:
        if mask & bit:
            index = index + bit - 2 * bit * (index // bit % 2)
        bit *= 2
    return index


class Net:
    def __init__(self, rows, cols, sends, recvs):
        self.rows, self.cols = rows, cols
        self.row, self.col = lax.axis_index("row"), lax.axis_index("col")
        self.sends, self.recvs, self.used = sends, recvs, 0
        self.pending = []

    def place(self, row_k, col_k):
        return (flip(self.row, row_k), flip(self.col, col_k))

    def meet(self, row_ks, col_ks):
        barrier = pltpu.get_barrier_semaphore()
        places = [self.place(k, 0) for k in row_ks] + [self.place(0, k) for k in col_ks]
        for place in places:
            pl.semaphore_signal(barrier, inc=1, device_id=place, device_id_type=MESH)
        pl.semaphore_wait(barrier, len(places))

    def send(self, src, dst, row_k=0, col_k=0):
        assert self.used < self.sends.shape[0]
        copy = pltpu.make_async_remote_copy(
            src_ref=src,
            dst_ref=dst,
            send_sem=self.sends.at[self.used],
            recv_sem=self.recvs.at[self.used],
            device_id=self.place(row_k, col_k),
            device_id_type=MESH,
        )
        copy.start()
        self.used += 1
        self.pending.append(copy)
        return copy

    def drain(self):
        for copy in self.pending:
            copy.wait_send()

    def gather_start(self, src, view, first=True):
        copies = [self.send(src, view(self.row), row_k=2 * j) for j in range(1, self.rows // 2)]
        return copies, self.send(src, view(self.row), row_k=1)

    def gather_pass(self, view, started):
        copies, sibling = started
        passed = []
        for j, copy in enumerate(copies):
            copy.wait_recv()
            there = flip(self.row, 2 * (j + 1))
            passed.append(self.send(view(there), view(there), row_k=1))
        return [sibling] + passed

    def scatter_start(self, view, across):
        twin = flip(self.row, 1)
        return [
            self.send(view(flip(twin, 2 * j)), across.at[j], row_k=1)
            for j in range(self.rows // 2)
        ]

    def scatter_pass(self, view, across, started, outgoing, incoming):
        moved = []
        for j in range(1, self.rows // 2):
            started[j].wait_recv()
            block = view(flip(self.row, 2 * j))[...] + across[j]
            outgoing[j - 1] = block.astype(outgoing.dtype)
            moved.append(self.send(outgoing.at[j - 1], incoming.at[j - 1], row_k=2 * j))
        return moved

    def scatter_end(self, view, across, started, incoming, moved):
        started[0].wait_recv()
        total = view(self.row)[...] + across[0]
        for j, copy in enumerate(moved):
            copy.wait_recv()
            total = total + incoming[j].astype(F32)
        return total

    def columns_start(self, view):
        return [self.send(view(self.col), view(self.col), col_k=k) for k in range(1, self.cols)]


def wait_all(copies):
    for copy in copies:
        copy.wait_recv()


def rows_of(ref, count):
    return lambda index: ref.at[pl.ds(pl.multiple_of(index * count, count), count), :]


def columns_of(ref, count):
    return lambda index: ref.at[:, pl.ds(pl.multiple_of(index * count, count), count)]


def one_hot_rows(positions, slots):
    places = lax.broadcasted_iota(jnp.int32, (positions.shape[0], slots), 1)
    return jnp.where(positions == places, 1.0, 0.0).astype(LOW)


def one_hot_columns(positions, slots):
    places = lax.broadcasted_iota(jnp.int32, (slots, positions.shape[1]), 0)
    return jnp.where(positions == places, 1.0, 0.0).astype(LOW)


def pack_for_rows(net, packed, values, positions):
    slots = packed.shape[0]
    packed[...] = jnp.dot(
        one_hot_columns(positions, slots), values, preferred_element_type=F32
    ).astype(LOW)


def exchange_start(net, packed, got, capacity):
    mine = rows_of(got, capacity)
    theirs = rows_of(packed, capacity)
    copies = [
        net.send(theirs(flip(net.row, k)), mine(net.row), row_k=k) for k in range(1, net.rows)
    ]
    mine(net.row)[...] = theirs(net.row)[...]
    return copies


def unpack(got, positions):
    return jnp.dot(
        one_hot_rows(positions, got.shape[0]), got[...], preferred_element_type=F32
    )


def share_sums(net, sums, mine, theirs):
    tokens = sums.shape[0]
    mine[...] = jnp.broadcast_to(sums, (tokens, LANES)).T[:8]
    copies = [net.send(mine, theirs.at[k], col_k=k) for k in range(1, net.cols)]
    wait_all(copies)
    total = mine[...]
    for k in range(1, net.cols):
        total = total + theirs[k]
    return jnp.broadcast_to(total[:1], (LANES, tokens)).T


def widen(lanes, width):
    return jnp.concatenate([lanes] * (width // LANES), axis=1)


def reduce_start(net, part, outgoing, incoming):
    width = part.shape[1] // net.cols
    view = columns_of(part, width)
    copies = []
    for k in range(1, net.cols):
        outgoing[k - 1] = view(flip(net.col, k))[...].astype(LOW)
        copies.append(net.send(outgoing.at[k - 1], incoming.at[k - 1], col_k=k))
    return copies


def reduce_end(net, part, incoming, copies):
    total = columns_of(part, part.shape[1] // net.cols)(net.col)[...].astype(F32)
    for k, copy in enumerate(copies):
        copy.wait_recv()
        total = total + incoming[k].astype(F32)
    return total


def deal_kernel(
    rows, cols, tokens_ref, send_row, recv_col, shard, full, weights, packed, got, sends, recvs
):
    net = Net(rows, cols, sends, recvs)
    capacity = packed.shape[0] // rows
    pack_for_rows(net, packed, tokens_ref[...], send_row[...])
    net.meet(range(1, rows), range(1, cols))
    copies = exchange_start(net, packed, got, capacity)
    count = shard.shape[0]
    place = rows_of(weights, count)
    gather = net.gather_start(shard, place)
    place(net.row)[...] = shard[...]
    wait_all(copies)
    mine = columns_of(full, tokens_ref.shape[1])
    mine(net.col)[...] = unpack(got, recv_col[...]).astype(LOW)
    spread = net.columns_start(mine)
    wait_all(net.gather_pass(place, gather))
    wait_all(spread)
    net.drain()


def norm_kernel(
    rows,
    cols,
    part,
    dealt,
    gain,
    cot,
    send_row,
    recv_col,
    shard,
    keys,
    picks,
    hidden,
    resid,
    factor,
    full,
    weights,
    key_table,
    all_picks,
    packed,
    got,
    outgoing,
    incoming,
    mine,
    theirs,
    sends,
    recvs,
):
    net = Net(rows, cols, sends, recvs)
    capacity = packed.shape[0] // rows
    width = dealt.shape[1]
    net.meet(range(1, rows), range(1, cols))
    reduce = reduce_start(net, part, outgoing, incoming)
    pack_for_rows(net, packed, cot[...], send_row[...])
    copies = exchange_start(net, packed, got, capacity)
    place = rows_of(weights, shard.shape[0])
    gather = net.gather_start(shard, place)
    span = keys.shape[1]
    key_place = lambda index: key_table.at[:, pl.ds(pl.multiple_of(index * span, span), span), :]
    key_gather = net.gather_start(keys, key_place)
    pick_place = rows_of(all_picks, picks.shape[0])
    pick_gather = net.gather_start(picks, pick_place)
    place(net.row)[...] = shard[...]
    key_place(net.row)[...] = keys[...]
    pick_place(net.row)[...] = picks[...]
    values = dealt[...] + reduce_end(net, part, incoming, reduce)
    resid[...] = values
    square = share_sums(net, jnp.sum(values * values, axis=1, keepdims=True), mine, theirs)
    scale = lax.rsqrt(square / D + EPS)
    factor[...] = scale
    own = columns_of(hidden, width)
    own(net.col)[...] = (resid[...] * widen(scale, width) * gain[...]).astype(LOW)
    spread = net.columns_start(own)
    wait_all(copies)
    own_cot = columns_of(full, width)
    own_cot(net.col)[...] = unpack(got, recv_col[...]).astype(LOW)
    cot_spread = net.columns_start(own_cot)
    left = net.gather_pass(place, gather)
    left += net.gather_pass(key_place, key_gather)
    left += net.gather_pass(pick_place, pick_gather)
    wait_all(spread)
    wait_all(cot_spread)
    wait_all(left)
    net.drain()


def score_kernel(
    rows, cols, part, grads, weights, all_low, all_grads, scores, sends, recvs
):
    net = Net(rows, cols, sends, recvs)
    net.meet([1] + [2 * j for j in range(1, rows // 2)], range(1, cols))
    place = rows_of(scores, part.shape[0])
    copies = [net.send(part, place(net.col), col_k=k) for k in range(1, cols)]
    grad_place = rows_of(all_grads, grads.shape[0])
    grad_gather = net.gather_start(grads, grad_place)
    place(net.col)[...] = part[...]
    grad_place(net.row)[...] = grads[...]
    wait_all(copies)
    low_place = lambda index: all_low.at[index]
    for m in range(MH):
        score = (
            scores[2 * m * PICKS : (2 * m + 1) * PICKS]
            + scores[(2 * m + 1) * PICKS : (2 * m + 2) * PICKS]
        )
        shifted = jnp.exp(score - jnp.max(score, axis=0, keepdims=True))
        share = shifted / jnp.sum(shifted, axis=0, keepdims=True)
        weights[m * PICKS : (m + 1) * PICKS] = share
    low_place(net.row)[...] = weights[...].astype(LOW)
    low_gather = net.gather_start(low_place(net.row), low_place)
    left = net.gather_pass(grad_place, grad_gather)
    left += net.gather_pass(low_place, low_gather)
    wait_all(left)
    net.drain()


def memory_sum_kernel(
    rows,
    cols,
    mem_part,
    dw_part,
    memory,
    dw,
    mem_across,
    mem_out,
    mem_in,
    dw_across,
    dw_sum,
    dw_cols,
    dw_out,
    dw_in,
    sends,
    recvs,
):
    net = Net(rows, cols, sends, recvs)
    tokens = memory.shape[0]
    half = rows // 2
    net.meet([1] + [2 * j for j in range(1, half)], range(1, cols))
    dw_view = lambda index: dw_part.at[index]
    dw_started = net.scatter_start(dw_view, dw_across)
    mem_view = rows_of(mem_part, tokens)
    mem_started = net.scatter_start(mem_view, mem_across)
    for j in range(half):
        dw_started[j].wait_recv()
        dw_sum[j] = dw_view(flip(net.row, 2 * j))[...] + dw_across[j]
    head = lambda col: pl.ds(pl.multiple_of(col * MH // cols * PICKS, PICKS), PICKS)
    moved = [
        net.send(dw_sum.at[:, head(flip(net.col, k)), :], dw_cols.at[k - 1], col_k=k)
        for k in range(1, cols)
    ]
    mem_moved = net.scatter_pass(mem_view, mem_across, mem_started, mem_out, mem_in)
    wait_all(moved)
    for j in range(half):
        total = dw_sum[j, head(net.col), :]
        for k in range(1, cols):
            total = total + dw_cols[k - 1, j]
        dw_out[j] = total
    last = [
        net.send(dw_out.at[j], dw_in.at[j - 1], row_k=2 * j) for j in range(1, half)
    ]
    memory[...] = net.scatter_end(mem_view, mem_across, mem_started, mem_in, mem_moved)
    total = dw_out[0]
    for j, copy in enumerate(last):
        copy.wait_recv()
        total = total + dw_in[j]
    dw[...] = total
    net.drain()


def norm_grad(net, grad_hidden, values, scale, gain, extra, mine, theirs):
    width = values.shape[1]
    scaled = grad_hidden * gain
    inner = share_sums(net, jnp.sum(scaled * values, axis=1, keepdims=True), mine, theirs)
    wide = widen(scale, width)
    grads = wide * scaled - values * (wide * wide * wide) * widen(inner, width) / D
    grad_gain = jnp.sum(grad_hidden * values * wide, axis=0, keepdims=True)
    return grads + extra, grad_gain


def back_two_kernel(
    rows,
    cols,
    part,
    result_part,
    resid,
    factor,
    gain,
    cot,
    recv_row,
    send_col,
    weight_grad,
    key_grad,
    grad_low,
    grad_resid,
    result,
    own_weight,
    own_keys,
    gain_grad,
    outgoing,
    incoming,
    res_outgoing,
    res_incoming,
    mine,
    theirs,
    packed,
    got,
    across,
    w_out,
    w_in,
    k_across,
    k_out,
    k_in,
    sends,
    recvs,
):
    net = Net(rows, cols, sends, recvs)
    capacity = packed.shape[0] // rows
    width = resid.shape[1]
    net.meet(range(1, rows), range(1, cols))
    reduce = reduce_start(net, part, outgoing, incoming)
    res_reduce = reduce_start(net, result_part, res_outgoing, res_incoming)
    view = rows_of(weight_grad, own_weight.shape[0])
    span = own_keys.shape[1]
    key_view = lambda index: key_grad.at[:, pl.ds(pl.multiple_of(index * span, span), span), :]
    started = net.scatter_start(view, across)
    key_started = net.scatter_start(key_view, k_across)
    grad_hidden = reduce_end(net, part, incoming, reduce)
    grads, gain_sum = norm_grad(
        net, grad_hidden, resid[...], factor[...], gain[...], cot[...].astype(F32), mine, theirs
    )
    grad_resid[...] = grads
    gain_grad[...] = jnp.broadcast_to(gain_sum, gain_grad.shape)
    own = columns_of(grad_low, width)
    own(net.col)[...] = grads.astype(LOW)
    spread = net.columns_start(own)
    block = resid[...] + reduce_end(net, result_part, res_incoming, res_reduce)
    pack_for_rows(net, packed, block.astype(LOW), recv_row[...])
    copies = exchange_start(net, packed, got, capacity)
    moved = net.scatter_pass(view, across, started, w_out, w_in)
    key_moved = net.scatter_pass(key_view, k_across, key_started, k_out, k_in)
    wait_all(copies)
    result[...] = unpack(got, send_col[...])
    own_weight[...] = net.scatter_end(view, across, started, w_in, moved)
    own_keys[...] = net.scatter_end(key_view, k_across, key_started, k_in, key_moved)
    wait_all(spread)
    net.drain()


def back_one_kernel(
    rows,
    cols,
    part,
    dealt,
    factor,
    gain,
    extra,
    recv_row,
    send_col,
    weight_grad,
    gain_two,
    result,
    own_weight,
    gains,
    outgoing,
    incoming,
    mine,
    theirs,
    packed,
    got,
    across,
    w_out,
    w_in,
    my_gains,
    their_gains,
    sends,
    recvs,
):
    net = Net(rows, cols, sends, recvs)
    capacity = packed.shape[0] // rows
    net.meet(range(1, rows), range(1, cols))
    reduce = reduce_start(net, part, outgoing, incoming)
    view = rows_of(weight_grad, own_weight.shape[0])
    started = net.scatter_start(view, across)
    grad_hidden = reduce_end(net, part, incoming, reduce)
    grads, gain_sum = norm_grad(
        net, grad_hidden, dealt[...], factor[...], gain[...], extra[...], mine, theirs
    )
    pack_for_rows(net, packed, grads.astype(LOW), recv_row[...])
    copies = exchange_start(net, packed, got, capacity)
    places = lax.broadcasted_iota(jnp.int32, my_gains.shape, 0)
    my_gains[...] = jnp.where(places == 0, gain_sum, gain_two[...])
    gain_copies = [
        net.send(my_gains, their_gains.at[k], row_k=k) for k in range(1, rows)
    ]
    moved = net.scatter_pass(view, across, started, w_out, w_in)
    wait_all(copies)
    result[...] = unpack(got, send_col[...])
    total = my_gains[...]
    for k, copy in enumerate(gain_copies):
        copy.wait_recv()
        total = total + their_gains[k + 1]
    gains[...] = total
    own_weight[...] = net.scatter_end(view, across, started, w_in, moved)
    net.drain()


def remote_call(kernel, rows, cols, number, copies, ins, outs, scratch):
    return pl.pallas_call(
        functools.partial(kernel, rows, cols),
        out_shape=[jax.ShapeDtypeStruct(shape, dtype) for shape, dtype in outs],
        in_specs=[VMEM_SPEC] * len(ins),
        out_specs=[VMEM_SPEC] * len(outs),
        scratch_shapes=[pltpu.VMEM(shape, dtype) for shape, dtype in scratch]
        + [pltpu.SemaphoreType.DMA((copies,)), pltpu.SemaphoreType.DMA((copies,))],
        compiler_params=pltpu.CompilerParams(
            collective_id=number, has_side_effects=True, vmem_limit_bytes=VMEM_BYTES
        ),
    )(*ins)


def plain_call(kernel, ins, outs):
    return pl.pallas_call(
        kernel,
        out_shape=[jax.ShapeDtypeStruct(shape, dtype) for shape, dtype in outs],
        in_specs=[VMEM_SPEC] * len(ins),
        out_specs=[VMEM_SPEC] * len(outs),
        compiler_params=pltpu.CompilerParams(vmem_limit_bytes=VMEM_BYTES),
    )(*ins)


def middle_kernel(
    halves, hidden, weights, keys, cot, index, queries, gate, grad_mixed, grad_memory, part
):
    width = gate.shape[1]
    depth = halves * QD
    for h in range(halves):
        columns = slice(h * QD, (h + 1) * QD)
        queries[:, columns] = jnp.dot(
            hidden[...], weights[:, columns], preferred_element_type=F32
        ).astype(LOW)
    open_gate = jnp.dot(
        hidden[...], weights[:, depth : depth + width], preferred_element_type=F32
    )
    gate[...] = open_gate
    back = jnp.dot(cot[...], weights[:, depth + width :], preferred_element_type=F32)
    grad_mixed[...] = back
    grad_memory[...] = (back * (open_gate * jax.nn.sigmoid(open_gate))).astype(LOW)
    lanes = lax.broadcasted_iota(jnp.int32, index.shape, 1)
    low_index = index[...] % LANES
    upper = index[...] >= LANES
    found = jnp.zeros(index.shape, F32)
    for h in range(halves):
        scores = lax.dot_general(
            queries[:, h * QD : (h + 1) * QD], keys[h], NT_DIMS, preferred_element_type=F32
        )
        first = jnp.take_along_axis(scores[:, :LANES], low_index, axis=1)
        second = jnp.take_along_axis(scores[:, LANES:], low_index, axis=1)
        found = jnp.where(lanes // PICKS == h, jnp.where(upper, second, first), found)
    part[...] = found.T[: halves * PICKS]


def spread_kernel(halves, weights, dw, index, out):
    tokens = weights.shape[1]
    change = dw[...]
    share = weights[...]
    grad = share * (change - jnp.sum(share * change, axis=0, keepdims=True))
    block = 128
    places = lax.broadcasted_iota(jnp.int32, (NK, block), 0)
    for h in range(halves):
        for b in range(tokens // block):
            columns = slice(b * block, (b + 1) * block)
            total = jnp.zeros((NK, block), F32)
            for k in range(PICKS):
                row = index[h * PICKS + k : h * PICKS + k + 1, columns]
                total = total + jnp.where(places == row, grad[k : k + 1, columns], 0.0)
            out[columns, h * NK : (h + 1) * NK] = total.T.astype(LOW)


def memory_kernel(
    groups, tok_block, iters, picks_ref, w_ref, dm_ref, table_ref, mem_ref, dw_ref, gt_ref, dense, gacc, hi_ref, lo_ref, wide_ref, found_ref
):
    spans = groups * NK // LANES
    pitch = spans + 8
    per_tok = tok_block // iters
    per_span = spans // iters
    step = pl.program_id(0)

    @pl.when(step == 0)
    def _():
        gacc[...] = jnp.zeros_like(gacc)

    picks = picks_ref[...].astype(jnp.int32) + 32768
    hi_ref[...] = (picks // LANES - lax.axis_index("row") * spans).astype(F32)
    lo_ref[...] = (picks % LANES).astype(F32)
    wide_ref[...] = w_ref[0].astype(F32).T
    places_lo = lax.broadcasted_iota(jnp.int32, (LANES, LANES), 0).astype(F32).astype(LOW)
    places_hi = lax.broadcasted_iota(jnp.int32, (spans, LANES), 0).astype(F32).astype(LOW)
    ones = jnp.ones((LANES, LANES), LOW)
    zeros = jnp.zeros((LANES, LANES), LOW)
    blank = jnp.zeros((spans, LANES), LOW)
    grads = dm_ref[...]
    grads_t = grads.T
    mem_ref[...] = jnp.zeros_like(mem_ref)
    found_ref[...] = jnp.zeros_like(found_ref)
    lo_int = picks % LANES
    hi_all = hi_ref[...]

    def token_pair(first):
        rights, lefts = [], []
        for token in (first, first + 1):
            lo_row = jnp.broadcast_to(lo_ref[pl.ds(token, 1), :], (LANES, LANES)).astype(LOW)
            hi_row = jnp.broadcast_to(hi_ref[pl.ds(token, 1), :], (spans, LANES)).astype(LOW)
            w_row = jnp.broadcast_to(wide_ref[pl.ds(token, 1), :], (spans, LANES)).astype(LOW)
            rights.append(jnp.where(lo_row == places_lo, ones, zeros))
            lefts.append(jnp.where(hi_row == places_hi, w_row, blank))
        right = jnp.concatenate(rights, axis=1)
        left = jnp.concatenate(
            [
                jnp.concatenate([lefts[0], blank], axis=1),
                jnp.concatenate([blank, lefts[1]], axis=1),
            ],
            axis=0,
        )
        both = lax.dot_general(left, right, NT_DIMS, preferred_element_type=F32)
        for j in range(2):
            dense[pl.ds(pl.multiple_of((first + j) * pitch, 8), spans), :] = both[
                j * spans : (j + 1) * spans
            ]

    def build(it, _):
        rows = pl.ds(pl.multiple_of(it * per_span * LANES, LANES), per_span * LANES)
        products = lax.dot_general(grads, table_ref[rows, :], NT_DIMS, preferred_element_type=F32)
        found = found_ref[...]
        pairs = per_tok // 2 // per_span
        for j in range(per_span):
            picked = jnp.take_along_axis(products[:, LANES * j : LANES * (j + 1)], lo_int, axis=1)
            found = jnp.where(hi_all == (it * per_span + j).astype(F32), picked, found)
            for u in range(pairs):
                token_pair(it * per_tok + (j * pairs + u) * 2)
        found_ref[...] = found
        return 0

    lax.fori_loop(0, iters, build, 0)
    dw_ref[0] = found_ref[...].T

    def multiply(it, _):
        rows = pl.ds(pl.multiple_of(it * per_span * LANES, LANES), per_span * LANES)
        weights = jnp.concatenate(
            [
                dense[pl.ds(it * per_span + j, tok_block, stride=pitch), :].astype(LOW)
                for j in range(per_span)
            ],
            axis=1,
        )
        mem_ref[...] += jnp.dot(weights, table_ref[rows, :], preferred_element_type=F32)
        gacc[:, rows] += jnp.dot(grads_t, weights, preferred_element_type=F32)
        return 0

    lax.fori_loop(0, iters, multiply, 0)

    @pl.when(step == pl.num_programs(0) - 1)
    def _():
        def turn(i, _):
            rows = pl.ds(pl.multiple_of(i * NK, NK), NK)
            gt_ref[rows, :] = gacc[:, rows].T
            return 0

        lax.fori_loop(0, groups, turn, 0)


def memory_call(picks, weights, grads, table):
    tokens, count = picks.shape
    rows, width = table.shape
    groups = rows // NK
    block = weights.shape[2]
    spec = lambda n: pl.BlockSpec((block, n), lambda i: (i, 0))
    turned = pl.BlockSpec((1, count, block), lambda i: (i, 0, 0))
    return pl.pallas_call(
        functools.partial(memory_kernel, groups, block, 4),
        grid=(tokens // block,),
        in_specs=[spec(count), turned, spec(width), pl.BlockSpec((rows, width), lambda i: (0, 0))],
        out_specs=[
            spec(width),
            turned,
            pl.BlockSpec((rows, width), lambda i: (0, 0), pipeline_mode=pl.Buffered(1)),
        ],
        out_shape=[
            jax.ShapeDtypeStruct((tokens, width), F32),
            jax.ShapeDtypeStruct((tokens // block, count, block), F32),
            jax.ShapeDtypeStruct((rows, width), F32),
        ],
        scratch_shapes=[
            pltpu.VMEM((block * (rows // LANES + 8), LANES), F32),
            pltpu.VMEM((width, rows), F32),
        ]
        + [pltpu.VMEM((block, count), F32)] * 4,
        compiler_params=pltpu.CompilerParams(vmem_limit_bytes=62 * 2**20),
    )(picks, weights, grads, table)


def attention_forward(queries, key_rows, value_rows, allowed, score_scale):
    scores = (
        jnp.einsum("qhd,khd->hqk", queries, key_rows, preferred_element_type=F32) * score_scale
    )
    scores = jnp.where(allowed[None], scores, MASKED)
    row_max = jnp.max(scores, axis=2, keepdims=True)
    shifted_exp = jnp.exp(scores - row_max)
    row_total = jnp.sum(shifted_exp, axis=2, keepdims=True)
    weights_low = (shifted_exp / row_total).astype(LOW)
    weighted = jnp.einsum("hqk,khd->qhd", weights_low, value_rows, preferred_element_type=F32)
    mixed = weighted.astype(LOW).reshape(queries.shape[0], -1)
    return mixed, row_max + jnp.log(row_total)


def attention_backward(queries, key_rows, value_rows, grad_out, log_total, allowed, score_scale):
    scores = (
        jnp.einsum("qhd,khd->hqk", queries, key_rows, preferred_element_type=F32) * score_scale
    )
    scores = jnp.where(allowed[None], scores, MASKED)
    probs = jnp.exp(scores - log_total)
    grad_prob = jnp.einsum("qhd,khd->hqk", grad_out, value_rows, preferred_element_type=F32)
    inner = jnp.sum(probs * grad_prob, axis=2, keepdims=True)
    grad_score = (probs * (grad_prob - inner)).astype(LOW)
    query_grad = (
        jnp.einsum("hqk,khd->qhd", grad_score, key_rows, preferred_element_type=F32) * score_scale
    )
    key_grad = (
        jnp.einsum("hqk,qhd->khd", grad_score, queries, preferred_element_type=F32) * score_scale
    )
    value_grad = jnp.einsum(
        "hqk,qhd->khd", probs.astype(LOW), grad_out, preferred_element_type=F32
    )
    return query_grad, key_grad, value_grad


def per_device(
    tokens,
    cotangent,
    deal_order,
    seq_lengths,
    value_picks,
    norm1_gain,
    w_qkv,
    w_attn_out,
    norm2_gain,
    w_query,
    sub_keys,
    value_table,
    w_gate,
    w_mem_out,
):
    rows, cols = lax.axis_size("row"), lax.axis_size("col")
    row_index, col_index = lax.axis_index("row"), lax.axis_index("col")
    count, width = tokens.shape
    capacity = 2 * count // rows
    slots = rows * capacity
    shard_rows = w_qkv.shape[0]
    heads_here = width // HD
    halves = sub_keys.shape[0]
    depth = halves * QD
    score_scale = HD ** (-0.5)

    my_slots = lax.dynamic_slice_in_dim(deal_order, row_index * count, count)
    source = my_slots // count
    from_source = (source[:, None] == jnp.arange(rows, dtype=jnp.int32)[None, :]).astype(jnp.int32)
    earlier = jnp.cumsum(from_source, axis=0) - from_source
    recv_pos = source * capacity + jnp.sum(earlier * from_source, axis=1)
    owned = (deal_order // count == row_index).astype(jnp.int32).reshape(rows, count)
    rank = jnp.cumsum(owned, axis=1) - owned
    slot_pos = (jnp.arange(rows, dtype=jnp.int32)[:, None] * capacity + rank).reshape(-1)
    mine = (deal_order - row_index * count)[None, :] == jnp.arange(count, dtype=jnp.int32)[:, None]
    send_pos = jnp.sum(jnp.where(mine, slot_pos[None, :], 0), axis=1)
    send_row, send_col = send_pos[None, :], send_pos[:, None]
    recv_row, recv_col = recv_pos[None, :], recv_pos[:, None]

    shard_one = jnp.concatenate([w_qkv.astype(LOW), w_attn_out.astype(LOW).T], axis=1)
    shard_two = jnp.concatenate(
        [w_query.astype(LOW), w_gate.astype(LOW), w_mem_out.astype(LOW).T], axis=1
    )
    gain_one = norm1_gain.astype(LOW).astype(F32)[None, :]
    gain_two = norm2_gain.astype(LOW).astype(F32)[None, :]
    gain_all = lax.all_gather(norm1_gain.astype(LOW), "col", axis=0, tiled=True).astype(F32)
    swap = [((slots, width), LOW), ((slots, width), LOW)]

    full_tokens, weights_one = remote_call(
        deal_kernel,
        rows,
        cols,
        0,
        rows - 1 + cols - 1 + rows,
        [tokens, send_row, recv_col, shard_one],
        [((count, D), LOW), ((D, shard_one.shape[1]), LOW)],
        swap,
    )
    qkv_weight, attn_weight = weights_one[:, : 3 * width], weights_one[:, 3 * width :]
    dealt = full_tokens.astype(F32)
    factor_one = lax.rsqrt(jnp.mean(dealt * dealt, axis=1, keepdims=True) + EPS)
    hidden_one = (dealt * factor_one * gain_all).astype(LOW)
    dealt_own = lax.dynamic_slice_in_dim(dealt, col_index * width, width, 1)

    places = jnp.arange(count, dtype=jnp.int32)
    seq_ids = jnp.sum(
        (places[:, None] >= jnp.cumsum(seq_lengths[0])[None, :]).astype(jnp.int32), axis=1
    )
    allowed = (seq_ids[:, None] == seq_ids[None, :]) & (places[:, None] >= places[None, :])
    qkv = (
        jnp.dot(hidden_one, qkv_weight, preferred_element_type=F32)
        .astype(LOW)
        .reshape(count, heads_here, 3, HD)
    )
    queries, key_rows, value_rows = qkv[:, :, 0, :], qkv[:, :, 1, :], qkv[:, :, 2, :]
    mixed, log_total = attention_forward(queries, key_rows, value_rows, allowed, score_scale)
    attn_part = lax.dot_general(mixed, attn_weight, NT_DIMS, preferred_element_type=F32)

    flat_picks = value_picks.reshape(count, MH * PICKS)
    sums = [
        ((cols - 1, count, width), LOW),
        ((cols - 1, count, width), LOW),
        ((8, count), F32),
        ((cols, 8, count), F32),
    ]
    hidden_two, resid, factor_two, full_cot, weights_two, key_table, all_picks = remote_call(
        norm_kernel,
        rows,
        cols,
        1,
        rows - 1 + 4 * (cols - 1) + 3 * rows,
        [
            attn_part,
            dealt_own,
            gain_two,
            cotangent,
            send_row,
            recv_col,
            shard_two,
            sub_keys.astype(LOW),
            (flat_picks - 32768).astype(jnp.int16),
        ],
        [
            ((count, D), LOW),
            ((count, width), F32),
            ((count, LANES), F32),
            ((count, D), LOW),
            ((D, shard_two.shape[1]), LOW),
            ((halves, NK, QD), LOW),
            ((rows * count, MH * PICKS), jnp.int16),
        ],
        swap + sums,
    )
    half_ids = col_index * halves + jnp.arange(halves, dtype=jnp.int32)
    head = half_ids[0] // 2
    head_picks = lax.dynamic_index_in_dim(value_picks, head, 1, keepdims=False)
    sub_index = jnp.concatenate(
        [
            jnp.where(half_ids[h] % 2 == 0, head_picks // NK, head_picks % NK)
            for h in range(halves)
        ],
        axis=1,
    )
    padded_index = jnp.pad(sub_index, ((0, 0), (0, LANES - halves * PICKS)))
    mem_queries, gate, grad_mixed, grad_memory, score_part = plain_call(
        functools.partial(middle_kernel, halves),
        [hidden_two, weights_two, key_table, full_cot, padded_index],
        [
            ((count, depth), LOW),
            ((count, width), F32),
            ((count, width), F32),
            ((count, width), LOW),
            ((halves * PICKS, count), F32),
        ],
    )
    pick_weights, all_low, all_grads = remote_call(
        score_kernel,
        rows,
        cols,
        2,
        cols - 1 + 2 * rows,
        [score_part, grad_memory],
        [
            ((MH * PICKS, count), F32),
            ((rows, MH * PICKS, count), LOW),
            ((rows * count, width), LOW),
        ],
        [((2 * MH * PICKS, count), F32)],
    )
    mem_part, dw_part, grad_table = memory_call(
        all_picks, all_low, all_grads, value_table.astype(LOW)
    )
    half = rows // 2
    memory, grad_pick = remote_call(
        memory_sum_kernel,
        rows,
        cols,
        3,
        2 * half + 2 * (half - 1) + cols - 1,
        [mem_part, dw_part],
        [((count, width), F32), ((PICKS, count), F32)],
        [
            ((half, count, width), F32),
            ((half - 1, count, width), LOW),
            ((half - 1, count, width), LOW),
            ((half, MH * PICKS, count), F32),
            ((half, MH * PICKS, count), F32),
            ((cols - 1, half, PICKS, count), F32),
            ((half, PICKS, count), F32),
            ((half - 1, PICKS, count), F32),
        ],
    )
    own_weights = lax.dynamic_slice_in_dim(pick_weights, head * PICKS, PICKS, 0)
    (grad_sub,) = plain_call(
        functools.partial(spread_kernel, halves),
        [own_weights, grad_pick, sub_index.T],
        [((count, halves * NK), LOW)],
    )
    sigmoid_gate = jax.nn.sigmoid(gate)
    mixed_two = (memory * gate * sigmoid_gate).astype(LOW)
    grad_gate = (
        grad_mixed * memory * sigmoid_gate * (1.0 + gate * (1.0 - sigmoid_gate))
    ).astype(LOW)
    memout_part = lax.dot_general(
        mixed_two, weights_two[:, depth + width :], NT_DIMS, preferred_element_type=F32
    )
    grad_sub = grad_sub.reshape(count, halves, NK)
    grad_queries = (
        jnp.einsum("tnj,njq->tnq", grad_sub, key_table, preferred_element_type=F32)
        .astype(LOW)
        .reshape(count, depth)
    )
    grad_keys = jnp.einsum(
        "tnj,tnq->njq",
        grad_sub,
        mem_queries.reshape(count, halves, QD),
        preferred_element_type=F32,
    )
    grad_both = jnp.concatenate([grad_queries, grad_gate], axis=1)
    hidden_two_part = lax.dot_general(
        grad_both, weights_two[:, : depth + width], NT_DIMS, preferred_element_type=F32
    )
    grad_two = jnp.concatenate(
        [
            jnp.einsum("tD,tm->Dm", hidden_two, grad_both, preferred_element_type=F32),
            jnp.einsum("tD,tc->Dc", full_cot, mixed_two, preferred_element_type=F32),
        ],
        axis=1,
    )
    own_cot = lax.dynamic_slice_in_dim(full_cot, col_index * width, width, 1)
    grad_low, grad_resid, output, own_two, own_keys, gain_two_part = remote_call(
        back_two_kernel,
        rows,
        cols,
        4,
        4 * (cols - 1) + rows - 1 + 2 * (half + half - 1),
        [
            hidden_two_part,
            memout_part,
            resid,
            factor_two,
            gain_two,
            own_cot,
            recv_row,
            send_col,
            grad_two,
            grad_keys,
        ],
        [
            ((count, D), LOW),
            ((count, width), F32),
            ((count, width), F32),
            (shard_two.shape, F32),
            (sub_keys.shape, F32),
            ((8, width), F32),
        ],
        [
            ((cols - 1, count, width), LOW),
            ((cols - 1, count, width), LOW),
            *sums,
            *swap,
            ((half,) + shard_two.shape, F32),
            ((half - 1,) + shard_two.shape, LOW),
            ((half - 1,) + shard_two.shape, LOW),
            ((half,) + sub_keys.shape, F32),
            ((half - 1,) + sub_keys.shape, LOW),
            ((half - 1,) + sub_keys.shape, LOW),
        ],
    )
    grad_heads = (
        jnp.dot(grad_low, attn_weight, preferred_element_type=F32)
        .astype(LOW)
        .reshape(count, heads_here, HD)
    )
    grad_qkv = (
        jnp.stack(
            attention_backward(
                queries, key_rows, value_rows, grad_heads, log_total, allowed, score_scale
            ),
            axis=2,
        )
        .astype(LOW)
        .reshape(count, heads_here * 3 * HD)
    )
    grad_one = jnp.concatenate(
        [
            jnp.einsum("tD,tm->Dm", hidden_one, grad_qkv, preferred_element_type=F32),
            jnp.einsum("tD,tc->Dc", grad_low, mixed, preferred_element_type=F32),
        ],
        axis=1,
    )
    hidden_one_part = lax.dot_general(grad_qkv, qkv_weight, NT_DIMS, preferred_element_type=F32)
    grad_tokens, own_one, gains = remote_call(
        back_one_kernel,
        rows,
        cols,
        5,
        2 * (cols - 1) + 2 * (rows - 1) + half + half - 1,
        [
            hidden_one_part,
            dealt_own,
            jnp.broadcast_to(factor_one, (count, LANES)),
            gain_one,
            grad_resid,
            recv_row,
            send_col,
            grad_one,
            gain_two_part,
        ],
        [((count, width), F32), (shard_one.shape, F32), ((8, width), F32)],
        [
            *sums,
            *swap,
            ((half,) + shard_one.shape, F32),
            ((half - 1,) + shard_one.shape, LOW),
            ((half - 1,) + shard_one.shape, LOW),
            ((8, width), F32),
            ((rows, 8, width), F32),
        ],
    )
    gain_span = width // rows
    gain_one_grad = lax.dynamic_slice_in_dim(gains[0], row_index * gain_span, gain_span)
    gain_two_grad = lax.dynamic_slice_in_dim(gains[1], row_index * gain_span, gain_span)
    return (
        output,
        grad_tokens,
        gain_one_grad,
        own_one[:, : 3 * width],
        own_one[:, 3 * width :].T,
        gain_two_grad,
        own_two[:, :depth],
        own_keys,
        grad_table,
        own_two[:, depth : depth + width],
        own_two[:, depth + width :].T,
    )


def solution(mesh):
    return jax.shard_map(
        per_device,
        mesh=mesh,
        in_specs=(
            P("row", "col"),
            P("row", "col"),
            P(),
            P("row", None),
            P("row", None, None),
            P("col"),
            P("row", "col"),
            P("col", "row"),
            P("col"),
            P("row", "col"),
            P("col", "row", None),
            P("row", "col"),
            P("row", "col"),
            P("col", "row"),
        ),
        out_specs=(
            P("row", "col"),
            P("row", "col"),
            P(("col", "row")),
            P("row", "col"),
            P("col", "row"),
            P(("col", "row")),
            P("row", "col"),
            P("col", "row", None),
            P("row", "col"),
            P("row", "col"),
            P("col", "row"),
        ),
        check_vma=False,
    )
```

```python
import functools

import jax
import jax.numpy as jnp
from jax import lax
from jax.experimental import pallas as pl
from jax.experimental.pallas import tpu as pltpu
from jax.sharding import PartitionSpec as P

D = 1024
HD = 64
MH = 4
QD = 512
NK = 256
PICKS = 32
LANES = 128
EPS = 1e-05
MASKED = -1e30
F32 = jnp.float32
LOW = jnp.bfloat16
MESH = pl.DeviceIdType.MESH
NT_DIMS = (((1,), (1,)), ((), ()))
VMEM_SPEC = pl.BlockSpec(memory_space=pltpu.VMEM)
VMEM_BYTES = 60 * 2**20


def flip(index, mask):
    bit = 1
    while bit <= mask:
        if mask & bit:
            index = index + bit - 2 * bit * (index // bit % 2)
        bit *= 2
    return index


def cross(index, mask, size):
    total, bit = 0, 1
    while bit < size:
        a, b = index // bit % 2, mask // bit % 2
        total = total + bit * (a + b - 2 * a * b)
        bit *= 2
    return total


class Net:
    def __init__(self, rows, cols, sends, recvs):
        self.rows, self.cols = rows, cols
        self.row, self.col = lax.axis_index("row"), lax.axis_index("col")
        self.sends, self.recvs, self.used = sends, recvs, 0
        self.pending = []

    def place(self, row_k, col_k):
        return (flip(self.row, row_k), flip(self.col, col_k))

    def meet(self, row_ks, col_ks):
        barrier = pltpu.get_barrier_semaphore()
        places = [self.place(k, 0) for k in row_ks] + [self.place(0, k) for k in col_ks]
        for place in places:
            pl.semaphore_signal(barrier, inc=1, device_id=place, device_id_type=MESH)
        pl.semaphore_wait(barrier, len(places))

    def copy(self, src, dst, number, row_k=0, col_k=0):
        assert number < self.sends.shape[0]
        return pltpu.make_async_remote_copy(
            src_ref=src,
            dst_ref=dst,
            send_sem=self.sends.at[number],
            recv_sem=self.recvs.at[number],
            device_id=self.place(row_k, col_k),
            device_id_type=MESH,
        )

    def send(self, src, dst, row_k=0, col_k=0):
        copy = self.copy(src, dst, self.used, row_k, col_k)
        copy.start()
        self.used += 1
        self.pending.append(copy)
        return copy

    def drain(self):
        for copy in self.pending:
            copy.wait_send()

    def gather_start(self, src, view, first=True):
        copies = [self.send(src, view(self.row), row_k=2 * j) for j in range(1, self.rows // 2)]
        return copies, self.send(src, view(self.row), row_k=1)

    def gather_pass(self, view, started):
        copies, sibling = started
        passed = []
        for j, copy in enumerate(copies):
            copy.wait_recv()
            there = flip(self.row, 2 * (j + 1))
            passed.append(self.send(view(there), view(there), row_k=1))
        return [sibling] + passed

    def scatter_start(self, view, across):
        twin = flip(self.row, 1)
        return [
            self.send(view(flip(twin, 2 * j)), across.at[j], row_k=1)
            for j in range(self.rows // 2)
        ]

    def scatter_pass(self, view, across, started, outgoing, incoming):
        moved = []
        for j in range(1, self.rows // 2):
            started[j].wait_recv()
            block = view(flip(self.row, 2 * j))[...] + across[j]
            outgoing[j - 1] = block.astype(outgoing.dtype)
            moved.append(self.send(outgoing.at[j - 1], incoming.at[j - 1], row_k=2 * j))
        return moved

    def scatter_end(self, view, across, started, incoming, moved):
        started[0].wait_recv()
        total = view(self.row)[...] + across[0]
        for j, copy in enumerate(moved):
            copy.wait_recv()
            total = total + incoming[j].astype(F32)
        return total

    def columns_start(self, view):
        return [self.send(view(self.col), view(self.col), col_k=k) for k in range(1, self.cols)]


def wait_all(copies):
    for copy in copies:
        copy.wait_recv()


def rows_of(ref, count):
    return lambda index: ref.at[pl.ds(pl.multiple_of(index * count, count), count), :]


def columns_of(ref, count):
    return lambda index: ref.at[:, pl.ds(pl.multiple_of(index * count, count), count)]


def one_hot_rows(positions, slots):
    places = lax.broadcasted_iota(jnp.int32, (positions.shape[0], slots), 1)
    return jnp.where(positions == places, 1.0, 0.0).astype(LOW)


def one_hot_columns(positions, slots):
    places = lax.broadcasted_iota(jnp.int32, (slots, positions.shape[1]), 0)
    return jnp.where(positions == places, 1.0, 0.0).astype(LOW)


def pack_for_rows(net, packed, values, positions):
    slots = packed.shape[0]
    packed[...] = jnp.dot(
        one_hot_columns(positions, slots), values, preferred_element_type=F32
    ).astype(LOW)


def exchange_start(net, packed, got, capacity):
    mine = rows_of(got, capacity)
    theirs = rows_of(packed, capacity)
    copies = [
        net.send(theirs(flip(net.row, k)), mine(net.row), row_k=k) for k in range(1, net.rows)
    ]
    mine(net.row)[...] = theirs(net.row)[...]
    return copies


def unpack(got, positions):
    return jnp.dot(
        one_hot_rows(positions, got.shape[0]), got[...], preferred_element_type=F32
    )


def share_sums(net, sums, mine, theirs):
    tokens = sums.shape[0]
    mine[...] = jnp.broadcast_to(sums, (tokens, LANES)).T[:8]
    copies = [net.send(mine, theirs.at[k], col_k=k) for k in range(1, net.cols)]
    wait_all(copies)
    total = mine[...]
    for k in range(1, net.cols):
        total = total + theirs[k]
    return jnp.broadcast_to(total[:1], (LANES, tokens)).T


def widen(lanes, width):
    return jnp.concatenate([lanes] * (width // LANES), axis=1)


def reduce_start(net, part, outgoing, incoming):
    width = part.shape[1] // net.cols
    view = columns_of(part, width)
    copies = []
    for k in range(1, net.cols):
        outgoing[k - 1] = view(flip(net.col, k))[...].astype(LOW)
        copies.append(net.send(outgoing.at[k - 1], incoming.at[k - 1], col_k=k))
    return copies


def reduce_end(net, part, incoming, copies):
    total = columns_of(part, part.shape[1] // net.cols)(net.col)[...].astype(F32)
    for k, copy in enumerate(copies):
        copy.wait_recv()
        total = total + incoming[k].astype(F32)
    return total


def deal_kernel(
    rows, cols, tokens_ref, send_row, recv_col, shard, full, weights, packed, got, sends, recvs
):
    net = Net(rows, cols, sends, recvs)
    capacity = packed.shape[0] // rows
    pack_for_rows(net, packed, tokens_ref[...], send_row[...])
    net.meet(range(1, rows), range(1, cols))
    copies = exchange_start(net, packed, got, capacity)
    count = shard.shape[0]
    place = rows_of(weights, count)
    gather = net.gather_start(shard, place)
    place(net.row)[...] = shard[...]
    wait_all(copies)
    mine = columns_of(full, tokens_ref.shape[1])
    mine(net.col)[...] = unpack(got, recv_col[...]).astype(LOW)
    spread = net.columns_start(mine)
    wait_all(net.gather_pass(place, gather))
    wait_all(spread)
    net.drain()


def norm_kernel(
    rows,
    cols,
    part,
    dealt,
    gain,
    cot,
    send_row,
    recv_col,
    shard,
    keys,
    hidden,
    resid,
    factor,
    full,
    weights,
    key_table,
    packed,
    got,
    outgoing,
    incoming,
    mine,
    theirs,
    sends,
    recvs,
):
    net = Net(rows, cols, sends, recvs)
    capacity = packed.shape[0] // rows
    width = dealt.shape[1]
    net.meet(range(1, rows), range(1, cols))
    reduce = reduce_start(net, part, outgoing, incoming)
    pack_for_rows(net, packed, cot[...], send_row[...])
    copies = exchange_start(net, packed, got, capacity)
    place = rows_of(weights, shard.shape[0])
    gather = net.gather_start(shard, place)
    span = keys.shape[1]
    key_place = lambda index: key_table.at[:, pl.ds(pl.multiple_of(index * span, span), span), :]
    key_gather = net.gather_start(keys, key_place)
    place(net.row)[...] = shard[...]
    key_place(net.row)[...] = keys[...]
    values = dealt[...] + reduce_end(net, part, incoming, reduce)
    resid[...] = values
    square = share_sums(net, jnp.sum(values * values, axis=1, keepdims=True), mine, theirs)
    scale = lax.rsqrt(square / D + EPS)
    factor[...] = scale
    own = columns_of(hidden, width)
    own(net.col)[...] = (resid[...] * widen(scale, width) * gain[...]).astype(LOW)
    spread = net.columns_start(own)
    wait_all(copies)
    own_cot = columns_of(full, width)
    own_cot(net.col)[...] = unpack(got, recv_col[...]).astype(LOW)
    cot_spread = net.columns_start(own_cot)
    left = net.gather_pass(place, gather)
    left += net.gather_pass(key_place, key_gather)
    wait_all(spread)
    wait_all(cot_spread)
    wait_all(left)
    net.drain()


def norm_grad(net, grad_hidden, values, scale, gain, extra, mine, theirs):
    width = values.shape[1]
    scaled = grad_hidden * gain
    inner = share_sums(net, jnp.sum(scaled * values, axis=1, keepdims=True), mine, theirs)
    wide = widen(scale, width)
    grads = wide * scaled - values * (wide * wide * wide) * widen(inner, width) / D
    grad_gain = jnp.sum(grad_hidden * values * wide, axis=0, keepdims=True)
    return grads + extra, grad_gain


def back_two_kernel(
    rows,
    cols,
    part,
    result_part,
    resid,
    factor,
    gain,
    cot,
    recv_row,
    send_col,
    weight_grad,
    key_grad,
    grad_low,
    grad_resid,
    result,
    own_weight,
    own_keys,
    gain_grad,
    outgoing,
    incoming,
    res_outgoing,
    res_incoming,
    mine,
    theirs,
    packed,
    got,
    across,
    w_out,
    w_in,
    k_across,
    k_out,
    k_in,
    sends,
    recvs,
):
    net = Net(rows, cols, sends, recvs)
    capacity = packed.shape[0] // rows
    width = resid.shape[1]
    net.meet(range(1, rows), range(1, cols))
    reduce = reduce_start(net, part, outgoing, incoming)
    res_reduce = reduce_start(net, result_part, res_outgoing, res_incoming)
    view = rows_of(weight_grad, own_weight.shape[0])
    span = own_keys.shape[1]
    key_view = lambda index: key_grad.at[:, pl.ds(pl.multiple_of(index * span, span), span), :]
    started = net.scatter_start(view, across)
    key_started = net.scatter_start(key_view, k_across)
    grad_hidden = reduce_end(net, part, incoming, reduce)
    grads, gain_sum = norm_grad(
        net, grad_hidden, resid[...], factor[...], gain[...], cot[...].astype(F32), mine, theirs
    )
    grad_resid[...] = grads
    gain_grad[...] = jnp.broadcast_to(gain_sum, gain_grad.shape)
    own = columns_of(grad_low, width)
    own(net.col)[...] = grads.astype(LOW)
    spread = net.columns_start(own)
    block = resid[...] + reduce_end(net, result_part, res_incoming, res_reduce)
    pack_for_rows(net, packed, block.astype(LOW), recv_row[...])
    copies = exchange_start(net, packed, got, capacity)
    moved = net.scatter_pass(view, across, started, w_out, w_in)
    key_moved = net.scatter_pass(key_view, k_across, key_started, k_out, k_in)
    wait_all(copies)
    result[...] = unpack(got, send_col[...])
    own_weight[...] = net.scatter_end(view, across, started, w_in, moved)
    own_keys[...] = net.scatter_end(key_view, k_across, key_started, k_in, key_moved)
    wait_all(spread)
    net.drain()


def back_one_kernel(
    rows,
    cols,
    part,
    dealt,
    factor,
    gain,
    extra,
    recv_row,
    send_col,
    weight_grad,
    gain_two,
    result,
    own_weight,
    gains,
    outgoing,
    incoming,
    mine,
    theirs,
    packed,
    got,
    across,
    w_out,
    w_in,
    my_gains,
    their_gains,
    sends,
    recvs,
):
    net = Net(rows, cols, sends, recvs)
    capacity = packed.shape[0] // rows
    net.meet(range(1, rows), range(1, cols))
    reduce = reduce_start(net, part, outgoing, incoming)
    view = rows_of(weight_grad, own_weight.shape[0])
    started = net.scatter_start(view, across)
    grad_hidden = reduce_end(net, part, incoming, reduce)
    grads, gain_sum = norm_grad(
        net, grad_hidden, dealt[...], factor[...], gain[...], extra[...], mine, theirs
    )
    pack_for_rows(net, packed, grads.astype(LOW), recv_row[...])
    copies = exchange_start(net, packed, got, capacity)
    places = lax.broadcasted_iota(jnp.int32, my_gains.shape, 0)
    my_gains[...] = jnp.where(places == 0, gain_sum, gain_two[...])
    gain_copies = [
        net.send(my_gains, their_gains.at[k], row_k=k) for k in range(1, rows)
    ]
    moved = net.scatter_pass(view, across, started, w_out, w_in)
    wait_all(copies)
    result[...] = unpack(got, send_col[...])
    total = my_gains[...]
    for k, copy in enumerate(gain_copies):
        copy.wait_recv()
        total = total + their_gains[k + 1]
    gains[...] = total
    own_weight[...] = net.scatter_end(view, across, started, w_in, moved)
    net.drain()


def remote_call(kernel, rows, cols, number, copies, ins, outs, scratch):
    return pl.pallas_call(
        functools.partial(kernel, rows, cols),
        out_shape=[jax.ShapeDtypeStruct(shape, dtype) for shape, dtype in outs],
        in_specs=[VMEM_SPEC] * len(ins),
        out_specs=[VMEM_SPEC] * len(outs),
        scratch_shapes=[pltpu.VMEM(shape, dtype) for shape, dtype in scratch]
        + [pltpu.SemaphoreType.DMA((copies,)), pltpu.SemaphoreType.DMA((copies,))],
        compiler_params=pltpu.CompilerParams(
            collective_id=number, has_side_effects=True, vmem_limit_bytes=VMEM_BYTES
        ),
    )(*ins)


def plain_call(kernel, ins, outs):
    return pl.pallas_call(
        kernel,
        out_shape=[jax.ShapeDtypeStruct(shape, dtype) for shape, dtype in outs],
        in_specs=[VMEM_SPEC] * len(ins),
        out_specs=[VMEM_SPEC] * len(outs),
        compiler_params=pltpu.CompilerParams(vmem_limit_bytes=VMEM_BYTES),
    )(*ins)


def middle_kernel(
    halves, hidden, weights, keys, cot, index, queries, gate, grad_mixed, grad_memory, part
):
    width = gate.shape[1]
    depth = halves * QD
    for h in range(halves):
        columns = slice(h * QD, (h + 1) * QD)
        queries[:, columns] = jnp.dot(
            hidden[...], weights[:, columns], preferred_element_type=F32
        ).astype(LOW)
    open_gate = jnp.dot(
        hidden[...], weights[:, depth : depth + width], preferred_element_type=F32
    )
    gate[...] = open_gate
    back = jnp.dot(cot[...], weights[:, depth + width :], preferred_element_type=F32)
    grad_mixed[...] = back
    grad_memory[...] = (back * (open_gate * jax.nn.sigmoid(open_gate))).astype(LOW)
    lanes = lax.broadcasted_iota(jnp.int32, index.shape, 1)
    low_index = index[...] % LANES
    upper = index[...] >= LANES
    found = jnp.zeros(index.shape, F32)
    for h in range(halves):
        scores = lax.dot_general(
            queries[:, h * QD : (h + 1) * QD], keys[h], NT_DIMS, preferred_element_type=F32
        )
        first = jnp.take_along_axis(scores[:, :LANES], low_index, axis=1)
        second = jnp.take_along_axis(scores[:, LANES:], low_index, axis=1)
        found = jnp.where(lanes // PICKS == h, jnp.where(upper, second, first), found)
    part[...] = found.T[: halves * PICKS]


def spread_kernel(halves, weights, dw, index, out):
    tokens = weights.shape[1]
    change = dw[...]
    share = weights[...]
    grad = share * (change - jnp.sum(share * change, axis=0, keepdims=True))
    block = 128
    places = lax.broadcasted_iota(jnp.int32, (NK, block), 0)
    for h in range(halves):
        for b in range(tokens // block):
            columns = slice(b * block, (b + 1) * block)
            total = jnp.zeros((NK, block), F32)
            for k in range(PICKS):
                row = index[h * PICKS + k : h * PICKS + k + 1, columns]
                total = total + jnp.where(places == row, grad[k : k + 1, columns], 0.0)
            out[columns, h * NK : (h + 1) * NK] = total.T.astype(LOW)


def memory_kernel(
    rows,
    cols,
    part,
    own_picks,
    own_grads,
    table_f32,
    weights,
    memory,
    dw,
    gacc,
    table,
    stage,
    scores,
    picks_of,
    grads_of,
    low_of,
    dense,
    hi_ref,
    lo_ref,
    wide_ref,
    found_ref,
    mem_all,
    mem_twin,
    mem_out,
    mem_in,
    dw_all,
    dw_twin,
    dw_out,
    dw_in,
    dw_cols,
    stage_sems,
    sends,
    recvs,
):
    net = Net(rows, cols, sends, recvs)
    half = rows // 2
    tok_block = own_picks.shape[0]
    span_rows, width = table.shape
    spans = span_rows // LANES
    pitch = spans + 8
    iters = 4
    per_tok = tok_block // iters
    per_span = spans // iters

    grads_at = rows_of(grads_of, tok_block)
    picks_at = rows_of(picks_of, tok_block)
    low_at = lambda index: low_of.at[index]
    views = (grads_at, picks_at, low_at)
    first_pass = 3 * half
    first_twin = first_pass + 3 * half
    first_out = first_twin + 2 * half
    first_col = first_out + 2 * half

    def gather(a, j):
        mine = views[a](net.row)
        return net.copy(mine, mine, 3 * j + a, row_k=2 * j if j else 1)

    def passing(a, j):
        there = views[a](flip(net.row, 2 * j))
        return net.copy(there, there, first_pass + 3 * j + a, row_k=1)

    def twin(a, j):
        src, dst = ((mem_all, mem_twin), (dw_all, dw_twin))[a]
        return net.copy(src.at[2 * j + 1], dst.at[j], first_twin + 2 * j + a, row_k=1)

    def outward(a, j):
        src, dst = ((mem_out, mem_in), (dw_out, dw_in))[a]
        return net.copy(src.at[j - 1], dst.at[j - 1], first_out + 2 * j + a, row_k=2 * j)

    head = lambda col: pl.ds(pl.multiple_of(col * MH // cols * PICKS, PICKS), PICKS)

    def score_copy(k):
        return net.copy(part, rows_of(scores, part.shape[0])(net.col), first_col + k, col_k=k)

    def dw_copy(k):
        return net.copy(
            dw_all.at[0, head(flip(net.col, k)), :],
            dw_cols.at[k - 1],
            first_col + cols + k,
            col_k=k,
        )

    stage_rows = stage.shape[1]

    def stage_copy(i):
        source = table_f32.at[pl.ds(i * stage_rows, stage_rows), :]
        return pltpu.make_async_copy(source, stage.at[i % 2], stage_sems.at[i % 2])

    stage_copy(0).start()
    net.meet([1] + [2 * j for j in range(1, half)], range(1, cols))
    for k in range(1, cols):
        score_copy(k).start()
    grads_at(net.row)[...] = own_grads[...]
    picks_at(net.row)[...] = own_picks[...]
    for j in range(half):
        for a in range(2):
            gather(a, j).start()
    rows_of(scores, part.shape[0])(net.col)[...] = part[...]
    for i in range(span_rows // stage_rows):
        if (i + 1) * stage_rows < span_rows:
            stage_copy(i + 1).start()
        stage_copy(i).wait()
        table[i * stage_rows : (i + 1) * stage_rows, :] = stage[i % 2].astype(LOW)
    for k in range(1, cols):
        score_copy(k).wait_recv()
    for m in range(MH):
        score = (
            scores[2 * m * PICKS : (2 * m + 1) * PICKS]
            + scores[(2 * m + 1) * PICKS : (2 * m + 2) * PICKS]
        )
        shifted = jnp.exp(score - jnp.max(score, axis=0, keepdims=True))
        weights[m * PICKS : (m + 1) * PICKS] = shifted / jnp.sum(shifted, axis=0, keepdims=True)
    low_at(net.row)[...] = weights[...].astype(LOW)
    for j in range(half):
        gather(2, j).start()
    gacc[...] = jnp.zeros_like(gacc)
    mem_all[...] = jnp.zeros_like(mem_all)

    def one_block(step, _):
        k = jnp.where(step == 0, 0, jnp.where(step == rows - 1, 1, step + 1))
        there = cross(net.row, k, rows)
        for j in range(1, half):

            @pl.when(step == 2 * j - 1)
            def _():
                for a in range(3):
                    gather(a, j).wait_recv()
                    passing(a, j).start()

            @pl.when(step == 2 * j)
            def _():
                for a in range(3):
                    passing(a, j).wait_recv()

        @pl.when(step == rows - 1)
        def _():
            for a in range(3):
                gather(a, 0).wait_recv()

        picks = picks_at(there)[...].astype(jnp.int32) + 32768
        hi_ref[...] = (picks // LANES - net.row * spans).astype(F32)
        lo_ref[...] = (picks % LANES).astype(F32)
        wide_ref[...] = low_of[there].astype(F32).T
        places_lo = lax.broadcasted_iota(jnp.int32, (LANES, LANES), 0).astype(F32).astype(LOW)
        places_hi = lax.broadcasted_iota(jnp.int32, (spans, LANES), 0).astype(F32).astype(LOW)
        ones = jnp.ones((LANES, LANES), LOW)
        zeros = jnp.zeros((LANES, LANES), LOW)
        blank = jnp.zeros((spans, LANES), LOW)
        grads = grads_at(there)[...]
        grads_t = grads.T
        found_ref[...] = jnp.zeros_like(found_ref)
        lo_int = picks % LANES
        hi_all = hi_ref[...]

        def token_pair(first):
            rights, lefts = [], []
            for token in (first, first + 1):
                lo_row = jnp.broadcast_to(lo_ref[pl.ds(token, 1), :], (LANES, LANES)).astype(LOW)
                hi_row = jnp.broadcast_to(hi_ref[pl.ds(token, 1), :], (spans, LANES)).astype(LOW)
                w_row = jnp.broadcast_to(wide_ref[pl.ds(token, 1), :], (spans, LANES)).astype(LOW)
                rights.append(jnp.where(lo_row == places_lo, ones, zeros))
                lefts.append(jnp.where(hi_row == places_hi, w_row, blank))
            right = jnp.concatenate(rights, axis=1)
            left = jnp.concatenate(
                [
                    jnp.concatenate([lefts[0], blank], axis=1),
                    jnp.concatenate([blank, lefts[1]], axis=1),
                ],
                axis=0,
            )
            both = lax.dot_general(left, right, NT_DIMS, preferred_element_type=F32)
            for j in range(2):
                dense[pl.ds(pl.multiple_of((first + j) * pitch, 8), spans), :] = both[
                    j * spans : (j + 1) * spans
                ]

        def build(it, _):
            for j in range(1, half):

                @pl.when((it == 1) & (step == 2 * j + 1))
                def _():
                    twin(0, j).wait_recv()
                    twin(1, j).wait_recv()
                    mem_out[j - 1] = (mem_all[2 * j] + mem_twin[j]).astype(LOW)
                    outward(0, j).start()
                    dw_out[j - 1] = dw_all[2 * j] + dw_twin[j]
                    outward(1, j).start()

            span = pl.ds(pl.multiple_of(it * per_span * LANES, LANES), per_span * LANES)
            products = lax.dot_general(
                grads, table[span, :], NT_DIMS, preferred_element_type=F32
            )
            found = found_ref[...]
            pairs = per_tok // 2 // per_span
            for j in range(per_span):
                picked = jnp.take_along_axis(
                    products[:, LANES * j : LANES * (j + 1)], lo_int, axis=1
                )
                found = jnp.where(hi_all == (it * per_span + j).astype(F32), picked, found)
                for u in range(pairs):
                    token_pair(it * per_tok + (j * pairs + u) * 2)
            found_ref[...] = found
            return 0

        lax.fori_loop(0, iters, build, 0)
        dw_all[k] = found_ref[...].T

        def multiply(it, _):
            span = pl.ds(pl.multiple_of(it * per_span * LANES, LANES), per_span * LANES)
            chosen = jnp.concatenate(
                [
                    dense[pl.ds(it * per_span + j, tok_block, stride=pitch), :].astype(LOW)
                    for j in range(per_span)
                ],
                axis=1,
            )
            mem_all[k] += jnp.dot(chosen, table[span, :], preferred_element_type=F32)
            gacc[:, span] += jnp.dot(grads_t, chosen, preferred_element_type=F32)
            return 0

        lax.fori_loop(0, iters, multiply, 0)
        for j in range(half):

            @pl.when(step == (2 * j if j else rows - 1))
            def _():
                twin(0, j).start()
                twin(1, j).start()

        return 0

    lax.fori_loop(0, rows, one_block, 0)
    twin(1, 0).wait_recv()
    total = dw_all[0] + dw_twin[0]
    for j in range(1, half):
        outward(1, j).wait_recv()
        total = total + dw_in[j - 1]
    dw_all[0] = total
    for k in range(1, cols):
        dw_copy(k).start()
    twin(0, 0).wait_recv()
    total = mem_all[0] + mem_twin[0]
    for j in range(1, half):
        outward(0, j).wait_recv()
        total = total + mem_in[j - 1].astype(F32)
    memory[...] = total
    total = dw_all[0, head(net.col), :]
    for k in range(1, cols):
        dw_copy(k).wait_recv()
        total = total + dw_cols[k - 1]
    dw[...] = total
    for k in range(1, cols):
        score_copy(k).wait_send()
        dw_copy(k).wait_send()
    for j in range(half):
        for a in range(3):
            gather(a, j).wait_send()
            if j:
                passing(a, j).wait_send()
        for a in range(2):
            twin(a, j).wait_send()
            if j:
                outward(a, j).wait_send()


def memory_call(rows, cols, number, part, picks, grads, table):
    tokens, count = picks.shape
    span_rows, width = table.shape
    half = rows // 2
    copies = 10 * half + 2 * cols
    vmem = pltpu.VMEM
    return pl.pallas_call(
        functools.partial(memory_kernel, rows, cols),
        in_specs=[VMEM_SPEC, VMEM_SPEC, VMEM_SPEC, pl.BlockSpec(memory_space=pl.ANY)],
        out_specs=[VMEM_SPEC] * 4,
        out_shape=[
            jax.ShapeDtypeStruct((count, tokens), F32),
            jax.ShapeDtypeStruct((tokens, width), F32),
            jax.ShapeDtypeStruct((PICKS, tokens), F32),
            jax.ShapeDtypeStruct((width, span_rows), F32),
        ],
        scratch_shapes=[
            vmem((span_rows, width), LOW),
            vmem((2, 1024, width), F32),
            vmem((2 * count, tokens), F32),
            vmem((rows * tokens, count), jnp.int16),
            vmem((rows * tokens, width), LOW),
            vmem((rows, count, tokens), LOW),
            vmem((tokens * (span_rows // LANES + 8), LANES), F32),
            vmem((tokens, count), F32),
            vmem((tokens, count), F32),
            vmem((tokens, count), F32),
            vmem((tokens, count), F32),
            vmem((rows, tokens, width), F32),
            vmem((half, tokens, width), F32),
            vmem((half - 1, tokens, width), LOW),
            vmem((half - 1, tokens, width), LOW),
            vmem((rows, count, tokens), F32),
            vmem((half, count, tokens), F32),
            vmem((half - 1, count, tokens), F32),
            vmem((half - 1, count, tokens), F32),
            vmem((cols - 1, PICKS, tokens), F32),
            pltpu.SemaphoreType.DMA((2,)),
            pltpu.SemaphoreType.DMA((copies,)),
            pltpu.SemaphoreType.DMA((copies,)),
        ],
        compiler_params=pltpu.CompilerParams(
            collective_id=number, has_side_effects=True, vmem_limit_bytes=63 * 2**20
        ),
    )(part, picks, grads, table)


def attention_forward(queries, key_rows, value_rows, allowed, score_scale):
    scores = (
        jnp.einsum("qhd,khd->hqk", queries, key_rows, preferred_element_type=F32) * score_scale
    )
    scores = jnp.where(allowed[None], scores, MASKED)
    row_max = jnp.max(scores, axis=2, keepdims=True)
    shifted_exp = jnp.exp(scores - row_max)
    row_total = jnp.sum(shifted_exp, axis=2, keepdims=True)
    weights_low = (shifted_exp / row_total).astype(LOW)
    weighted = jnp.einsum("hqk,khd->qhd", weights_low, value_rows, preferred_element_type=F32)
    mixed = weighted.astype(LOW).reshape(queries.shape[0], -1)
    return mixed, row_max + jnp.log(row_total)


def attention_backward(queries, key_rows, value_rows, grad_out, log_total, allowed, score_scale):
    scores = (
        jnp.einsum("qhd,khd->hqk", queries, key_rows, preferred_element_type=F32) * score_scale
    )
    scores = jnp.where(allowed[None], scores, MASKED)
    probs = jnp.exp(scores - log_total)
    grad_prob = jnp.einsum("qhd,khd->hqk", grad_out, value_rows, preferred_element_type=F32)
    inner = jnp.sum(probs * grad_prob, axis=2, keepdims=True)
    grad_score = (probs * (grad_prob - inner)).astype(LOW)
    query_grad = (
        jnp.einsum("hqk,khd->qhd", grad_score, key_rows, preferred_element_type=F32) * score_scale
    )
    key_grad = (
        jnp.einsum("hqk,qhd->khd", grad_score, queries, preferred_element_type=F32) * score_scale
    )
    value_grad = jnp.einsum(
        "hqk,qhd->khd", probs.astype(LOW), grad_out, preferred_element_type=F32
    )
    return query_grad, key_grad, value_grad


def per_device(
    tokens,
    cotangent,
    deal_order,
    seq_lengths,
    value_picks,
    norm1_gain,
    w_qkv,
    w_attn_out,
    norm2_gain,
    w_query,
    sub_keys,
    value_table,
    w_gate,
    w_mem_out,
):
    rows, cols = lax.axis_size("row"), lax.axis_size("col")
    row_index, col_index = lax.axis_index("row"), lax.axis_index("col")
    count, width = tokens.shape
    capacity = 2 * count // rows
    slots = rows * capacity
    shard_rows = w_qkv.shape[0]
    heads_here = width // HD
    halves = sub_keys.shape[0]
    depth = halves * QD
    score_scale = HD ** (-0.5)

    my_slots = lax.dynamic_slice_in_dim(deal_order, row_index * count, count)
    source = my_slots // count
    from_source = (source[:, None] == jnp.arange(rows, dtype=jnp.int32)[None, :]).astype(jnp.int32)
    earlier = jnp.cumsum(from_source, axis=0) - from_source
    recv_pos = source * capacity + jnp.sum(earlier * from_source, axis=1)
    owned = (deal_order // count == row_index).astype(jnp.int32).reshape(rows, count)
    rank = jnp.cumsum(owned, axis=1) - owned
    slot_pos = (jnp.arange(rows, dtype=jnp.int32)[:, None] * capacity + rank).reshape(-1)
    mine = (deal_order - row_index * count)[None, :] == jnp.arange(count, dtype=jnp.int32)[:, None]
    send_pos = jnp.sum(jnp.where(mine, slot_pos[None, :], 0), axis=1)
    send_row, send_col = send_pos[None, :], send_pos[:, None]
    recv_row, recv_col = recv_pos[None, :], recv_pos[:, None]

    shard_one = jnp.concatenate([w_qkv.astype(LOW), w_attn_out.astype(LOW).T], axis=1)
    shard_two = jnp.concatenate(
        [w_query.astype(LOW), w_gate.astype(LOW), w_mem_out.astype(LOW).T], axis=1
    )
    gain_one = norm1_gain.astype(LOW).astype(F32)[None, :]
    gain_two = norm2_gain.astype(LOW).astype(F32)[None, :]
    gain_all = lax.all_gather(norm1_gain.astype(LOW), "col", axis=0, tiled=True).astype(F32)
    swap = [((slots, width), LOW), ((slots, width), LOW)]

    full_tokens, weights_one = remote_call(
        deal_kernel,
        rows,
        cols,
        0,
        rows - 1 + cols - 1 + rows,
        [tokens, send_row, recv_col, shard_one],
        [((count, D), LOW), ((D, shard_one.shape[1]), LOW)],
        swap,
    )
    qkv_weight, attn_weight = weights_one[:, : 3 * width], weights_one[:, 3 * width :]
    dealt = full_tokens.astype(F32)
    factor_one = lax.rsqrt(jnp.mean(dealt * dealt, axis=1, keepdims=True) + EPS)
    hidden_one = (dealt * factor_one * gain_all).astype(LOW)
    dealt_own = lax.dynamic_slice_in_dim(dealt, col_index * width, width, 1)

    places = jnp.arange(count, dtype=jnp.int32)
    seq_ids = jnp.sum(
        (places[:, None] >= jnp.cumsum(seq_lengths[0])[None, :]).astype(jnp.int32), axis=1
    )
    allowed = (seq_ids[:, None] == seq_ids[None, :]) & (places[:, None] >= places[None, :])
    qkv = (
        jnp.dot(hidden_one, qkv_weight, preferred_element_type=F32)
        .astype(LOW)
        .reshape(count, heads_here, 3, HD)
    )
    queries, key_rows, value_rows = qkv[:, :, 0, :], qkv[:, :, 1, :], qkv[:, :, 2, :]
    mixed, log_total = attention_forward(queries, key_rows, value_rows, allowed, score_scale)
    attn_part = lax.dot_general(mixed, attn_weight, NT_DIMS, preferred_element_type=F32)

    flat_picks = value_picks.reshape(count, MH * PICKS)
    sums = [
        ((cols - 1, count, width), LOW),
        ((cols - 1, count, width), LOW),
        ((8, count), F32),
        ((cols, 8, count), F32),
    ]
    hidden_two, resid, factor_two, full_cot, weights_two, key_table = remote_call(
        norm_kernel,
        rows,
        cols,
        1,
        rows - 1 + 4 * (cols - 1) + 3 * rows,
        [
            attn_part,
            dealt_own,
            gain_two,
            cotangent,
            send_row,
            recv_col,
            shard_two,
            sub_keys.astype(LOW),
        ],
        [
            ((count, D), LOW),
            ((count, width), F32),
            ((count, LANES), F32),
            ((count, D), LOW),
            ((D, shard_two.shape[1]), LOW),
            ((halves, NK, QD), LOW),
        ],
        swap + sums,
    )
    half_ids = col_index * halves + jnp.arange(halves, dtype=jnp.int32)
    head = half_ids[0] // 2
    head_picks = lax.dynamic_index_in_dim(value_picks, head, 1, keepdims=False)
    sub_index = jnp.concatenate(
        [
            jnp.where(half_ids[h] % 2 == 0, head_picks // NK, head_picks % NK)
            for h in range(halves)
        ],
        axis=1,
    )
    padded_index = jnp.pad(sub_index, ((0, 0), (0, LANES - halves * PICKS)))
    mem_queries, gate, grad_mixed, grad_memory, score_part = plain_call(
        functools.partial(middle_kernel, halves),
        [hidden_two, weights_two, key_table, full_cot, padded_index],
        [
            ((count, depth), LOW),
            ((count, width), F32),
            ((count, width), F32),
            ((count, width), LOW),
            ((halves * PICKS, count), F32),
        ],
    )
    half = rows // 2
    pick_weights, memory, grad_pick, grad_table = memory_call(
        rows,
        cols,
        2,
        score_part,
        (flat_picks - 32768).astype(jnp.int16),
        grad_memory,
        value_table,
    )
    own_weights = lax.dynamic_slice_in_dim(pick_weights, head * PICKS, PICKS, 0)
    (grad_sub,) = plain_call(
        functools.partial(spread_kernel, halves),
        [own_weights, grad_pick, sub_index.T],
        [((count, halves * NK), LOW)],
    )
    sigmoid_gate = jax.nn.sigmoid(gate)
    mixed_two = (memory * gate * sigmoid_gate).astype(LOW)
    grad_gate = (
        grad_mixed * memory * sigmoid_gate * (1.0 + gate * (1.0 - sigmoid_gate))
    ).astype(LOW)
    memout_part = lax.dot_general(
        mixed_two, weights_two[:, depth + width :], NT_DIMS, preferred_element_type=F32
    )
    grad_sub = grad_sub.reshape(count, halves, NK)
    grad_queries = (
        jnp.einsum("tnj,njq->tnq", grad_sub, key_table, preferred_element_type=F32)
        .astype(LOW)
        .reshape(count, depth)
    )
    grad_keys = jnp.einsum(
        "tnj,tnq->njq",
        grad_sub,
        mem_queries.reshape(count, halves, QD),
        preferred_element_type=F32,
    )
    grad_both = jnp.concatenate([grad_queries, grad_gate], axis=1)
    hidden_two_part = lax.dot_general(
        grad_both, weights_two[:, : depth + width], NT_DIMS, preferred_element_type=F32
    )
    grad_two = jnp.concatenate(
        [
            jnp.einsum("tD,tm->Dm", hidden_two, grad_both, preferred_element_type=F32),
            jnp.einsum("tD,tc->Dc", full_cot, mixed_two, preferred_element_type=F32),
        ],
        axis=1,
    )
    own_cot = lax.dynamic_slice_in_dim(full_cot, col_index * width, width, 1)
    grad_low, grad_resid, output, own_two, own_keys, gain_two_part = remote_call(
        back_two_kernel,
        rows,
        cols,
        4,
        4 * (cols - 1) + rows - 1 + 2 * (half + half - 1),
        [
            hidden_two_part,
            memout_part,
            resid,
            factor_two,
            gain_two,
            own_cot,
            recv_row,
            send_col,
            grad_two,
            grad_keys,
        ],
        [
            ((count, D), LOW),
            ((count, width), F32),
            ((count, width), F32),
            (shard_two.shape, F32),
            (sub_keys.shape, F32),
            ((8, width), F32),
        ],
        [
            ((cols - 1, count, width), LOW),
            ((cols - 1, count, width), LOW),
            *sums,
            *swap,
            ((half,) + shard_two.shape, F32),
            ((half - 1,) + shard_two.shape, LOW),
            ((half - 1,) + shard_two.shape, LOW),
            ((half,) + sub_keys.shape, F32),
            ((half - 1,) + sub_keys.shape, LOW),
            ((half - 1,) + sub_keys.shape, LOW),
        ],
    )
    grad_heads = (
        jnp.dot(grad_low, attn_weight, preferred_element_type=F32)
        .astype(LOW)
        .reshape(count, heads_here, HD)
    )
    grad_qkv = (
        jnp.stack(
            attention_backward(
                queries, key_rows, value_rows, grad_heads, log_total, allowed, score_scale
            ),
            axis=2,
        )
        .astype(LOW)
        .reshape(count, heads_here * 3 * HD)
    )
    grad_one = jnp.concatenate(
        [
            jnp.einsum("tD,tm->Dm", hidden_one, grad_qkv, preferred_element_type=F32),
            jnp.einsum("tD,tc->Dc", grad_low, mixed, preferred_element_type=F32),
        ],
        axis=1,
    )
    hidden_one_part = lax.dot_general(grad_qkv, qkv_weight, NT_DIMS, preferred_element_type=F32)
    grad_tokens, own_one, gains = remote_call(
        back_one_kernel,
        rows,
        cols,
        5,
        2 * (cols - 1) + 2 * (rows - 1) + half + half - 1,
        [
            hidden_one_part,
            dealt_own,
            jnp.broadcast_to(factor_one, (count, LANES)),
            gain_one,
            grad_resid,
            recv_row,
            send_col,
            grad_one,
            gain_two_part,
        ],
        [((count, width), F32), (shard_one.shape, F32), ((8, width), F32)],
        [
            *sums,
            *swap,
            ((half,) + shard_one.shape, F32),
            ((half - 1,) + shard_one.shape, LOW),
            ((half - 1,) + shard_one.shape, LOW),
            ((8, width), F32),
            ((rows, 8, width), F32),
        ],
    )
    gain_span = width // rows
    gain_one_grad = lax.dynamic_slice_in_dim(gains[0], row_index * gain_span, gain_span)
    gain_two_grad = lax.dynamic_slice_in_dim(gains[1], row_index * gain_span, gain_span)
    return (
        output,
        grad_tokens,
        gain_one_grad,
        own_one[:, : 3 * width],
        own_one[:, 3 * width :].T,
        gain_two_grad,
        own_two[:, :depth],
        own_keys,
        grad_table.T,
        own_two[:, depth : depth + width],
        own_two[:, depth + width :].T,
    )


def solution(mesh):
    return jax.shard_map(
        per_device,
        mesh=mesh,
        in_specs=(
            P("row", "col"),
            P("row", "col"),
            P(),
            P("row", None),
            P("row", None, None),
            P("col"),
            P("row", "col"),
            P("col", "row"),
            P("col"),
            P("row", "col"),
            P("col", "row", None),
            P("row", "col"),
            P("row", "col"),
            P("col", "row"),
        ),
        out_specs=(
            P("row", "col"),
            P("row", "col"),
            P(("col", "row")),
            P("row", "col"),
            P("col", "row"),
            P(("col", "row")),
            P("row", "col"),
            P("col", "row", None),
            P("row", "col"),
            P("row", "col"),
            P("col", "row"),
        ),
        check_vma=False,
    )
```

```python
import functools

import jax
import jax.numpy as jnp
from jax import lax
from jax.experimental import pallas as pl
from jax.experimental.pallas import tpu as pltpu
from jax.sharding import PartitionSpec as P

D = 1024
HD = 64
MH = 4
QD = 512
NK = 256
PICKS = 32
LANES = 128
EPS = 1e-05
MASKED = -1e30
F32 = jnp.float32
LOW = jnp.bfloat16
MESH = pl.DeviceIdType.MESH
NT_DIMS = (((1,), (1,)), ((), ()))
VMEM_SPEC = pl.BlockSpec(memory_space=pltpu.VMEM)
VMEM_BYTES = 60 * 2**20


def flip(index, mask):
    bit = 1
    while bit <= mask:
        if mask & bit:
            index = index + bit - 2 * bit * (index // bit % 2)
        bit *= 2
    return index


def cross(index, mask, size):
    total, bit = 0, 1
    while bit < size:
        a, b = index // bit % 2, mask // bit % 2
        total = total + bit * (a + b - 2 * a * b)
        bit *= 2
    return total


class Net:
    def __init__(self, rows, cols, sends, recvs):
        self.rows, self.cols = rows, cols
        self.row, self.col = lax.axis_index("row"), lax.axis_index("col")
        self.sends, self.recvs, self.used = sends, recvs, 0
        self.pending = []

    def place(self, row_k, col_k):
        return (flip(self.row, row_k), flip(self.col, col_k))

    def meet(self, row_ks, col_ks):
        barrier = pltpu.get_barrier_semaphore()
        places = [self.place(k, 0) for k in row_ks] + [self.place(0, k) for k in col_ks]
        for place in places:
            pl.semaphore_signal(barrier, inc=1, device_id=place, device_id_type=MESH)
        pl.semaphore_wait(barrier, len(places))

    def copy(self, src, dst, number, row_k=0, col_k=0):
        assert number < self.sends.shape[0]
        return pltpu.make_async_remote_copy(
            src_ref=src,
            dst_ref=dst,
            send_sem=self.sends.at[number],
            recv_sem=self.recvs.at[number],
            device_id=self.place(row_k, col_k),
            device_id_type=MESH,
        )

    def send(self, src, dst, row_k=0, col_k=0):
        copy = self.copy(src, dst, self.used, row_k, col_k)
        copy.start()
        self.used += 1
        self.pending.append(copy)
        return copy

    def drain(self):
        for copy in self.pending:
            copy.wait_send()

    def gather_start(self, src, view, first=True):
        copies = [self.send(src, view(self.row), row_k=2 * j) for j in range(1, self.rows // 2)]
        return copies, self.send(src, view(self.row), row_k=1)

    def gather_pass(self, view, started):
        copies, sibling = started
        passed = []
        for j, copy in enumerate(copies):
            copy.wait_recv()
            there = flip(self.row, 2 * (j + 1))
            passed.append(self.send(view(there), view(there), row_k=1))
        return [sibling] + passed

    def scatter_start(self, view, across):
        twin = flip(self.row, 1)
        return [
            self.send(view(flip(twin, 2 * j)), across.at[j], row_k=1)
            for j in range(self.rows // 2)
        ]

    def scatter_pass(self, view, across, started, outgoing, incoming):
        moved = []
        for j in range(1, self.rows // 2):
            started[j].wait_recv()
            block = view(flip(self.row, 2 * j))[...] + across[j]
            outgoing[j - 1] = block.astype(outgoing.dtype)
            moved.append(self.send(outgoing.at[j - 1], incoming.at[j - 1], row_k=2 * j))
        return moved

    def scatter_end(self, view, across, started, incoming, moved):
        started[0].wait_recv()
        total = view(self.row)[...] + across[0]
        for j, copy in enumerate(moved):
            copy.wait_recv()
            total = total + incoming[j].astype(F32)
        return total

    def columns_start(self, view):
        return [self.send(view(self.col), view(self.col), col_k=k) for k in range(1, self.cols)]


def wait_all(copies):
    for copy in copies:
        copy.wait_recv()


def rows_of(ref, count):
    return lambda index: ref.at[pl.ds(pl.multiple_of(index * count, count), count), :]


def columns_of(ref, count):
    return lambda index: ref.at[:, pl.ds(pl.multiple_of(index * count, count), count)]


def one_hot_rows(positions, slots):
    places = lax.broadcasted_iota(jnp.int32, (positions.shape[0], slots), 1)
    return jnp.where(positions == places, 1.0, 0.0).astype(LOW)


def one_hot_columns(positions, slots):
    places = lax.broadcasted_iota(jnp.int32, (slots, positions.shape[1]), 0)
    return jnp.where(positions == places, 1.0, 0.0).astype(LOW)


def pack_for_rows(net, packed, values, positions):
    slots = packed.shape[0]
    packed[...] = jnp.dot(
        one_hot_columns(positions, slots), values, preferred_element_type=F32
    ).astype(LOW)


def exchange_start(net, packed, got, capacity):
    mine = rows_of(got, capacity)
    theirs = rows_of(packed, capacity)
    copies = [
        net.send(theirs(flip(net.row, k)), mine(net.row), row_k=k) for k in range(1, net.rows)
    ]
    mine(net.row)[...] = theirs(net.row)[...]
    return copies


def unpack(got, positions):
    return jnp.dot(
        one_hot_rows(positions, got.shape[0]), got[...], preferred_element_type=F32
    )


def share_sums(net, sums, mine, theirs):
    tokens = sums.shape[0]
    mine[...] = jnp.broadcast_to(sums, (tokens, LANES)).T[:8]
    copies = [net.send(mine, theirs.at[k], col_k=k) for k in range(1, net.cols)]
    wait_all(copies)
    total = mine[...]
    for k in range(1, net.cols):
        total = total + theirs[k]
    return jnp.broadcast_to(total[:1], (LANES, tokens)).T


def widen(lanes, width):
    return jnp.concatenate([lanes] * (width // LANES), axis=1)


def reduce_start(net, part, outgoing, incoming):
    width = part.shape[1] // net.cols
    view = columns_of(part, width)
    copies = []
    for k in range(1, net.cols):
        outgoing[k - 1] = view(flip(net.col, k))[...].astype(LOW)
        copies.append(net.send(outgoing.at[k - 1], incoming.at[k - 1], col_k=k))
    return copies


def reduce_end(net, part, incoming, copies):
    total = columns_of(part, part.shape[1] // net.cols)(net.col)[...].astype(F32)
    for k, copy in enumerate(copies):
        copy.wait_recv()
        total = total + incoming[k].astype(F32)
    return total


def deal_kernel(
    rows, cols, tokens_ref, send_row, recv_col, shard, full, weights, packed, got, sends, recvs
):
    net = Net(rows, cols, sends, recvs)
    capacity = packed.shape[0] // rows
    pack_for_rows(net, packed, tokens_ref[...], send_row[...])
    net.meet(range(1, rows), range(1, cols))
    copies = exchange_start(net, packed, got, capacity)
    count = shard.shape[0]
    place = rows_of(weights, count)
    gather = net.gather_start(shard, place)
    place(net.row)[...] = shard[...]
    wait_all(copies)
    mine = columns_of(full, tokens_ref.shape[1])
    mine(net.col)[...] = unpack(got, recv_col[...]).astype(LOW)
    spread = net.columns_start(mine)
    wait_all(net.gather_pass(place, gather))
    wait_all(spread)
    net.drain()


def norm_kernel(
    rows,
    cols,
    part,
    dealt,
    gain,
    cot,
    send_row,
    recv_col,
    shard,
    keys,
    hidden,
    resid,
    factor,
    full,
    weights,
    key_table,
    packed,
    got,
    outgoing,
    incoming,
    mine,
    theirs,
    sends,
    recvs,
):
    net = Net(rows, cols, sends, recvs)
    capacity = packed.shape[0] // rows
    width = dealt.shape[1]
    net.meet(range(1, rows), range(1, cols))
    reduce = reduce_start(net, part, outgoing, incoming)
    pack_for_rows(net, packed, cot[...], send_row[...])
    copies = exchange_start(net, packed, got, capacity)
    place = rows_of(weights, shard.shape[0])
    gather = net.gather_start(shard, place)
    span = keys.shape[1]
    key_place = lambda index: key_table.at[:, pl.ds(pl.multiple_of(index * span, span), span), :]
    key_gather = net.gather_start(keys, key_place)
    place(net.row)[...] = shard[...]
    key_place(net.row)[...] = keys[...]
    values = dealt[...] + reduce_end(net, part, incoming, reduce)
    resid[...] = values
    square = share_sums(net, jnp.sum(values * values, axis=1, keepdims=True), mine, theirs)
    scale = lax.rsqrt(square / D + EPS)
    factor[...] = scale
    own = columns_of(hidden, width)
    own(net.col)[...] = (resid[...] * widen(scale, width) * gain[...]).astype(LOW)
    spread = net.columns_start(own)
    wait_all(copies)
    own_cot = columns_of(full, width)
    own_cot(net.col)[...] = unpack(got, recv_col[...]).astype(LOW)
    cot_spread = net.columns_start(own_cot)
    left = net.gather_pass(place, gather)
    left += net.gather_pass(key_place, key_gather)
    wait_all(spread)
    wait_all(cot_spread)
    wait_all(left)
    net.drain()


def norm_grad(net, grad_hidden, values, scale, gain, mine, theirs):
    width = values.shape[1]
    scaled = grad_hidden * gain
    inner = share_sums(net, jnp.sum(scaled * values, axis=1, keepdims=True), mine, theirs)
    wide = widen(scale, width)
    grads = wide * scaled - values * (wide * wide * wide) * widen(inner, width) / D
    grad_gain = jnp.sum(grad_hidden * values * wide, axis=0, keepdims=True)
    return grads, grad_gain


def project_start(net, left, weights, outgoing, incoming):
    width = outgoing.shape[2]

    def block(col):
        rows = rows_of(weights, width)(col)[...]
        return lax.dot_general(left, rows, NT_DIMS, preferred_element_type=F32)

    copies = []
    for k in range(1, net.cols):
        outgoing[k - 1] = block(flip(net.col, k)).astype(LOW)
        copies.append(net.send(outgoing.at[k - 1], incoming.at[k - 1], col_k=k))
    return block(net.col), copies


def project_end(total, incoming, copies):
    for k, copy in enumerate(copies):
        copy.wait_recv()
        total = total + incoming[k].astype(F32)
    return total


def attention_scores(qkv, head, ids_col, ids_row):
    parts = [qkv[:, (3 * head + j) * HD : (3 * head + j + 1) * HD] for j in range(3)]
    scores = lax.dot_general(parts[0], parts[1], NT_DIMS, preferred_element_type=F32) * HD ** (
        -0.5
    )
    asks = lax.broadcasted_iota(jnp.int32, scores.shape, 0)
    offers = lax.broadcasted_iota(jnp.int32, scores.shape, 1)
    allowed = (ids_col == ids_row) & (asks >= offers)
    scores = jnp.where(allowed, scores, MASKED)
    shifted = jnp.exp(scores - jnp.max(scores, axis=1, keepdims=True))
    return parts, shifted / jnp.sum(shifted, axis=1, keepdims=True)


def spread_picks(halves, weights, dw, index, out):
    tokens = weights.shape[1]
    change = dw[...]
    share = weights[...]
    grad = share * (change - jnp.sum(share * change, axis=0, keepdims=True))
    block = 128
    places = lax.broadcasted_iota(jnp.int32, (NK, block), 0)
    for h in range(halves):
        for b in range(tokens // block):
            columns = slice(b * block, (b + 1) * block)
            total = jnp.zeros((NK, block), F32)
            for k in range(PICKS):
                row = index[h * PICKS + k : h * PICKS + k + 1, columns]
                total = total + jnp.where(places == row, grad[k : k + 1, columns], 0.0)
            out[columns, h * NK : (h + 1) * NK] = total.T.astype(LOW)


def back_kernel(
    rows,
    cols,
    halves,
    share,
    dw,
    index,
    memory,
    gate,
    grad_mixed,
    queries,
    hidden_two,
    cot,
    weights_two,
    keys,
    resid,
    factor_two,
    gain_two,
    recv_row,
    send_col,
    qkv,
    mixed,
    ids_col,
    ids_row,
    hidden_one,
    weights_one,
    dealt,
    factor_one,
    gain_one,
    output,
    grad_tokens,
    own_one,
    own_two,
    own_keys,
    gains,
    grad_sub,
    both,
    mixed_two,
    grad_two,
    grad_keys,
    grad_low,
    grad_resid,
    grad_qkv,
    grad_one,
    one_outgoing,
    one_incoming,
    res_outgoing,
    res_incoming,
    two_outgoing,
    two_incoming,
    mine,
    theirs,
    mine_one,
    theirs_one,
    packed,
    got,
    packed_one,
    got_one,
    across_two,
    two_out,
    two_in,
    across_keys,
    keys_out,
    keys_in,
    across_one,
    one_out,
    one_in,
    my_gains,
    their_gains,
    sends,
    recvs,
):
    net = Net(rows, cols, sends, recvs)
    capacity = packed.shape[0] // rows
    width = resid.shape[1]
    depth = halves * QD
    net.meet(range(1, rows), range(1, cols))
    spread_picks(halves, share, dw, index, grad_sub)
    for h in range(halves):
        both[:, h * QD : (h + 1) * QD] = jnp.dot(
            grad_sub[:, h * NK : (h + 1) * NK], keys[h], preferred_element_type=F32
        ).astype(LOW)
    open_gate, back, read = gate[...], grad_mixed[...], memory[...]
    sigmoid = jax.nn.sigmoid(open_gate)
    both[:, depth:] = (back * read * sigmoid * (1.0 + open_gate * (1.0 - sigmoid))).astype(LOW)
    mixed_two[...] = (read * open_gate * sigmoid).astype(LOW)
    own_part, reduce_two = project_start(
        net, both[...], weights_two.at[:, : depth + width], two_outgoing, two_incoming
    )
    hidden_t = hidden_two[...].T
    grad_two[:, : depth + width] = jnp.dot(hidden_t, both[...], preferred_element_type=F32)
    grad_two[:, depth + width :] = jnp.dot(
        cot[...].T, mixed_two[...], preferred_element_type=F32
    )
    for h in range(halves):
        grad_keys[h] = jnp.dot(
            grad_sub[:, h * NK : (h + 1) * NK].T,
            queries[:, h * QD : (h + 1) * QD],
            preferred_element_type=F32,
        )
    view_two = rows_of(grad_two, own_two.shape[0])
    span = own_keys.shape[1]
    view_keys = lambda at: grad_keys.at[:, pl.ds(pl.multiple_of(at * span, span), span), :]
    started_two = net.scatter_start(view_two, across_two)
    started_keys = net.scatter_start(view_keys, across_keys)
    moved_two = net.scatter_pass(view_two, across_two, started_two, two_out, two_in)
    moved_keys = net.scatter_pass(view_keys, across_keys, started_keys, keys_out, keys_in)
    grad_hidden = project_end(own_part, two_incoming, reduce_two)
    grads, gain_two_sum = norm_grad(
        net, grad_hidden, resid[...], factor_two[...], gain_two[...], mine, theirs
    )
    own_cot = columns_of(cot, width)(net.col)[...]
    grads = grads + own_cot.astype(F32)
    grad_resid[...] = grads
    own = columns_of(grad_low, width)
    own(net.col)[...] = grads.astype(LOW)
    spread = net.columns_start(own)
    wait_all(spread)
    own_res, reduce_res = project_start(
        net, mixed_two[...], weights_two.at[:, depth + width :], res_outgoing, res_incoming
    )
    grad_heads = jnp.dot(
        grad_low[...], weights_one[:, 3 * width :], preferred_element_type=F32
    ).astype(LOW)
    for head in range(width // HD):
        (query, key, value), probs = attention_scores(qkv, head, ids_col[...], ids_row[...])
        grad_out = grad_heads[:, head * HD : (head + 1) * HD]
        grad_prob = lax.dot_general(grad_out, value, NT_DIMS, preferred_element_type=F32)
        inner = jnp.sum(probs * grad_prob, axis=1, keepdims=True)
        grad_score = (probs * (grad_prob - inner)).astype(LOW)
        pieces = (
            jnp.dot(grad_score, key, preferred_element_type=F32) * HD ** (-0.5),
            jnp.dot(grad_score.T, query, preferred_element_type=F32) * HD ** (-0.5),
            jnp.dot(probs.astype(LOW).T, grad_out, preferred_element_type=F32),
        )
        for j in range(3):
            grad_qkv[:, (3 * head + j) * HD : (3 * head + j + 1) * HD] = pieces[j].astype(LOW)
    own_part, reduce_one = project_start(
        net, grad_qkv[...], weights_one.at[:, : 3 * width], one_outgoing, one_incoming
    )
    grad_one[:, : 3 * width] = jnp.dot(
        hidden_one[...].T, grad_qkv[...], preferred_element_type=F32
    )
    grad_one[:, 3 * width :] = jnp.dot(grad_low[...].T, mixed[...], preferred_element_type=F32)
    view_one = rows_of(grad_one, own_one.shape[0])
    started_one = net.scatter_start(view_one, across_one)
    block = resid[...] + project_end(own_res, res_incoming, reduce_res)
    pack_for_rows(net, packed, block.astype(LOW), recv_row[...])
    copies = exchange_start(net, packed, got, capacity)
    moved_one = net.scatter_pass(view_one, across_one, started_one, one_out, one_in)
    grad_hidden = project_end(own_part, one_incoming, reduce_one)
    grads, gain_one_sum = norm_grad(
        net, grad_hidden, dealt[...], factor_one[...], gain_one[...], mine_one, theirs_one
    )
    grads = grads + grad_resid[...]
    pack_for_rows(net, packed_one, grads.astype(LOW), recv_row[...])
    last = exchange_start(net, packed_one, got_one, capacity)
    places = lax.broadcasted_iota(jnp.int32, my_gains.shape, 0)
    my_gains[...] = jnp.where(places == 0, gain_one_sum, gain_two_sum)
    gain_copies = [net.send(my_gains, their_gains.at[k], row_k=k) for k in range(1, rows)]
    own_two[...] = net.scatter_end(view_two, across_two, started_two, two_in, moved_two)
    own_keys[...] = net.scatter_end(view_keys, across_keys, started_keys, keys_in, moved_keys)
    wait_all(copies)
    output[...] = unpack(got, send_col[...])
    own_one[...] = net.scatter_end(view_one, across_one, started_one, one_in, moved_one)
    total = my_gains[...]
    for k, copy in enumerate(gain_copies):
        copy.wait_recv()
        total = total + their_gains[k + 1]
    gains[...] = total
    wait_all(last)
    grad_tokens[...] = unpack(got_one, send_col[...])
    net.drain()


def remote_call(kernel, rows, cols, number, copies, ins, outs, scratch, *sizes):
    return pl.pallas_call(
        functools.partial(kernel, rows, cols, *sizes),
        out_shape=[jax.ShapeDtypeStruct(shape, dtype) for shape, dtype in outs],
        in_specs=[VMEM_SPEC] * len(ins),
        out_specs=[VMEM_SPEC] * len(outs),
        scratch_shapes=[pltpu.VMEM(shape, dtype) for shape, dtype in scratch]
        + [pltpu.SemaphoreType.DMA((copies,)), pltpu.SemaphoreType.DMA((copies,))],
        compiler_params=pltpu.CompilerParams(
            collective_id=number, has_side_effects=True, vmem_limit_bytes=VMEM_BYTES
        ),
    )(*ins)


def plain_call(kernel, ins, outs):
    return pl.pallas_call(
        kernel,
        out_shape=[jax.ShapeDtypeStruct(shape, dtype) for shape, dtype in outs],
        in_specs=[VMEM_SPEC] * len(ins),
        out_specs=[VMEM_SPEC] * len(outs),
        compiler_params=pltpu.CompilerParams(vmem_limit_bytes=VMEM_BYTES),
    )(*ins)


def middle_kernel(
    halves, hidden, weights, keys, cot, index, queries, gate, grad_mixed, grad_memory, part
):
    width = gate.shape[1]
    depth = halves * QD
    for h in range(halves):
        columns = slice(h * QD, (h + 1) * QD)
        queries[:, columns] = jnp.dot(
            hidden[...], weights[:, columns], preferred_element_type=F32
        ).astype(LOW)
    open_gate = jnp.dot(
        hidden[...], weights[:, depth : depth + width], preferred_element_type=F32
    )
    gate[...] = open_gate
    back = jnp.dot(cot[...], weights[:, depth + width :], preferred_element_type=F32)
    grad_mixed[...] = back
    grad_memory[...] = (back * (open_gate * jax.nn.sigmoid(open_gate))).astype(LOW)
    lanes = lax.broadcasted_iota(jnp.int32, index.shape, 1)
    low_index = index[...] % LANES
    upper = index[...] >= LANES
    found = jnp.zeros(index.shape, F32)
    for h in range(halves):
        scores = lax.dot_general(
            queries[:, h * QD : (h + 1) * QD], keys[h], NT_DIMS, preferred_element_type=F32
        )
        first = jnp.take_along_axis(scores[:, :LANES], low_index, axis=1)
        second = jnp.take_along_axis(scores[:, LANES:], low_index, axis=1)
        found = jnp.where(lanes // PICKS == h, jnp.where(upper, second, first), found)
    part[...] = found.T[: halves * PICKS]


def memory_kernel(
    rows,
    cols,
    part,
    own_picks,
    own_grads,
    table_f32,
    weights,
    memory,
    dw,
    gacc,
    table,
    stage,
    scores,
    picks_of,
    grads_of,
    low_of,
    dense,
    hi_ref,
    lo_ref,
    wide_ref,
    found_ref,
    mem_all,
    mem_twin,
    mem_out,
    mem_in,
    dw_all,
    dw_twin,
    dw_out,
    dw_in,
    dw_cols,
    stage_sems,
    sends,
    recvs,
):
    net = Net(rows, cols, sends, recvs)
    half = rows // 2
    tok_block = own_picks.shape[0]
    span_rows, width = table.shape
    spans = span_rows // LANES
    pitch = spans + 8
    iters = 4
    per_tok = tok_block // iters
    per_span = spans // iters

    grads_at = rows_of(grads_of, tok_block)
    picks_at = rows_of(picks_of, tok_block)
    low_at = lambda index: low_of.at[index]
    views = (grads_at, picks_at, low_at)
    first_pass = 3 * half
    first_twin = first_pass + 3 * half
    first_out = first_twin + 2 * half
    first_col = first_out + 2 * half

    def gather(a, j):
        mine = views[a](net.row)
        return net.copy(mine, mine, 3 * j + a, row_k=2 * j if j else 1)

    def passing(a, j):
        there = views[a](flip(net.row, 2 * j))
        return net.copy(there, there, first_pass + 3 * j + a, row_k=1)

    def twin(a, j):
        src, dst = ((mem_all, mem_twin), (dw_all, dw_twin))[a]
        return net.copy(src.at[2 * j + 1], dst.at[j], first_twin + 2 * j + a, row_k=1)

    def outward(a, j):
        src, dst = ((mem_out, mem_in), (dw_out, dw_in))[a]
        return net.copy(src.at[j - 1], dst.at[j - 1], first_out + 2 * j + a, row_k=2 * j)

    head = lambda col: pl.ds(pl.multiple_of(col * MH // cols * PICKS, PICKS), PICKS)

    def score_copy(k):
        return net.copy(part, rows_of(scores, part.shape[0])(net.col), first_col + k, col_k=k)

    def dw_copy(k):
        return net.copy(
            dw_all.at[0, head(flip(net.col, k)), :],
            dw_cols.at[k - 1],
            first_col + cols + k,
            col_k=k,
        )

    stage_rows = stage.shape[1]

    def stage_copy(i):
        source = table_f32.at[pl.ds(i * stage_rows, stage_rows), :]
        return pltpu.make_async_copy(source, stage.at[i % 2], stage_sems.at[i % 2])

    stage_copy(0).start()
    net.meet([1] + [2 * j for j in range(1, half)], range(1, cols))
    for k in range(1, cols):
        score_copy(k).start()
    grads_at(net.row)[...] = own_grads[...]
    picks_at(net.row)[...] = own_picks[...]
    for j in range(half):
        for a in range(2):
            gather(a, j).start()
    rows_of(scores, part.shape[0])(net.col)[...] = part[...]
    for i in range(span_rows // stage_rows):
        if (i + 1) * stage_rows < span_rows:
            stage_copy(i + 1).start()
        stage_copy(i).wait()
        table[i * stage_rows : (i + 1) * stage_rows, :] = stage[i % 2].astype(LOW)
    for k in range(1, cols):
        score_copy(k).wait_recv()
    for m in range(MH):
        score = (
            scores[2 * m * PICKS : (2 * m + 1) * PICKS]
            + scores[(2 * m + 1) * PICKS : (2 * m + 2) * PICKS]
        )
        shifted = jnp.exp(score - jnp.max(score, axis=0, keepdims=True))
        weights[m * PICKS : (m + 1) * PICKS] = shifted / jnp.sum(shifted, axis=0, keepdims=True)
    low_at(net.row)[...] = weights[...].astype(LOW)
    for j in range(half):
        gather(2, j).start()
    gacc[...] = jnp.zeros_like(gacc)
    mem_all[...] = jnp.zeros_like(mem_all)

    def one_block(step, _):
        k = jnp.where(step == 0, 0, jnp.where(step == rows - 1, 1, step + 1))
        there = cross(net.row, k, rows)
        for j in range(1, half):

            @pl.when(step == 2 * j - 1)
            def _():
                for a in range(3):
                    gather(a, j).wait_recv()
                    passing(a, j).start()

            @pl.when(step == 2 * j)
            def _():
                for a in range(3):
                    passing(a, j).wait_recv()

        @pl.when(step == rows - 1)
        def _():
            for a in range(3):
                gather(a, 0).wait_recv()

        picks = picks_at(there)[...].astype(jnp.int32) + 32768
        hi_ref[...] = (picks // LANES - net.row * spans).astype(F32)
        lo_ref[...] = (picks % LANES).astype(F32)
        wide_ref[...] = low_of[there].astype(F32).T
        places_lo = lax.broadcasted_iota(jnp.int32, (LANES, LANES), 0).astype(F32).astype(LOW)
        places_hi = lax.broadcasted_iota(jnp.int32, (spans, LANES), 0).astype(F32).astype(LOW)
        ones = jnp.ones((LANES, LANES), LOW)
        zeros = jnp.zeros((LANES, LANES), LOW)
        blank = jnp.zeros((spans, LANES), LOW)
        grads = grads_at(there)[...]
        grads_t = grads.T
        found_ref[...] = jnp.zeros_like(found_ref)
        lo_int = picks % LANES
        hi_all = hi_ref[...]

        def token_pair(first):
            rights, lefts = [], []
            for token in (first, first + 1):
                lo_row = jnp.broadcast_to(lo_ref[pl.ds(token, 1), :], (LANES, LANES)).astype(LOW)
                hi_row = jnp.broadcast_to(hi_ref[pl.ds(token, 1), :], (spans, LANES)).astype(LOW)
                w_row = jnp.broadcast_to(wide_ref[pl.ds(token, 1), :], (spans, LANES)).astype(LOW)
                rights.append(jnp.where(lo_row == places_lo, ones, zeros))
                lefts.append(jnp.where(hi_row == places_hi, w_row, blank))
            right = jnp.concatenate(rights, axis=1)
            left = jnp.concatenate(
                [
                    jnp.concatenate([lefts[0], blank], axis=1),
                    jnp.concatenate([blank, lefts[1]], axis=1),
                ],
                axis=0,
            )
            both = lax.dot_general(left, right, NT_DIMS, preferred_element_type=F32)
            for j in range(2):
                dense[pl.ds(pl.multiple_of((first + j) * pitch, 8), spans), :] = both[
                    j * spans : (j + 1) * spans
                ]

        def build(it, _):
            for j in range(1, half):

                @pl.when((it == 1) & (step == 2 * j + 1))
                def _():
                    twin(0, j).wait_recv()
                    twin(1, j).wait_recv()
                    mem_out[j - 1] = (mem_all[2 * j] + mem_twin[j]).astype(LOW)
                    outward(0, j).start()
                    dw_out[j - 1] = dw_all[2 * j] + dw_twin[j]
                    outward(1, j).start()

            span = pl.ds(pl.multiple_of(it * per_span * LANES, LANES), per_span * LANES)
            products = lax.dot_general(
                grads, table[span, :], NT_DIMS, preferred_element_type=F32
            )
            found = found_ref[...]
            pairs = per_tok // 2 // per_span
            for j in range(per_span):
                picked = jnp.take_along_axis(
                    products[:, LANES * j : LANES * (j + 1)], lo_int, axis=1
                )
                found = jnp.where(hi_all == (it * per_span + j).astype(F32), picked, found)
                for u in range(pairs):
                    token_pair(it * per_tok + (j * pairs + u) * 2)
            found_ref[...] = found
            return 0

        lax.fori_loop(0, iters, build, 0)
        dw_all[k] = found_ref[...].T

        def multiply(it, _):
            span = pl.ds(pl.multiple_of(it * per_span * LANES, LANES), per_span * LANES)
            chosen = jnp.concatenate(
                [
                    dense[pl.ds(it * per_span + j, tok_block, stride=pitch), :].astype(LOW)
                    for j in range(per_span)
                ],
                axis=1,
            )
            mem_all[k] += jnp.dot(chosen, table[span, :], preferred_element_type=F32)
            gacc[:, span] += jnp.dot(grads_t, chosen, preferred_element_type=F32)
            return 0

        lax.fori_loop(0, iters, multiply, 0)
        for j in range(half):

            @pl.when(step == (2 * j if j else rows - 1))
            def _():
                twin(0, j).start()
                twin(1, j).start()

        return 0

    lax.fori_loop(0, rows, one_block, 0)
    twin(1, 0).wait_recv()
    total = dw_all[0] + dw_twin[0]
    for j in range(1, half):
        outward(1, j).wait_recv()
        total = total + dw_in[j - 1]
    dw_all[0] = total
    for k in range(1, cols):
        dw_copy(k).start()
    twin(0, 0).wait_recv()
    total = mem_all[0] + mem_twin[0]
    for j in range(1, half):
        outward(0, j).wait_recv()
        total = total + mem_in[j - 1].astype(F32)
    memory[...] = total
    total = dw_all[0, head(net.col), :]
    for k in range(1, cols):
        dw_copy(k).wait_recv()
        total = total + dw_cols[k - 1]
    dw[...] = total
    for k in range(1, cols):
        score_copy(k).wait_send()
        dw_copy(k).wait_send()
    for j in range(half):
        for a in range(3):
            gather(a, j).wait_send()
            if j:
                passing(a, j).wait_send()
        for a in range(2):
            twin(a, j).wait_send()
            if j:
                outward(a, j).wait_send()


def memory_call(rows, cols, number, part, picks, grads, table):
    tokens, count = picks.shape
    span_rows, width = table.shape
    half = rows // 2
    copies = 10 * half + 2 * cols
    vmem = pltpu.VMEM
    return pl.pallas_call(
        functools.partial(memory_kernel, rows, cols),
        in_specs=[VMEM_SPEC, VMEM_SPEC, VMEM_SPEC, pl.BlockSpec(memory_space=pl.ANY)],
        out_specs=[VMEM_SPEC] * 4,
        out_shape=[
            jax.ShapeDtypeStruct((count, tokens), F32),
            jax.ShapeDtypeStruct((tokens, width), F32),
            jax.ShapeDtypeStruct((PICKS, tokens), F32),
            jax.ShapeDtypeStruct((width, span_rows), F32),
        ],
        scratch_shapes=[
            vmem((span_rows, width), LOW),
            vmem((2, 1024, width), F32),
            vmem((2 * count, tokens), F32),
            vmem((rows * tokens, count), jnp.int16),
            vmem((rows * tokens, width), LOW),
            vmem((rows, count, tokens), LOW),
            vmem((tokens * (span_rows // LANES + 8), LANES), F32),
            vmem((tokens, count), F32),
            vmem((tokens, count), F32),
            vmem((tokens, count), F32),
            vmem((tokens, count), F32),
            vmem((rows, tokens, width), F32),
            vmem((half, tokens, width), F32),
            vmem((half - 1, tokens, width), LOW),
            vmem((half - 1, tokens, width), LOW),
            vmem((rows, count, tokens), F32),
            vmem((half, count, tokens), F32),
            vmem((half - 1, count, tokens), F32),
            vmem((half - 1, count, tokens), F32),
            vmem((cols - 1, PICKS, tokens), F32),
            pltpu.SemaphoreType.DMA((2,)),
            pltpu.SemaphoreType.DMA((copies,)),
            pltpu.SemaphoreType.DMA((copies,)),
        ],
        compiler_params=pltpu.CompilerParams(
            collective_id=number, has_side_effects=True, vmem_limit_bytes=63 * 2**20
        ),
    )(part, picks, grads, table)


def attention_forward(queries, key_rows, value_rows, allowed, score_scale):
    scores = (
        jnp.einsum("qhd,khd->hqk", queries, key_rows, preferred_element_type=F32) * score_scale
    )
    scores = jnp.where(allowed[None], scores, MASKED)
    row_max = jnp.max(scores, axis=2, keepdims=True)
    shifted_exp = jnp.exp(scores - row_max)
    row_total = jnp.sum(shifted_exp, axis=2, keepdims=True)
    weights_low = (shifted_exp / row_total).astype(LOW)
    weighted = jnp.einsum("hqk,khd->qhd", weights_low, value_rows, preferred_element_type=F32)
    mixed = weighted.astype(LOW).reshape(queries.shape[0], -1)
    return mixed


def per_device(
    tokens,
    cotangent,
    deal_order,
    seq_lengths,
    value_picks,
    norm1_gain,
    w_qkv,
    w_attn_out,
    norm2_gain,
    w_query,
    sub_keys,
    value_table,
    w_gate,
    w_mem_out,
):
    rows, cols = lax.axis_size("row"), lax.axis_size("col")
    row_index, col_index = lax.axis_index("row"), lax.axis_index("col")
    count, width = tokens.shape
    capacity = 2 * count // rows
    slots = rows * capacity
    shard_rows = w_qkv.shape[0]
    heads_here = width // HD
    halves = sub_keys.shape[0]
    depth = halves * QD
    score_scale = HD ** (-0.5)

    my_slots = lax.dynamic_slice_in_dim(deal_order, row_index * count, count)
    source = my_slots // count
    from_source = (source[:, None] == jnp.arange(rows, dtype=jnp.int32)[None, :]).astype(jnp.int32)
    earlier = jnp.cumsum(from_source, axis=0) - from_source
    recv_pos = source * capacity + jnp.sum(earlier * from_source, axis=1)
    owned = (deal_order // count == row_index).astype(jnp.int32).reshape(rows, count)
    rank = jnp.cumsum(owned, axis=1) - owned
    slot_pos = (jnp.arange(rows, dtype=jnp.int32)[:, None] * capacity + rank).reshape(-1)
    mine = (deal_order - row_index * count)[None, :] == jnp.arange(count, dtype=jnp.int32)[:, None]
    send_pos = jnp.sum(jnp.where(mine, slot_pos[None, :], 0), axis=1)
    send_row, send_col = send_pos[None, :], send_pos[:, None]
    recv_row, recv_col = recv_pos[None, :], recv_pos[:, None]

    shard_one = jnp.concatenate([w_qkv.astype(LOW), w_attn_out.astype(LOW).T], axis=1)
    shard_two = jnp.concatenate(
        [w_query.astype(LOW), w_gate.astype(LOW), w_mem_out.astype(LOW).T], axis=1
    )
    gain_one = norm1_gain.astype(LOW).astype(F32)[None, :]
    gain_two = norm2_gain.astype(LOW).astype(F32)[None, :]
    gain_all = lax.all_gather(norm1_gain.astype(LOW), "col", axis=0, tiled=True).astype(F32)
    swap = [((slots, width), LOW), ((slots, width), LOW)]

    full_tokens, weights_one = remote_call(
        deal_kernel,
        rows,
        cols,
        0,
        rows - 1 + cols - 1 + rows,
        [tokens, send_row, recv_col, shard_one],
        [((count, D), LOW), ((D, shard_one.shape[1]), LOW)],
        swap,
    )
    qkv_weight, attn_weight = weights_one[:, : 3 * width], weights_one[:, 3 * width :]
    dealt = full_tokens.astype(F32)
    factor_one = lax.rsqrt(jnp.mean(dealt * dealt, axis=1, keepdims=True) + EPS)
    hidden_one = (dealt * factor_one * gain_all).astype(LOW)
    dealt_own = lax.dynamic_slice_in_dim(dealt, col_index * width, width, 1)

    places = jnp.arange(count, dtype=jnp.int32)
    seq_ids = jnp.sum(
        (places[:, None] >= jnp.cumsum(seq_lengths[0])[None, :]).astype(jnp.int32), axis=1
    )
    allowed = (seq_ids[:, None] == seq_ids[None, :]) & (places[:, None] >= places[None, :])
    qkv = jnp.dot(hidden_one, qkv_weight, preferred_element_type=F32).astype(LOW)
    by_head = qkv.reshape(count, heads_here, 3, HD)
    queries, key_rows, value_rows = by_head[:, :, 0], by_head[:, :, 1], by_head[:, :, 2]
    mixed = attention_forward(queries, key_rows, value_rows, allowed, score_scale)
    attn_part = lax.dot_general(mixed, attn_weight, NT_DIMS, preferred_element_type=F32)

    flat_picks = value_picks.reshape(count, MH * PICKS)
    sums = [
        ((cols - 1, count, width), LOW),
        ((cols - 1, count, width), LOW),
        ((8, count), F32),
        ((cols, 8, count), F32),
    ]
    hidden_two, resid, factor_two, full_cot, weights_two, key_table = remote_call(
        norm_kernel,
        rows,
        cols,
        1,
        rows - 1 + 4 * (cols - 1) + 3 * rows,
        [
            attn_part,
            dealt_own,
            gain_two,
            cotangent,
            send_row,
            recv_col,
            shard_two,
            sub_keys.astype(LOW),
        ],
        [
            ((count, D), LOW),
            ((count, width), F32),
            ((count, LANES), F32),
            ((count, D), LOW),
            ((D, shard_two.shape[1]), LOW),
            ((halves, NK, QD), LOW),
        ],
        swap + sums,
    )
    half_ids = col_index * halves + jnp.arange(halves, dtype=jnp.int32)
    head = half_ids[0] // 2
    head_picks = lax.dynamic_index_in_dim(value_picks, head, 1, keepdims=False)
    sub_index = jnp.concatenate(
        [
            jnp.where(half_ids[h] % 2 == 0, head_picks // NK, head_picks % NK)
            for h in range(halves)
        ],
        axis=1,
    )
    padded_index = jnp.pad(sub_index, ((0, 0), (0, LANES - halves * PICKS)))
    mem_queries, gate, grad_mixed, grad_memory, score_part = plain_call(
        functools.partial(middle_kernel, halves),
        [hidden_two, weights_two, key_table, full_cot, padded_index],
        [
            ((count, depth), LOW),
            ((count, width), F32),
            ((count, width), F32),
            ((count, width), LOW),
            ((halves * PICKS, count), F32),
        ],
    )
    half = rows // 2
    pick_weights, memory, grad_pick, grad_table = memory_call(
        rows,
        cols,
        2,
        score_part,
        (flat_picks - 32768).astype(jnp.int16),
        grad_memory,
        value_table,
    )
    own_weights = lax.dynamic_slice_in_dim(pick_weights, head * PICKS, PICKS, 0)
    block = ((count, width), F32)
    moving = ((cols - 1, count, width), LOW)
    scattered = [
        [((half,) + shape, F32), ((half - 1,) + shape, LOW), ((half - 1,) + shape, LOW)]
        for shape in (shard_two.shape, sub_keys.shape, shard_one.shape)
    ]
    output, grad_tokens, own_one, own_two, own_keys, gains = remote_call(
        back_kernel,
        rows,
        cols,
        3,
        6 * (cols - 1) + 3 * (rows - 1) + 3 * (half + half - 1),
        [
            own_weights,
            grad_pick,
            sub_index.T,
            memory,
            gate,
            grad_mixed,
            mem_queries,
            hidden_two,
            full_cot,
            weights_two,
            key_table,
            resid,
            factor_two,
            gain_two,
            recv_row,
            send_col,
            qkv,
            mixed,
            seq_ids[:, None],
            seq_ids[None, :],
            hidden_one,
            weights_one,
            dealt_own,
            jnp.broadcast_to(factor_one, (count, LANES)),
            gain_one,
        ],
        [
            block,
            block,
            (shard_one.shape, F32),
            (shard_two.shape, F32),
            (sub_keys.shape, F32),
            ((8, width), F32),
        ],
        [
            ((count, halves * NK), LOW),
            ((count, depth + width), LOW),
            ((count, width), LOW),
            ((D, shard_two.shape[1]), F32),
            ((halves, NK, QD), F32),
            ((count, D), LOW),
            block,
            ((count, 3 * width), LOW),
            ((D, shard_one.shape[1]), F32),
            *[moving] * 6,
            *sums[2:],
            *sums[2:],
            *swap,
            *swap,
            *scattered[0],
            *scattered[1],
            *scattered[2],
            ((8, width), F32),
            ((rows, 8, width), F32),
        ],
        halves,
    )
    gain_span = width // rows
    gain_one_grad = lax.dynamic_slice_in_dim(gains[0], row_index * gain_span, gain_span)
    gain_two_grad = lax.dynamic_slice_in_dim(gains[1], row_index * gain_span, gain_span)
    return (
        output,
        grad_tokens,
        gain_one_grad,
        own_one[:, : 3 * width],
        own_one[:, 3 * width :].T,
        gain_two_grad,
        own_two[:, :depth],
        own_keys,
        grad_table.T,
        own_two[:, depth : depth + width],
        own_two[:, depth + width :].T,
    )


def solution(mesh):
    return jax.shard_map(
        per_device,
        mesh=mesh,
        in_specs=(
            P("row", "col"),
            P("row", "col"),
            P(),
            P("row", None),
            P("row", None, None),
            P("col"),
            P("row", "col"),
            P("col", "row"),
            P("col"),
            P("row", "col"),
            P("col", "row", None),
            P("row", "col"),
            P("row", "col"),
            P("col", "row"),
        ),
        out_specs=(
            P("row", "col"),
            P("row", "col"),
            P(("col", "row")),
            P("row", "col"),
            P("col", "row"),
            P(("col", "row")),
            P("row", "col"),
            P("col", "row", None),
            P("row", "col"),
            P("row", "col"),
            P("col", "row"),
        ),
        check_vma=False,
    )
```

```python
import functools

import jax
import jax.numpy as jnp
from jax import lax
from jax.experimental import pallas as pl
from jax.experimental.pallas import tpu as pltpu
from jax.sharding import PartitionSpec as P

D = 1024
HD = 64
MH = 4
QD = 512
NK = 256
PICKS = 32
LANES = 128
EPS = 1e-05
MASKED = -1e30
F32 = jnp.float32
LOW = jnp.bfloat16
MESH = pl.DeviceIdType.MESH
NT_DIMS = (((1,), (1,)), ((), ()))
VMEM_SPEC = pl.BlockSpec(memory_space=pltpu.VMEM)
VMEM_BYTES = 60 * 2**20


def flip(index, mask):
    bit = 1
    while bit <= mask:
        if mask & bit:
            index = index + bit - 2 * bit * (index // bit % 2)
        bit *= 2
    return index


def cross(index, mask, size):
    total, bit = 0, 1
    while bit < size:
        a, b = index // bit % 2, mask // bit % 2
        total = total + bit * (a + b - 2 * a * b)
        bit *= 2
    return total


class Net:
    def __init__(self, rows, cols, sends, recvs):
        self.rows, self.cols = rows, cols
        self.row, self.col = lax.axis_index("row"), lax.axis_index("col")
        self.sends, self.recvs, self.used = sends, recvs, 0
        self.pending = []

    def place(self, row_k, col_k):
        return (flip(self.row, row_k), flip(self.col, col_k))

    def greet(self, row_ks, col_ks):
        barrier = pltpu.get_barrier_semaphore()
        places = [self.place(k, 0) for k in row_ks] + [self.place(0, k) for k in col_ks]
        for place in places:
            pl.semaphore_signal(barrier, inc=1, device_id=place, device_id_type=MESH)
        return len(places)

    def meet(self, greeted):
        pl.semaphore_wait(pltpu.get_barrier_semaphore(), greeted)

    def copy(self, src, dst, number, row_k=0, col_k=0):
        assert number < self.sends.shape[0]
        return pltpu.make_async_remote_copy(
            src_ref=src,
            dst_ref=dst,
            send_sem=self.sends.at[number],
            recv_sem=self.recvs.at[number],
            device_id=self.place(row_k, col_k),
            device_id_type=MESH,
        )

    def send(self, src, dst, row_k=0, col_k=0):
        copy = self.copy(src, dst, self.used, row_k, col_k)
        copy.start()
        self.used += 1
        self.pending.append(copy)
        return copy

    def drain(self):
        for copy in self.pending:
            copy.wait_send()

    def gather_start(self, src, view, first=True):
        copies = [self.send(src, view(self.row), row_k=2 * j) for j in range(1, self.rows // 2)]
        return copies, self.send(src, view(self.row), row_k=1)

    def gather_pass(self, view, started):
        copies, sibling = started
        passed = []
        for j, copy in enumerate(copies):
            copy.wait_recv()
            there = flip(self.row, 2 * (j + 1))
            passed.append(self.send(view(there), view(there), row_k=1))
        return [sibling] + passed

    def scatter_start(self, view, across):
        twin = flip(self.row, 1)
        return [
            self.send(view(flip(twin, 2 * j)), across.at[j], row_k=1)
            for j in range(self.rows // 2)
        ]

    def scatter_pass(self, view, across, started, outgoing, incoming):
        moved = []
        for j in range(1, self.rows // 2):
            started[j].wait_recv()
            block = view(flip(self.row, 2 * j))[...] + across[j]
            outgoing[j - 1] = block.astype(outgoing.dtype)
            moved.append(self.send(outgoing.at[j - 1], incoming.at[j - 1], row_k=2 * j))
        return moved

    def scatter_end(self, view, across, started, incoming, moved):
        started[0].wait_recv()
        total = view(self.row)[...] + across[0]
        for j, copy in enumerate(moved):
            copy.wait_recv()
            total = total + incoming[j].astype(F32)
        return total

    def columns_start(self, view):
        return [self.send(view(self.col), view(self.col), col_k=k) for k in range(1, self.cols)]


def wait_all(copies):
    for copy in copies:
        copy.wait_recv()


def rows_of(ref, count):
    return lambda index: ref.at[pl.ds(pl.multiple_of(index * count, count), count), :]


def columns_of(ref, count):
    return lambda index: ref.at[:, pl.ds(pl.multiple_of(index * count, count), count)]


def one_hot_rows(positions, slots):
    places = lax.broadcasted_iota(jnp.int32, (positions.shape[0], slots), 1)
    return jnp.where(positions == places, 1.0, 0.0).astype(LOW)


def one_hot_columns(positions, slots):
    places = lax.broadcasted_iota(jnp.int32, (slots, positions.shape[1]), 0)
    return jnp.where(positions == places, 1.0, 0.0).astype(LOW)


def pack_for_rows(net, packed, values, positions):
    slots = packed.shape[0]
    packed[...] = jnp.dot(
        one_hot_columns(positions, slots), values, preferred_element_type=F32
    ).astype(LOW)


def exchange_start(net, packed, got, capacity):
    mine = rows_of(got, capacity)
    theirs = rows_of(packed, capacity)
    copies = [
        net.send(theirs(flip(net.row, k)), mine(net.row), row_k=k) for k in range(1, net.rows)
    ]
    mine(net.row)[...] = theirs(net.row)[...]
    return copies


def unpack(got, positions):
    return jnp.dot(
        one_hot_rows(positions, got.shape[0]), got[...], preferred_element_type=F32
    )


def share_sums(net, sums, mine, theirs):
    tokens = sums.shape[0]
    mine[...] = jnp.broadcast_to(sums, (tokens, LANES)).T[:8]
    copies = [net.send(mine, theirs.at[k], col_k=k) for k in range(1, net.cols)]
    wait_all(copies)
    total = mine[...]
    for k in range(1, net.cols):
        total = total + theirs[k]
    return jnp.broadcast_to(total[:1], (LANES, tokens)).T


def widen(lanes, width):
    return jnp.concatenate([lanes] * (width // LANES), axis=1)


def first_of(size, mask):
    earlier = lax.broadcasted_iota(jnp.int32, (size, size), 0)
    later = lax.broadcasted_iota(jnp.int32, (size, size), 1)
    triangle = jnp.where(earlier < later, 1.0, 0.0).astype(LOW)
    return jnp.dot(mask.astype(LOW), triangle, preferred_element_type=F32)


def find_places(rows, row, order, send_row, send_col, recv_row, recv_col):
    count = order.shape[1]
    capacity = 2 * count // rows
    owner = order[...] // count
    owned = jnp.where(owner == row, 1.0, 0.0)
    rank = first_of(count, owned)
    low_order = order[...].astype(F32).T
    tokens = lax.broadcasted_iota(jnp.int32, (count, count), 1).astype(F32)
    first = (row * count).astype(F32)
    sent = jnp.zeros((1, count), F32)
    pick = lax.broadcasted_iota(jnp.int32, (8, count), 0)
    for d in range(rows):
        match = jnp.where(low_order[:, d : d + 1] - first == tokens, 1.0, 0.0).astype(LOW)
        pair = jnp.where(pick == 0, rank[d : d + 1] * owned[d : d + 1], owned[d : d + 1])
        found = jnp.dot(pair.astype(LOW), match, preferred_element_type=F32)
        sent = sent + found[:1] + found[1:2] * (d * capacity)
    send_row[...] = sent.astype(jnp.int32)
    send_col[...] = jnp.broadcast_to(sent, (LANES, count)).T[:, :1].astype(jnp.int32)
    blocks = lax.broadcasted_iota(jnp.int32, (rows, count), 0)
    mine = jnp.sum(jnp.where(blocks == row, order[...], 0), axis=0, keepdims=True)
    source = mine // count
    came = jnp.where(source == lax.broadcasted_iota(jnp.int32, (LANES, count), 0), 1.0, 0.0)
    place = jnp.sum(first_of(count, came) * came, axis=0, keepdims=True)
    place = place + source.astype(F32) * capacity
    recv_row[...] = place.astype(jnp.int32)
    recv_col[...] = jnp.broadcast_to(place, (LANES, count)).T[:, :1].astype(jnp.int32)


def sequence_ids(lengths, count, axis):
    places = lax.broadcasted_iota(jnp.int32, (1, count) if axis else (count, 1), axis)
    end = jnp.zeros((1, 1), jnp.int32)
    ids = jnp.zeros(places.shape, jnp.int32)
    for j in range(lengths.shape[1]):
        end = end + lengths[:, j : j + 1]
        ids = ids + jnp.where(places >= end, 1, 0)
    return ids


def front_kernel(
    rows,
    cols,
    halves,
    order,
    picks,
    lengths,
    tokens_ref,
    cot,
    w_qkv,
    w_attn,
    w_query,
    w_gate,
    w_mem,
    sub_keys,
    norm_one,
    norm_two,
    send_row,
    send_col,
    recv_row,
    recv_col,
    hidden_one,
    dealt,
    factor_one,
    weights_one,
    qkv,
    mixed,
    hidden_two,
    resid,
    factor_two,
    full_cot,
    weights_two,
    keys,
    queries,
    gate,
    grad_mixed,
    grad_memory,
    part,
    index,
    low_picks,
    full,
    gains,
    packed,
    got,
    packed_cot,
    got_cot,
    outgoing,
    incoming,
    mine,
    theirs,
    turned,
    sends,
    recvs,
):
    net = Net(rows, cols, sends, recvs)
    greeted = net.greet(range(1, rows), range(1, cols))
    count, width = tokens_ref.shape
    capacity = packed.shape[0] // rows
    depth = halves * QD
    find_places(rows, net.row, order, send_row, send_col, recv_row, recv_col)
    pack_for_rows(net, packed, tokens_ref[...], send_row[...])
    net.meet(greeted)
    copies = exchange_start(net, packed, got, capacity)
    own_gain = columns_of(gains, width)
    own_gain(net.col)[...] = jnp.broadcast_to(
        norm_one[...].astype(LOW).astype(F32), (8, width)
    )
    gain_spread = net.columns_start(own_gain)
    place_one = rows_of(weights_one, w_qkv.shape[0])
    place_one(net.row)[:, : 3 * width] = w_qkv[...].astype(LOW)
    place_one(net.row)[:, 3 * width :] = w_attn[...].T.astype(LOW)
    gather_one = net.gather_start(place_one(net.row), place_one)
    pack_for_rows(net, packed_cot, cot[...], send_row[...])
    cot_copies = exchange_start(net, packed_cot, got_cot, capacity)
    place_two = rows_of(weights_two, w_query.shape[0])
    place_two(net.row)[:, :depth] = w_query[...].astype(LOW)
    place_two(net.row)[:, depth : depth + width] = w_gate[...].astype(LOW)
    place_two(net.row)[:, depth + width :] = w_mem[...].T.astype(LOW)
    gather_two = net.gather_start(place_two(net.row), place_two)
    span = sub_keys.shape[1]
    place_keys = lambda at: keys.at[:, pl.ds(pl.multiple_of(at * span, span), span), :]
    place_keys(net.row)[...] = sub_keys[...].astype(LOW)
    gather_keys = net.gather_start(place_keys(net.row), place_keys)
    wait_all(copies)
    own = columns_of(full, width)
    values = unpack(got, recv_col[...])
    own(net.col)[...] = values.astype(LOW)
    spread = net.columns_start(own)
    dealt[...] = values
    low_picks[...] = (picks[...] - 32768).astype(jnp.int16)
    head = net.col * halves // 2
    head_rows = pl.ds(pl.multiple_of(head * PICKS, PICKS), PICKS)
    halves_of = []
    for h in range(halves):
        even = (net.col * halves + h) % 2 == 0
        halves_of.append(jnp.where(even, picks[...] // NK, picks[...] % NK))
        turned[...] = halves_of[h].astype(F32).T
        index[h * PICKS : (h + 1) * PICKS] = turned[head_rows, :].astype(jnp.int32)
    ids_col = sequence_ids(lengths[...], count, 0)
    ids_row = sequence_ids(lengths[...], count, 1)
    wait_all(spread)
    wait_all(gain_spread)
    values = full[...].astype(F32)
    scale = lax.rsqrt(jnp.mean(values * values, axis=1, keepdims=True) + EPS)
    hidden_one[...] = (values * scale * gains[:1]).astype(LOW)
    factor_one[...] = jnp.broadcast_to(scale, (count, LANES))
    wait_all(net.gather_pass(place_one, gather_one))
    qkv[...] = jnp.dot(
        hidden_one[...], weights_one[:, : 3 * width], preferred_element_type=F32
    ).astype(LOW)
    for h in range(width // HD):
        (_, _, value), probs = attention_scores(qkv, h, ids_col, ids_row)
        mixed[:, h * HD : (h + 1) * HD] = jnp.dot(
            probs.astype(LOW), value, preferred_element_type=F32
        ).astype(LOW)
    own_part, reduce = project_start(
        net, mixed[...], weights_one.at[:, 3 * width :], outgoing, incoming
    )
    values = dealt[...] + project_end(own_part, incoming, reduce)
    resid[...] = values
    square = share_sums(net, jnp.sum(values * values, axis=1, keepdims=True), mine, theirs)
    scale = lax.rsqrt(square / D + EPS)
    factor_two[...] = scale
    own = columns_of(hidden_two, width)
    gain_two = norm_two[...].astype(LOW).astype(F32)
    own(net.col)[...] = (resid[...] * widen(scale, width) * gain_two).astype(LOW)
    spread = net.columns_start(own)
    wait_all(cot_copies)
    own_cot = columns_of(full_cot, width)
    own_cot(net.col)[...] = unpack(got_cot, recv_col[...]).astype(LOW)
    cot_spread = net.columns_start(own_cot)
    left = net.gather_pass(place_two, gather_two) + net.gather_pass(place_keys, gather_keys)
    wait_all(spread)
    wait_all(left)
    for h in range(halves):
        columns = slice(h * QD, (h + 1) * QD)
        queries[:, columns] = jnp.dot(
            hidden_two[...], weights_two[:, columns], preferred_element_type=F32
        ).astype(LOW)
        scores = lax.dot_general(
            queries[:, columns], keys[h], NT_DIMS, preferred_element_type=F32
        )
        low_index = halves_of[h] % LANES
        first = jnp.take_along_axis(scores[:, :LANES], low_index, axis=1)
        second = jnp.take_along_axis(scores[:, LANES:], low_index, axis=1)
        turned[...] = jnp.where(halves_of[h] >= LANES, second, first).T
        part[h * PICKS : (h + 1) * PICKS] = turned[head_rows, :]
    open_gate = jnp.dot(
        hidden_two[...], weights_two[:, depth : depth + width], preferred_element_type=F32
    )
    gate[...] = open_gate
    wait_all(cot_spread)
    back = jnp.dot(full_cot[...], weights_two[:, depth + width :], preferred_element_type=F32)
    grad_mixed[...] = back
    grad_memory[...] = (back * (open_gate * jax.nn.sigmoid(open_gate))).astype(LOW)
    net.drain()


def norm_grad(net, grad_hidden, values, scale, gain, mine, theirs):
    width = values.shape[1]
    scaled = grad_hidden * gain
    inner = share_sums(net, jnp.sum(scaled * values, axis=1, keepdims=True), mine, theirs)
    wide = widen(scale, width)
    grads = wide * scaled - values * (wide * wide * wide) * widen(inner, width) / D
    grad_gain = jnp.sum(grad_hidden * values * wide, axis=0, keepdims=True)
    return grads, grad_gain


def project_start(net, left, weights, outgoing, incoming):
    width = outgoing.shape[2]

    def block(col):
        rows = rows_of(weights, width)(col)[...]
        return lax.dot_general(left, rows, NT_DIMS, preferred_element_type=F32)

    copies = []
    for k in range(1, net.cols):
        outgoing[k - 1] = block(flip(net.col, k)).astype(LOW)
        copies.append(net.send(outgoing.at[k - 1], incoming.at[k - 1], col_k=k))
    return block(net.col), copies


def project_end(total, incoming, copies):
    for k, copy in enumerate(copies):
        copy.wait_recv()
        total = total + incoming[k].astype(F32)
    return total


def attention_scores(qkv, head, ids_col, ids_row):
    parts = [qkv[:, (3 * head + j) * HD : (3 * head + j + 1) * HD] for j in range(3)]
    scores = lax.dot_general(parts[0], parts[1], NT_DIMS, preferred_element_type=F32) * HD ** (
        -0.5
    )
    asks = lax.broadcasted_iota(jnp.int32, scores.shape, 0)
    offers = lax.broadcasted_iota(jnp.int32, scores.shape, 1)
    allowed = (ids_col == ids_row) & (asks >= offers)
    scores = jnp.where(allowed, scores, MASKED)
    shifted = jnp.exp(scores - jnp.max(scores, axis=1, keepdims=True))
    return parts, shifted / jnp.sum(shifted, axis=1, keepdims=True)


def spread_picks(halves, weights, dw, index, out):
    tokens = weights.shape[1]
    grad = weights * (dw - jnp.sum(weights * dw, axis=0, keepdims=True))
    block = 128
    places = lax.broadcasted_iota(jnp.int32, (NK, block), 0)
    for h in range(halves):
        for b in range(tokens // block):
            columns = slice(b * block, (b + 1) * block)
            total = jnp.zeros((NK, block), F32)
            for k in range(PICKS):
                row = index[h * PICKS + k : h * PICKS + k + 1, columns]
                total = total + jnp.where(places == row, grad[k : k + 1, columns], 0.0)
            out[columns, h * NK : (h + 1) * NK] = total.T.astype(LOW)


def back_kernel(
    rows,
    cols,
    halves,
    share,
    dw,
    index,
    memory,
    gate,
    grad_mixed,
    queries,
    hidden_two,
    cot,
    weights_two,
    keys,
    resid,
    factor_two,
    gain_two,
    recv_row,
    send_col,
    qkv,
    mixed,
    lengths,
    hidden_one,
    weights_one,
    dealt,
    factor_one,
    gain_one,
    output,
    grad_tokens,
    own_one,
    own_two,
    own_keys,
    gains,
    grad_sub,
    both,
    mixed_two,
    grad_two,
    grad_keys,
    grad_low,
    grad_resid,
    grad_qkv,
    grad_one,
    one_outgoing,
    one_incoming,
    res_outgoing,
    res_incoming,
    two_outgoing,
    two_incoming,
    mine,
    theirs,
    mine_one,
    theirs_one,
    packed,
    got,
    packed_one,
    got_one,
    across_two,
    two_out,
    two_in,
    across_keys,
    keys_out,
    keys_in,
    across_one,
    one_out,
    one_in,
    my_gains,
    their_gains,
    sends,
    recvs,
):
    net = Net(rows, cols, sends, recvs)
    capacity = packed.shape[0] // rows
    width = resid.shape[1]
    depth = halves * QD
    greeted = net.greet(range(1, rows), range(1, cols))
    head = net.col * halves // 2
    own_share = share[pl.ds(pl.multiple_of(head * PICKS, PICKS), PICKS), :]
    spread_picks(halves, own_share, dw[...], index, grad_sub)
    ids_col = sequence_ids(lengths[...], memory.shape[0], 0)
    ids_row = sequence_ids(lengths[...], memory.shape[0], 1)
    for h in range(halves):
        both[:, h * QD : (h + 1) * QD] = jnp.dot(
            grad_sub[:, h * NK : (h + 1) * NK], keys[h], preferred_element_type=F32
        ).astype(LOW)
    open_gate, back, read = gate[...], grad_mixed[...], memory[...]
    sigmoid = jax.nn.sigmoid(open_gate)
    both[:, depth:] = (back * read * sigmoid * (1.0 + open_gate * (1.0 - sigmoid))).astype(LOW)
    mixed_two[...] = (read * open_gate * sigmoid).astype(LOW)
    net.meet(greeted)
    own_part, reduce_two = project_start(
        net, both[...], weights_two.at[:, : depth + width], two_outgoing, two_incoming
    )
    hidden_t = hidden_two[...].T
    grad_two[:, : depth + width] = jnp.dot(hidden_t, both[...], preferred_element_type=F32)
    grad_two[:, depth + width :] = jnp.dot(
        cot[...].T, mixed_two[...], preferred_element_type=F32
    )
    for h in range(halves):
        grad_keys[h] = jnp.dot(
            grad_sub[:, h * NK : (h + 1) * NK].T,
            queries[:, h * QD : (h + 1) * QD],
            preferred_element_type=F32,
        )
    view_two = rows_of(grad_two, own_two.shape[0])
    span = own_keys.shape[1]
    view_keys = lambda at: grad_keys.at[:, pl.ds(pl.multiple_of(at * span, span), span), :]
    started_two = net.scatter_start(view_two, across_two)
    started_keys = net.scatter_start(view_keys, across_keys)
    moved_two = net.scatter_pass(view_two, across_two, started_two, two_out, two_in)
    moved_keys = net.scatter_pass(view_keys, across_keys, started_keys, keys_out, keys_in)
    grad_hidden = project_end(own_part, two_incoming, reduce_two)
    grads, gain_two_sum = norm_grad(
        net, grad_hidden, resid[...], factor_two[...], gain_two[...].astype(LOW).astype(F32), mine, theirs
    )
    own_cot = columns_of(cot, width)(net.col)[...]
    grads = grads + own_cot.astype(F32)
    grad_resid[...] = grads
    own = columns_of(grad_low, width)
    own(net.col)[...] = grads.astype(LOW)
    spread = net.columns_start(own)
    wait_all(spread)
    own_res, reduce_res = project_start(
        net, mixed_two[...], weights_two.at[:, depth + width :], res_outgoing, res_incoming
    )
    grad_heads = jnp.dot(
        grad_low[...], weights_one[:, 3 * width :], preferred_element_type=F32
    ).astype(LOW)
    for head in range(width // HD):
        (query, key, value), probs = attention_scores(qkv, head, ids_col, ids_row)
        grad_out = grad_heads[:, head * HD : (head + 1) * HD]
        grad_prob = lax.dot_general(grad_out, value, NT_DIMS, preferred_element_type=F32)
        inner = jnp.sum(probs * grad_prob, axis=1, keepdims=True)
        grad_score = (probs * (grad_prob - inner)).astype(LOW)
        pieces = (
            jnp.dot(grad_score, key, preferred_element_type=F32) * HD ** (-0.5),
            jnp.dot(grad_score.T, query, preferred_element_type=F32) * HD ** (-0.5),
            jnp.dot(probs.astype(LOW).T, grad_out, preferred_element_type=F32),
        )
        for j in range(3):
            grad_qkv[:, (3 * head + j) * HD : (3 * head + j + 1) * HD] = pieces[j].astype(LOW)
    own_part, reduce_one = project_start(
        net, grad_qkv[...], weights_one.at[:, : 3 * width], one_outgoing, one_incoming
    )
    grad_one[:, : 3 * width] = jnp.dot(
        hidden_one[...].T, grad_qkv[...], preferred_element_type=F32
    )
    grad_one[:, 3 * width :] = jnp.dot(grad_low[...].T, mixed[...], preferred_element_type=F32)
    view_one = rows_of(grad_one, own_one.shape[0])
    started_one = net.scatter_start(view_one, across_one)
    block = resid[...] + project_end(own_res, res_incoming, reduce_res)
    pack_for_rows(net, packed, block.astype(LOW), recv_row[...])
    copies = exchange_start(net, packed, got, capacity)
    moved_one = net.scatter_pass(view_one, across_one, started_one, one_out, one_in)
    grad_hidden = project_end(own_part, one_incoming, reduce_one)
    grads, gain_one_sum = norm_grad(
        net,
        grad_hidden,
        dealt[...],
        factor_one[...],
        gain_one[...].astype(LOW).astype(F32),
        mine_one,
        theirs_one,
    )
    grads = grads + grad_resid[...]
    pack_for_rows(net, packed_one, grads.astype(LOW), recv_row[...])
    last = exchange_start(net, packed_one, got_one, capacity)
    places = lax.broadcasted_iota(jnp.int32, my_gains.shape, 0)
    my_gains[...] = jnp.where(places == 0, gain_one_sum, gain_two_sum)
    gain_copies = [net.send(my_gains, their_gains.at[k], row_k=k) for k in range(1, rows)]
    own_two[...] = net.scatter_end(view_two, across_two, started_two, two_in, moved_two)
    own_keys[...] = net.scatter_end(view_keys, across_keys, started_keys, keys_in, moved_keys)
    wait_all(copies)
    output[...] = unpack(got, send_col[...])
    own_one[...] = net.scatter_end(view_one, across_one, started_one, one_in, moved_one)
    total = my_gains[...]
    for k, copy in enumerate(gain_copies):
        copy.wait_recv()
        total = total + their_gains[k + 1]
    gains[...] = total
    wait_all(last)
    grad_tokens[...] = unpack(got_one, send_col[...])
    net.drain()


def remote_call(kernel, rows, cols, number, copies, ins, outs, scratch, *sizes):
    return pl.pallas_call(
        functools.partial(kernel, rows, cols, *sizes),
        out_shape=[jax.ShapeDtypeStruct(shape, dtype) for shape, dtype in outs],
        in_specs=[VMEM_SPEC] * len(ins),
        out_specs=[VMEM_SPEC] * len(outs),
        scratch_shapes=[pltpu.VMEM(shape, dtype) for shape, dtype in scratch]
        + [pltpu.SemaphoreType.DMA((copies,)), pltpu.SemaphoreType.DMA((copies,))],
        compiler_params=pltpu.CompilerParams(
            collective_id=number, has_side_effects=True, vmem_limit_bytes=VMEM_BYTES
        ),
    )(*ins)


def memory_kernel(
    rows,
    cols,
    part,
    own_picks,
    own_grads,
    table_f32,
    weights,
    memory,
    dw,
    gacc,
    table,
    stage,
    scores,
    picks_of,
    grads_of,
    low_of,
    dense,
    hi_ref,
    lo_ref,
    wide_ref,
    found_ref,
    mem_all,
    mem_twin,
    mem_out,
    mem_in,
    dw_all,
    dw_twin,
    dw_out,
    dw_in,
    dw_cols,
    stage_sems,
    sends,
    recvs,
):
    net = Net(rows, cols, sends, recvs)
    half = rows // 2
    tok_block = own_picks.shape[0]
    span_rows, width = table.shape
    spans = span_rows // LANES
    pitch = spans + 8
    iters = 4
    per_tok = tok_block // iters
    per_span = spans // iters

    grads_at = rows_of(grads_of, tok_block)
    picks_at = rows_of(picks_of, tok_block)
    low_at = lambda index: low_of.at[index]
    views = (grads_at, picks_at, low_at)
    first_pass = 3 * half
    first_twin = first_pass + 3 * half
    first_out = first_twin + 2 * half
    first_col = first_out + 2 * half

    def gather(a, j):
        mine = views[a](net.row)
        return net.copy(mine, mine, 3 * j + a, row_k=2 * j if j else 1)

    def passing(a, j):
        there = views[a](flip(net.row, 2 * j))
        return net.copy(there, there, first_pass + 3 * j + a, row_k=1)

    def twin(a, j):
        src, dst = ((mem_all, mem_twin), (dw_all, dw_twin))[a]
        return net.copy(src.at[2 * j + 1], dst.at[j], first_twin + 2 * j + a, row_k=1)

    def outward(a, j):
        src, dst = ((mem_out, mem_in), (dw_out, dw_in))[a]
        return net.copy(src.at[j - 1], dst.at[j - 1], first_out + 2 * j + a, row_k=2 * j)

    head = lambda col: pl.ds(pl.multiple_of(col * MH // cols * PICKS, PICKS), PICKS)

    def score_copy(k):
        return net.copy(part, rows_of(scores, part.shape[0])(net.col), first_col + k, col_k=k)

    def dw_copy(k):
        return net.copy(
            dw_all.at[0, head(flip(net.col, k)), :],
            dw_cols.at[k - 1],
            first_col + cols + k,
            col_k=k,
        )

    stage_rows = stage.shape[1]

    def stage_copy(i):
        source = table_f32.at[pl.ds(i * stage_rows, stage_rows), :]
        return pltpu.make_async_copy(source, stage.at[i % 2], stage_sems.at[i % 2])

    stage_copy(0).start()
    net.meet(net.greet([1] + [2 * j for j in range(1, half)], range(1, cols)))
    for k in range(1, cols):
        score_copy(k).start()
    grads_at(net.row)[...] = own_grads[...]
    picks_at(net.row)[...] = own_picks[...]
    for j in range(half):
        for a in range(2):
            gather(a, j).start()
    rows_of(scores, part.shape[0])(net.col)[...] = part[...]
    for i in range(span_rows // stage_rows):
        if (i + 1) * stage_rows < span_rows:
            stage_copy(i + 1).start()
        stage_copy(i).wait()
        table[i * stage_rows : (i + 1) * stage_rows, :] = stage[i % 2].astype(LOW)
    for k in range(1, cols):
        score_copy(k).wait_recv()
    for m in range(MH):
        score = (
            scores[2 * m * PICKS : (2 * m + 1) * PICKS]
            + scores[(2 * m + 1) * PICKS : (2 * m + 2) * PICKS]
        )
        shifted = jnp.exp(score - jnp.max(score, axis=0, keepdims=True))
        weights[m * PICKS : (m + 1) * PICKS] = shifted / jnp.sum(shifted, axis=0, keepdims=True)
    low_at(net.row)[...] = weights[...].astype(LOW)
    for j in range(half):
        gather(2, j).start()
    gacc[...] = jnp.zeros_like(gacc)
    mem_all[...] = jnp.zeros_like(mem_all)

    def one_block(step, _):
        k = jnp.where(step == 0, 0, jnp.where(step == rows - 1, 1, step + 1))
        there = cross(net.row, k, rows)
        for j in range(1, half):

            @pl.when(step == 2 * j - 1)
            def _():
                for a in range(3):
                    gather(a, j).wait_recv()
                    passing(a, j).start()

            @pl.when(step == 2 * j)
            def _():
                for a in range(3):
                    passing(a, j).wait_recv()

        @pl.when(step == rows - 1)
        def _():
            for a in range(3):
                gather(a, 0).wait_recv()

        picks = picks_at(there)[...].astype(jnp.int32) + 32768
        hi_ref[...] = (picks // LANES - net.row * spans).astype(F32)
        lo_ref[...] = (picks % LANES).astype(F32)
        wide_ref[...] = low_of[there].astype(F32).T
        places_lo = lax.broadcasted_iota(jnp.int32, (LANES, LANES), 0).astype(F32).astype(LOW)
        places_hi = lax.broadcasted_iota(jnp.int32, (spans, LANES), 0).astype(F32).astype(LOW)
        ones = jnp.ones((LANES, LANES), LOW)
        zeros = jnp.zeros((LANES, LANES), LOW)
        blank = jnp.zeros((spans, LANES), LOW)
        grads = grads_at(there)[...]
        grads_t = grads.T
        found_ref[...] = jnp.zeros_like(found_ref)
        lo_int = picks % LANES
        hi_all = hi_ref[...]

        def token_pair(first):
            rights, lefts = [], []
            for token in (first, first + 1):
                lo_row = jnp.broadcast_to(lo_ref[pl.ds(token, 1), :], (LANES, LANES)).astype(LOW)
                hi_row = jnp.broadcast_to(hi_ref[pl.ds(token, 1), :], (spans, LANES)).astype(LOW)
                w_row = jnp.broadcast_to(wide_ref[pl.ds(token, 1), :], (spans, LANES)).astype(LOW)
                rights.append(jnp.where(lo_row == places_lo, ones, zeros))
                lefts.append(jnp.where(hi_row == places_hi, w_row, blank))
            right = jnp.concatenate(rights, axis=1)
            left = jnp.concatenate(
                [
                    jnp.concatenate([lefts[0], blank], axis=1),
                    jnp.concatenate([blank, lefts[1]], axis=1),
                ],
                axis=0,
            )
            both = lax.dot_general(left, right, NT_DIMS, preferred_element_type=F32)
            for j in range(2):
                dense[pl.ds(pl.multiple_of((first + j) * pitch, 8), spans), :] = both[
                    j * spans : (j + 1) * spans
                ]

        def build(it, _):
            for j in range(1, half):

                @pl.when((it == 1) & (step == 2 * j + 1))
                def _():
                    twin(0, j).wait_recv()
                    twin(1, j).wait_recv()
                    mem_out[j - 1] = (mem_all[2 * j] + mem_twin[j]).astype(LOW)
                    outward(0, j).start()
                    dw_out[j - 1] = dw_all[2 * j] + dw_twin[j]
                    outward(1, j).start()

            span = pl.ds(pl.multiple_of(it * per_span * LANES, LANES), per_span * LANES)
            products = lax.dot_general(
                grads, table[span, :], NT_DIMS, preferred_element_type=F32
            )
            found = found_ref[...]
            pairs = per_tok // 2 // per_span
            for j in range(per_span):
                picked = jnp.take_along_axis(
                    products[:, LANES * j : LANES * (j + 1)], lo_int, axis=1
                )
                found = jnp.where(hi_all == (it * per_span + j).astype(F32), picked, found)
                for u in range(pairs):
                    token_pair(it * per_tok + (j * pairs + u) * 2)
            found_ref[...] = found
            return 0

        lax.fori_loop(0, iters, build, 0)
        dw_all[k] = found_ref[...].T

        def multiply(it, _):
            span = pl.ds(pl.multiple_of(it * per_span * LANES, LANES), per_span * LANES)
            chosen = jnp.concatenate(
                [
                    dense[pl.ds(it * per_span + j, tok_block, stride=pitch), :].astype(LOW)
                    for j in range(per_span)
                ],
                axis=1,
            )
            mem_all[k] += jnp.dot(chosen, table[span, :], preferred_element_type=F32)
            gacc[:, span] += jnp.dot(grads_t, chosen, preferred_element_type=F32)
            return 0

        lax.fori_loop(0, iters, multiply, 0)
        for j in range(half):

            @pl.when(step == (2 * j if j else rows - 1))
            def _():
                twin(0, j).start()
                twin(1, j).start()

        return 0

    lax.fori_loop(0, rows, one_block, 0)
    twin(1, 0).wait_recv()
    total = dw_all[0] + dw_twin[0]
    for j in range(1, half):
        outward(1, j).wait_recv()
        total = total + dw_in[j - 1]
    dw_all[0] = total
    for k in range(1, cols):
        dw_copy(k).start()
    twin(0, 0).wait_recv()
    total = mem_all[0] + mem_twin[0]
    for j in range(1, half):
        outward(0, j).wait_recv()
        total = total + mem_in[j - 1].astype(F32)
    memory[...] = total
    total = dw_all[0, head(net.col), :]
    for k in range(1, cols):
        dw_copy(k).wait_recv()
        total = total + dw_cols[k - 1]
    dw[...] = total
    for k in range(1, cols):
        score_copy(k).wait_send()
        dw_copy(k).wait_send()
    for j in range(half):
        for a in range(3):
            gather(a, j).wait_send()
            if j:
                passing(a, j).wait_send()
        for a in range(2):
            twin(a, j).wait_send()
            if j:
                outward(a, j).wait_send()


def memory_call(rows, cols, number, part, picks, grads, table):
    tokens, count = picks.shape
    span_rows, width = table.shape
    half = rows // 2
    copies = 10 * half + 2 * cols
    vmem = pltpu.VMEM
    return pl.pallas_call(
        functools.partial(memory_kernel, rows, cols),
        in_specs=[VMEM_SPEC, VMEM_SPEC, VMEM_SPEC, pl.BlockSpec(memory_space=pl.ANY)],
        out_specs=[VMEM_SPEC] * 4,
        out_shape=[
            jax.ShapeDtypeStruct((count, tokens), F32),
            jax.ShapeDtypeStruct((tokens, width), F32),
            jax.ShapeDtypeStruct((PICKS, tokens), F32),
            jax.ShapeDtypeStruct((width, span_rows), F32),
        ],
        scratch_shapes=[
            vmem((span_rows, width), LOW),
            vmem((2, 1024, width), F32),
            vmem((2 * count, tokens), F32),
            vmem((rows * tokens, count), jnp.int16),
            vmem((rows * tokens, width), LOW),
            vmem((rows, count, tokens), LOW),
            vmem((tokens * (span_rows // LANES + 8), LANES), F32),
            vmem((tokens, count), F32),
            vmem((tokens, count), F32),
            vmem((tokens, count), F32),
            vmem((tokens, count), F32),
            vmem((rows, tokens, width), F32),
            vmem((half, tokens, width), F32),
            vmem((half - 1, tokens, width), LOW),
            vmem((half - 1, tokens, width), LOW),
            vmem((rows, count, tokens), F32),
            vmem((half, count, tokens), F32),
            vmem((half - 1, count, tokens), F32),
            vmem((half - 1, count, tokens), F32),
            vmem((cols - 1, PICKS, tokens), F32),
            pltpu.SemaphoreType.DMA((2,)),
            pltpu.SemaphoreType.DMA((copies,)),
            pltpu.SemaphoreType.DMA((copies,)),
        ],
        compiler_params=pltpu.CompilerParams(
            collective_id=number, has_side_effects=True, vmem_limit_bytes=63 * 2**20
        ),
    )(part, picks, grads, table)


def per_device(
    tokens,
    cotangent,
    deal_order,
    seq_lengths,
    value_picks,
    norm1_gain,
    w_qkv,
    w_attn_out,
    norm2_gain,
    w_query,
    sub_keys,
    value_table,
    w_gate,
    w_mem_out,
):
    rows, cols = lax.axis_size("row"), lax.axis_size("col")
    row_index = lax.axis_index("row")
    count, width = tokens.shape
    slots = 2 * count
    half = rows // 2
    halves = sub_keys.shape[0]
    depth = halves * QD
    span_one, span_two = 4 * width, depth + 2 * width
    shard_rows = w_qkv.shape[0]
    flat_picks = value_picks.reshape(count, MH * PICKS)
    gain_one, gain_two = norm1_gain[None, :], norm2_gain[None, :]
    swap = [((slots, width), LOW), ((slots, width), LOW)]
    sums = [((8, count), F32), ((cols, 8, count), F32)]
    moving = ((cols - 1, count, width), LOW)
    (
        send_row,
        send_col,
        recv_row,
        recv_col,
        hidden_one,
        dealt,
        factor_one,
        weights_one,
        qkv,
        mixed,
        hidden_two,
        resid,
        factor_two,
        full_cot,
        weights_two,
        keys,
        queries,
        gate,
        grad_mixed,
        grad_memory,
        score_part,
        index,
        low_picks,
    ) = remote_call(
        front_kernel,
        rows,
        cols,
        0,
        6 * (cols - 1) + 5 * (rows - 1),
        [
            deal_order.reshape(rows, count),
            flat_picks,
            seq_lengths,
            tokens,
            cotangent,
            w_qkv,
            w_attn_out,
            w_query,
            w_gate,
            w_mem_out,
            sub_keys,
            gain_one,
            gain_two,
        ],
        [
            ((1, count), jnp.int32),
            ((count, 1), jnp.int32),
            ((1, count), jnp.int32),
            ((count, 1), jnp.int32),
            ((count, D), LOW),
            ((count, width), F32),
            ((count, LANES), F32),
            ((D, span_one), LOW),
            ((count, 3 * width), LOW),
            ((count, width), LOW),
            ((count, D), LOW),
            ((count, width), F32),
            ((count, LANES), F32),
            ((count, D), LOW),
            ((D, span_two), LOW),
            ((halves, NK, QD), LOW),
            ((count, depth), LOW),
            ((count, width), F32),
            ((count, width), F32),
            ((count, width), LOW),
            ((halves * PICKS, count), F32),
            ((halves * PICKS, count), jnp.int32),
            ((count, MH * PICKS), jnp.int16),
        ],
        [((count, D), LOW), ((8, D), F32), *swap, *swap, moving, moving, *sums]
        + [((MH * PICKS, count), F32)],
        halves,
    )
    pick_weights, memory, grad_pick, grad_table = memory_call(
        rows, cols, 1, score_part, low_picks, grad_memory, value_table
    )
    block = ((count, width), F32)
    scattered = [
        [((half,) + shape, F32), ((half - 1,) + shape, LOW), ((half - 1,) + shape, LOW)]
        for shape in ((shard_rows, span_two), sub_keys.shape, (shard_rows, span_one))
    ]
    output, grad_tokens, own_one, own_two, own_keys, gains = remote_call(
        back_kernel,
        rows,
        cols,
        2,
        6 * (cols - 1) + 3 * (rows - 1) + 3 * (half + half - 1),
        [
            pick_weights,
            grad_pick,
            index,
            memory,
            gate,
            grad_mixed,
            queries,
            hidden_two,
            full_cot,
            weights_two,
            keys,
            resid,
            factor_two,
            gain_two,
            recv_row,
            send_col,
            qkv,
            mixed,
            seq_lengths,
            hidden_one,
            weights_one,
            dealt,
            factor_one,
            gain_one,
        ],
        [
            block,
            block,
            ((shard_rows, span_one), F32),
            ((shard_rows, span_two), F32),
            (sub_keys.shape, F32),
            ((8, width), F32),
        ],
        [
            ((count, halves * NK), LOW),
            ((count, depth + width), LOW),
            ((count, width), LOW),
            ((D, span_two), F32),
            ((halves, NK, QD), F32),
            ((count, D), LOW),
            block,
            ((count, 3 * width), LOW),
            ((D, span_one), F32),
            *[moving] * 6,
            *sums,
            *sums,
            *swap,
            *swap,
            *scattered[0],
            *scattered[1],
            *scattered[2],
            ((8, width), F32),
            ((rows, 8, width), F32),
        ],
        halves,
    )
    gain_span = width // rows
    gain_one_grad = lax.dynamic_slice_in_dim(gains[0], row_index * gain_span, gain_span)
    gain_two_grad = lax.dynamic_slice_in_dim(gains[1], row_index * gain_span, gain_span)
    return (
        output,
        grad_tokens,
        gain_one_grad,
        own_one[:, : 3 * width],
        own_one[:, 3 * width :].T,
        gain_two_grad,
        own_two[:, :depth],
        own_keys,
        grad_table.T,
        own_two[:, depth : depth + width],
        own_two[:, depth + width :].T,
    )


def solution(mesh):
    return jax.shard_map(
        per_device,
        mesh=mesh,
        in_specs=(
            P("row", "col"),
            P("row", "col"),
            P(),
            P("row", None),
            P("row", None, None),
            P("col"),
            P("row", "col"),
            P("col", "row"),
            P("col"),
            P("row", "col"),
            P("col", "row", None),
            P("row", "col"),
            P("row", "col"),
            P("col", "row"),
        ),
        out_specs=(
            P("row", "col"),
            P("row", "col"),
            P(("col", "row")),
            P("row", "col"),
            P("col", "row"),
            P(("col", "row")),
            P("row", "col"),
            P("col", "row", None),
            P("row", "col"),
            P("row", "col"),
            P("col", "row"),
        ),
        check_vma=False,
    )
```

```python
import functools

import jax
import jax.numpy as jnp
from jax import lax
from jax.experimental import pallas as pl
from jax.experimental.pallas import tpu as pltpu
from jax.sharding import PartitionSpec as P

D = 1024
HD = 64
MH = 4
QD = 512
NK = 256
PICKS = 32
LANES = 128
EPS = 1e-05
MASKED = -1e30
F32 = jnp.float32
LOW = jnp.bfloat16
MESH = pl.DeviceIdType.MESH
NT_DIMS = (((1,), (1,)), ((), ()))
VMEM_SPEC = pl.BlockSpec(memory_space=pltpu.VMEM)
VMEM_BYTES = 60 * 2**20


def flip(index, mask):
    bit = 1
    while bit <= mask:
        if mask & bit:
            index = index + bit - 2 * bit * (index // bit % 2)
        bit *= 2
    return index


def cross(index, mask, size):
    total, bit = 0, 1
    while bit < size:
        a, b = index // bit % 2, mask // bit % 2
        total = total + bit * (a + b - 2 * a * b)
        bit *= 2
    return total


class Net:
    def __init__(self, rows, cols, sends, recvs):
        self.rows, self.cols = rows, cols
        self.row, self.col = lax.axis_index("row"), lax.axis_index("col")
        self.sends, self.recvs, self.used = sends, recvs, 0
        self.pending = []

    def place(self, row_k, col_k):
        return (flip(self.row, row_k), flip(self.col, col_k))

    def greet(self, row_ks, col_ks):
        barrier = pltpu.get_barrier_semaphore()
        places = [self.place(k, 0) for k in row_ks] + [self.place(0, k) for k in col_ks]
        for place in places:
            pl.semaphore_signal(barrier, inc=1, device_id=place, device_id_type=MESH)
        return len(places)

    def meet(self, greeted):
        pl.semaphore_wait(pltpu.get_barrier_semaphore(), greeted)

    def copy(self, src, dst, number, row_k=0, col_k=0):
        assert number < self.sends.shape[0]
        return pltpu.make_async_remote_copy(
            src_ref=src,
            dst_ref=dst,
            send_sem=self.sends.at[number],
            recv_sem=self.recvs.at[number],
            device_id=self.place(row_k, col_k),
            device_id_type=MESH,
        )

    def send(self, src, dst, row_k=0, col_k=0):
        copy = self.copy(src, dst, self.used, row_k, col_k)
        copy.start()
        self.used += 1
        self.pending.append(copy)
        return copy

    def drain(self):
        for copy in self.pending:
            copy.wait_send()

    def gather_start(self, src, view):
        sent = {b: self.send(src, view(self.row), row_k=2 * b) for b in reversed(self.bits())}
        return sent, self.send(src, view(self.row), row_k=1)

    def gather_pass(self, view, started):
        sent, sibling = started
        passed = [sibling]
        for m in sorted(range(1, self.rows // 2), key=lambda m: (-(m & -m), m.bit_count())):
            sent[m].wait_recv()
            block = view(flip(self.row, 2 * m))
            for b in self.bits():
                if b < (m & -m):
                    sent[m ^ b] = self.send(block, block, row_k=2 * b)
            passed.append(self.send(block, block, row_k=1))
        return passed

    def bits(self):
        return [1 << i for i in range((self.rows // 2 - 1).bit_length())]

    def scatter_start(self, view, across):
        twin = flip(self.row, 1)
        return [
            self.send(view(flip(twin, 2 * j)), across.at[j], row_k=1)
            for j in range(self.rows // 2)
        ]

    def scatter_pass(self, view, across, started, outgoing, incoming, moved, near):
        masks = [m for m in range(1, self.rows // 2) if (m % 2 == 1) == near]
        for m in sorted(masks, key=lambda m: ((m & -m), -m.bit_count())):
            started[m].wait_recv()
            block = view(flip(self.row, 2 * m))[...] + across[m]
            for b in self.bits():
                if b < (m & -m):
                    moved[m ^ b].wait_recv()
                    block = block + incoming[(m ^ b) - 1].astype(F32)
            outgoing[m - 1] = block.astype(outgoing.dtype)
            moved[m] = self.send(outgoing.at[m - 1], incoming.at[m - 1], row_k=2 * (m & -m))
        return moved

    def scatter_end(self, view, across, started, incoming, moved):
        started[0].wait_recv()
        total = view(self.row)[...] + across[0]
        for b in self.bits():
            moved[b].wait_recv()
            total = total + incoming[b - 1].astype(F32)
        return total

    def columns_start(self, view):
        return [self.send(view(self.col), view(self.col), col_k=k) for k in range(1, self.cols)]


def wait_all(copies):
    for copy in copies:
        copy.wait_recv()


def rows_of(ref, count):
    return lambda index: ref.at[pl.ds(pl.multiple_of(index * count, count), count), :]


def columns_of(ref, count):
    return lambda index: ref.at[:, pl.ds(pl.multiple_of(index * count, count), count)]


def one_hot_rows(positions, slots):
    places = lax.broadcasted_iota(jnp.int32, (positions.shape[0], slots), 1)
    return jnp.where(positions == places, 1.0, 0.0).astype(LOW)


def one_hot_columns(positions, slots):
    places = lax.broadcasted_iota(jnp.int32, (slots, positions.shape[1]), 0)
    return jnp.where(positions == places, 1.0, 0.0).astype(LOW)


def pack_for_rows(net, packed, values, positions):
    slots = packed.shape[0]
    packed[...] = jnp.dot(
        one_hot_columns(positions, slots), values, preferred_element_type=F32
    ).astype(LOW)


def exchange_start(net, packed, got, capacity):
    mine = rows_of(got, capacity)
    theirs = rows_of(packed, capacity)
    copies = [
        net.send(theirs(flip(net.row, k)), mine(net.row), row_k=k) for k in range(1, net.rows)
    ]
    mine(net.row)[...] = theirs(net.row)[...]
    return copies


def unpack(got, positions):
    return jnp.dot(
        one_hot_rows(positions, got.shape[0]), got[...], preferred_element_type=F32
    )


def share_sums(net, sums, mine, theirs):
    tokens = sums.shape[0]
    mine[...] = jnp.broadcast_to(sums, (tokens, LANES)).T[:8]
    copies = [net.send(mine, theirs.at[k], col_k=k) for k in range(1, net.cols)]
    wait_all(copies)
    total = mine[...]
    for k in range(1, net.cols):
        total = total + theirs[k]
    return jnp.broadcast_to(total[:1], (LANES, tokens)).T


def widen(lanes, width):
    return jnp.concatenate([lanes] * (width // LANES), axis=1)


def first_of(size, mask):
    earlier = lax.broadcasted_iota(jnp.int32, (size, size), 0)
    later = lax.broadcasted_iota(jnp.int32, (size, size), 1)
    triangle = jnp.where(earlier < later, 1.0, 0.0).astype(LOW)
    return jnp.dot(mask.astype(LOW), triangle, preferred_element_type=F32)


def find_places(rows, row, order, send_row, send_col, recv_row, recv_col):
    count = order.shape[1]
    capacity = 2 * count // rows
    owner = order[...] // count
    owned = jnp.where(owner == row, 1.0, 0.0)
    rank = first_of(count, owned)
    low_order = order[...].astype(F32).T
    tokens = lax.broadcasted_iota(jnp.int32, (count, count), 1).astype(F32)
    first = (row * count).astype(F32)
    sent = jnp.zeros((1, count), F32)
    pick = lax.broadcasted_iota(jnp.int32, (8, count), 0)
    for d in range(rows):
        match = jnp.where(low_order[:, d : d + 1] - first == tokens, 1.0, 0.0).astype(LOW)
        pair = jnp.where(pick == 0, rank[d : d + 1] * owned[d : d + 1], owned[d : d + 1])
        found = jnp.dot(pair.astype(LOW), match, preferred_element_type=F32)
        sent = sent + found[:1] + found[1:2] * (d * capacity)
    send_row[...] = sent.astype(jnp.int32)
    send_col[...] = jnp.broadcast_to(sent, (LANES, count)).T[:, :1].astype(jnp.int32)
    blocks = lax.broadcasted_iota(jnp.int32, (rows, count), 0)
    mine = jnp.sum(jnp.where(blocks == row, order[...], 0), axis=0, keepdims=True)
    source = mine // count
    came = jnp.where(source == lax.broadcasted_iota(jnp.int32, (LANES, count), 0), 1.0, 0.0)
    place = jnp.sum(first_of(count, came) * came, axis=0, keepdims=True)
    place = place + source.astype(F32) * capacity
    recv_row[...] = place.astype(jnp.int32)
    recv_col[...] = jnp.broadcast_to(place, (LANES, count)).T[:, :1].astype(jnp.int32)


def sequence_ids(lengths, count, axis):
    places = lax.broadcasted_iota(jnp.int32, (1, count) if axis else (count, 1), axis)
    end = jnp.zeros((1, 1), jnp.int32)
    ids = jnp.zeros(places.shape, jnp.int32)
    for j in range(lengths.shape[1]):
        end = end + lengths[:, j : j + 1]
        ids = ids + jnp.where(places >= end, 1, 0)
    return ids


def front_kernel(
    rows,
    cols,
    halves,
    order,
    picks,
    lengths,
    tokens_ref,
    cot,
    w_qkv,
    w_attn,
    w_query,
    w_gate,
    w_mem,
    sub_keys,
    norm_one,
    norm_two,
    send_row,
    send_col,
    recv_row,
    recv_col,
    hidden_one,
    dealt,
    factor_one,
    weights_one,
    qkv,
    mixed,
    hidden_two,
    resid,
    factor_two,
    full_cot,
    weights_two,
    keys,
    queries,
    gate,
    grad_mixed,
    grad_memory,
    index,
    low_picks,
    weights,
    scores_of,
    full,
    gains,
    packed,
    got,
    packed_cot,
    got_cot,
    outgoing,
    incoming,
    mine,
    theirs,
    turned,
    sends,
    recvs,
):
    net = Net(rows, cols, sends, recvs)
    greeted = net.greet(range(1, rows), range(1, cols))
    count, width = tokens_ref.shape
    capacity = packed.shape[0] // rows
    depth = halves * QD
    find_places(rows, net.row, order, send_row, send_col, recv_row, recv_col)
    pack_for_rows(net, packed, tokens_ref[...], send_row[...])
    net.meet(greeted)
    copies = exchange_start(net, packed, got, capacity)
    own_gain = columns_of(gains, width)
    own_gain(net.col)[...] = jnp.broadcast_to(
        norm_one[...].astype(LOW).astype(F32), (8, width)
    )
    gain_spread = net.columns_start(own_gain)
    place_one = rows_of(weights_one, w_qkv.shape[0])
    place_one(net.row)[:, : 3 * width] = w_qkv[...].astype(LOW)
    place_one(net.row)[:, 3 * width :] = w_attn[...].T.astype(LOW)
    gather_one = net.gather_start(place_one(net.row), place_one)
    pack_for_rows(net, packed_cot, cot[...], send_row[...])
    cot_copies = exchange_start(net, packed_cot, got_cot, capacity)
    place_two = rows_of(weights_two, w_query.shape[0])
    place_two(net.row)[:, :depth] = w_query[...].astype(LOW)
    place_two(net.row)[:, depth : depth + width] = w_gate[...].astype(LOW)
    place_two(net.row)[:, depth + width :] = w_mem[...].T.astype(LOW)
    gather_two = net.gather_start(place_two(net.row), place_two)
    span = sub_keys.shape[1]
    place_keys = lambda at: keys.at[:, pl.ds(pl.multiple_of(at * span, span), span), :]
    place_keys(net.row)[...] = sub_keys[...].astype(LOW)
    gather_keys = net.gather_start(place_keys(net.row), place_keys)
    wait_all(copies)
    own = columns_of(full, width)
    values = unpack(got, recv_col[...])
    own(net.col)[...] = values.astype(LOW)
    spread = net.columns_start(own)
    dealt[...] = values
    low_picks[...] = (picks[...] - 32768).astype(jnp.int16)
    head = net.col * halves // 2
    head_rows = pl.ds(pl.multiple_of(head * PICKS, PICKS), PICKS)
    halves_of = []
    for h in range(halves):
        even = (net.col * halves + h) % 2 == 0
        halves_of.append(jnp.where(even, picks[...] // NK, picks[...] % NK))
        turned[...] = halves_of[h].astype(F32).T
        index[h * PICKS : (h + 1) * PICKS] = turned[head_rows, :].astype(jnp.int32)
    ids_col = sequence_ids(lengths[...], count, 0)
    ids_row = sequence_ids(lengths[...], count, 1)
    wait_all(spread)
    wait_all(gain_spread)
    values = full[...].astype(F32)
    scale = lax.rsqrt(jnp.mean(values * values, axis=1, keepdims=True) + EPS)
    hidden_one[...] = (values * scale * gains[:1]).astype(LOW)
    factor_one[...] = jnp.broadcast_to(scale, (count, LANES))
    wait_all(net.gather_pass(place_one, gather_one))
    qkv[...] = jnp.dot(
        hidden_one[...], weights_one[:, : 3 * width], preferred_element_type=F32
    ).astype(LOW)
    for h in range(width // HD):
        (_, _, value), probs = attention_scores(qkv, h, ids_col, ids_row)
        mixed[:, h * HD : (h + 1) * HD] = jnp.dot(
            probs.astype(LOW), value, preferred_element_type=F32
        ).astype(LOW)
    own_part, reduce = project_start(
        net, mixed[...], weights_one.at[:, 3 * width :], outgoing, incoming
    )
    values = dealt[...] + project_end(own_part, incoming, reduce)
    resid[...] = values
    square = share_sums(net, jnp.sum(values * values, axis=1, keepdims=True), mine, theirs)
    scale = lax.rsqrt(square / D + EPS)
    factor_two[...] = scale
    own = columns_of(hidden_two, width)
    gain_two = norm_two[...].astype(LOW).astype(F32)
    own(net.col)[...] = (resid[...] * widen(scale, width) * gain_two).astype(LOW)
    spread = net.columns_start(own)
    wait_all(cot_copies)
    own_cot = columns_of(full_cot, width)
    own_cot(net.col)[...] = unpack(got_cot, recv_col[...]).astype(LOW)
    cot_spread = net.columns_start(own_cot)
    left = net.gather_pass(place_two, gather_two) + net.gather_pass(place_keys, gather_keys)
    wait_all(spread)
    wait_all(left)
    for h in range(halves):
        columns = slice(h * QD, (h + 1) * QD)
        queries[:, columns] = jnp.dot(
            hidden_two[...], weights_two[:, columns], preferred_element_type=F32
        ).astype(LOW)
        scores = lax.dot_general(
            queries[:, columns], keys[h], NT_DIMS, preferred_element_type=F32
        )
        low_index = halves_of[h] % LANES
        first = jnp.take_along_axis(scores[:, :LANES], low_index, axis=1)
        second = jnp.take_along_axis(scores[:, LANES:], low_index, axis=1)
        turned[...] = jnp.where(halves_of[h] >= LANES, second, first).T
        first_row = (net.col * halves + h) * PICKS
        scores_of[pl.ds(pl.multiple_of(first_row, PICKS), PICKS), :] = turned[head_rows, :]
    own_scores = rows_of(scores_of, halves * PICKS)
    score_spread = net.columns_start(own_scores)
    open_gate = jnp.dot(
        hidden_two[...], weights_two[:, depth : depth + width], preferred_element_type=F32
    )
    gate[...] = open_gate
    wait_all(cot_spread)
    back = jnp.dot(full_cot[...], weights_two[:, depth + width :], preferred_element_type=F32)
    grad_mixed[...] = back
    grad_memory[...] = (back * (open_gate * jax.nn.sigmoid(open_gate))).astype(LOW)
    wait_all(score_spread)
    for m in range(MH):
        score = (
            scores_of[2 * m * PICKS : (2 * m + 1) * PICKS]
            + scores_of[(2 * m + 1) * PICKS : (2 * m + 2) * PICKS]
        )
        shifted = jnp.exp(score - jnp.max(score, axis=0, keepdims=True))
        weights[m * PICKS : (m + 1) * PICKS] = shifted / jnp.sum(shifted, axis=0, keepdims=True)
    net.drain()


def norm_grad(net, grad_hidden, values, scale, gain, mine, theirs):
    width = values.shape[1]
    scaled = grad_hidden * gain
    inner = share_sums(net, jnp.sum(scaled * values, axis=1, keepdims=True), mine, theirs)
    wide = widen(scale, width)
    grads = wide * scaled - values * (wide * wide * wide) * widen(inner, width) / D
    grad_gain = jnp.sum(grad_hidden * values * wide, axis=0, keepdims=True)
    return grads, grad_gain


def project_start(net, left, weights, outgoing, incoming):
    width = outgoing.shape[2]

    def block(col):
        rows = rows_of(weights, width)(col)[...]
        return lax.dot_general(left, rows, NT_DIMS, preferred_element_type=F32)

    copies = []
    for k in range(1, net.cols):
        outgoing[k - 1] = block(flip(net.col, k)).astype(LOW)
        copies.append(net.send(outgoing.at[k - 1], incoming.at[k - 1], col_k=k))
    return block(net.col), copies


def project_end(total, incoming, copies):
    for k, copy in enumerate(copies):
        copy.wait_recv()
        total = total + incoming[k].astype(F32)
    return total


def attention_scores(qkv, head, ids_col, ids_row):
    parts = [qkv[:, (3 * head + j) * HD : (3 * head + j + 1) * HD] for j in range(3)]
    scores = lax.dot_general(parts[0], parts[1], NT_DIMS, preferred_element_type=F32) * HD ** (
        -0.5
    )
    asks = lax.broadcasted_iota(jnp.int32, scores.shape, 0)
    offers = lax.broadcasted_iota(jnp.int32, scores.shape, 1)
    allowed = (ids_col == ids_row) & (asks >= offers)
    scores = jnp.where(allowed, scores, MASKED)
    shifted = jnp.exp(scores - jnp.max(scores, axis=1, keepdims=True))
    return parts, shifted / jnp.sum(shifted, axis=1, keepdims=True)


def spread_picks(halves, weights, dw, index, out):
    tokens = weights.shape[1]
    grad = weights * (dw - jnp.sum(weights * dw, axis=0, keepdims=True))
    block = 128
    places = lax.broadcasted_iota(jnp.int32, (NK, block), 0)
    for h in range(halves):
        for b in range(tokens // block):
            columns = slice(b * block, (b + 1) * block)
            total = jnp.zeros((NK, block), F32)
            for k in range(PICKS):
                row = index[h * PICKS + k : h * PICKS + k + 1, columns]
                total = total + jnp.where(places == row, grad[k : k + 1, columns], 0.0)
            out[columns, h * NK : (h + 1) * NK] = total.T.astype(LOW)


def back_kernel(
    rows,
    cols,
    halves,
    share,
    dw,
    index,
    memory,
    gate,
    grad_mixed,
    queries,
    hidden_two,
    cot,
    weights_two,
    keys,
    resid,
    factor_two,
    gain_two,
    recv_row,
    send_col,
    qkv,
    mixed,
    lengths,
    hidden_one,
    weights_one,
    dealt,
    factor_one,
    gain_one,
    output,
    grad_tokens,
    own_qkv,
    own_attn,
    own_query,
    own_gate,
    own_mem,
    own_keys,
    gains,
    grad_sub,
    both,
    mixed_two,
    grad_two,
    grad_keys,
    grad_low,
    grad_resid,
    grad_qkv,
    grad_one,
    one_outgoing,
    one_incoming,
    res_outgoing,
    res_incoming,
    two_outgoing,
    two_incoming,
    mine,
    theirs,
    mine_one,
    theirs_one,
    packed,
    got,
    packed_one,
    got_one,
    across_two,
    two_out,
    two_in,
    across_keys,
    keys_out,
    keys_in,
    across_one,
    one_out,
    one_in,
    my_gains,
    their_gains,
    sends,
    recvs,
):
    net = Net(rows, cols, sends, recvs)
    capacity = packed.shape[0] // rows
    width = resid.shape[1]
    depth = halves * QD
    greeted = net.greet(range(1, rows), range(1, cols))
    head = net.col * halves // 2
    own_share = share[pl.ds(pl.multiple_of(head * PICKS, PICKS), PICKS), :]
    spread_picks(halves, own_share, dw[...], index, grad_sub)
    ids_col = sequence_ids(lengths[...], memory.shape[0], 0)
    ids_row = sequence_ids(lengths[...], memory.shape[0], 1)
    for h in range(halves):
        both[:, h * QD : (h + 1) * QD] = jnp.dot(
            grad_sub[:, h * NK : (h + 1) * NK], keys[h], preferred_element_type=F32
        ).astype(LOW)
    open_gate, back, read = gate[...], grad_mixed[...], memory[...]
    sigmoid = jax.nn.sigmoid(open_gate)
    both[:, depth:] = (back * read * sigmoid * (1.0 + open_gate * (1.0 - sigmoid))).astype(LOW)
    mixed_two[...] = (read * open_gate * sigmoid).astype(LOW)
    net.meet(greeted)
    own_part, reduce_two = project_start(
        net, both[...], weights_two.at[:, : depth + width], two_outgoing, two_incoming
    )
    hidden_t = hidden_two[...].T
    grad_two[:, : depth + width] = jnp.dot(hidden_t, both[...], preferred_element_type=F32)
    grad_two[:, depth + width :] = jnp.dot(
        cot[...].T, mixed_two[...], preferred_element_type=F32
    )
    for h in range(halves):
        grad_keys[h] = jnp.dot(
            grad_sub[:, h * NK : (h + 1) * NK].T,
            queries[:, h * QD : (h + 1) * QD],
            preferred_element_type=F32,
        )
    view_two = rows_of(grad_two, own_query.shape[0])
    span = own_keys.shape[1]
    view_keys = lambda at: grad_keys.at[:, pl.ds(pl.multiple_of(at * span, span), span), :]
    started_two = net.scatter_start(view_two, across_two)
    started_keys = net.scatter_start(view_keys, across_keys)
    moved_two, moved_keys, moved_one = {}, {}, {}
    pass_two = (view_two, across_two, started_two, two_out, two_in, moved_two)
    pass_keys = (view_keys, across_keys, started_keys, keys_out, keys_in, moved_keys)
    net.scatter_pass(*pass_two, True)
    net.scatter_pass(*pass_keys, True)
    grad_hidden = project_end(own_part, two_incoming, reduce_two)
    grads, gain_two_sum = norm_grad(
        net, grad_hidden, resid[...], factor_two[...], gain_two[...].astype(LOW).astype(F32), mine, theirs
    )
    own_cot = columns_of(cot, width)(net.col)[...]
    grads = grads + own_cot.astype(F32)
    grad_resid[...] = grads
    own = columns_of(grad_low, width)
    own(net.col)[...] = grads.astype(LOW)
    spread = net.columns_start(own)
    net.scatter_pass(*pass_two, False)
    net.scatter_pass(*pass_keys, False)
    wait_all(spread)
    own_res, reduce_res = project_start(
        net, mixed_two[...], weights_two.at[:, depth + width :], res_outgoing, res_incoming
    )
    grad_heads = jnp.dot(
        grad_low[...], weights_one[:, 3 * width :], preferred_element_type=F32
    ).astype(LOW)
    for head in range(width // HD):
        (query, key, value), probs = attention_scores(qkv, head, ids_col, ids_row)
        grad_out = grad_heads[:, head * HD : (head + 1) * HD]
        grad_prob = lax.dot_general(grad_out, value, NT_DIMS, preferred_element_type=F32)
        inner = jnp.sum(probs * grad_prob, axis=1, keepdims=True)
        grad_score = (probs * (grad_prob - inner)).astype(LOW)
        pieces = (
            jnp.dot(grad_score, key, preferred_element_type=F32) * HD ** (-0.5),
            jnp.dot(grad_score.T, query, preferred_element_type=F32) * HD ** (-0.5),
            jnp.dot(probs.astype(LOW).T, grad_out, preferred_element_type=F32),
        )
        for j in range(3):
            grad_qkv[:, (3 * head + j) * HD : (3 * head + j + 1) * HD] = pieces[j].astype(LOW)
    own_part, reduce_one = project_start(
        net, grad_qkv[...], weights_one.at[:, : 3 * width], one_outgoing, one_incoming
    )
    grad_one[:, : 3 * width] = jnp.dot(
        hidden_one[...].T, grad_qkv[...], preferred_element_type=F32
    )
    grad_one[:, 3 * width :] = jnp.dot(grad_low[...].T, mixed[...], preferred_element_type=F32)
    view_one = rows_of(grad_one, own_qkv.shape[0])
    started_one = net.scatter_start(view_one, across_one)
    block = resid[...] + project_end(own_res, res_incoming, reduce_res)
    pack_for_rows(net, packed, block.astype(LOW), recv_row[...])
    copies = exchange_start(net, packed, got, capacity)
    pass_one = (view_one, across_one, started_one, one_out, one_in, moved_one)
    net.scatter_pass(*pass_one, True)
    grad_hidden = project_end(own_part, one_incoming, reduce_one)
    grads, gain_one_sum = norm_grad(
        net,
        grad_hidden,
        dealt[...],
        factor_one[...],
        gain_one[...].astype(LOW).astype(F32),
        mine_one,
        theirs_one,
    )
    grads = grads + grad_resid[...]
    pack_for_rows(net, packed_one, grads.astype(LOW), recv_row[...])
    last = exchange_start(net, packed_one, got_one, capacity)
    net.scatter_pass(*pass_one, False)
    places = lax.broadcasted_iota(jnp.int32, my_gains.shape, 0)
    my_gains[...] = jnp.where(places == 0, gain_one_sum, gain_two_sum)
    gain_copies = [net.send(my_gains, their_gains.at[k], row_k=k) for k in range(1, rows)]
    total = net.scatter_end(view_two, across_two, started_two, two_in, moved_two)
    own_query[...] = total[:, :depth]
    own_gate[...] = total[:, depth : depth + width]
    own_mem[...] = total[:, depth + width :].T
    own_keys[...] = net.scatter_end(view_keys, across_keys, started_keys, keys_in, moved_keys)
    wait_all(copies)
    output[...] = unpack(got, send_col[...])
    total = net.scatter_end(view_one, across_one, started_one, one_in, moved_one)
    own_qkv[...] = total[:, : 3 * width]
    own_attn[...] = total[:, 3 * width :].T
    total = my_gains[...]
    for k, copy in enumerate(gain_copies):
        copy.wait_recv()
        total = total + their_gains[k + 1]
    gains[...] = total
    wait_all(last)
    grad_tokens[...] = unpack(got_one, send_col[...])
    net.drain()


def remote_call(kernel, rows, cols, number, copies, ins, outs, scratch, *sizes):
    return pl.pallas_call(
        functools.partial(kernel, rows, cols, *sizes),
        out_shape=[jax.ShapeDtypeStruct(shape, dtype) for shape, dtype in outs],
        in_specs=[VMEM_SPEC] * len(ins),
        out_specs=[VMEM_SPEC] * len(outs),
        scratch_shapes=[pltpu.VMEM(shape, dtype) for shape, dtype in scratch]
        + [pltpu.SemaphoreType.DMA((copies,)), pltpu.SemaphoreType.DMA((copies,))],
        compiler_params=pltpu.CompilerParams(
            collective_id=number, has_side_effects=True, vmem_limit_bytes=VMEM_BYTES
        ),
    )(*ins)


def memory_kernel(
    rows,
    cols,
    own_weights,
    own_picks,
    own_grads,
    table_f32,
    memory,
    dw,
    gacc,
    table,
    stage,
    picks_of,
    grads_of,
    low_of,
    dense,
    hi_ref,
    lo_ref,
    wide_ref,
    found_ref,
    mem_all,
    mem_twin,
    mem_out,
    mem_in,
    dw_all,
    dw_twin,
    dw_out,
    dw_in,
    dw_cols,
    stage_sems,
    sends,
    recvs,
):
    net = Net(rows, cols, sends, recvs)
    half = rows // 2
    tok_block = own_picks.shape[0]
    span_rows, width = table.shape
    spans = span_rows // LANES
    pitch = spans + 8
    iters = 4
    per_tok = tok_block // iters
    per_span = spans // iters

    grads_at = rows_of(grads_of, tok_block)
    picks_at = rows_of(picks_of, tok_block)
    low_at = lambda index: low_of.at[index]
    views = (grads_at, picks_at, low_at)
    first_pass = 3 * half
    first_twin = first_pass + 3 * half
    first_out = first_twin + 2 * half
    first_col = first_out + 2 * half

    def gather(a, j):
        mine = views[a](net.row)
        return net.copy(mine, mine, 3 * j + a, row_k=2 * j if j else 1)

    def passing(a, j):
        there = views[a](flip(net.row, 2 * j))
        return net.copy(there, there, first_pass + 3 * j + a, row_k=1)

    def twin(a, j):
        src, dst = ((mem_all, mem_twin), (dw_all, dw_twin))[a]
        return net.copy(src.at[2 * j + 1], dst.at[j], first_twin + 2 * j + a, row_k=1)

    def outward(a, j):
        src, dst = ((mem_out, mem_in), (dw_out, dw_in))[a]
        return net.copy(src.at[j - 1], dst.at[j - 1], first_out + 2 * j + a, row_k=2 * j)

    head = lambda col: pl.ds(pl.multiple_of(col * MH // cols * PICKS, PICKS), PICKS)

    def dw_copy(k):
        return net.copy(
            dw_all.at[0, head(flip(net.col, k)), :],
            dw_cols.at[k - 1],
            first_col + k,
            col_k=k,
        )

    stage_rows = stage.shape[1]

    def stage_copy(i):
        source = table_f32.at[pl.ds(i * stage_rows, stage_rows), :]
        return pltpu.make_async_copy(source, stage.at[i % 2], stage_sems.at[i % 2])

    stage_copy(0).start()
    net.meet(net.greet([1] + [2 * j for j in range(1, half)], range(1, cols)))
    grads_at(net.row)[...] = own_grads[...]
    picks_at(net.row)[...] = own_picks[...]
    low_at(net.row)[...] = own_weights[...].astype(LOW)
    for j in range(half):
        for a in range(3):
            gather(a, j).start()
    for i in range(span_rows // stage_rows):
        if (i + 1) * stage_rows < span_rows:
            stage_copy(i + 1).start()
        stage_copy(i).wait()
        table[i * stage_rows : (i + 1) * stage_rows, :] = stage[i % 2].astype(LOW)
    gacc[...] = jnp.zeros_like(gacc)
    mem_all[...] = jnp.zeros_like(mem_all)

    def one_block(step, _):
        k = jnp.where(step == 0, 0, jnp.where(step == rows - 1, 1, step + 1))
        there = cross(net.row, k, rows)
        for j in range(1, half):

            @pl.when(step == 2 * j - 1)
            def _():
                for a in range(3):
                    gather(a, j).wait_recv()
                    passing(a, j).start()

            @pl.when(step == 2 * j)
            def _():
                for a in range(3):
                    passing(a, j).wait_recv()

        @pl.when(step == rows - 1)
        def _():
            for a in range(3):
                gather(a, 0).wait_recv()

        picks = picks_at(there)[...].astype(jnp.int32) + 32768
        hi_ref[...] = (picks // LANES - net.row * spans).astype(F32)
        lo_ref[...] = (picks % LANES).astype(F32)
        wide_ref[...] = low_of[there].astype(F32).T
        places_lo = lax.broadcasted_iota(jnp.int32, (LANES, LANES), 0).astype(F32).astype(LOW)
        places_hi = lax.broadcasted_iota(jnp.int32, (spans, LANES), 0).astype(F32).astype(LOW)
        ones = jnp.ones((LANES, LANES), LOW)
        zeros = jnp.zeros((LANES, LANES), LOW)
        blank = jnp.zeros((spans, LANES), LOW)
        grads = grads_at(there)[...]
        grads_t = grads.T
        found_ref[...] = jnp.zeros_like(found_ref)
        lo_int = picks % LANES
        hi_all = hi_ref[...]

        def token_pair(first):
            rights, lefts = [], []
            for token in (first, first + 1):
                lo_row = jnp.broadcast_to(lo_ref[pl.ds(token, 1), :], (LANES, LANES)).astype(LOW)
                hi_row = jnp.broadcast_to(hi_ref[pl.ds(token, 1), :], (spans, LANES)).astype(LOW)
                w_row = jnp.broadcast_to(wide_ref[pl.ds(token, 1), :], (spans, LANES)).astype(LOW)
                rights.append(jnp.where(lo_row == places_lo, ones, zeros))
                lefts.append(jnp.where(hi_row == places_hi, w_row, blank))
            right = jnp.concatenate(rights, axis=1)
            left = jnp.concatenate(
                [
                    jnp.concatenate([lefts[0], blank], axis=1),
                    jnp.concatenate([blank, lefts[1]], axis=1),
                ],
                axis=0,
            )
            both = lax.dot_general(left, right, NT_DIMS, preferred_element_type=F32)
            for j in range(2):
                dense[pl.ds(pl.multiple_of((first + j) * pitch, 8), spans), :] = both[
                    j * spans : (j + 1) * spans
                ]

        def look(found, first, number, between=None):
            span = pl.ds(pl.multiple_of(first * LANES, LANES), number * LANES)
            products = lax.dot_general(
                grads, table[span, :], NT_DIMS, preferred_element_type=F32
            )
            for j in range(number):
                picked = jnp.take_along_axis(
                    products[:, LANES * j : LANES * (j + 1)], lo_int, axis=1
                )
                found = jnp.where(hi_all == (first + j).astype(F32), picked, found)
                if between:
                    between(j)
            return found

        early = per_span // 2
        late = per_span - early

        def build(it, _):
            for j in range(1, half):

                @pl.when((it == 1) & (step == 2 * j + 1))
                def _():
                    twin(0, j).wait_recv()
                    twin(1, j).wait_recv()
                    mem_out[j - 1] = (mem_all[2 * j] + mem_twin[j]).astype(LOW)
                    outward(0, j).start()
                    dw_out[j - 1] = dw_all[2 * j] + dw_twin[j]
                    outward(1, j).start()

            pairs = per_tok // 2 // early

            def some_pairs(j):
                for u in range(pairs):
                    token_pair(it * per_tok + (j * pairs + u) * 2)

            found_ref[...] = look(found_ref[...], it * early, early, some_pairs)
            return 0

        lax.fori_loop(0, iters, build, 0)
        parts = min(4, late)

        def multiply(it, _):
            found, total = found_ref[...], None
            for c in range(parts):
                low, high = c * late // parts, (c + 1) * late // parts
                found = look(found, early * iters + it * late + low, high - low)
                low, high = c * per_span // parts, (c + 1) * per_span // parts
                first = it * per_span + low
                chosen = jnp.concatenate(
                    [
                        dense[pl.ds(first + j, tok_block, stride=pitch), :].astype(LOW)
                        for j in range(high - low)
                    ],
                    axis=1,
                )
                span = pl.ds(pl.multiple_of(first * LANES, LANES), (high - low) * LANES)
                gacc[:, span] += jnp.dot(grads_t, chosen, preferred_element_type=F32)
                read = jnp.dot(chosen, table[span, :], preferred_element_type=F32)
                total = read if total is None else total + read
            mem_all[k] += total
            found_ref[...] = found
            return 0

        lax.fori_loop(0, iters, multiply, 0)
        dw_all[k] = found_ref[...].T
        for j in range(half):

            @pl.when(step == (2 * j if j else rows - 1))
            def _():
                twin(0, j).start()
                twin(1, j).start()

        return 0

    lax.fori_loop(0, rows, one_block, 0)
    twin(1, 0).wait_recv()
    total = dw_all[0] + dw_twin[0]
    for j in range(1, half):
        outward(1, j).wait_recv()
        total = total + dw_in[j - 1]
    dw_all[0] = total
    for k in range(1, cols):
        dw_copy(k).start()
    twin(0, 0).wait_recv()
    total = mem_all[0] + mem_twin[0]
    for j in range(1, half):
        outward(0, j).wait_recv()
        total = total + mem_in[j - 1].astype(F32)
    memory[...] = total
    total = dw_all[0, head(net.col), :]
    for k in range(1, cols):
        dw_copy(k).wait_recv()
        total = total + dw_cols[k - 1]
    dw[...] = total
    for k in range(1, cols):
        dw_copy(k).wait_send()
    for j in range(half):
        for a in range(3):
            gather(a, j).wait_send()
            if j:
                passing(a, j).wait_send()
        for a in range(2):
            twin(a, j).wait_send()
            if j:
                outward(a, j).wait_send()


def turn_kernel(source, out):
    out[...] = source[...].T


def turn_call(table):
    width, span_rows = table.shape
    block = 1024
    return pl.pallas_call(
        turn_kernel,
        grid=(span_rows // block,),
        in_specs=[pl.BlockSpec((width, block), lambda i: (0, i))],
        out_specs=pl.BlockSpec((block, width), lambda i: (i, 0)),
        out_shape=jax.ShapeDtypeStruct((span_rows, width), F32),
    )(table)


def memory_call(rows, cols, number, weights, picks, grads, table):
    tokens, count = picks.shape
    span_rows, width = table.shape
    half = rows // 2
    copies = 10 * half + cols
    vmem = pltpu.VMEM
    return pl.pallas_call(
        functools.partial(memory_kernel, rows, cols),
        in_specs=[VMEM_SPEC, VMEM_SPEC, VMEM_SPEC, pl.BlockSpec(memory_space=pl.ANY)],
        out_specs=[VMEM_SPEC] * 3,
        out_shape=[
            jax.ShapeDtypeStruct((tokens, width), F32),
            jax.ShapeDtypeStruct((PICKS, tokens), F32),
            jax.ShapeDtypeStruct((width, span_rows), F32),
        ],
        scratch_shapes=[
            vmem((span_rows, width), LOW),
            vmem((2, 1024, width), F32),
            vmem((rows * tokens, count), jnp.int16),
            vmem((rows * tokens, width), LOW),
            vmem((rows, count, tokens), LOW),
            vmem((tokens * (span_rows // LANES + 8), LANES), F32),
            vmem((tokens, count), F32),
            vmem((tokens, count), F32),
            vmem((tokens, count), F32),
            vmem((tokens, count), F32),
            vmem((rows, tokens, width), F32),
            vmem((half, tokens, width), F32),
            vmem((half - 1, tokens, width), LOW),
            vmem((half - 1, tokens, width), LOW),
            vmem((rows, count, tokens), F32),
            vmem((half, count, tokens), F32),
            vmem((half - 1, count, tokens), F32),
            vmem((half - 1, count, tokens), F32),
            vmem((cols - 1, PICKS, tokens), F32),
            pltpu.SemaphoreType.DMA((2,)),
            pltpu.SemaphoreType.DMA((copies,)),
            pltpu.SemaphoreType.DMA((copies,)),
        ],
        compiler_params=pltpu.CompilerParams(
            collective_id=number, has_side_effects=True, vmem_limit_bytes=63 * 2**20
        ),
    )(weights, picks, grads, table)


def per_device(
    tokens,
    cotangent,
    deal_order,
    seq_lengths,
    value_picks,
    norm1_gain,
    w_qkv,
    w_attn_out,
    norm2_gain,
    w_query,
    sub_keys,
    value_table,
    w_gate,
    w_mem_out,
):
    rows, cols = lax.axis_size("row"), lax.axis_size("col")
    row_index = lax.axis_index("row")
    count, width = tokens.shape
    slots = 2 * count
    half = rows // 2
    halves = sub_keys.shape[0]
    depth = halves * QD
    span_one, span_two = 4 * width, depth + 2 * width
    shard_rows = w_qkv.shape[0]
    flat_picks = value_picks.reshape(count, MH * PICKS)
    gain_one, gain_two = norm1_gain[None, :], norm2_gain[None, :]
    swap = [((slots, width), LOW), ((slots, width), LOW)]
    sums = [((8, count), F32), ((cols, 8, count), F32)]
    moving = ((cols - 1, count, width), LOW)
    (
        send_row,
        send_col,
        recv_row,
        recv_col,
        hidden_one,
        dealt,
        factor_one,
        weights_one,
        qkv,
        mixed,
        hidden_two,
        resid,
        factor_two,
        full_cot,
        weights_two,
        keys,
        queries,
        gate,
        grad_mixed,
        grad_memory,
        index,
        low_picks,
        pick_weights,
    ) = remote_call(
        front_kernel,
        rows,
        cols,
        0,
        7 * (cols - 1) + 5 * (rows - 1),
        [
            deal_order.reshape(rows, count),
            flat_picks,
            seq_lengths,
            tokens,
            cotangent,
            w_qkv,
            w_attn_out,
            w_query,
            w_gate,
            w_mem_out,
            sub_keys,
            gain_one,
            gain_two,
        ],
        [
            ((1, count), jnp.int32),
            ((count, 1), jnp.int32),
            ((1, count), jnp.int32),
            ((count, 1), jnp.int32),
            ((count, D), LOW),
            ((count, width), F32),
            ((count, LANES), F32),
            ((D, span_one), LOW),
            ((count, 3 * width), LOW),
            ((count, width), LOW),
            ((count, D), LOW),
            ((count, width), F32),
            ((count, LANES), F32),
            ((count, D), LOW),
            ((D, span_two), LOW),
            ((halves, NK, QD), LOW),
            ((count, depth), LOW),
            ((count, width), F32),
            ((count, width), F32),
            ((count, width), LOW),
            ((halves * PICKS, count), jnp.int32),
            ((count, MH * PICKS), jnp.int16),
            ((MH * PICKS, count), F32),
        ],
        [((2 * MH * PICKS, count), F32), ((count, D), LOW), ((8, D), F32), *swap, *swap, moving, moving, *sums]
        + [((MH * PICKS, count), F32)],
        halves,
    )
    memory, grad_pick, grad_table = memory_call(
        rows, cols, 1, pick_weights, low_picks, grad_memory, value_table
    )
    block = ((count, width), F32)
    scattered = [
        [((half,) + shape, F32), ((half - 1,) + shape, LOW), ((half - 1,) + shape, LOW)]
        for shape in ((shard_rows, span_two), sub_keys.shape, (shard_rows, span_one))
    ]
    output, grad_tokens, own_qkv, own_attn, own_query, own_gate, own_mem, own_keys, gains = remote_call(
        back_kernel,
        rows,
        cols,
        2,
        6 * (cols - 1) + 3 * (rows - 1) + 3 * (half + half - 1),
        [
            pick_weights,
            grad_pick,
            index,
            memory,
            gate,
            grad_mixed,
            queries,
            hidden_two,
            full_cot,
            weights_two,
            keys,
            resid,
            factor_two,
            gain_two,
            recv_row,
            send_col,
            qkv,
            mixed,
            seq_lengths,
            hidden_one,
            weights_one,
            dealt,
            factor_one,
            gain_one,
        ],
        [
            block,
            block,
            (w_qkv.shape, F32),
            (w_attn_out.shape, F32),
            (w_query.shape, F32),
            (w_gate.shape, F32),
            (w_mem_out.shape, F32),
            (sub_keys.shape, F32),
            ((8, width), F32),
        ],
        [
            ((count, halves * NK), LOW),
            ((count, depth + width), LOW),
            ((count, width), LOW),
            ((D, span_two), F32),
            ((halves, NK, QD), F32),
            ((count, D), LOW),
            block,
            ((count, 3 * width), LOW),
            ((D, span_one), F32),
            *[moving] * 6,
            *sums,
            *sums,
            *swap,
            *swap,
            *scattered[0],
            *scattered[1],
            *scattered[2],
            ((8, width), F32),
            ((rows, 8, width), F32),
        ],
        halves,
    )
    gain_span = width // rows
    gain_one_grad = lax.dynamic_slice_in_dim(gains[0], row_index * gain_span, gain_span)
    gain_two_grad = lax.dynamic_slice_in_dim(gains[1], row_index * gain_span, gain_span)
    return (
        output,
        grad_tokens,
        gain_one_grad,
        own_qkv,
        own_attn,
        gain_two_grad,
        own_query,
        own_keys,
        turn_call(grad_table),
        own_gate,
        own_mem,
    )


def solution(mesh):
    return jax.shard_map(
        per_device,
        mesh=mesh,
        in_specs=(
            P("row", "col"),
            P("row", "col"),
            P(),
            P("row", None),
            P("row", None, None),
            P("col"),
            P("row", "col"),
            P("col", "row"),
            P("col"),
            P("row", "col"),
            P("col", "row", None),
            P("row", "col"),
            P("row", "col"),
            P("col", "row"),
        ),
        out_specs=(
            P("row", "col"),
            P("row", "col"),
            P(("col", "row")),
            P("row", "col"),
            P("col", "row"),
            P(("col", "row")),
            P("row", "col"),
            P("col", "row", None),
            P("row", "col"),
            P("row", "col"),
            P("col", "row"),
        ),
        check_vma=False,
    )
```

```python
import functools

import jax
import jax.numpy as jnp
from jax import lax
from jax.experimental import pallas as pl
from jax.experimental.pallas import tpu as pltpu
from jax.sharding import PartitionSpec as P

D = 1024
HD = 64
MH = 4
QD = 512
NK = 256
PICKS = 32
LANES = 128
EPS = 1e-05
MASKED = -1e30
F32 = jnp.float32
LOW = jnp.bfloat16
MESH = pl.DeviceIdType.MESH
NT_DIMS = (((1,), (1,)), ((), ()))
VMEM_SPEC = pl.BlockSpec(memory_space=pltpu.VMEM)
VMEM_BYTES = 60 * 2**20


def flip(index, mask):
    bit = 1
    while bit <= mask:
        if mask & bit:
            index = index + bit - 2 * bit * (index // bit % 2)
        bit *= 2
    return index


def cross(index, mask, size):
    total, bit = 0, 1
    while bit < size:
        a, b = index // bit % 2, mask // bit % 2
        total = total + bit * (a + b - 2 * a * b)
        bit *= 2
    return total


class Net:
    def __init__(self, rows, cols, sends, recvs):
        self.rows, self.cols = rows, cols
        self.row, self.col = lax.axis_index("row"), lax.axis_index("col")
        self.sends, self.recvs, self.used = sends, recvs, 0
        self.pending = []

    def place(self, row_k, col_k):
        return (flip(self.row, row_k), flip(self.col, col_k))

    def greet(self, row_ks, col_ks):
        barrier = pltpu.get_barrier_semaphore()
        places = [self.place(k, 0) for k in row_ks] + [self.place(0, k) for k in col_ks]
        for place in places:
            pl.semaphore_signal(barrier, inc=1, device_id=place, device_id_type=MESH)
        return len(places)

    def meet(self, greeted):
        pl.semaphore_wait(pltpu.get_barrier_semaphore(), greeted)

    def copy(self, src, dst, number, row_k=0, col_k=0):
        assert number < self.sends.shape[0]
        return pltpu.make_async_remote_copy(
            src_ref=src,
            dst_ref=dst,
            send_sem=self.sends.at[number],
            recv_sem=self.recvs.at[number],
            device_id=self.place(row_k, col_k),
            device_id_type=MESH,
        )

    def send(self, src, dst, row_k=0, col_k=0):
        copy = self.copy(src, dst, self.used, row_k, col_k)
        copy.start()
        self.used += 1
        self.pending.append(copy)
        return copy

    def drain(self):
        for copy in self.pending:
            copy.wait_send()

    def gather_start(self, src, view):
        sent = {b: self.send(src, view(self.row), row_k=2 * b) for b in reversed(self.bits())}
        return sent, self.send(src, view(self.row), row_k=1)

    def gather_pass(self, view, started, near):
        sent, sibling = started
        passed = [sibling] if near else []
        masks = [m for m in range(1, self.rows // 2) if (m % 2 == 1) == near]
        for m in sorted(masks, key=lambda m: (-(m & -m), m.bit_count())):
            sent[m].wait_recv()
            block = view(flip(self.row, 2 * m))
            for b in self.bits():
                if b < (m & -m):
                    sent[m ^ b] = self.send(block, block, row_k=2 * b)
            passed.append(self.send(block, block, row_k=1))
        return passed

    def bits(self):
        return [1 << i for i in range((self.rows // 2 - 1).bit_length())]

    def scatter_start(self, view, across):
        twin = flip(self.row, 1)
        return [
            self.send(view(flip(twin, 2 * j)), across.at[j], row_k=1)
            for j in range(self.rows // 2)
        ]

    def scatter_pass(self, view, across, started, outgoing, incoming, moved, near):
        masks = [m for m in range(1, self.rows // 2) if (m % 2 == 1) == near]
        for m in sorted(masks, key=lambda m: ((m & -m), -m.bit_count())):
            started[m].wait_recv()
            block = view(flip(self.row, 2 * m))[...] + across[m]
            for b in self.bits():
                if b < (m & -m):
                    moved[m ^ b].wait_recv()
                    block = block + incoming[(m ^ b) - 1].astype(F32)
            outgoing[m - 1] = block.astype(outgoing.dtype)
            moved[m] = self.send(outgoing.at[m - 1], incoming.at[m - 1], row_k=2 * (m & -m))
        return moved

    def scatter_end(self, view, across, started, incoming, moved):
        started[0].wait_recv()
        total = view(self.row)[...] + across[0]
        for b in self.bits():
            moved[b].wait_recv()
            total = total + incoming[b - 1].astype(F32)
        return total

    def columns_start(self, view):
        return [self.send(view(self.col), view(self.col), col_k=k) for k in range(1, self.cols)]


def wait_all(copies):
    for copy in copies:
        copy.wait_recv()


def rows_of(ref, count):
    return lambda index: ref.at[pl.ds(pl.multiple_of(index * count, count), count), :]


def columns_of(ref, count):
    return lambda index: ref.at[:, pl.ds(pl.multiple_of(index * count, count), count)]


def one_hot_rows(positions, slots):
    places = lax.broadcasted_iota(jnp.int32, (positions.shape[0], slots), 1)
    return jnp.where(positions == places, 1.0, 0.0).astype(LOW)


def one_hot_columns(positions, slots):
    places = lax.broadcasted_iota(jnp.int32, (slots, positions.shape[1]), 0)
    return jnp.where(positions == places, 1.0, 0.0).astype(LOW)


def pack_for_rows(net, packed, values, positions):
    slots = packed.shape[0]
    packed[...] = jnp.dot(
        one_hot_columns(positions, slots), values, preferred_element_type=F32
    ).astype(LOW)


def exchange_start(net, packed, got, capacity):
    mine = rows_of(got, capacity)
    theirs = rows_of(packed, capacity)
    copies = [
        net.send(theirs(flip(net.row, k)), mine(net.row), row_k=k) for k in range(1, net.rows)
    ]
    mine(net.row)[...] = theirs(net.row)[...]
    return copies


def unpack(got, positions):
    return jnp.dot(
        one_hot_rows(positions, got.shape[0]), got[...], preferred_element_type=F32
    )


def share_sums(net, sums, mine, theirs):
    tokens = sums.shape[0]
    mine[...] = jnp.broadcast_to(sums, (tokens, LANES)).T[:8]
    copies = [net.send(mine, theirs.at[k], col_k=k) for k in range(1, net.cols)]
    wait_all(copies)
    total = mine[...]
    for k in range(1, net.cols):
        total = total + theirs[k]
    return jnp.broadcast_to(total[:1], (LANES, tokens)).T


def widen(lanes, width):
    return jnp.concatenate([lanes] * (width // LANES), axis=1)


def first_of(size, mask):
    earlier = lax.broadcasted_iota(jnp.int32, (size, size), 0)
    later = lax.broadcasted_iota(jnp.int32, (size, size), 1)
    triangle = jnp.where(earlier < later, 1.0, 0.0).astype(LOW)
    return jnp.dot(mask.astype(LOW), triangle, preferred_element_type=F32)


def find_places(rows, row, order, send_row, send_col, recv_row, recv_col):
    count = order.shape[1]
    capacity = 2 * count // rows
    owner = order[...] // count
    owned = jnp.where(owner == row, 1.0, 0.0)
    rank = first_of(count, owned)
    low_order = order[...].astype(F32).T
    tokens = lax.broadcasted_iota(jnp.int32, (count, count), 1).astype(F32)
    first = (row * count).astype(F32)
    sent = jnp.zeros((1, count), F32)
    pick = lax.broadcasted_iota(jnp.int32, (8, count), 0)
    for d in range(rows):
        match = jnp.where(low_order[:, d : d + 1] - first == tokens, 1.0, 0.0).astype(LOW)
        pair = jnp.where(pick == 0, rank[d : d + 1] * owned[d : d + 1], owned[d : d + 1])
        found = jnp.dot(pair.astype(LOW), match, preferred_element_type=F32)
        sent = sent + found[:1] + found[1:2] * (d * capacity)
    send_row[...] = sent.astype(jnp.int32)
    send_col[...] = jnp.broadcast_to(sent, (LANES, count)).T[:, :1].astype(jnp.int32)
    blocks = lax.broadcasted_iota(jnp.int32, (rows, count), 0)
    mine = jnp.sum(jnp.where(blocks == row, order[...], 0), axis=0, keepdims=True)
    source = mine // count
    came = jnp.where(source == lax.broadcasted_iota(jnp.int32, (LANES, count), 0), 1.0, 0.0)
    place = jnp.sum(first_of(count, came) * came, axis=0, keepdims=True)
    place = place + source.astype(F32) * capacity
    recv_row[...] = place.astype(jnp.int32)
    recv_col[...] = jnp.broadcast_to(place, (LANES, count)).T[:, :1].astype(jnp.int32)


def sequence_ids(lengths, count, axis):
    places = lax.broadcasted_iota(jnp.int32, (1, count) if axis else (count, 1), axis)
    end = jnp.zeros((1, 1), jnp.int32)
    ids = jnp.zeros(places.shape, jnp.int32)
    for j in range(lengths.shape[1]):
        end = end + lengths[:, j : j + 1]
        ids = ids + jnp.where(places >= end, 1, 0)
    return ids


def front_kernel(
    rows,
    cols,
    halves,
    need,
    flush,
    order,
    picks,
    lengths,
    tokens_ref,
    cot,
    w_qkv,
    w_attn,
    w_query,
    w_gate,
    w_mem,
    sub_keys,
    norm_one,
    norm_two,
    send_row,
    send_col,
    recv_row,
    recv_col,
    hidden_one,
    dealt,
    factor_one,
    weights_one,
    qkv,
    mixed,
    hidden_two,
    resid,
    factor_two,
    full_cot,
    weights_two,
    keys,
    queries,
    gate,
    grad_mixed,
    grad_memory,
    index,
    low_picks,
    weights,
    scores_of,
    full,
    gains,
    packed,
    got,
    packed_cot,
    got_cot,
    outgoing,
    incoming,
    mine,
    theirs,
    turned,
    sends,
    recvs,
):
    net = Net(rows, cols, sends, recvs)
    greeted = net.greet(range(1, rows), range(1, cols))
    count, width = tokens_ref.shape
    capacity = packed.shape[0] // rows
    depth = halves * QD
    need(order, tokens_ref)
    find_places(rows, net.row, order, send_row, send_col, recv_row, recv_col)
    pack_for_rows(net, packed, tokens_ref[...], send_row[...])
    net.meet(greeted)
    copies = exchange_start(net, packed, got, capacity)
    need(norm_one, norm_two, w_qkv, w_attn, cot, w_query, w_gate, w_mem, sub_keys, picks, lengths)
    own_gain = columns_of(gains, width)
    own_gain(net.col)[...] = jnp.broadcast_to(
        norm_one[...].astype(LOW).astype(F32), (8, width)
    )
    gain_spread = net.columns_start(own_gain)
    place_one = rows_of(weights_one, w_qkv.shape[0])
    place_one(net.row)[:, : 3 * width] = w_qkv[...].astype(LOW)
    place_one(net.row)[:, 3 * width :] = w_attn[...].T.astype(LOW)
    gather_one = net.gather_start(place_one(net.row), place_one)
    pack_for_rows(net, packed_cot, cot[...], send_row[...])
    cot_copies = exchange_start(net, packed_cot, got_cot, capacity)
    place_two = rows_of(weights_two, w_query.shape[0])
    place_two(net.row)[:, :depth] = w_query[...].astype(LOW)
    place_two(net.row)[:, depth : depth + width] = w_gate[...].astype(LOW)
    place_two(net.row)[:, depth + width :] = w_mem[...].T.astype(LOW)
    gather_two = net.gather_start(place_two(net.row), place_two)
    span = sub_keys.shape[1]
    place_keys = lambda at: keys.at[:, pl.ds(pl.multiple_of(at * span, span), span), :]
    place_keys(net.row)[...] = sub_keys[...].astype(LOW)
    gather_keys = net.gather_start(place_keys(net.row), place_keys)
    wait_all(copies)
    own = columns_of(full, width)
    values = unpack(got, recv_col[...])
    own(net.col)[...] = values.astype(LOW)
    spread = net.columns_start(own)
    dealt[...] = values
    left_one = net.gather_pass(place_one, gather_one, False)
    low_picks[...] = (picks[...] - 32768).astype(jnp.int16)
    head = net.col * halves // 2
    head_rows = pl.ds(pl.multiple_of(head * PICKS, PICKS), PICKS)
    halves_of = []
    for h in range(halves):
        even = (net.col * halves + h) % 2 == 0
        halves_of.append(jnp.where(even, picks[...] // NK, picks[...] % NK))
        turned[...] = halves_of[h].astype(F32).T
        index[h * PICKS : (h + 1) * PICKS] = turned[head_rows, :].astype(jnp.int32)
    ids_col = sequence_ids(lengths[...], count, 0)
    ids_row = sequence_ids(lengths[...], count, 1)
    wait_all(spread)
    wait_all(gain_spread)
    values = full[...].astype(F32)
    scale = lax.rsqrt(jnp.mean(values * values, axis=1, keepdims=True) + EPS)
    hidden_one[...] = (values * scale * gains[:1]).astype(LOW)
    factor_one[...] = jnp.broadcast_to(scale, (count, LANES))
    flush(hidden_one, factor_one, dealt, index, low_picks, send_row, send_col, recv_row, recv_col)
    wait_all(left_one + net.gather_pass(place_one, gather_one, True))
    flush(weights_one)
    qkv[...] = jnp.dot(
        hidden_one[...], weights_one[:, : 3 * width], preferred_element_type=F32
    ).astype(LOW)
    for h in range(width // HD):
        (_, _, value), probs = attention_scores(qkv, h, ids_col, ids_row)
        mixed[:, h * HD : (h + 1) * HD] = jnp.dot(
            probs.astype(LOW), value, preferred_element_type=F32
        ).astype(LOW)
    flush(qkv, mixed)
    own_part, reduce = project_start(
        net, mixed[...], weights_one.at[:, 3 * width :], outgoing, incoming
    )
    values = dealt[...] + project_end(own_part, incoming, reduce)
    resid[...] = values
    left = net.gather_pass(place_two, gather_two, False)
    left += net.gather_pass(place_keys, gather_keys, False)
    square = share_sums(net, jnp.sum(values * values, axis=1, keepdims=True), mine, theirs)
    scale = lax.rsqrt(square / D + EPS)
    factor_two[...] = scale
    flush(resid, factor_two)
    own = columns_of(hidden_two, width)
    gain_two = norm_two[...].astype(LOW).astype(F32)
    own(net.col)[...] = (resid[...] * widen(scale, width) * gain_two).astype(LOW)
    spread = net.columns_start(own)
    wait_all(cot_copies)
    own_cot = columns_of(full_cot, width)
    own_cot(net.col)[...] = unpack(got_cot, recv_col[...]).astype(LOW)
    cot_spread = net.columns_start(own_cot)
    left += net.gather_pass(place_two, gather_two, True)
    left += net.gather_pass(place_keys, gather_keys, True)
    wait_all(spread)
    wait_all(left)
    flush(hidden_two, weights_two, keys)
    for h in range(halves):
        columns = slice(h * QD, (h + 1) * QD)
        queries[:, columns] = jnp.dot(
            hidden_two[...], weights_two[:, columns], preferred_element_type=F32
        ).astype(LOW)
        scores = lax.dot_general(
            queries[:, columns], keys[h], NT_DIMS, preferred_element_type=F32
        )
        low_index = halves_of[h] % LANES
        first = jnp.take_along_axis(scores[:, :LANES], low_index, axis=1)
        second = jnp.take_along_axis(scores[:, LANES:], low_index, axis=1)
        turned[...] = jnp.where(halves_of[h] >= LANES, second, first).T
        first_row = (net.col * halves + h) * PICKS
        scores_of[pl.ds(pl.multiple_of(first_row, PICKS), PICKS), :] = turned[head_rows, :]
    own_scores = rows_of(scores_of, halves * PICKS)
    score_spread = net.columns_start(own_scores)
    open_gate = jnp.dot(
        hidden_two[...], weights_two[:, depth : depth + width], preferred_element_type=F32
    )
    gate[...] = open_gate
    wait_all(cot_spread)
    flush(full_cot, queries, gate)
    back = jnp.dot(full_cot[...], weights_two[:, depth + width :], preferred_element_type=F32)
    grad_mixed[...] = back
    grad_memory[...] = (back * (open_gate * jax.nn.sigmoid(open_gate))).astype(LOW)
    wait_all(score_spread)
    for m in range(MH):
        score = (
            scores_of[2 * m * PICKS : (2 * m + 1) * PICKS]
            + scores_of[(2 * m + 1) * PICKS : (2 * m + 2) * PICKS]
        )
        shifted = jnp.exp(score - jnp.max(score, axis=0, keepdims=True))
        weights[m * PICKS : (m + 1) * PICKS] = shifted / jnp.sum(shifted, axis=0, keepdims=True)
    net.drain()


def norm_grad(net, grad_hidden, values, scale, gain, mine, theirs):
    width = values.shape[1]
    scaled = grad_hidden * gain
    inner = share_sums(net, jnp.sum(scaled * values, axis=1, keepdims=True), mine, theirs)
    wide = widen(scale, width)
    grads = wide * scaled - values * (wide * wide * wide) * widen(inner, width) / D
    grad_gain = jnp.sum(grad_hidden * values * wide, axis=0, keepdims=True)
    return grads, grad_gain


def project_start(net, left, weights, outgoing, incoming):
    width = outgoing.shape[2]

    def block(col):
        rows = rows_of(weights, width)(col)[...]
        return lax.dot_general(left, rows, NT_DIMS, preferred_element_type=F32)

    copies = []
    for k in range(1, net.cols):
        outgoing[k - 1] = block(flip(net.col, k)).astype(LOW)
        copies.append(net.send(outgoing.at[k - 1], incoming.at[k - 1], col_k=k))
    return block(net.col), copies


def project_end(total, incoming, copies):
    for k, copy in enumerate(copies):
        copy.wait_recv()
        total = total + incoming[k].astype(F32)
    return total


def attention_scores(qkv, head, ids_col, ids_row):
    parts = [qkv[:, (3 * head + j) * HD : (3 * head + j + 1) * HD] for j in range(3)]
    scores = lax.dot_general(parts[0], parts[1], NT_DIMS, preferred_element_type=F32) * HD ** (
        -0.5
    )
    asks = lax.broadcasted_iota(jnp.int32, scores.shape, 0)
    offers = lax.broadcasted_iota(jnp.int32, scores.shape, 1)
    allowed = (ids_col == ids_row) & (asks >= offers)
    scores = jnp.where(allowed, scores, MASKED)
    shifted = jnp.exp(scores - jnp.max(scores, axis=1, keepdims=True))
    return parts, shifted / jnp.sum(shifted, axis=1, keepdims=True)


def spread_picks(halves, weights, dw, index, out):
    tokens = weights.shape[1]
    grad = weights * (dw - jnp.sum(weights * dw, axis=0, keepdims=True))
    block = 128
    places = lax.broadcasted_iota(jnp.int32, (NK, block), 0)
    for h in range(halves):
        for b in range(tokens // block):
            columns = slice(b * block, (b + 1) * block)
            total = jnp.zeros((NK, block), F32)
            for k in range(PICKS):
                row = index[h * PICKS + k : h * PICKS + k + 1, columns]
                total = total + jnp.where(places == row, grad[k : k + 1, columns], 0.0)
            out[columns, h * NK : (h + 1) * NK] = total.T.astype(LOW)


def back_kernel(
    rows,
    cols,
    halves,
    need,
    flush,
    share,
    dw,
    index,
    memory,
    gate,
    grad_mixed,
    queries,
    hidden_two,
    cot,
    weights_two,
    keys,
    resid,
    factor_two,
    gain_two,
    recv_row,
    send_col,
    qkv,
    mixed,
    lengths,
    hidden_one,
    weights_one,
    dealt,
    factor_one,
    gain_one,
    output,
    grad_tokens,
    own_qkv,
    own_attn,
    own_query,
    own_gate,
    own_mem,
    own_keys,
    gains,
    grad_sub,
    both,
    mixed_two,
    grad_two,
    grad_keys,
    grad_low,
    grad_resid,
    grad_qkv,
    grad_one,
    one_outgoing,
    one_incoming,
    res_outgoing,
    res_incoming,
    two_outgoing,
    two_incoming,
    mine,
    theirs,
    mine_one,
    theirs_one,
    packed,
    got,
    packed_one,
    got_one,
    across_two,
    two_out,
    two_in,
    across_keys,
    keys_out,
    keys_in,
    across_one,
    one_out,
    one_in,
    my_gains,
    their_gains,
    sends,
    recvs,
):
    net = Net(rows, cols, sends, recvs)
    capacity = packed.shape[0] // rows
    width = resid.shape[1]
    depth = halves * QD
    greeted = net.greet(range(1, rows), range(1, cols))
    need(share, dw, index, keys, gate, grad_mixed, memory, weights_two)
    head = net.col * halves // 2
    own_share = share[pl.ds(pl.multiple_of(head * PICKS, PICKS), PICKS), :]
    spread_picks(halves, own_share, dw[...], index, grad_sub)
    need(lengths)
    ids_col = sequence_ids(lengths[...], memory.shape[0], 0)
    ids_row = sequence_ids(lengths[...], memory.shape[0], 1)
    for h in range(halves):
        both[:, h * QD : (h + 1) * QD] = jnp.dot(
            grad_sub[:, h * NK : (h + 1) * NK], keys[h], preferred_element_type=F32
        ).astype(LOW)
    open_gate, back, read = gate[...], grad_mixed[...], memory[...]
    sigmoid = jax.nn.sigmoid(open_gate)
    both[:, depth:] = (back * read * sigmoid * (1.0 + open_gate * (1.0 - sigmoid))).astype(LOW)
    mixed_two[...] = (read * open_gate * sigmoid).astype(LOW)
    net.meet(greeted)
    own_part, reduce_two = project_start(
        net, both[...], weights_two.at[:, : depth + width], two_outgoing, two_incoming
    )
    need(hidden_two, cot, queries)
    hidden_t = hidden_two[...].T
    grad_two[:, : depth + width] = jnp.dot(hidden_t, both[...], preferred_element_type=F32)
    grad_two[:, depth + width :] = jnp.dot(
        cot[...].T, mixed_two[...], preferred_element_type=F32
    )
    for h in range(halves):
        grad_keys[h] = jnp.dot(
            grad_sub[:, h * NK : (h + 1) * NK].T,
            queries[:, h * QD : (h + 1) * QD],
            preferred_element_type=F32,
        )
    view_two = rows_of(grad_two, own_query.shape[0])
    span = own_keys.shape[1]
    view_keys = lambda at: grad_keys.at[:, pl.ds(pl.multiple_of(at * span, span), span), :]
    started_two = net.scatter_start(view_two, across_two)
    started_keys = net.scatter_start(view_keys, across_keys)
    moved_two, moved_keys, moved_one = {}, {}, {}
    pass_two = (view_two, across_two, started_two, two_out, two_in, moved_two)
    pass_keys = (view_keys, across_keys, started_keys, keys_out, keys_in, moved_keys)
    net.scatter_pass(*pass_two, True)
    net.scatter_pass(*pass_keys, True)
    need(resid, factor_two, gain_two)
    grad_hidden = project_end(own_part, two_incoming, reduce_two)
    grads, gain_two_sum = norm_grad(
        net, grad_hidden, resid[...], factor_two[...], gain_two[...].astype(LOW).astype(F32), mine, theirs
    )
    own_cot = columns_of(cot, width)(net.col)[...]
    grads = grads + own_cot.astype(F32)
    grad_resid[...] = grads
    own = columns_of(grad_low, width)
    own(net.col)[...] = grads.astype(LOW)
    spread = net.columns_start(own)
    net.scatter_pass(*pass_two, False)
    net.scatter_pass(*pass_keys, False)
    wait_all(spread)
    own_res, reduce_res = project_start(
        net, mixed_two[...], weights_two.at[:, depth + width :], res_outgoing, res_incoming
    )
    need(weights_one, qkv, hidden_one, mixed, recv_row, send_col, dealt, factor_one, gain_one)
    grad_heads = jnp.dot(
        grad_low[...], weights_one[:, 3 * width :], preferred_element_type=F32
    ).astype(LOW)
    for head in range(width // HD):
        (query, key, value), probs = attention_scores(qkv, head, ids_col, ids_row)
        grad_out = grad_heads[:, head * HD : (head + 1) * HD]
        grad_prob = lax.dot_general(grad_out, value, NT_DIMS, preferred_element_type=F32)
        inner = jnp.sum(probs * grad_prob, axis=1, keepdims=True)
        grad_score = (probs * (grad_prob - inner)).astype(LOW)
        pieces = (
            jnp.dot(grad_score, key, preferred_element_type=F32) * HD ** (-0.5),
            jnp.dot(grad_score.T, query, preferred_element_type=F32) * HD ** (-0.5),
            jnp.dot(probs.astype(LOW).T, grad_out, preferred_element_type=F32),
        )
        for j in range(3):
            grad_qkv[:, (3 * head + j) * HD : (3 * head + j + 1) * HD] = pieces[j].astype(LOW)
    own_part, reduce_one = project_start(
        net, grad_qkv[...], weights_one.at[:, : 3 * width], one_outgoing, one_incoming
    )
    grad_one[:, : 3 * width] = jnp.dot(
        hidden_one[...].T, grad_qkv[...], preferred_element_type=F32
    )
    grad_one[:, 3 * width :] = jnp.dot(grad_low[...].T, mixed[...], preferred_element_type=F32)
    view_one = rows_of(grad_one, own_qkv.shape[0])
    started_one = net.scatter_start(view_one, across_one)
    block = resid[...] + project_end(own_res, res_incoming, reduce_res)
    pack_for_rows(net, packed, block.astype(LOW), recv_row[...])
    copies = exchange_start(net, packed, got, capacity)
    pass_one = (view_one, across_one, started_one, one_out, one_in, moved_one)
    net.scatter_pass(*pass_one, True)
    grad_hidden = project_end(own_part, one_incoming, reduce_one)
    grads, gain_one_sum = norm_grad(
        net,
        grad_hidden,
        dealt[...],
        factor_one[...],
        gain_one[...].astype(LOW).astype(F32),
        mine_one,
        theirs_one,
    )
    grads = grads + grad_resid[...]
    pack_for_rows(net, packed_one, grads.astype(LOW), recv_row[...])
    last = exchange_start(net, packed_one, got_one, capacity)
    net.scatter_pass(*pass_one, False)
    places = lax.broadcasted_iota(jnp.int32, my_gains.shape, 0)
    my_gains[...] = jnp.where(places == 0, gain_one_sum, gain_two_sum)
    gain_copies = [net.send(my_gains, their_gains.at[k], row_k=k) for k in range(1, rows)]
    total = net.scatter_end(view_two, across_two, started_two, two_in, moved_two)
    own_query[...] = total[:, :depth]
    own_gate[...] = total[:, depth : depth + width]
    own_mem[...] = total[:, depth + width :].T
    own_keys[...] = net.scatter_end(view_keys, across_keys, started_keys, keys_in, moved_keys)
    wait_all(copies)
    output[...] = unpack(got, send_col[...])
    flush(output)
    total = net.scatter_end(view_one, across_one, started_one, one_in, moved_one)
    own_qkv[...] = total[:, : 3 * width]
    own_attn[...] = total[:, 3 * width :].T
    total = my_gains[...]
    for k, copy in enumerate(gain_copies):
        copy.wait_recv()
        total = total + their_gains[k + 1]
    gains[...] = total
    wait_all(last)
    grad_tokens[...] = unpack(got_one, send_col[...])
    net.drain()


def staged(kernel, rows, cols, sizes, ins, outs, *refs):
    given, results = refs[:ins], refs[ins : ins + outs]
    rest = refs[ins + outs :]
    twins, rest = rest[: ins + outs], rest[ins + outs :]
    sems, rest = rest[0], rest[1:]
    sources, targets = twins[:ins], twins[ins:]
    waited, left = set(), []

    def moving(i):
        return pltpu.make_async_copy(given[i], sources[i], sems.at[i])

    def need(*wanted):
        for ref in wanted:
            i = [j for j in range(ins) if sources[j] is ref][0]
            if i not in waited:
                moving(i).wait()
                waited.add(i)

    def flush(*done):
        for ref in done:
            i = [j for j in range(outs) if targets[j] is ref][0]
            copy = pltpu.make_async_copy(targets[i], results[i], sems.at[ins + i])
            copy.start()
            left.append((i, copy))

    for i in range(ins):
        moving(i).start()
    kernel(rows, cols, *sizes, need, flush, *sources, *targets, *rest)
    assert len(waited) == ins
    flush(*[targets[i] for i in range(outs) if i not in [j for j, _ in left]])
    for _, copy in left:
        copy.wait()


def remote_call(kernel, rows, cols, number, copies, ins, outs, scratch, *sizes):
    twins = [(x.shape, x.dtype) for x in ins] + outs
    anywhere = pl.BlockSpec(memory_space=pl.ANY)
    return pl.pallas_call(
        functools.partial(staged, kernel, rows, cols, sizes, len(ins), len(outs)),
        out_shape=[jax.ShapeDtypeStruct(shape, dtype) for shape, dtype in outs],
        in_specs=[anywhere] * len(ins),
        out_specs=[anywhere] * len(outs),
        scratch_shapes=[pltpu.VMEM(shape, dtype) for shape, dtype in twins]
        + [pltpu.SemaphoreType.DMA((len(twins),))]
        + [pltpu.VMEM(shape, dtype) for shape, dtype in scratch]
        + [pltpu.SemaphoreType.DMA((copies,)), pltpu.SemaphoreType.DMA((copies,))],
        compiler_params=pltpu.CompilerParams(
            collective_id=number, has_side_effects=True, vmem_limit_bytes=VMEM_BYTES
        ),
    )(*ins)


def memory_kernel(
    rows,
    cols,
    own_weights,
    own_picks,
    own_grads,
    table_f32,
    memory,
    dw,
    gacc_out,
    gacc,
    table,
    stage,
    picks_of,
    grads_of,
    low_of,
    dense,
    hi_ref,
    lo_ref,
    wide_ref,
    found_ref,
    mem_all,
    mem_twin,
    mem_out,
    mem_in,
    dw_all,
    dw_twin,
    dw_out,
    dw_in,
    dw_cols,
    stage_sems,
    sends,
    recvs,
):
    net = Net(rows, cols, sends, recvs)
    half = rows // 2
    tok_block = own_picks.shape[0]
    span_rows, width = table.shape
    spans = span_rows // LANES
    pitch = spans + 8
    iters = 4
    per_tok = tok_block // iters
    per_span = spans // iters

    grads_at = rows_of(grads_of, tok_block)
    picks_at = rows_of(picks_of, tok_block)
    low_at = lambda index: low_of.at[index]
    views = (grads_at, picks_at, low_at)
    first_pass = 3 * half
    first_twin = first_pass + 3 * half
    first_out = first_twin + 2 * half
    first_col = first_out + 2 * half

    def gather(a, j):
        mine = views[a](net.row)
        return net.copy(mine, mine, 3 * j + a, row_k=2 * j if j else 1)

    def passing(a, j):
        there = views[a](flip(net.row, 2 * j))
        return net.copy(there, there, first_pass + 3 * j + a, row_k=1)

    def twin(a, j):
        src, dst = ((mem_all, mem_twin), (dw_all, dw_twin))[a]
        return net.copy(src.at[2 * j + 1], dst.at[j], first_twin + 2 * j + a, row_k=1)

    def outward(a, j):
        src, dst = ((mem_out, mem_in), (dw_out, dw_in))[a]
        return net.copy(src.at[j - 1], dst.at[j - 1], first_out + 2 * j + a, row_k=2 * j)

    head = lambda col: pl.ds(pl.multiple_of(col * MH // cols * PICKS, PICKS), PICKS)

    def dw_copy(k):
        return net.copy(
            dw_all.at[0, head(flip(net.col, k)), :],
            dw_cols.at[k - 1],
            first_col + k,
            col_k=k,
        )

    stage_rows = stage.shape[1]

    def stage_copy(i):
        source = table_f32.at[pl.ds(i * stage_rows, stage_rows), :]
        return pltpu.make_async_copy(source, stage.at[i % 2], stage_sems.at[i % 2])

    stage_copy(0).start()
    greeted = net.greet([1] + [2 * j for j in range(1, half)], range(1, cols))
    for i in range(span_rows // stage_rows):
        if (i + 1) * stage_rows < span_rows:
            stage_copy(i + 1).start()
        stage_copy(i).wait()
        table[i * stage_rows : (i + 1) * stage_rows, :] = stage[i % 2].astype(LOW)
    net.meet(greeted)
    grads_at(net.row)[...] = own_grads[...]
    picks_at(net.row)[...] = own_picks[...]
    low_at(net.row)[...] = own_weights[...].astype(LOW)
    for j in range(half):
        for a in range(3):
            gather(a, j).start()
    gacc[...] = jnp.zeros_like(gacc)
    mem_all[...] = jnp.zeros_like(mem_all)

    def one_block(step, _):
        k = jnp.where(step == 0, 0, jnp.where(step == rows - 1, 1, step + 1))
        there = cross(net.row, k, rows)
        for j in range(1, half):

            @pl.when(step == 2 * j - 1)
            def _():
                for a in range(3):
                    gather(a, j).wait_recv()
                    passing(a, j).start()

            @pl.when(step == 2 * j)
            def _():
                for a in range(3):
                    passing(a, j).wait_recv()

        @pl.when(step == rows - 1)
        def _():
            for a in range(3):
                gather(a, 0).wait_recv()

        picks = picks_at(there)[...].astype(jnp.int32) + 32768
        hi_ref[...] = (picks // LANES - net.row * spans).astype(F32)
        lo_ref[...] = (picks % LANES).astype(F32)
        wide_ref[...] = low_of[there].astype(F32).T
        places_lo = lax.broadcasted_iota(jnp.int32, (LANES, LANES), 0).astype(F32).astype(LOW)
        places_hi = lax.broadcasted_iota(jnp.int32, (spans, LANES), 0).astype(F32).astype(LOW)
        ones = jnp.ones((LANES, LANES), LOW)
        zeros = jnp.zeros((LANES, LANES), LOW)
        blank = jnp.zeros((spans, LANES), LOW)
        grads = grads_at(there)[...]
        grads_t = grads.T
        found_ref[...] = jnp.zeros_like(found_ref)
        lo_int = picks % LANES
        hi_all = hi_ref[...]

        def token_pair(first):
            rights, lefts = [], []
            for token in (first, first + 1):
                lo_row = jnp.broadcast_to(lo_ref[pl.ds(token, 1), :], (LANES, LANES)).astype(LOW)
                hi_row = jnp.broadcast_to(hi_ref[pl.ds(token, 1), :], (spans, LANES)).astype(LOW)
                w_row = jnp.broadcast_to(wide_ref[pl.ds(token, 1), :], (spans, LANES)).astype(LOW)
                rights.append(jnp.where(lo_row == places_lo, ones, zeros))
                lefts.append(jnp.where(hi_row == places_hi, w_row, blank))
            right = jnp.concatenate(rights, axis=1)
            left = jnp.concatenate(
                [
                    jnp.concatenate([lefts[0], blank], axis=1),
                    jnp.concatenate([blank, lefts[1]], axis=1),
                ],
                axis=0,
            )
            both = lax.dot_general(left, right, NT_DIMS, preferred_element_type=F32)
            for j in range(2):
                dense[pl.ds(pl.multiple_of((first + j) * pitch, 8), spans), :] = both[
                    j * spans : (j + 1) * spans
                ]

        def look(found, first, number, between=None):
            span = pl.ds(pl.multiple_of(first * LANES, LANES), number * LANES)
            products = lax.dot_general(
                grads, table[span, :], NT_DIMS, preferred_element_type=F32
            )
            for j in range(number):
                picked = jnp.take_along_axis(
                    products[:, LANES * j : LANES * (j + 1)], lo_int, axis=1
                )
                found = jnp.where(hi_all == (first + j).astype(F32), picked, found)
                if between:
                    between(j)
            return found

        early = per_span // 2
        late = per_span - early

        def build(it, _):
            for j in range(1, half):

                @pl.when((it == 1) & (step == 2 * j + 1))
                def _():
                    twin(0, j).wait_recv()
                    twin(1, j).wait_recv()
                    mem_out[j - 1] = (mem_all[2 * j] + mem_twin[j]).astype(LOW)
                    outward(0, j).start()
                    dw_out[j - 1] = dw_all[2 * j] + dw_twin[j]
                    outward(1, j).start()

            pairs = per_tok // 2 // early

            def some_pairs(j):
                for u in range(pairs):
                    token_pair(it * per_tok + (j * pairs + u) * 2)

            found_ref[...] = look(found_ref[...], it * early, early, some_pairs)
            return 0

        lax.fori_loop(0, iters, build, 0)
        parts = min(4, late)

        def multiply(it, _):
            found, total = found_ref[...], None
            for c in range(parts):
                low, high = c * late // parts, (c + 1) * late // parts
                found = look(found, early * iters + it * late + low, high - low)
                low, high = c * per_span // parts, (c + 1) * per_span // parts
                first = it * per_span + low
                chosen = jnp.concatenate(
                    [
                        dense[pl.ds(first + j, tok_block, stride=pitch), :].astype(LOW)
                        for j in range(high - low)
                    ],
                    axis=1,
                )
                span = pl.ds(pl.multiple_of(first * LANES, LANES), (high - low) * LANES)
                gacc[:, span] += jnp.dot(grads_t, chosen, preferred_element_type=F32)
                read = jnp.dot(chosen, table[span, :], preferred_element_type=F32)
                total = read if total is None else total + read
            mem_all[k] += total
            found_ref[...] = found
            return 0

        lax.fori_loop(0, iters, multiply, 0)
        dw_all[k] = found_ref[...].T
        for j in range(half):

            @pl.when(step == (2 * j if j else rows - 1))
            def _():
                twin(0, j).start()
                twin(1, j).start()

        return 0

    lax.fori_loop(0, rows, one_block, 0)
    leaving = pltpu.make_async_copy(gacc, gacc_out, stage_sems.at[2])
    leaving.start()
    twin(1, 0).wait_recv()
    total = dw_all[0] + dw_twin[0]
    for j in range(1, half):
        outward(1, j).wait_recv()
        total = total + dw_in[j - 1]
    dw_all[0] = total
    for k in range(1, cols):
        dw_copy(k).start()
    twin(0, 0).wait_recv()
    total = mem_all[0] + mem_twin[0]
    for j in range(1, half):
        outward(0, j).wait_recv()
        total = total + mem_in[j - 1].astype(F32)
    memory[...] = total
    total = dw_all[0, head(net.col), :]
    for k in range(1, cols):
        dw_copy(k).wait_recv()
        total = total + dw_cols[k - 1]
    dw[...] = total
    for k in range(1, cols):
        dw_copy(k).wait_send()
    for j in range(half):
        for a in range(3):
            gather(a, j).wait_send()
            if j:
                passing(a, j).wait_send()
        for a in range(2):
            twin(a, j).wait_send()
            if j:
                outward(a, j).wait_send()
    leaving.wait()


def turn_kernel(source, out):
    out[...] = source[...].T


def turn_call(table):
    width, span_rows = table.shape
    block = 1024
    return pl.pallas_call(
        turn_kernel,
        grid=(span_rows // block,),
        in_specs=[pl.BlockSpec((width, block), lambda i: (0, i))],
        out_specs=pl.BlockSpec((block, width), lambda i: (i, 0)),
        out_shape=jax.ShapeDtypeStruct((span_rows, width), F32),
    )(table)


def memory_call(rows, cols, number, weights, picks, grads, table):
    tokens, count = picks.shape
    span_rows, width = table.shape
    half = rows // 2
    copies = 10 * half + cols
    vmem = pltpu.VMEM
    return pl.pallas_call(
        functools.partial(memory_kernel, rows, cols),
        in_specs=[VMEM_SPEC, VMEM_SPEC, VMEM_SPEC, pl.BlockSpec(memory_space=pl.ANY)],
        out_specs=[VMEM_SPEC, VMEM_SPEC, pl.BlockSpec(memory_space=pl.ANY)],
        out_shape=[
            jax.ShapeDtypeStruct((tokens, width), F32),
            jax.ShapeDtypeStruct((PICKS, tokens), F32),
            jax.ShapeDtypeStruct((width, span_rows), F32),
        ],
        scratch_shapes=[
            vmem((width, span_rows), F32),
            vmem((span_rows, width), LOW),
            vmem((2, 1024, width), F32),
            vmem((rows * tokens, count), jnp.int16),
            vmem((rows * tokens, width), LOW),
            vmem((rows, count, tokens), LOW),
            vmem((tokens * (span_rows // LANES + 8), LANES), F32),
            vmem((tokens, count), F32),
            vmem((tokens, count), F32),
            vmem((tokens, count), F32),
            vmem((tokens, count), F32),
            vmem((rows, tokens, width), F32),
            vmem((half, tokens, width), F32),
            vmem((half - 1, tokens, width), LOW),
            vmem((half - 1, tokens, width), LOW),
            vmem((rows, count, tokens), F32),
            vmem((half, count, tokens), F32),
            vmem((half - 1, count, tokens), F32),
            vmem((half - 1, count, tokens), F32),
            vmem((cols - 1, PICKS, tokens), F32),
            pltpu.SemaphoreType.DMA((3,)),
            pltpu.SemaphoreType.DMA((copies,)),
            pltpu.SemaphoreType.DMA((copies,)),
        ],
        compiler_params=pltpu.CompilerParams(
            collective_id=number, has_side_effects=True, vmem_limit_bytes=63 * 2**20
        ),
    )(weights, picks, grads, table)


def per_device(
    tokens,
    cotangent,
    deal_order,
    seq_lengths,
    value_picks,
    norm1_gain,
    w_qkv,
    w_attn_out,
    norm2_gain,
    w_query,
    sub_keys,
    value_table,
    w_gate,
    w_mem_out,
):
    rows, cols = lax.axis_size("row"), lax.axis_size("col")
    row_index = lax.axis_index("row")
    count, width = tokens.shape
    slots = 2 * count
    half = rows // 2
    halves = sub_keys.shape[0]
    depth = halves * QD
    span_one, span_two = 4 * width, depth + 2 * width
    shard_rows = w_qkv.shape[0]
    flat_picks = value_picks.reshape(count, MH * PICKS)
    gain_one, gain_two = norm1_gain[None, :], norm2_gain[None, :]
    swap = [((slots, width), LOW), ((slots, width), LOW)]
    sums = [((8, count), F32), ((cols, 8, count), F32)]
    moving = ((cols - 1, count, width), LOW)
    (
        send_row,
        send_col,
        recv_row,
        recv_col,
        hidden_one,
        dealt,
        factor_one,
        weights_one,
        qkv,
        mixed,
        hidden_two,
        resid,
        factor_two,
        full_cot,
        weights_two,
        keys,
        queries,
        gate,
        grad_mixed,
        grad_memory,
        index,
        low_picks,
        pick_weights,
    ) = remote_call(
        front_kernel,
        rows,
        cols,
        0,
        7 * (cols - 1) + 5 * (rows - 1),
        [
            deal_order.reshape(rows, count),
            flat_picks,
            seq_lengths,
            tokens,
            cotangent,
            w_qkv,
            w_attn_out,
            w_query,
            w_gate,
            w_mem_out,
            sub_keys,
            gain_one,
            gain_two,
        ],
        [
            ((1, count), jnp.int32),
            ((count, 1), jnp.int32),
            ((1, count), jnp.int32),
            ((count, 1), jnp.int32),
            ((count, D), LOW),
            ((count, width), F32),
            ((count, LANES), F32),
            ((D, span_one), LOW),
            ((count, 3 * width), LOW),
            ((count, width), LOW),
            ((count, D), LOW),
            ((count, width), F32),
            ((count, LANES), F32),
            ((count, D), LOW),
            ((D, span_two), LOW),
            ((halves, NK, QD), LOW),
            ((count, depth), LOW),
            ((count, width), F32),
            ((count, width), F32),
            ((count, width), LOW),
            ((halves * PICKS, count), jnp.int32),
            ((count, MH * PICKS), jnp.int16),
            ((MH * PICKS, count), F32),
        ],
        [((2 * MH * PICKS, count), F32), ((count, D), LOW), ((8, D), F32), *swap, *swap, moving, moving, *sums]
        + [((MH * PICKS, count), F32)],
        halves,
    )
    memory, grad_pick, grad_table = memory_call(
        rows, cols, 1, pick_weights, low_picks, grad_memory, value_table
    )
    block = ((count, width), F32)
    scattered = [
        [((half,) + shape, F32), ((half - 1,) + shape, LOW), ((half - 1,) + shape, LOW)]
        for shape in ((shard_rows, span_two), sub_keys.shape, (shard_rows, span_one))
    ]
    output, grad_tokens, own_qkv, own_attn, own_query, own_gate, own_mem, own_keys, gains = remote_call(
        back_kernel,
        rows,
        cols,
        2,
        6 * (cols - 1) + 3 * (rows - 1) + 3 * (half + half - 1),
        [
            pick_weights,
            grad_pick,
            index,
            memory,
            gate,
            grad_mixed,
            queries,
            hidden_two,
            full_cot,
            weights_two,
            keys,
            resid,
            factor_two,
            gain_two,
            recv_row,
            send_col,
            qkv,
            mixed,
            seq_lengths,
            hidden_one,
            weights_one,
            dealt,
            factor_one,
            gain_one,
        ],
        [
            block,
            block,
            (w_qkv.shape, F32),
            (w_attn_out.shape, F32),
            (w_query.shape, F32),
            (w_gate.shape, F32),
            (w_mem_out.shape, F32),
            (sub_keys.shape, F32),
            ((8, width), F32),
        ],
        [
            ((count, halves * NK), LOW),
            ((count, depth + width), LOW),
            ((count, width), LOW),
            ((D, span_two), F32),
            ((halves, NK, QD), F32),
            ((count, D), LOW),
            block,
            ((count, 3 * width), LOW),
            ((D, span_one), F32),
            *[moving] * 6,
            *sums,
            *sums,
            *swap,
            *swap,
            *scattered[0],
            *scattered[1],
            *scattered[2],
            ((8, width), F32),
            ((rows, 8, width), F32),
        ],
        halves,
    )
    gain_span = width // rows
    gain_one_grad = lax.dynamic_slice_in_dim(gains[0], row_index * gain_span, gain_span)
    gain_two_grad = lax.dynamic_slice_in_dim(gains[1], row_index * gain_span, gain_span)
    return (
        output,
        grad_tokens,
        gain_one_grad,
        own_qkv,
        own_attn,
        gain_two_grad,
        own_query,
        own_keys,
        turn_call(grad_table),
        own_gate,
        own_mem,
    )


def solution(mesh):
    return jax.shard_map(
        per_device,
        mesh=mesh,
        in_specs=(
            P("row", "col"),
            P("row", "col"),
            P(),
            P("row", None),
            P("row", None, None),
            P("col"),
            P("row", "col"),
            P("col", "row"),
            P("col"),
            P("row", "col"),
            P("col", "row", None),
            P("row", "col"),
            P("row", "col"),
            P("col", "row"),
        ),
        out_specs=(
            P("row", "col"),
            P("row", "col"),
            P(("col", "row")),
            P("row", "col"),
            P("col", "row"),
            P(("col", "row")),
            P("row", "col"),
            P("col", "row", None),
            P("row", "col"),
            P("row", "col"),
            P("col", "row"),
        ),
        check_vma=False,
    )
```

```python
import functools

import jax
import jax.numpy as jnp
from jax import lax
from jax.experimental import pallas as pl
from jax.experimental.pallas import tpu as pltpu
from jax.sharding import PartitionSpec as P

D = 1024
HD = 64
MH = 4
QD = 512
NK = 256
PICKS = 32
LANES = 128
EPS = 1e-05
MASKED = -1e30
F32 = jnp.float32
LOW = jnp.bfloat16
MESH = pl.DeviceIdType.MESH
NT_DIMS = (((1,), (1,)), ((), ()))
VMEM_SPEC = pl.BlockSpec(memory_space=pltpu.VMEM)
VMEM_BYTES = 60 * 2**20


def flip(index, mask):
    bit = 1
    while bit <= mask:
        if mask & bit:
            index = index + bit - 2 * bit * (index // bit % 2)
        bit *= 2
    return index


def cross(index, mask, size):
    total, bit = 0, 1
    while bit < size:
        a, b = index // bit % 2, mask // bit % 2
        total = total + bit * (a + b - 2 * a * b)
        bit *= 2
    return total


class Net:
    def __init__(self, rows, cols, sends, recvs):
        self.rows, self.cols = rows, cols
        self.row, self.col = lax.axis_index("row"), lax.axis_index("col")
        self.sends, self.recvs, self.used = sends, recvs, 0
        self.pending = []

    def place(self, row_k, col_k):
        return (flip(self.row, row_k), flip(self.col, col_k))

    def greet(self, row_ks, col_ks):
        barrier = pltpu.get_barrier_semaphore()
        places = [self.place(k, 0) for k in row_ks] + [self.place(0, k) for k in col_ks]
        for place in places:
            pl.semaphore_signal(barrier, inc=1, device_id=place, device_id_type=MESH)
        return len(places)

    def meet(self, greeted):
        pl.semaphore_wait(pltpu.get_barrier_semaphore(), greeted)

    def copy(self, src, dst, number, row_k=0, col_k=0):
        assert number < self.sends.shape[0]
        return pltpu.make_async_remote_copy(
            src_ref=src,
            dst_ref=dst,
            send_sem=self.sends.at[number],
            recv_sem=self.recvs.at[number],
            device_id=self.place(row_k, col_k),
            device_id_type=MESH,
        )

    def send(self, src, dst, row_k=0, col_k=0):
        copy = self.copy(src, dst, self.used, row_k, col_k)
        copy.start()
        self.used += 1
        self.pending.append(copy)
        return copy

    def drain(self):
        for copy in self.pending:
            copy.wait_send()

    def gather_start(self, src, view):
        sent = {b: self.send(src, view(self.row), row_k=2 * b) for b in reversed(self.bits())}
        return sent, self.send(src, view(self.row), row_k=1)

    def gather_pass(self, view, started, near):
        sent, sibling = started
        passed = [sibling] if near else []
        masks = [m for m in range(1, self.rows // 2) if (m % 2 == 1) == near]
        for m in sorted(masks, key=lambda m: (-(m & -m), m.bit_count())):
            sent[m].wait_recv()
            block = view(flip(self.row, 2 * m))
            for b in self.bits():
                if b < (m & -m):
                    sent[m ^ b] = self.send(block, block, row_k=2 * b)
            passed.append(self.send(block, block, row_k=1))
        return passed

    def bits(self):
        return [1 << i for i in range((self.rows // 2 - 1).bit_length())]

    def scatter_start(self, view, across):
        twin = flip(self.row, 1)
        return [
            self.send(view(flip(twin, 2 * j)), across.at[j], row_k=1)
            for j in range(self.rows // 2)
        ]

    def scatter_pass(self, view, across, started, outgoing, incoming, moved, near):
        masks = [m for m in range(1, self.rows // 2) if (m % 2 == 1) == near]
        for m in sorted(masks, key=lambda m: ((m & -m), -m.bit_count())):
            started[m].wait_recv()
            block = view(flip(self.row, 2 * m))[...] + across[m]
            for b in self.bits():
                if b < (m & -m):
                    moved[m ^ b].wait_recv()
                    block = block + incoming[(m ^ b) - 1].astype(F32)
            outgoing[m - 1] = block.astype(outgoing.dtype)
            moved[m] = self.send(outgoing.at[m - 1], incoming.at[m - 1], row_k=2 * (m & -m))
        return moved

    def scatter_end(self, view, across, started, incoming, moved):
        started[0].wait_recv()
        total = view(self.row)[...] + across[0]
        for b in self.bits():
            moved[b].wait_recv()
            total = total + incoming[b - 1].astype(F32)
        return total

    def columns_start(self, view):
        return [self.send(view(self.col), view(self.col), col_k=k) for k in range(1, self.cols)]


def wait_all(copies):
    for copy in copies:
        copy.wait_recv()


def rows_of(ref, count):
    return lambda index: ref.at[pl.ds(pl.multiple_of(index * count, count), count), :]


def columns_of(ref, count):
    return lambda index: ref.at[:, pl.ds(pl.multiple_of(index * count, count), count)]


def one_hot_rows(positions, slots):
    places = lax.broadcasted_iota(jnp.int32, (positions.shape[0], slots), 1)
    return jnp.where(positions == places, 1.0, 0.0).astype(LOW)


def one_hot_columns(positions, slots):
    places = lax.broadcasted_iota(jnp.int32, (slots, positions.shape[1]), 0)
    return jnp.where(positions == places, 1.0, 0.0).astype(LOW)


def pack_for_rows(net, packed, values, positions):
    slots = packed.shape[0]
    packed[...] = jnp.dot(
        one_hot_columns(positions, slots), values, preferred_element_type=F32
    ).astype(LOW)


def exchange_start(net, packed, got, capacity):
    mine = rows_of(got, capacity)
    theirs = rows_of(packed, capacity)
    copies = [
        net.send(theirs(flip(net.row, k)), mine(net.row), row_k=k) for k in range(1, net.rows)
    ]
    mine(net.row)[...] = theirs(net.row)[...]
    return copies


def unpack(got, positions):
    return jnp.dot(
        one_hot_rows(positions, got.shape[0]), got[...], preferred_element_type=F32
    )


def share_sums(net, sums, mine, theirs):
    tokens = sums.shape[0]
    mine[...] = jnp.broadcast_to(sums, (tokens, LANES)).T[:8]
    copies = [net.send(mine, theirs.at[k], col_k=k) for k in range(1, net.cols)]
    wait_all(copies)
    total = mine[...]
    for k in range(1, net.cols):
        total = total + theirs[k]
    return jnp.broadcast_to(total[:1], (LANES, tokens)).T


def widen(lanes, width):
    return jnp.concatenate([lanes] * (width // LANES), axis=1)


def first_of(size, mask):
    earlier = lax.broadcasted_iota(jnp.int32, (size, size), 0)
    later = lax.broadcasted_iota(jnp.int32, (size, size), 1)
    triangle = jnp.where(earlier < later, 1.0, 0.0).astype(LOW)
    return jnp.dot(mask.astype(LOW), triangle, preferred_element_type=F32)


def find_places(rows, row, order, send_row, send_col, recv_row, recv_col):
    count = order.shape[1]
    capacity = 2 * count // rows
    owner = order[...] // count
    owned = jnp.where(owner == row, 1.0, 0.0)
    rank = first_of(count, owned)
    low_order = order[...].astype(F32).T
    tokens = lax.broadcasted_iota(jnp.int32, (count, count), 1).astype(F32)
    first = (row * count).astype(F32)
    sent = jnp.zeros((1, count), F32)
    pick = lax.broadcasted_iota(jnp.int32, (8, count), 0)
    for d in range(rows):
        match = jnp.where(low_order[:, d : d + 1] - first == tokens, 1.0, 0.0).astype(LOW)
        pair = jnp.where(pick == 0, rank[d : d + 1] * owned[d : d + 1], owned[d : d + 1])
        found = jnp.dot(pair.astype(LOW), match, preferred_element_type=F32)
        sent = sent + found[:1] + found[1:2] * (d * capacity)
    send_row[...] = sent.astype(jnp.int32)
    send_col[...] = jnp.broadcast_to(sent, (LANES, count)).T[:, :1].astype(jnp.int32)
    blocks = lax.broadcasted_iota(jnp.int32, (rows, count), 0)
    mine = jnp.sum(jnp.where(blocks == row, order[...], 0), axis=0, keepdims=True)
    source = mine // count
    came = jnp.where(source == lax.broadcasted_iota(jnp.int32, (LANES, count), 0), 1.0, 0.0)
    place = jnp.sum(first_of(count, came) * came, axis=0, keepdims=True)
    place = place + source.astype(F32) * capacity
    recv_row[...] = place.astype(jnp.int32)
    recv_col[...] = jnp.broadcast_to(place, (LANES, count)).T[:, :1].astype(jnp.int32)


def sequence_ids(lengths, count, axis):
    places = lax.broadcasted_iota(jnp.int32, (1, count) if axis else (count, 1), axis)
    end = jnp.zeros((1, 1), jnp.int32)
    ids = jnp.zeros(places.shape, jnp.int32)
    for j in range(lengths.shape[1]):
        end = end + lengths[:, j : j + 1]
        ids = ids + jnp.where(places >= end, 1, 0)
    return ids


def front_kernel(
    rows,
    cols,
    halves,
    need,
    flush,
    order,
    picks,
    lengths,
    tokens_ref,
    cot,
    w_qkv,
    w_attn,
    w_query,
    w_gate,
    w_mem,
    sub_keys,
    norm_one,
    norm_two,
    send_row,
    send_col,
    recv_row,
    recv_col,
    hidden_one,
    dealt,
    factor_one,
    weights_one,
    qkv,
    mixed,
    hidden_two,
    resid,
    factor_two,
    full_cot,
    weights_two,
    keys,
    queries,
    gate,
    grad_mixed,
    grad_memory,
    index,
    low_picks,
    weights,
    scores_of,
    full,
    gains,
    packed,
    got,
    packed_cot,
    got_cot,
    outgoing,
    incoming,
    mine,
    theirs,
    turned,
    sends,
    recvs,
):
    net = Net(rows, cols, sends, recvs)
    greeted = net.greet(range(1, rows), range(1, cols))
    count, width = tokens_ref.shape
    capacity = packed.shape[0] // rows
    depth = halves * QD
    need(w_qkv, w_attn)
    place_one = rows_of(weights_one, w_qkv.shape[0])
    place_one(net.row)[:, : 3 * width] = w_qkv[...].astype(LOW)
    place_one(net.row)[:, 3 * width :] = w_attn[...].T.astype(LOW)
    net.meet(greeted)
    gather_one = net.gather_start(place_one(net.row), place_one)
    need(order, tokens_ref)
    find_places(rows, net.row, order, send_row, send_col, recv_row, recv_col)
    pack_for_rows(net, packed, tokens_ref[...], send_row[...])
    copies = exchange_start(net, packed, got, capacity)
    need(norm_one, norm_two, cot, w_query, w_gate, w_mem, sub_keys, picks, lengths)
    own_gain = columns_of(gains, width)
    own_gain(net.col)[...] = jnp.broadcast_to(
        norm_one[...].astype(LOW).astype(F32), (8, width)
    )
    gain_spread = net.columns_start(own_gain)
    pack_for_rows(net, packed_cot, cot[...], send_row[...])
    cot_copies = exchange_start(net, packed_cot, got_cot, capacity)
    place_two = rows_of(weights_two, w_query.shape[0])
    place_two(net.row)[:, :depth] = w_query[...].astype(LOW)
    place_two(net.row)[:, depth : depth + width] = w_gate[...].astype(LOW)
    place_two(net.row)[:, depth + width :] = w_mem[...].T.astype(LOW)
    span = sub_keys.shape[1]
    place_keys = lambda at: keys.at[:, pl.ds(pl.multiple_of(at * span, span), span), :]
    place_keys(net.row)[...] = sub_keys[...].astype(LOW)
    wait_all(copies)
    own = columns_of(full, width)
    values = unpack(got, recv_col[...])
    own(net.col)[...] = values.astype(LOW)
    spread = net.columns_start(own)
    dealt[...] = values
    left_one = net.gather_pass(place_one, gather_one, False)
    gather_two = net.gather_start(place_two(net.row), place_two)
    gather_keys = net.gather_start(place_keys(net.row), place_keys)
    low_picks[...] = (picks[...] - 32768).astype(jnp.int16)
    head = net.col * halves // 2
    head_rows = pl.ds(pl.multiple_of(head * PICKS, PICKS), PICKS)
    halves_of = []
    for h in range(halves):
        even = (net.col * halves + h) % 2 == 0
        halves_of.append(jnp.where(even, picks[...] // NK, picks[...] % NK))
        turned[...] = halves_of[h].astype(F32).T
        index[h * PICKS : (h + 1) * PICKS] = turned[head_rows, :].astype(jnp.int32)
    ids_col = sequence_ids(lengths[...], count, 0)
    ids_row = sequence_ids(lengths[...], count, 1)
    wait_all(spread)
    wait_all(gain_spread)
    values = full[...].astype(F32)
    scale = lax.rsqrt(jnp.mean(values * values, axis=1, keepdims=True) + EPS)
    hidden_one[...] = (values * scale * gains[:1]).astype(LOW)
    factor_one[...] = jnp.broadcast_to(scale, (count, LANES))
    flush(hidden_one, factor_one, dealt, index, low_picks, send_row, send_col, recv_row, recv_col)
    wait_all(left_one + net.gather_pass(place_one, gather_one, True))
    flush(weights_one)
    qkv[...] = jnp.dot(
        hidden_one[...], weights_one[:, : 3 * width], preferred_element_type=F32
    ).astype(LOW)
    for h in range(width // HD):
        (_, _, value), probs = attention_scores(qkv, h, ids_col, ids_row)
        mixed[:, h * HD : (h + 1) * HD] = jnp.dot(
            probs.astype(LOW), value, preferred_element_type=F32
        ).astype(LOW)
    flush(qkv, mixed)
    own_part, reduce = project_start(
        net, mixed[...], weights_one.at[:, 3 * width :], outgoing, incoming
    )
    values = dealt[...] + project_end(own_part, incoming, reduce)
    resid[...] = values
    left = net.gather_pass(place_two, gather_two, False)
    left += net.gather_pass(place_keys, gather_keys, False)
    square = share_sums(net, jnp.sum(values * values, axis=1, keepdims=True), mine, theirs)
    scale = lax.rsqrt(square / D + EPS)
    factor_two[...] = scale
    flush(resid, factor_two)
    own = columns_of(hidden_two, width)
    gain_two = norm_two[...].astype(LOW).astype(F32)
    own(net.col)[...] = (resid[...] * widen(scale, width) * gain_two).astype(LOW)
    spread = net.columns_start(own)
    wait_all(cot_copies)
    own_cot = columns_of(full_cot, width)
    own_cot(net.col)[...] = unpack(got_cot, recv_col[...]).astype(LOW)
    cot_spread = net.columns_start(own_cot)
    left += net.gather_pass(place_two, gather_two, True)
    left += net.gather_pass(place_keys, gather_keys, True)
    wait_all(spread)
    wait_all(left)
    flush(hidden_two, weights_two, keys)
    for h in range(halves):
        columns = slice(h * QD, (h + 1) * QD)
        queries[:, columns] = jnp.dot(
            hidden_two[...], weights_two[:, columns], preferred_element_type=F32
        ).astype(LOW)
        scores = lax.dot_general(
            queries[:, columns], keys[h], NT_DIMS, preferred_element_type=F32
        )
        low_index = halves_of[h] % LANES
        first = jnp.take_along_axis(scores[:, :LANES], low_index, axis=1)
        second = jnp.take_along_axis(scores[:, LANES:], low_index, axis=1)
        turned[...] = jnp.where(halves_of[h] >= LANES, second, first).T
        first_row = (net.col * halves + h) * PICKS
        scores_of[pl.ds(pl.multiple_of(first_row, PICKS), PICKS), :] = turned[head_rows, :]
    own_scores = rows_of(scores_of, halves * PICKS)
    score_spread = net.columns_start(own_scores)
    open_gate = jnp.dot(
        hidden_two[...], weights_two[:, depth : depth + width], preferred_element_type=F32
    )
    gate[...] = open_gate
    wait_all(cot_spread)
    flush(full_cot, queries, gate)
    back = jnp.dot(full_cot[...], weights_two[:, depth + width :], preferred_element_type=F32)
    grad_mixed[...] = back
    grad_memory[...] = (back * (open_gate * jax.nn.sigmoid(open_gate))).astype(LOW)
    wait_all(score_spread)
    for m in range(MH):
        score = (
            scores_of[2 * m * PICKS : (2 * m + 1) * PICKS]
            + scores_of[(2 * m + 1) * PICKS : (2 * m + 2) * PICKS]
        )
        shifted = jnp.exp(score - jnp.max(score, axis=0, keepdims=True))
        weights[m * PICKS : (m + 1) * PICKS] = shifted / jnp.sum(shifted, axis=0, keepdims=True)
    net.drain()


def norm_grad(net, grad_hidden, values, scale, gain, mine, theirs):
    width = values.shape[1]
    scaled = grad_hidden * gain
    inner = share_sums(net, jnp.sum(scaled * values, axis=1, keepdims=True), mine, theirs)
    wide = widen(scale, width)
    grads = wide * scaled - values * (wide * wide * wide) * widen(inner, width) / D
    grad_gain = jnp.sum(grad_hidden * values * wide, axis=0, keepdims=True)
    return grads, grad_gain


def project_start(net, left, weights, outgoing, incoming):
    width = outgoing.shape[2]

    def block(col):
        rows = rows_of(weights, width)(col)[...]
        return lax.dot_general(left, rows, NT_DIMS, preferred_element_type=F32)

    copies = []
    for k in range(1, net.cols):
        outgoing[k - 1] = block(flip(net.col, k)).astype(LOW)
        copies.append(net.send(outgoing.at[k - 1], incoming.at[k - 1], col_k=k))
    return block(net.col), copies


def project_end(total, incoming, copies):
    for k, copy in enumerate(copies):
        copy.wait_recv()
        total = total + incoming[k].astype(F32)
    return total


def attention_scores(qkv, head, ids_col, ids_row):
    parts = [qkv[:, (3 * head + j) * HD : (3 * head + j + 1) * HD] for j in range(3)]
    scores = lax.dot_general(parts[0], parts[1], NT_DIMS, preferred_element_type=F32) * HD ** (
        -0.5
    )
    asks = lax.broadcasted_iota(jnp.int32, scores.shape, 0)
    offers = lax.broadcasted_iota(jnp.int32, scores.shape, 1)
    allowed = (ids_col == ids_row) & (asks >= offers)
    scores = jnp.where(allowed, scores, MASKED)
    shifted = jnp.exp(scores - jnp.max(scores, axis=1, keepdims=True))
    return parts, shifted / jnp.sum(shifted, axis=1, keepdims=True)


def spread_picks(halves, weights, dw, index, out):
    tokens = weights.shape[1]
    grad = weights * (dw - jnp.sum(weights * dw, axis=0, keepdims=True))
    block = 128
    places = lax.broadcasted_iota(jnp.int32, (NK, block), 0)
    for h in range(halves):
        for b in range(tokens // block):
            columns = slice(b * block, (b + 1) * block)
            total = jnp.zeros((NK, block), F32)
            for k in range(PICKS):
                row = index[h * PICKS + k : h * PICKS + k + 1, columns]
                total = total + jnp.where(places == row, grad[k : k + 1, columns], 0.0)
            out[columns, h * NK : (h + 1) * NK] = total.T.astype(LOW)


def back_kernel(
    rows,
    cols,
    halves,
    need,
    flush,
    share,
    dw,
    index,
    memory,
    gate,
    grad_mixed,
    queries,
    hidden_two,
    cot,
    weights_two,
    keys,
    resid,
    factor_two,
    gain_two,
    recv_row,
    send_col,
    qkv,
    mixed,
    lengths,
    hidden_one,
    weights_one,
    dealt,
    factor_one,
    gain_one,
    output,
    grad_tokens,
    own_qkv,
    own_attn,
    own_query,
    own_gate,
    own_mem,
    own_keys,
    gains,
    grad_sub,
    both,
    mixed_two,
    grad_mem,
    grad_two,
    grad_keys,
    grad_low,
    grad_resid,
    grad_qkv,
    grad_one,
    one_outgoing,
    one_incoming,
    res_outgoing,
    res_incoming,
    two_outgoing,
    two_incoming,
    mine,
    theirs,
    mine_one,
    theirs_one,
    packed,
    got,
    packed_one,
    got_one,
    across_two,
    two_out,
    two_in,
    across_keys,
    keys_out,
    keys_in,
    across_one,
    one_out,
    one_in,
    across_mem,
    mem_out,
    mem_in,
    my_gains,
    their_gains,
    sends,
    recvs,
):
    net = Net(rows, cols, sends, recvs)
    capacity = packed.shape[0] // rows
    width = resid.shape[1]
    depth = halves * QD
    greeted = net.greet(range(1, rows), range(1, cols))
    need(gate, grad_mixed, memory)
    open_gate, back, read = gate[...], grad_mixed[...], memory[...]
    sigmoid = jax.nn.sigmoid(open_gate)
    both[:, depth:] = (back * read * sigmoid * (1.0 + open_gate * (1.0 - sigmoid))).astype(LOW)
    mixed_two[...] = (read * open_gate * sigmoid).astype(LOW)
    need(weights_two)
    net.meet(greeted)
    own_res, reduce_res = project_start(
        net, mixed_two[...], weights_two.at[:, depth + width :], res_outgoing, res_incoming
    )
    need(cot)
    grad_mem[...] = jnp.dot(cot[...].T, mixed_two[...], preferred_element_type=F32)
    moved_mem, moved_two, moved_keys, moved_one = {}, {}, {}, {}
    view_mem = rows_of(grad_mem, own_query.shape[0])
    started_mem = net.scatter_start(view_mem, across_mem)
    pass_mem = (view_mem, across_mem, started_mem, mem_out, mem_in, moved_mem)
    need(share, dw, index, keys)
    head = net.col * halves // 2
    own_share = share[pl.ds(pl.multiple_of(head * PICKS, PICKS), PICKS), :]
    spread_picks(halves, own_share, dw[...], index, grad_sub)
    net.scatter_pass(*pass_mem, True)
    for h in range(halves):
        both[:, h * QD : (h + 1) * QD] = jnp.dot(
            grad_sub[:, h * NK : (h + 1) * NK], keys[h], preferred_element_type=F32
        ).astype(LOW)
    own_part, reduce_two = project_start(
        net, both[...], weights_two.at[:, : depth + width], two_outgoing, two_incoming
    )
    need(resid, recv_row)
    block = resid[...] + project_end(own_res, res_incoming, reduce_res)
    pack_for_rows(net, packed, block.astype(LOW), recv_row[...])
    copies = exchange_start(net, packed, got, capacity)
    need(hidden_two, queries)
    grad_two[...] = jnp.dot(hidden_two[...].T, both[...], preferred_element_type=F32)
    for h in range(halves):
        grad_keys[h] = jnp.dot(
            grad_sub[:, h * NK : (h + 1) * NK].T,
            queries[:, h * QD : (h + 1) * QD],
            preferred_element_type=F32,
        )
    view_two = rows_of(grad_two, own_query.shape[0])
    span = own_keys.shape[1]
    view_keys = lambda at: grad_keys.at[:, pl.ds(pl.multiple_of(at * span, span), span), :]
    started_two = net.scatter_start(view_two, across_two)
    started_keys = net.scatter_start(view_keys, across_keys)
    pass_two = (view_two, across_two, started_two, two_out, two_in, moved_two)
    pass_keys = (view_keys, across_keys, started_keys, keys_out, keys_in, moved_keys)
    net.scatter_pass(*pass_two, True)
    net.scatter_pass(*pass_keys, True)
    net.scatter_pass(*pass_mem, False)
    need(lengths)
    ids_col = sequence_ids(lengths[...], memory.shape[0], 0)
    ids_row = sequence_ids(lengths[...], memory.shape[0], 1)
    need(factor_two, gain_two)
    grad_hidden = project_end(own_part, two_incoming, reduce_two)
    grads, gain_two_sum = norm_grad(
        net, grad_hidden, resid[...], factor_two[...], gain_two[...].astype(LOW).astype(F32), mine, theirs
    )
    own_cot = columns_of(cot, width)(net.col)[...]
    grads = grads + own_cot.astype(F32)
    grad_resid[...] = grads
    own = columns_of(grad_low, width)
    own(net.col)[...] = grads.astype(LOW)
    spread = net.columns_start(own)
    wait_all(spread)
    net.scatter_pass(*pass_two, False)
    net.scatter_pass(*pass_keys, False)
    need(weights_one, qkv, hidden_one, mixed, send_col, dealt, factor_one, gain_one)
    grad_heads = jnp.dot(
        grad_low[...], weights_one[:, 3 * width :], preferred_element_type=F32
    ).astype(LOW)
    for head in range(width // HD):
        (query, key, value), probs = attention_scores(qkv, head, ids_col, ids_row)
        grad_out = grad_heads[:, head * HD : (head + 1) * HD]
        grad_prob = lax.dot_general(grad_out, value, NT_DIMS, preferred_element_type=F32)
        inner = jnp.sum(probs * grad_prob, axis=1, keepdims=True)
        grad_score = (probs * (grad_prob - inner)).astype(LOW)
        pieces = (
            jnp.dot(grad_score, key, preferred_element_type=F32) * HD ** (-0.5),
            jnp.dot(grad_score.T, query, preferred_element_type=F32) * HD ** (-0.5),
            jnp.dot(probs.astype(LOW).T, grad_out, preferred_element_type=F32),
        )
        for j in range(3):
            grad_qkv[:, (3 * head + j) * HD : (3 * head + j + 1) * HD] = pieces[j].astype(LOW)
    own_part, reduce_one = project_start(
        net, grad_qkv[...], weights_one.at[:, : 3 * width], one_outgoing, one_incoming
    )
    grad_one[:, : 3 * width] = jnp.dot(
        hidden_one[...].T, grad_qkv[...], preferred_element_type=F32
    )
    grad_one[:, 3 * width :] = jnp.dot(grad_low[...].T, mixed[...], preferred_element_type=F32)
    view_one = rows_of(grad_one, own_qkv.shape[0])
    started_one = net.scatter_start(view_one, across_one)
    pass_one = (view_one, across_one, started_one, one_out, one_in, moved_one)
    net.scatter_pass(*pass_one, True)
    grad_hidden = project_end(own_part, one_incoming, reduce_one)
    grads, gain_one_sum = norm_grad(
        net,
        grad_hidden,
        dealt[...],
        factor_one[...],
        gain_one[...].astype(LOW).astype(F32),
        mine_one,
        theirs_one,
    )
    grads = grads + grad_resid[...]
    pack_for_rows(net, packed_one, grads.astype(LOW), recv_row[...])
    last = exchange_start(net, packed_one, got_one, capacity)
    net.scatter_pass(*pass_one, False)
    places = lax.broadcasted_iota(jnp.int32, my_gains.shape, 0)
    my_gains[...] = jnp.where(places == 0, gain_one_sum, gain_two_sum)
    gain_copies = [net.send(my_gains, their_gains.at[k], row_k=k) for k in range(1, rows)]
    total = net.scatter_end(view_two, across_two, started_two, two_in, moved_two)
    own_query[...] = total[:, :depth]
    own_gate[...] = total[:, depth:]
    own_mem[...] = net.scatter_end(view_mem, across_mem, started_mem, mem_in, moved_mem).T
    own_keys[...] = net.scatter_end(view_keys, across_keys, started_keys, keys_in, moved_keys)
    wait_all(copies)
    output[...] = unpack(got, send_col[...])
    flush(output)
    total = net.scatter_end(view_one, across_one, started_one, one_in, moved_one)
    own_qkv[...] = total[:, : 3 * width]
    own_attn[...] = total[:, 3 * width :].T
    total = my_gains[...]
    for k, copy in enumerate(gain_copies):
        copy.wait_recv()
        total = total + their_gains[k + 1]
    gains[...] = total
    wait_all(last)
    grad_tokens[...] = unpack(got_one, send_col[...])
    net.drain()


def staged(kernel, rows, cols, sizes, ins, outs, *refs):
    given, results = refs[:ins], refs[ins : ins + outs]
    rest = refs[ins + outs :]
    twins, rest = rest[: ins + outs], rest[ins + outs :]
    sems, rest = rest[0], rest[1:]
    sources, targets = twins[:ins], twins[ins:]
    waited, left = set(), []

    def moving(i):
        return pltpu.make_async_copy(given[i], sources[i], sems.at[i])

    def need(*wanted):
        for ref in wanted:
            i = [j for j in range(ins) if sources[j] is ref][0]
            if i not in waited:
                moving(i).wait()
                waited.add(i)

    def flush(*done):
        for ref in done:
            i = [j for j in range(outs) if targets[j] is ref][0]
            copy = pltpu.make_async_copy(targets[i], results[i], sems.at[ins + i])
            copy.start()
            left.append((i, copy))

    for i in range(ins):
        moving(i).start()
    kernel(rows, cols, *sizes, need, flush, *sources, *targets, *rest)
    assert len(waited) == ins
    flush(*[targets[i] for i in range(outs) if i not in [j for j, _ in left]])
    for _, copy in left:
        copy.wait()


def remote_call(kernel, rows, cols, number, copies, ins, outs, scratch, *sizes):
    twins = [(x.shape, x.dtype) for x in ins] + outs
    anywhere = pl.BlockSpec(memory_space=pl.ANY)
    return pl.pallas_call(
        functools.partial(staged, kernel, rows, cols, sizes, len(ins), len(outs)),
        out_shape=[jax.ShapeDtypeStruct(shape, dtype) for shape, dtype in outs],
        in_specs=[anywhere] * len(ins),
        out_specs=[anywhere] * len(outs),
        scratch_shapes=[pltpu.VMEM(shape, dtype) for shape, dtype in twins]
        + [pltpu.SemaphoreType.DMA((len(twins),))]
        + [pltpu.VMEM(shape, dtype) for shape, dtype in scratch]
        + [pltpu.SemaphoreType.DMA((copies,)), pltpu.SemaphoreType.DMA((copies,))],
        compiler_params=pltpu.CompilerParams(
            collective_id=number, has_side_effects=True, vmem_limit_bytes=VMEM_BYTES
        ),
    )(*ins)


def memory_kernel(
    rows,
    cols,
    own_weights,
    own_picks,
    own_grads,
    table_f32,
    memory,
    dw,
    gacc_out,
    gacc,
    table,
    stage,
    picks_of,
    grads_of,
    low_of,
    dense,
    hi_ref,
    lo_ref,
    wide_ref,
    found_ref,
    mem_all,
    mem_twin,
    mem_out,
    mem_in,
    dw_all,
    dw_twin,
    dw_out,
    dw_in,
    dw_cols,
    stage_sems,
    sends,
    recvs,
):
    net = Net(rows, cols, sends, recvs)
    half = rows // 2
    tok_block = own_picks.shape[0]
    span_rows, width = table.shape
    spans = span_rows // LANES
    pitch = spans + 8
    iters = 4
    per_tok = tok_block // iters
    per_span = spans // iters

    grads_at = rows_of(grads_of, tok_block)
    picks_at = rows_of(picks_of, tok_block)
    low_at = lambda index: low_of.at[index]
    views = (grads_at, picks_at, low_at)
    first_pass = 3 * half
    first_twin = first_pass + 3 * half
    first_out = first_twin + 2 * half
    first_col = first_out + 2 * half

    def gather(a, j):
        mine = views[a](net.row)
        return net.copy(mine, mine, 3 * j + a, row_k=2 * j if j else 1)

    def passing(a, j):
        there = views[a](flip(net.row, 2 * j))
        return net.copy(there, there, first_pass + 3 * j + a, row_k=1)

    def twin(a, j):
        src, dst = ((mem_all, mem_twin), (dw_all, dw_twin))[a]
        return net.copy(src.at[2 * j + 1], dst.at[j], first_twin + 2 * j + a, row_k=1)

    def outward(a, j):
        src, dst = ((mem_out, mem_in), (dw_out, dw_in))[a]
        return net.copy(src.at[j - 1], dst.at[j - 1], first_out + 2 * j + a, row_k=2 * j)

    head = lambda col: pl.ds(pl.multiple_of(col * MH // cols * PICKS, PICKS), PICKS)

    def dw_copy(k):
        return net.copy(
            dw_all.at[0, head(flip(net.col, k)), :],
            dw_cols.at[k - 1],
            first_col + k,
            col_k=k,
        )

    stage_rows = stage.shape[1]

    def stage_copy(i):
        source = table_f32.at[pl.ds(i * stage_rows, stage_rows), :]
        return pltpu.make_async_copy(source, stage.at[i % 2], stage_sems.at[i % 2])

    stage_copy(0).start()
    greeted = net.greet([1] + [2 * j for j in range(1, half)], range(1, cols))
    for i in range(span_rows // stage_rows):
        if (i + 1) * stage_rows < span_rows:
            stage_copy(i + 1).start()
        stage_copy(i).wait()
        table[i * stage_rows : (i + 1) * stage_rows, :] = stage[i % 2].astype(LOW)
    net.meet(greeted)
    grads_at(net.row)[...] = own_grads[...]
    picks_at(net.row)[...] = own_picks[...]
    low_at(net.row)[...] = own_weights[...].astype(LOW)
    for j in range(half):
        for a in range(3):
            gather(a, j).start()
    gacc[...] = jnp.zeros_like(gacc)
    mem_all[...] = jnp.zeros_like(mem_all)

    def one_block(step, _):
        k = jnp.where(step == 0, 0, jnp.where(step == rows - 1, 1, step + 1))
        there = cross(net.row, k, rows)
        for j in range(1, half):

            @pl.when(step == 2 * j - 1)
            def _():
                for a in range(3):
                    gather(a, j).wait_recv()
                    passing(a, j).start()

            @pl.when(step == 2 * j)
            def _():
                for a in range(3):
                    passing(a, j).wait_recv()

        @pl.when(step == rows - 1)
        def _():
            for a in range(3):
                gather(a, 0).wait_recv()

        picks = picks_at(there)[...].astype(jnp.int32) + 32768
        hi_ref[...] = (picks // LANES - net.row * spans).astype(F32)
        lo_ref[...] = (picks % LANES).astype(F32)
        wide_ref[...] = low_of[there].astype(F32).T
        places_lo = lax.broadcasted_iota(jnp.int32, (LANES, LANES), 0).astype(F32).astype(LOW)
        places_hi = lax.broadcasted_iota(jnp.int32, (spans, LANES), 0).astype(F32).astype(LOW)
        ones = jnp.ones((LANES, LANES), LOW)
        zeros = jnp.zeros((LANES, LANES), LOW)
        blank = jnp.zeros((spans, LANES), LOW)
        grads = grads_at(there)[...]
        grads_t = grads.T
        found_ref[...] = jnp.zeros_like(found_ref)
        lo_int = picks % LANES
        hi_all = hi_ref[...]

        def token_pair(first):
            rights, lefts = [], []
            for token in (first, first + 1):
                lo_row = jnp.broadcast_to(lo_ref[pl.ds(token, 1), :], (LANES, LANES)).astype(LOW)
                hi_row = jnp.broadcast_to(hi_ref[pl.ds(token, 1), :], (spans, LANES)).astype(LOW)
                w_row = jnp.broadcast_to(wide_ref[pl.ds(token, 1), :], (spans, LANES)).astype(LOW)
                rights.append(jnp.where(lo_row == places_lo, ones, zeros))
                lefts.append(jnp.where(hi_row == places_hi, w_row, blank))
            right = jnp.concatenate(rights, axis=1)
            left = jnp.concatenate(
                [
                    jnp.concatenate([lefts[0], blank], axis=1),
                    jnp.concatenate([blank, lefts[1]], axis=1),
                ],
                axis=0,
            )
            both = lax.dot_general(left, right, NT_DIMS, preferred_element_type=F32)
            for j in range(2):
                dense[pl.ds(pl.multiple_of((first + j) * pitch, 8), spans), :] = both[
                    j * spans : (j + 1) * spans
                ]

        def look(found, first, number, between=None):
            span = pl.ds(pl.multiple_of(first * LANES, LANES), number * LANES)
            products = lax.dot_general(
                grads, table[span, :], NT_DIMS, preferred_element_type=F32
            )
            for j in range(number):
                picked = jnp.take_along_axis(
                    products[:, LANES * j : LANES * (j + 1)], lo_int, axis=1
                )
                found = jnp.where(hi_all == (first + j).astype(F32), picked, found)
                if between:
                    between(j)
            return found

        early = per_span // 2
        late = per_span - early

        def build(it, _):
            for j in range(1, half):

                @pl.when((it == 1) & (step == 2 * j + 1))
                def _():
                    twin(0, j).wait_recv()
                    twin(1, j).wait_recv()
                    mem_out[j - 1] = (mem_all[2 * j] + mem_twin[j]).astype(LOW)
                    outward(0, j).start()
                    dw_out[j - 1] = dw_all[2 * j] + dw_twin[j]
                    outward(1, j).start()

            pairs = per_tok // 2 // early

            def some_pairs(j):
                for u in range(pairs):
                    token_pair(it * per_tok + (j * pairs + u) * 2)

            found_ref[...] = look(found_ref[...], it * early, early, some_pairs)
            return 0

        lax.fori_loop(0, iters, build, 0)
        parts = min(4, late)

        def multiply(it, _):
            found, total = found_ref[...], None
            for c in range(parts):
                low, high = c * late // parts, (c + 1) * late // parts
                found = look(found, early * iters + it * late + low, high - low)
                low, high = c * per_span // parts, (c + 1) * per_span // parts
                first = it * per_span + low
                chosen = jnp.concatenate(
                    [
                        dense[pl.ds(first + j, tok_block, stride=pitch), :].astype(LOW)
                        for j in range(high - low)
                    ],
                    axis=1,
                )
                span = pl.ds(pl.multiple_of(first * LANES, LANES), (high - low) * LANES)
                gacc[:, span] += jnp.dot(grads_t, chosen, preferred_element_type=F32)
                read = jnp.dot(chosen, table[span, :], preferred_element_type=F32)
                total = read if total is None else total + read
            mem_all[k] += total
            found_ref[...] = found
            return 0

        lax.fori_loop(0, iters, multiply, 0)
        dw_all[k] = found_ref[...].T
        for j in range(half):

            @pl.when(step == (2 * j if j else rows - 1))
            def _():
                twin(0, j).start()
                twin(1, j).start()

        return 0

    lax.fori_loop(0, rows, one_block, 0)
    leaving = pltpu.make_async_copy(gacc, gacc_out, stage_sems.at[2])
    leaving.start()
    twin(1, 0).wait_recv()
    total = dw_all[0] + dw_twin[0]
    for j in range(1, half):
        outward(1, j).wait_recv()
        total = total + dw_in[j - 1]
    dw_all[0] = total
    for k in range(1, cols):
        dw_copy(k).start()
    twin(0, 0).wait_recv()
    total = mem_all[0] + mem_twin[0]
    for j in range(1, half):
        outward(0, j).wait_recv()
        total = total + mem_in[j - 1].astype(F32)
    memory[...] = total
    total = dw_all[0, head(net.col), :]
    for k in range(1, cols):
        dw_copy(k).wait_recv()
        total = total + dw_cols[k - 1]
    dw[...] = total
    for k in range(1, cols):
        dw_copy(k).wait_send()
    for j in range(half):
        for a in range(3):
            gather(a, j).wait_send()
            if j:
                passing(a, j).wait_send()
        for a in range(2):
            twin(a, j).wait_send()
            if j:
                outward(a, j).wait_send()
    leaving.wait()


def turn_kernel(source, out):
    out[...] = source[...].T


def turn_call(table):
    width, span_rows = table.shape
    block = 1024
    return pl.pallas_call(
        turn_kernel,
        grid=(span_rows // block,),
        in_specs=[pl.BlockSpec((width, block), lambda i: (0, i))],
        out_specs=pl.BlockSpec((block, width), lambda i: (i, 0)),
        out_shape=jax.ShapeDtypeStruct((span_rows, width), F32),
    )(table)


def memory_call(rows, cols, number, weights, picks, grads, table):
    tokens, count = picks.shape
    span_rows, width = table.shape
    half = rows // 2
    copies = 10 * half + cols
    vmem = pltpu.VMEM
    return pl.pallas_call(
        functools.partial(memory_kernel, rows, cols),
        in_specs=[VMEM_SPEC, VMEM_SPEC, VMEM_SPEC, pl.BlockSpec(memory_space=pl.ANY)],
        out_specs=[VMEM_SPEC, VMEM_SPEC, pl.BlockSpec(memory_space=pl.ANY)],
        out_shape=[
            jax.ShapeDtypeStruct((tokens, width), F32),
            jax.ShapeDtypeStruct((PICKS, tokens), F32),
            jax.ShapeDtypeStruct((width, span_rows), F32),
        ],
        scratch_shapes=[
            vmem((width, span_rows), F32),
            vmem((span_rows, width), LOW),
            vmem((2, 1024, width), F32),
            vmem((rows * tokens, count), jnp.int16),
            vmem((rows * tokens, width), LOW),
            vmem((rows, count, tokens), LOW),
            vmem((tokens * (span_rows // LANES + 8), LANES), F32),
            vmem((tokens, count), F32),
            vmem((tokens, count), F32),
            vmem((tokens, count), F32),
            vmem((tokens, count), F32),
            vmem((rows, tokens, width), F32),
            vmem((half, tokens, width), F32),
            vmem((half - 1, tokens, width), LOW),
            vmem((half - 1, tokens, width), LOW),
            vmem((rows, count, tokens), F32),
            vmem((half, count, tokens), F32),
            vmem((half - 1, count, tokens), F32),
            vmem((half - 1, count, tokens), F32),
            vmem((cols - 1, PICKS, tokens), F32),
            pltpu.SemaphoreType.DMA((3,)),
            pltpu.SemaphoreType.DMA((copies,)),
            pltpu.SemaphoreType.DMA((copies,)),
        ],
        compiler_params=pltpu.CompilerParams(
            collective_id=number, has_side_effects=True, vmem_limit_bytes=63 * 2**20
        ),
    )(weights, picks, grads, table)


def per_device(
    tokens,
    cotangent,
    deal_order,
    seq_lengths,
    value_picks,
    norm1_gain,
    w_qkv,
    w_attn_out,
    norm2_gain,
    w_query,
    sub_keys,
    value_table,
    w_gate,
    w_mem_out,
):
    rows, cols = lax.axis_size("row"), lax.axis_size("col")
    row_index = lax.axis_index("row")
    count, width = tokens.shape
    slots = 2 * count
    half = rows // 2
    halves = sub_keys.shape[0]
    depth = halves * QD
    span_one, span_two = 4 * width, depth + 2 * width
    shard_rows = w_qkv.shape[0]
    flat_picks = value_picks.reshape(count, MH * PICKS)
    gain_one, gain_two = norm1_gain[None, :], norm2_gain[None, :]
    swap = [((slots, width), LOW), ((slots, width), LOW)]
    sums = [((8, count), F32), ((cols, 8, count), F32)]
    moving = ((cols - 1, count, width), LOW)
    (
        send_row,
        send_col,
        recv_row,
        recv_col,
        hidden_one,
        dealt,
        factor_one,
        weights_one,
        qkv,
        mixed,
        hidden_two,
        resid,
        factor_two,
        full_cot,
        weights_two,
        keys,
        queries,
        gate,
        grad_mixed,
        grad_memory,
        index,
        low_picks,
        pick_weights,
    ) = remote_call(
        front_kernel,
        rows,
        cols,
        0,
        7 * (cols - 1) + 5 * (rows - 1),
        [
            deal_order.reshape(rows, count),
            flat_picks,
            seq_lengths,
            tokens,
            cotangent,
            w_qkv,
            w_attn_out,
            w_query,
            w_gate,
            w_mem_out,
            sub_keys,
            gain_one,
            gain_two,
        ],
        [
            ((1, count), jnp.int32),
            ((count, 1), jnp.int32),
            ((1, count), jnp.int32),
            ((count, 1), jnp.int32),
            ((count, D), LOW),
            ((count, width), F32),
            ((count, LANES), F32),
            ((D, span_one), LOW),
            ((count, 3 * width), LOW),
            ((count, width), LOW),
            ((count, D), LOW),
            ((count, width), F32),
            ((count, LANES), F32),
            ((count, D), LOW),
            ((D, span_two), LOW),
            ((halves, NK, QD), LOW),
            ((count, depth), LOW),
            ((count, width), F32),
            ((count, width), F32),
            ((count, width), LOW),
            ((halves * PICKS, count), jnp.int32),
            ((count, MH * PICKS), jnp.int16),
            ((MH * PICKS, count), F32),
        ],
        [((2 * MH * PICKS, count), F32), ((count, D), LOW), ((8, D), F32), *swap, *swap, moving, moving, *sums]
        + [((MH * PICKS, count), F32)],
        halves,
    )
    memory, grad_pick, grad_table = memory_call(
        rows, cols, 1, pick_weights, low_picks, grad_memory, value_table
    )
    block = ((count, width), F32)
    scattered = [
        [((half,) + shape, F32), ((half - 1,) + shape, LOW), ((half - 1,) + shape, LOW)]
        for shape in (
            (shard_rows, depth + width),
            sub_keys.shape,
            (shard_rows, span_one),
            (shard_rows, width),
        )
    ]
    output, grad_tokens, own_qkv, own_attn, own_query, own_gate, own_mem, own_keys, gains = remote_call(
        back_kernel,
        rows,
        cols,
        2,
        6 * (cols - 1) + 3 * (rows - 1) + 4 * (half + half - 1),
        [
            pick_weights,
            grad_pick,
            index,
            memory,
            gate,
            grad_mixed,
            queries,
            hidden_two,
            full_cot,
            weights_two,
            keys,
            resid,
            factor_two,
            gain_two,
            recv_row,
            send_col,
            qkv,
            mixed,
            seq_lengths,
            hidden_one,
            weights_one,
            dealt,
            factor_one,
            gain_one,
        ],
        [
            block,
            block,
            (w_qkv.shape, F32),
            (w_attn_out.shape, F32),
            (w_query.shape, F32),
            (w_gate.shape, F32),
            (w_mem_out.shape, F32),
            (sub_keys.shape, F32),
            ((8, width), F32),
        ],
        [
            ((count, halves * NK), LOW),
            ((count, depth + width), LOW),
            ((count, width), LOW),
            ((D, width), F32),
            ((D, depth + width), F32),
            ((halves, NK, QD), F32),
            ((count, D), LOW),
            block,
            ((count, 3 * width), LOW),
            ((D, span_one), F32),
            *[moving] * 6,
            *sums,
            *sums,
            *swap,
            *swap,
            *scattered[0],
            *scattered[1],
            *scattered[2],
            *scattered[3],
            ((8, width), F32),
            ((rows, 8, width), F32),
        ],
        halves,
    )
    gain_span = width // rows
    gain_one_grad = lax.dynamic_slice_in_dim(gains[0], row_index * gain_span, gain_span)
    gain_two_grad = lax.dynamic_slice_in_dim(gains[1], row_index * gain_span, gain_span)
    return (
        output,
        grad_tokens,
        gain_one_grad,
        own_qkv,
        own_attn,
        gain_two_grad,
        own_query,
        own_keys,
        turn_call(grad_table),
        own_gate,
        own_mem,
    )


def solution(mesh):
    return jax.shard_map(
        per_device,
        mesh=mesh,
        in_specs=(
            P("row", "col"),
            P("row", "col"),
            P(),
            P("row", None),
            P("row", None, None),
            P("col"),
            P("row", "col"),
            P("col", "row"),
            P("col"),
            P("row", "col"),
            P("col", "row", None),
            P("row", "col"),
            P("row", "col"),
            P("col", "row"),
        ),
        out_specs=(
            P("row", "col"),
            P("row", "col"),
            P(("col", "row")),
            P("row", "col"),
            P("col", "row"),
            P(("col", "row")),
            P("row", "col"),
            P("col", "row", None),
            P("row", "col"),
            P("row", "col"),
            P("col", "row"),
        ),
        check_vma=False,
    )
```

```python
import functools

import jax
import jax.numpy as jnp
from jax import lax
from jax.experimental import pallas as pl
from jax.experimental.pallas import tpu as pltpu
from jax.sharding import PartitionSpec as P

D = 1024
HD = 64
MH = 4
QD = 512
NK = 256
PICKS = 32
LANES = 128
EPS = 1e-05
MASKED = -1e30
F32 = jnp.float32
LOW = jnp.bfloat16
MESH = pl.DeviceIdType.MESH
NT_DIMS = (((1,), (1,)), ((), ()))
VMEM_SPEC = pl.BlockSpec(memory_space=pltpu.VMEM)
VMEM_BYTES = 60 * 2**20


def flip(index, mask):
    bit = 1
    while bit <= mask:
        if mask & bit:
            index = index + bit - 2 * bit * (index // bit % 2)
        bit *= 2
    return index


def cross(index, mask, size):
    total, bit = 0, 1
    while bit < size:
        a, b = index // bit % 2, mask // bit % 2
        total = total + bit * (a + b - 2 * a * b)
        bit *= 2
    return total


class Net:
    def __init__(self, rows, cols, sends, recvs):
        self.rows, self.cols = rows, cols
        self.row, self.col = lax.axis_index("row"), lax.axis_index("col")
        self.sends, self.recvs, self.used = sends, recvs, 0
        self.pending = []

    def place(self, row_k, col_k):
        return (flip(self.row, row_k), flip(self.col, col_k))

    def greet(self, row_ks, col_ks):
        barrier = pltpu.get_barrier_semaphore()
        places = [self.place(k, 0) for k in row_ks] + [self.place(0, k) for k in col_ks]
        for place in places:
            pl.semaphore_signal(barrier, inc=1, device_id=place, device_id_type=MESH)
        return len(places)

    def meet(self, greeted):
        pl.semaphore_wait(pltpu.get_barrier_semaphore(), greeted)

    def copy(self, src, dst, number, row_k=0, col_k=0):
        assert number < self.sends.shape[0]
        return pltpu.make_async_remote_copy(
            src_ref=src,
            dst_ref=dst,
            send_sem=self.sends.at[number],
            recv_sem=self.recvs.at[number],
            device_id=self.place(row_k, col_k),
            device_id_type=MESH,
        )

    def send(self, src, dst, row_k=0, col_k=0):
        copy = self.copy(src, dst, self.used, row_k, col_k)
        copy.start()
        self.used += 1
        self.pending.append(copy)
        return copy

    def drain(self):
        for copy in self.pending:
            copy.wait_send()

    def gather_start(self, src, view):
        sent = {b: self.send(src, view(self.row), row_k=2 * b) for b in reversed(self.bits())}
        return sent, self.send(src, view(self.row), row_k=1)

    def gather_pass(self, view, started, near):
        sent, sibling = started
        passed = [sibling] if near else []
        masks = [m for m in range(1, self.rows // 2) if (m % 2 == 1) == near]
        for m in sorted(masks, key=lambda m: (-(m & -m), m.bit_count())):
            sent[m].wait_recv()
            block = view(flip(self.row, 2 * m))
            for b in self.bits():
                if b < (m & -m):
                    sent[m ^ b] = self.send(block, block, row_k=2 * b)
            passed.append(self.send(block, block, row_k=1))
        return passed

    def bits(self):
        return [1 << i for i in range((self.rows // 2 - 1).bit_length())]

    def scatter_start(self, view, across):
        twin = flip(self.row, 1)
        return [
            self.send(view(flip(twin, 2 * j)), across.at[j], row_k=1)
            for j in range(self.rows // 2)
        ]

    def scatter_pass(self, view, across, started, outgoing, incoming, moved, near):
        masks = [m for m in range(1, self.rows // 2) if (m % 2 == 1) == near]
        for m in sorted(masks, key=lambda m: ((m & -m), -m.bit_count())):
            started[m].wait_recv()
            block = view(flip(self.row, 2 * m))[...] + across[m]
            for b in self.bits():
                if b < (m & -m):
                    moved[m ^ b].wait_recv()
                    block = block + incoming[(m ^ b) - 1].astype(F32)
            outgoing[m - 1] = block.astype(outgoing.dtype)
            moved[m] = self.send(outgoing.at[m - 1], incoming.at[m - 1], row_k=2 * (m & -m))
        return moved

    def scatter_end(self, view, across, started, incoming, moved):
        started[0].wait_recv()
        total = view(self.row)[...] + across[0]
        for b in self.bits():
            moved[b].wait_recv()
            total = total + incoming[b - 1].astype(F32)
        return total

    def columns_start(self, view):
        return [self.send(view(self.col), view(self.col), col_k=k) for k in range(1, self.cols)]


def wait_all(copies):
    for copy in copies:
        copy.wait_recv()


def rows_of(ref, count):
    return lambda index: ref.at[pl.ds(pl.multiple_of(index * count, count), count), :]


def columns_of(ref, count):
    return lambda index: ref.at[:, pl.ds(pl.multiple_of(index * count, count), count)]


def one_hot_rows(positions, slots):
    places = lax.broadcasted_iota(jnp.int32, (positions.shape[0], slots), 1)
    return jnp.where(positions == places, 1.0, 0.0).astype(LOW)


def one_hot_columns(positions, slots):
    places = lax.broadcasted_iota(jnp.int32, (slots, positions.shape[1]), 0)
    return jnp.where(positions == places, 1.0, 0.0).astype(LOW)


def pack_for_rows(net, packed, values, positions):
    slots = packed.shape[0]
    packed[...] = jnp.dot(
        one_hot_columns(positions, slots), values, preferred_element_type=F32
    ).astype(LOW)


def exchange_start(net, packed, got, capacity):
    mine = rows_of(got, capacity)
    theirs = rows_of(packed, capacity)
    copies = [
        net.send(theirs(flip(net.row, k)), mine(net.row), row_k=k) for k in range(1, net.rows)
    ]
    mine(net.row)[...] = theirs(net.row)[...]
    return copies


def unpack(got, positions):
    return jnp.dot(
        one_hot_rows(positions, got.shape[0]), got[...], preferred_element_type=F32
    )


def share_sums(net, sums, mine, theirs):
    tokens = sums.shape[0]
    mine[...] = jnp.broadcast_to(sums, (tokens, LANES)).T[:8]
    copies = [net.send(mine, theirs.at[k], col_k=k) for k in range(1, net.cols)]
    wait_all(copies)
    total = mine[...]
    for k in range(1, net.cols):
        total = total + theirs[k]
    return jnp.broadcast_to(total[:1], (LANES, tokens)).T


def widen(lanes, width):
    return jnp.concatenate([lanes] * (width // LANES), axis=1)


def first_of(size, mask):
    earlier = lax.broadcasted_iota(jnp.int32, (size, size), 0)
    later = lax.broadcasted_iota(jnp.int32, (size, size), 1)
    triangle = jnp.where(earlier < later, 1.0, 0.0).astype(LOW)
    return jnp.dot(mask.astype(LOW), triangle, preferred_element_type=F32)


def find_places(rows, row, order, send_row, send_col, recv_row, recv_col):
    count = order.shape[1]
    capacity = 2 * count // rows
    owner = order[...] // count
    owned = jnp.where(owner == row, 1.0, 0.0)
    rank = first_of(count, owned)
    low_order = order[...].astype(F32).T
    tokens = lax.broadcasted_iota(jnp.int32, (count, count), 1).astype(F32)
    first = (row * count).astype(F32)
    sent = jnp.zeros((1, count), F32)
    pick = lax.broadcasted_iota(jnp.int32, (8, count), 0)
    for d in range(rows):
        match = jnp.where(low_order[:, d : d + 1] - first == tokens, 1.0, 0.0).astype(LOW)
        pair = jnp.where(pick == 0, rank[d : d + 1] * owned[d : d + 1], owned[d : d + 1])
        found = jnp.dot(pair.astype(LOW), match, preferred_element_type=F32)
        sent = sent + found[:1] + found[1:2] * (d * capacity)
    send_row[...] = sent.astype(jnp.int32)
    send_col[...] = jnp.broadcast_to(sent, (LANES, count)).T[:, :1].astype(jnp.int32)
    blocks = lax.broadcasted_iota(jnp.int32, (rows, count), 0)
    mine = jnp.sum(jnp.where(blocks == row, order[...], 0), axis=0, keepdims=True)
    source = mine // count
    came = jnp.where(source == lax.broadcasted_iota(jnp.int32, (LANES, count), 0), 1.0, 0.0)
    place = jnp.sum(first_of(count, came) * came, axis=0, keepdims=True)
    place = place + source.astype(F32) * capacity
    recv_row[...] = place.astype(jnp.int32)
    recv_col[...] = jnp.broadcast_to(place, (LANES, count)).T[:, :1].astype(jnp.int32)


def sequence_ids(lengths, count, axis):
    places = lax.broadcasted_iota(jnp.int32, (1, count) if axis else (count, 1), axis)
    end = jnp.zeros((1, 1), jnp.int32)
    ids = jnp.zeros(places.shape, jnp.int32)
    for j in range(lengths.shape[1]):
        end = end + lengths[:, j : j + 1]
        ids = ids + jnp.where(places >= end, 1, 0)
    return ids


def front_kernel(
    rows,
    cols,
    halves,
    need,
    flush,
    order,
    picks,
    lengths,
    tokens_ref,
    cot,
    w_qkv,
    w_attn,
    w_query,
    w_gate,
    w_mem,
    sub_keys,
    norm_one,
    norm_two,
    send_row,
    send_col,
    recv_row,
    recv_col,
    hidden_one,
    dealt,
    factor_one,
    weights_one,
    qkv,
    mixed,
    hidden_two,
    resid,
    factor_two,
    full_cot,
    weights_two,
    keys,
    queries,
    gate,
    grad_mixed,
    grad_memory,
    index,
    low_picks,
    weights,
    scores_of,
    full,
    gains,
    packed,
    got,
    packed_cot,
    got_cot,
    outgoing,
    incoming,
    mine,
    theirs,
    turned,
    sends,
    recvs,
):
    net = Net(rows, cols, sends, recvs)
    greeted = net.greet(range(1, rows), range(1, cols))
    count, width = tokens_ref.shape
    capacity = packed.shape[0] // rows
    depth = halves * QD
    need(w_qkv, w_attn)
    place_one = rows_of(weights_one, w_qkv.shape[0])
    place_one(net.row)[:, : 3 * width] = w_qkv[...].astype(LOW)
    place_one(net.row)[:, 3 * width :] = w_attn[...].T.astype(LOW)
    net.meet(greeted)
    gather_one = net.gather_start(place_one(net.row), place_one)
    need(order, tokens_ref)
    find_places(rows, net.row, order, send_row, send_col, recv_row, recv_col)
    pack_for_rows(net, packed, tokens_ref[...], send_row[...])
    copies = exchange_start(net, packed, got, capacity)
    need(norm_one, norm_two, cot, w_query, w_gate, w_mem, sub_keys, picks, lengths)
    own_gain = columns_of(gains, width)
    own_gain(net.col)[...] = jnp.broadcast_to(
        norm_one[...].astype(LOW).astype(F32), (8, width)
    )
    gain_spread = net.columns_start(own_gain)
    pack_for_rows(net, packed_cot, cot[...], send_row[...])
    cot_copies = exchange_start(net, packed_cot, got_cot, capacity)
    place_two = rows_of(weights_two, w_query.shape[0])
    place_two(net.row)[:, :depth] = w_query[...].astype(LOW)
    place_two(net.row)[:, depth : depth + width] = w_gate[...].astype(LOW)
    place_two(net.row)[:, depth + width :] = w_mem[...].T.astype(LOW)
    span = sub_keys.shape[1]
    place_keys = lambda at: keys.at[:, pl.ds(pl.multiple_of(at * span, span), span), :]
    place_keys(net.row)[...] = sub_keys[...].astype(LOW)
    wait_all(copies)
    own = columns_of(full, width)
    values = unpack(got, recv_col[...])
    own(net.col)[...] = values.astype(LOW)
    spread = net.columns_start(own)
    dealt[...] = values
    left_one = net.gather_pass(place_one, gather_one, False)
    gather_two = net.gather_start(place_two(net.row), place_two)
    gather_keys = net.gather_start(place_keys(net.row), place_keys)
    low_picks[...] = (picks[...] - 32768).astype(jnp.int16)
    head = net.col * halves // 2
    head_rows = pl.ds(pl.multiple_of(head * PICKS, PICKS), PICKS)
    halves_of = []
    for h in range(halves):
        even = (net.col * halves + h) % 2 == 0
        halves_of.append(jnp.where(even, picks[...] // NK, picks[...] % NK))
        turned[...] = halves_of[h].astype(F32).T
        index[h * PICKS : (h + 1) * PICKS] = turned[head_rows, :].astype(jnp.int32)
    ids_col = sequence_ids(lengths[...], count, 0)
    ids_row = sequence_ids(lengths[...], count, 1)
    wait_all(spread)
    wait_all(gain_spread)
    values = full[...].astype(F32)
    scale = lax.rsqrt(jnp.mean(values * values, axis=1, keepdims=True) + EPS)
    hidden_one[...] = (values * scale * gains[:1]).astype(LOW)
    factor_one[...] = jnp.broadcast_to(scale, (count, LANES))
    flush(hidden_one, factor_one, dealt, index, low_picks, send_row, send_col, recv_row, recv_col)
    wait_all(left_one + net.gather_pass(place_one, gather_one, True))
    flush(weights_one)
    qkv[...] = jnp.dot(
        hidden_one[...], weights_one[:, : 3 * width], preferred_element_type=F32
    ).astype(LOW)
    for h in range(width // HD):
        (_, _, value), probs = attention_scores(qkv, h, ids_col, ids_row)
        mixed[:, h * HD : (h + 1) * HD] = jnp.dot(
            probs.astype(LOW), value, preferred_element_type=F32
        ).astype(LOW)
    flush(qkv, mixed)
    own_part, reduce = project_start(
        net, mixed[...], weights_one.at[:, 3 * width :], outgoing, incoming
    )
    values = dealt[...] + project_end(own_part, incoming, reduce)
    resid[...] = values
    left = net.gather_pass(place_two, gather_two, False)
    left += net.gather_pass(place_keys, gather_keys, False)
    square = share_sums(net, jnp.sum(values * values, axis=1, keepdims=True), mine, theirs)
    scale = lax.rsqrt(square / D + EPS)
    factor_two[...] = scale
    flush(resid, factor_two)
    own = columns_of(hidden_two, width)
    gain_two = norm_two[...].astype(LOW).astype(F32)
    own(net.col)[...] = (resid[...] * widen(scale, width) * gain_two).astype(LOW)
    spread = net.columns_start(own)
    wait_all(cot_copies)
    own_cot = columns_of(full_cot, width)
    own_cot(net.col)[...] = unpack(got_cot, recv_col[...]).astype(LOW)
    cot_spread = net.columns_start(own_cot)
    left += net.gather_pass(place_two, gather_two, True)
    left += net.gather_pass(place_keys, gather_keys, True)
    wait_all(spread)
    wait_all(left)
    flush(hidden_two, weights_two, keys)
    for h in range(halves):
        columns = slice(h * QD, (h + 1) * QD)
        queries[:, columns] = jnp.dot(
            hidden_two[...], weights_two[:, columns], preferred_element_type=F32
        ).astype(LOW)
        scores = lax.dot_general(
            queries[:, columns], keys[h], NT_DIMS, preferred_element_type=F32
        )
        low_index = halves_of[h] % LANES
        first = jnp.take_along_axis(scores[:, :LANES], low_index, axis=1)
        second = jnp.take_along_axis(scores[:, LANES:], low_index, axis=1)
        turned[...] = jnp.where(halves_of[h] >= LANES, second, first).T
        first_row = (net.col * halves + h) * PICKS
        scores_of[pl.ds(pl.multiple_of(first_row, PICKS), PICKS), :] = turned[head_rows, :]
    own_scores = rows_of(scores_of, halves * PICKS)
    score_spread = net.columns_start(own_scores)
    open_gate = jnp.dot(
        hidden_two[...], weights_two[:, depth : depth + width], preferred_element_type=F32
    )
    gate[...] = open_gate
    wait_all(cot_spread)
    flush(full_cot, queries, gate)
    back = jnp.dot(full_cot[...], weights_two[:, depth + width :], preferred_element_type=F32)
    grad_mixed[...] = back
    grad_memory[...] = (back * (open_gate * jax.nn.sigmoid(open_gate))).astype(LOW)
    wait_all(score_spread)
    for m in range(MH):
        score = (
            scores_of[2 * m * PICKS : (2 * m + 1) * PICKS]
            + scores_of[(2 * m + 1) * PICKS : (2 * m + 2) * PICKS]
        )
        shifted = jnp.exp(score - jnp.max(score, axis=0, keepdims=True))
        weights[m * PICKS : (m + 1) * PICKS] = shifted / jnp.sum(shifted, axis=0, keepdims=True)
    net.drain()


def norm_grad(net, grad_hidden, values, scale, gain, mine, theirs):
    width = values.shape[1]
    scaled = grad_hidden * gain
    inner = share_sums(net, jnp.sum(scaled * values, axis=1, keepdims=True), mine, theirs)
    wide = widen(scale, width)
    grads = wide * scaled - values * (wide * wide * wide) * widen(inner, width) / D
    grad_gain = jnp.sum(grad_hidden * values * wide, axis=0, keepdims=True)
    return grads, grad_gain


def project_start(net, left, weights, outgoing, incoming):
    width = outgoing.shape[2]

    def block(col):
        rows = rows_of(weights, width)(col)[...]
        return lax.dot_general(left, rows, NT_DIMS, preferred_element_type=F32)

    copies = []
    for k in range(1, net.cols):
        outgoing[k - 1] = block(flip(net.col, k)).astype(LOW)
        copies.append(net.send(outgoing.at[k - 1], incoming.at[k - 1], col_k=k))
    return block(net.col), copies


def project_end(total, incoming, copies):
    for k, copy in enumerate(copies):
        copy.wait_recv()
        total = total + incoming[k].astype(F32)
    return total


def attention_scores(qkv, head, ids_col, ids_row):
    parts = [qkv[:, (3 * head + j) * HD : (3 * head + j + 1) * HD] for j in range(3)]
    scores = lax.dot_general(parts[0], parts[1], NT_DIMS, preferred_element_type=F32) * HD ** (
        -0.5
    )
    asks = lax.broadcasted_iota(jnp.int32, scores.shape, 0)
    offers = lax.broadcasted_iota(jnp.int32, scores.shape, 1)
    allowed = (ids_col == ids_row) & (asks >= offers)
    scores = jnp.where(allowed, scores, MASKED)
    shifted = jnp.exp(scores - jnp.max(scores, axis=1, keepdims=True))
    return parts, shifted / jnp.sum(shifted, axis=1, keepdims=True)


def spread_picks(halves, weights, dw, index, out):
    tokens = weights.shape[1]
    grad = weights * (dw - jnp.sum(weights * dw, axis=0, keepdims=True))
    block = 128
    places = lax.broadcasted_iota(jnp.int32, (NK, block), 0)
    for h in range(halves):
        for b in range(tokens // block):
            columns = slice(b * block, (b + 1) * block)
            total = jnp.zeros((NK, block), F32)
            for k in range(PICKS):
                row = index[h * PICKS + k : h * PICKS + k + 1, columns]
                total = total + jnp.where(places == row, grad[k : k + 1, columns], 0.0)
            out[columns, h * NK : (h + 1) * NK] = total.T.astype(LOW)


def back_kernel(
    rows,
    cols,
    halves,
    need,
    flush,
    share,
    dw,
    index,
    memory,
    gate,
    grad_mixed,
    queries,
    hidden_two,
    cot,
    weights_two,
    keys,
    resid,
    factor_two,
    gain_two,
    recv_row,
    send_col,
    qkv,
    mixed,
    lengths,
    hidden_one,
    weights_one,
    dealt,
    factor_one,
    gain_one,
    output,
    grad_tokens,
    own_qkv,
    own_attn,
    own_query,
    own_gate,
    own_mem,
    own_keys,
    gains,
    grad_sub,
    both,
    mixed_two,
    grad_mem,
    grad_two,
    grad_keys,
    grad_low,
    grad_resid,
    grad_qkv,
    grad_one,
    one_outgoing,
    one_incoming,
    res_outgoing,
    res_incoming,
    two_outgoing,
    two_incoming,
    mine,
    theirs,
    mine_one,
    theirs_one,
    packed,
    got,
    packed_one,
    got_one,
    across_two,
    two_out,
    two_in,
    across_keys,
    keys_out,
    keys_in,
    across_one,
    one_out,
    one_in,
    across_mem,
    mem_out,
    mem_in,
    my_gains,
    their_gains,
    sends,
    recvs,
):
    net = Net(rows, cols, sends, recvs)
    capacity = packed.shape[0] // rows
    width = resid.shape[1]
    depth = halves * QD
    greeted = net.greet(range(1, rows), range(1, cols))
    need(gate, grad_mixed, memory)
    open_gate, back, read = gate[...], grad_mixed[...], memory[...]
    sigmoid = jax.nn.sigmoid(open_gate)
    both[:, depth:] = (back * read * sigmoid * (1.0 + open_gate * (1.0 - sigmoid))).astype(LOW)
    mixed_two[...] = (read * open_gate * sigmoid).astype(LOW)
    need(weights_two)
    net.meet(greeted)
    own_res, reduce_res = project_start(
        net, mixed_two[...], weights_two.at[:, depth + width :], res_outgoing, res_incoming
    )
    need(cot)
    grad_mem[...] = jnp.dot(cot[...].T, mixed_two[...], preferred_element_type=F32)
    moved_mem, moved_two, moved_keys, moved_one = {}, {}, {}, {}
    view_mem = rows_of(grad_mem, own_query.shape[0])
    started_mem = net.scatter_start(view_mem, across_mem)
    pass_mem = (view_mem, across_mem, started_mem, mem_out, mem_in, moved_mem)
    need(share, dw, index, keys)
    head = net.col * halves // 2
    own_share = share[pl.ds(pl.multiple_of(head * PICKS, PICKS), PICKS), :]
    spread_picks(halves, own_share, dw[...], index, grad_sub)
    net.scatter_pass(*pass_mem, True)
    for h in range(halves):
        both[:, h * QD : (h + 1) * QD] = jnp.dot(
            grad_sub[:, h * NK : (h + 1) * NK], keys[h], preferred_element_type=F32
        ).astype(LOW)
    own_part, reduce_two = project_start(
        net, both[...], weights_two.at[:, : depth + width], two_outgoing, two_incoming
    )
    need(resid, recv_row)
    block = resid[...] + project_end(own_res, res_incoming, reduce_res)
    pack_for_rows(net, packed, block.astype(LOW), recv_row[...])
    copies = exchange_start(net, packed, got, capacity)
    need(hidden_two, queries)
    grad_two[...] = jnp.dot(hidden_two[...].T, both[...], preferred_element_type=F32)
    for h in range(halves):
        grad_keys[h] = jnp.dot(
            grad_sub[:, h * NK : (h + 1) * NK].T,
            queries[:, h * QD : (h + 1) * QD],
            preferred_element_type=F32,
        )
    view_two = rows_of(grad_two, own_query.shape[0])
    span = own_keys.shape[1]
    view_keys = lambda at: grad_keys.at[:, pl.ds(pl.multiple_of(at * span, span), span), :]
    started_two = net.scatter_start(view_two, across_two)
    started_keys = net.scatter_start(view_keys, across_keys)
    pass_two = (view_two, across_two, started_two, two_out, two_in, moved_two)
    pass_keys = (view_keys, across_keys, started_keys, keys_out, keys_in, moved_keys)
    net.scatter_pass(*pass_two, True)
    net.scatter_pass(*pass_keys, True)
    net.scatter_pass(*pass_mem, False)
    need(lengths)
    ids_col = sequence_ids(lengths[...], memory.shape[0], 0)
    ids_row = sequence_ids(lengths[...], memory.shape[0], 1)
    need(factor_two, gain_two)
    grad_hidden = project_end(own_part, two_incoming, reduce_two)
    grads, gain_two_sum = norm_grad(
        net, grad_hidden, resid[...], factor_two[...], gain_two[...].astype(LOW).astype(F32), mine, theirs
    )
    own_cot = columns_of(cot, width)(net.col)[...]
    grads = grads + own_cot.astype(F32)
    grad_resid[...] = grads
    own = columns_of(grad_low, width)
    own(net.col)[...] = grads.astype(LOW)
    spread = net.columns_start(own)
    wait_all(spread)
    net.scatter_pass(*pass_two, False)
    net.scatter_pass(*pass_keys, False)
    need(weights_one, qkv, hidden_one, mixed, send_col, dealt, factor_one, gain_one)
    grad_heads = jnp.dot(
        grad_low[...], weights_one[:, 3 * width :], preferred_element_type=F32
    ).astype(LOW)
    for head in range(width // HD):
        (query, key, value), probs = attention_scores(qkv, head, ids_col, ids_row)
        grad_out = grad_heads[:, head * HD : (head + 1) * HD]
        grad_prob = lax.dot_general(grad_out, value, NT_DIMS, preferred_element_type=F32)
        inner = jnp.sum(probs * grad_prob, axis=1, keepdims=True)
        grad_score = (probs * (grad_prob - inner)).astype(LOW)
        pieces = (
            jnp.dot(grad_score, key, preferred_element_type=F32) * HD ** (-0.5),
            jnp.dot(grad_score.T, query, preferred_element_type=F32) * HD ** (-0.5),
            jnp.dot(probs.astype(LOW).T, grad_out, preferred_element_type=F32),
        )
        for j in range(3):
            grad_qkv[:, (3 * head + j) * HD : (3 * head + j + 1) * HD] = pieces[j].astype(LOW)
    own_part, reduce_one = project_start(
        net, grad_qkv[...], weights_one.at[:, : 3 * width], one_outgoing, one_incoming
    )
    grad_one[:, : 3 * width] = jnp.dot(
        hidden_one[...].T, grad_qkv[...], preferred_element_type=F32
    )
    grad_one[:, 3 * width :] = jnp.dot(grad_low[...].T, mixed[...], preferred_element_type=F32)
    view_one = rows_of(grad_one, own_qkv.shape[0])
    started_one = net.scatter_start(view_one, across_one)
    pass_one = (view_one, across_one, started_one, one_out, one_in, moved_one)
    net.scatter_pass(*pass_one, True)
    grad_hidden = project_end(own_part, one_incoming, reduce_one)
    grads, gain_one_sum = norm_grad(
        net,
        grad_hidden,
        dealt[...],
        factor_one[...],
        gain_one[...].astype(LOW).astype(F32),
        mine_one,
        theirs_one,
    )
    grads = grads + grad_resid[...]
    pack_for_rows(net, packed_one, grads.astype(LOW), recv_row[...])
    last = exchange_start(net, packed_one, got_one, capacity)
    net.scatter_pass(*pass_one, False)
    places = lax.broadcasted_iota(jnp.int32, my_gains.shape, 0)
    my_gains[...] = jnp.where(places == 0, gain_one_sum, gain_two_sum)
    gain_copies = [net.send(my_gains, their_gains.at[k], row_k=k) for k in range(1, rows)]
    total = net.scatter_end(view_two, across_two, started_two, two_in, moved_two)
    own_query[...] = total[:, :depth]
    own_gate[...] = total[:, depth:]
    own_mem[...] = net.scatter_end(view_mem, across_mem, started_mem, mem_in, moved_mem).T
    own_keys[...] = net.scatter_end(view_keys, across_keys, started_keys, keys_in, moved_keys)
    wait_all(copies)
    output[...] = unpack(got, send_col[...])
    flush(output)
    total = net.scatter_end(view_one, across_one, started_one, one_in, moved_one)
    own_qkv[...] = total[:, : 3 * width]
    own_attn[...] = total[:, 3 * width :].T
    total = my_gains[...]
    for k, copy in enumerate(gain_copies):
        copy.wait_recv()
        total = total + their_gains[k + 1]
    gains[...] = total
    wait_all(last)
    grad_tokens[...] = unpack(got_one, send_col[...])
    net.drain()


def staged(kernel, rows, cols, sizes, ins, outs, *refs):
    given, results = refs[:ins], refs[ins : ins + outs]
    rest = refs[ins + outs :]
    twins, rest = rest[: ins + outs], rest[ins + outs :]
    sems, rest = rest[0], rest[1:]
    sources, targets = twins[:ins], twins[ins:]
    waited, left = set(), []

    def moving(i):
        return pltpu.make_async_copy(given[i], sources[i], sems.at[i])

    def need(*wanted):
        for ref in wanted:
            i = [j for j in range(ins) if sources[j] is ref][0]
            if i not in waited:
                moving(i).wait()
                waited.add(i)

    def flush(*done):
        for ref in done:
            i = [j for j in range(outs) if targets[j] is ref][0]
            copy = pltpu.make_async_copy(targets[i], results[i], sems.at[ins + i])
            copy.start()
            left.append((i, copy))

    for i in range(ins):
        moving(i).start()
    kernel(rows, cols, *sizes, need, flush, *sources, *targets, *rest)
    assert len(waited) == ins
    flush(*[targets[i] for i in range(outs) if i not in [j for j, _ in left]])
    for _, copy in left:
        copy.wait()


def remote_call(kernel, rows, cols, number, copies, ins, outs, scratch, *sizes):
    twins = [(x.shape, x.dtype) for x in ins] + outs
    anywhere = pl.BlockSpec(memory_space=pl.ANY)
    return pl.pallas_call(
        functools.partial(staged, kernel, rows, cols, sizes, len(ins), len(outs)),
        out_shape=[jax.ShapeDtypeStruct(shape, dtype) for shape, dtype in outs],
        in_specs=[anywhere] * len(ins),
        out_specs=[anywhere] * len(outs),
        scratch_shapes=[pltpu.VMEM(shape, dtype) for shape, dtype in twins]
        + [pltpu.SemaphoreType.DMA((len(twins),))]
        + [pltpu.VMEM(shape, dtype) for shape, dtype in scratch]
        + [pltpu.SemaphoreType.DMA((copies,)), pltpu.SemaphoreType.DMA((copies,))],
        compiler_params=pltpu.CompilerParams(
            collective_id=number, has_side_effects=True, vmem_limit_bytes=VMEM_BYTES
        ),
    )(*ins)


def memory_kernel(
    rows,
    cols,
    own_weights,
    own_picks,
    own_grads,
    table_f32,
    memory,
    dw,
    gacc_out,
    gacc,
    table,
    stage,
    picks_of,
    grads_of,
    low_of,
    dense,
    hi_ref,
    lo_ref,
    wide_ref,
    found_ref,
    mem_all,
    mem_twin,
    mem_out,
    mem_in,
    dw_all,
    dw_twin,
    dw_out,
    dw_in,
    dw_cols,
    stage_sems,
    sends,
    recvs,
):
    net = Net(rows, cols, sends, recvs)
    half = rows // 2
    tok_block = own_picks.shape[0]
    span_rows, width = table.shape
    spans = span_rows // LANES
    pitch = spans + 8
    iters = 4
    per_tok = tok_block // iters
    per_span = spans // iters

    grads_at = rows_of(grads_of, tok_block)
    picks_at = rows_of(picks_of, tok_block)
    low_at = lambda index: low_of.at[index]
    views = (grads_at, picks_at, low_at)
    first_pass = 3 * half
    first_twin = first_pass + 3 * half
    first_out = first_twin + 2 * half
    first_col = first_out + 2 * half

    def gather(a, j):
        mine = views[a](net.row)
        return net.copy(mine, mine, 3 * j + a, row_k=2 * j if j else 1)

    def passing(a, j):
        there = views[a](flip(net.row, 2 * j))
        return net.copy(there, there, first_pass + 3 * j + a, row_k=1)

    def twin(a, j):
        src, dst = ((mem_all, mem_twin), (dw_all, dw_twin))[a]
        return net.copy(src.at[2 * j + 1], dst.at[j], first_twin + 2 * j + a, row_k=1)

    def outward(a, j):
        src, dst = ((mem_out, mem_in), (dw_out, dw_in))[a]
        return net.copy(src.at[j - 1], dst.at[j - 1], first_out + 2 * j + a, row_k=2 * j)

    head = lambda col: pl.ds(pl.multiple_of(col * MH // cols * PICKS, PICKS), PICKS)

    def dw_copy(k):
        return net.copy(
            dw_all.at[0, head(flip(net.col, k)), :],
            dw_cols.at[k - 1],
            first_col + k,
            col_k=k,
        )

    stage_rows = stage.shape[1]

    def stage_copy(i):
        source = table_f32.at[pl.ds(i * stage_rows, stage_rows), :]
        return pltpu.make_async_copy(source, stage.at[i % 2], stage_sems.at[i % 2])

    stage_copy(0).start()
    greeted = net.greet([1] + [2 * j for j in range(1, half)], range(1, cols))
    for i in range(span_rows // stage_rows):
        if (i + 1) * stage_rows < span_rows:
            stage_copy(i + 1).start()
        stage_copy(i).wait()
        table[i * stage_rows : (i + 1) * stage_rows, :] = stage[i % 2].astype(LOW)
    net.meet(greeted)
    grads_at(net.row)[...] = own_grads[...]
    picks_at(net.row)[...] = own_picks[...]
    low_at(net.row)[...] = own_weights[...].astype(LOW)
    for j in range(2):
        for a in range(3):
            gather(a, j).start()
    gacc[...] = jnp.zeros_like(gacc)
    mem_all[...] = jnp.zeros_like(mem_all)

    def one_block(step, _):
        k = jnp.where(step == 0, 0, jnp.where(step == rows - 1, 1, step + 1))
        there = cross(net.row, k, rows)
        for j in range(1, half):

            @pl.when(step == 2 * j - 1)
            def _():
                for a in range(3):
                    gather(a, j).wait_recv()
                    passing(a, j).start()
                if j + 1 < half:
                    for a in range(3):
                        gather(a, j + 1).start()

            @pl.when(step == 2 * j)
            def _():
                for a in range(3):
                    passing(a, j).wait_recv()

        @pl.when(step == rows - 1)
        def _():
            for a in range(3):
                gather(a, 0).wait_recv()

        picks = picks_at(there)[...].astype(jnp.int32) + 32768
        hi_ref[...] = (picks // LANES - net.row * spans).astype(F32)
        lo_ref[...] = (picks % LANES).astype(F32)
        wide_ref[...] = low_of[there].astype(F32).T
        places_lo = lax.broadcasted_iota(jnp.int32, (LANES, LANES), 0).astype(F32).astype(LOW)
        places_hi = lax.broadcasted_iota(jnp.int32, (spans, LANES), 0).astype(F32).astype(LOW)
        ones = jnp.ones((LANES, LANES), LOW)
        zeros = jnp.zeros((LANES, LANES), LOW)
        blank = jnp.zeros((spans, LANES), LOW)
        grads = grads_at(there)[...]
        grads_t = grads.T
        found_ref[...] = jnp.zeros_like(found_ref)
        lo_int = picks % LANES
        hi_all = hi_ref[...]

        def token_pair(first):
            rights, lefts = [], []
            for token in (first, first + 1):
                lo_row = jnp.broadcast_to(lo_ref[pl.ds(token, 1), :], (LANES, LANES)).astype(LOW)
                hi_row = jnp.broadcast_to(hi_ref[pl.ds(token, 1), :], (spans, LANES)).astype(LOW)
                w_row = jnp.broadcast_to(wide_ref[pl.ds(token, 1), :], (spans, LANES)).astype(LOW)
                rights.append(jnp.where(lo_row == places_lo, ones, zeros))
                lefts.append(jnp.where(hi_row == places_hi, w_row, blank))
            right = jnp.concatenate(rights, axis=1)
            left = jnp.concatenate(
                [
                    jnp.concatenate([lefts[0], blank], axis=1),
                    jnp.concatenate([blank, lefts[1]], axis=1),
                ],
                axis=0,
            )
            both = lax.dot_general(left, right, NT_DIMS, preferred_element_type=F32)
            for j in range(2):
                dense[pl.ds(pl.multiple_of((first + j) * pitch, 8), spans), :] = both[
                    j * spans : (j + 1) * spans
                ]

        def look(found, first, number, between=None):
            span = pl.ds(pl.multiple_of(first * LANES, LANES), number * LANES)
            products = lax.dot_general(
                grads, table[span, :], NT_DIMS, preferred_element_type=F32
            )
            for j in range(number):
                picked = jnp.take_along_axis(
                    products[:, LANES * j : LANES * (j + 1)], lo_int, axis=1
                )
                found = jnp.where(hi_all == (first + j).astype(F32), picked, found)
                if between:
                    between(j)
            return found

        early = per_span // 2
        late = per_span - early

        def build(it, _):
            for j in range(1, half):

                @pl.when((it == 1) & (step == 2 * j + 1))
                def _():
                    twin(0, j).wait_recv()
                    twin(1, j).wait_recv()
                    mem_out[j - 1] = (mem_all[2 * j] + mem_twin[j]).astype(LOW)
                    outward(0, j).start()
                    dw_out[j - 1] = (dw_all[2 * j] + dw_twin[j]).astype(LOW)
                    outward(1, j).start()

            pairs = per_tok // 2 // early

            def some_pairs(j):
                for u in range(pairs):
                    token_pair(it * per_tok + (j * pairs + u) * 2)

            found_ref[...] = look(found_ref[...], it * early, early, some_pairs)
            return 0

        lax.fori_loop(0, iters, build, 0)
        parts = min(4, late)

        def multiply(it, _):
            found, total = found_ref[...], None
            for c in range(parts):
                low, high = c * late // parts, (c + 1) * late // parts
                found = look(found, early * iters + it * late + low, high - low)
                low, high = c * per_span // parts, (c + 1) * per_span // parts
                first = it * per_span + low
                chosen = jnp.concatenate(
                    [
                        dense[pl.ds(first + j, tok_block, stride=pitch), :].astype(LOW)
                        for j in range(high - low)
                    ],
                    axis=1,
                )
                span = pl.ds(pl.multiple_of(first * LANES, LANES), (high - low) * LANES)
                gacc[:, span] += jnp.dot(grads_t, chosen, preferred_element_type=F32)
                read = jnp.dot(chosen, table[span, :], preferred_element_type=F32)
                total = read if total is None else total + read
            mem_all[k] += total
            found_ref[...] = found
            return 0

        lax.fori_loop(0, iters, multiply, 0)
        dw_all[k] = found_ref[...].T
        for j in range(half):

            @pl.when(step == (2 * j if j else rows - 1))
            def _():
                twin(0, j).start()
                twin(1, j).start()

        return 0

    lax.fori_loop(0, rows, one_block, 0)
    leaving = pltpu.make_async_copy(gacc, gacc_out, stage_sems.at[2])
    leaving.start()
    twin(1, 0).wait_recv()
    total = dw_all[0] + dw_twin[0]
    for j in range(1, half):
        outward(1, j).wait_recv()
        total = total + dw_in[j - 1].astype(F32)
    dw_all[0] = total
    for k in range(1, cols):
        dw_copy(k).start()
    twin(0, 0).wait_recv()
    total = mem_all[0] + mem_twin[0]
    for j in range(1, half):
        outward(0, j).wait_recv()
        total = total + mem_in[j - 1].astype(F32)
    memory[...] = total
    total = dw_all[0, head(net.col), :]
    for k in range(1, cols):
        dw_copy(k).wait_recv()
        total = total + dw_cols[k - 1]
    dw[...] = total
    for k in range(1, cols):
        dw_copy(k).wait_send()
    for j in range(half):
        for a in range(3):
            gather(a, j).wait_send()
            if j:
                passing(a, j).wait_send()
        for a in range(2):
            twin(a, j).wait_send()
            if j:
                outward(a, j).wait_send()
    leaving.wait()


def turn_kernel(source, out):
    out[...] = source[...].T


def turn_call(table):
    width, span_rows = table.shape
    block = min(4096, span_rows)
    return pl.pallas_call(
        turn_kernel,
        grid=(span_rows // block,),
        in_specs=[pl.BlockSpec((width, block), lambda i: (0, i))],
        out_specs=pl.BlockSpec((block, width), lambda i: (i, 0)),
        out_shape=jax.ShapeDtypeStruct((span_rows, width), F32),
        compiler_params=pltpu.CompilerParams(vmem_limit_bytes=VMEM_BYTES),
    )(table)


def memory_call(rows, cols, number, weights, picks, grads, table):
    tokens, count = picks.shape
    span_rows, width = table.shape
    half = rows // 2
    copies = 10 * half + cols
    vmem = pltpu.VMEM
    return pl.pallas_call(
        functools.partial(memory_kernel, rows, cols),
        in_specs=[VMEM_SPEC, VMEM_SPEC, VMEM_SPEC, pl.BlockSpec(memory_space=pl.ANY)],
        out_specs=[VMEM_SPEC, VMEM_SPEC, pl.BlockSpec(memory_space=pl.ANY)],
        out_shape=[
            jax.ShapeDtypeStruct((tokens, width), F32),
            jax.ShapeDtypeStruct((PICKS, tokens), F32),
            jax.ShapeDtypeStruct((width, span_rows), F32),
        ],
        scratch_shapes=[
            vmem((width, span_rows), F32),
            vmem((span_rows, width), LOW),
            vmem((2, 1024, width), F32),
            vmem((rows * tokens, count), jnp.int16),
            vmem((rows * tokens, width), LOW),
            vmem((rows, count, tokens), LOW),
            vmem((tokens * (span_rows // LANES + 8), LANES), F32),
            vmem((tokens, count), F32),
            vmem((tokens, count), F32),
            vmem((tokens, count), F32),
            vmem((tokens, count), F32),
            vmem((rows, tokens, width), F32),
            vmem((half, tokens, width), F32),
            vmem((half - 1, tokens, width), LOW),
            vmem((half - 1, tokens, width), LOW),
            vmem((rows, count, tokens), F32),
            vmem((half, count, tokens), F32),
            vmem((half - 1, count, tokens), LOW),
            vmem((half - 1, count, tokens), LOW),
            vmem((cols - 1, PICKS, tokens), F32),
            pltpu.SemaphoreType.DMA((3,)),
            pltpu.SemaphoreType.DMA((copies,)),
            pltpu.SemaphoreType.DMA((copies,)),
        ],
        compiler_params=pltpu.CompilerParams(
            collective_id=number, has_side_effects=True, vmem_limit_bytes=63 * 2**20
        ),
    )(weights, picks, grads, table)


def per_device(
    tokens,
    cotangent,
    deal_order,
    seq_lengths,
    value_picks,
    norm1_gain,
    w_qkv,
    w_attn_out,
    norm2_gain,
    w_query,
    sub_keys,
    value_table,
    w_gate,
    w_mem_out,
):
    rows, cols = lax.axis_size("row"), lax.axis_size("col")
    row_index = lax.axis_index("row")
    count, width = tokens.shape
    slots = 2 * count
    half = rows // 2
    halves = sub_keys.shape[0]
    depth = halves * QD
    span_one, span_two = 4 * width, depth + 2 * width
    shard_rows = w_qkv.shape[0]
    flat_picks = value_picks.reshape(count, MH * PICKS)
    gain_one, gain_two = norm1_gain[None, :], norm2_gain[None, :]
    swap = [((slots, width), LOW), ((slots, width), LOW)]
    sums = [((8, count), F32), ((cols, 8, count), F32)]
    moving = ((cols - 1, count, width), LOW)
    (
        send_row,
        send_col,
        recv_row,
        recv_col,
        hidden_one,
        dealt,
        factor_one,
        weights_one,
        qkv,
        mixed,
        hidden_two,
        resid,
        factor_two,
        full_cot,
        weights_two,
        keys,
        queries,
        gate,
        grad_mixed,
        grad_memory,
        index,
        low_picks,
        pick_weights,
    ) = remote_call(
        front_kernel,
        rows,
        cols,
        0,
        7 * (cols - 1) + 5 * (rows - 1),
        [
            deal_order.reshape(rows, count),
            flat_picks,
            seq_lengths,
            tokens,
            cotangent,
            w_qkv,
            w_attn_out,
            w_query,
            w_gate,
            w_mem_out,
            sub_keys,
            gain_one,
            gain_two,
        ],
        [
            ((1, count), jnp.int32),
            ((count, 1), jnp.int32),
            ((1, count), jnp.int32),
            ((count, 1), jnp.int32),
            ((count, D), LOW),
            ((count, width), F32),
            ((count, LANES), F32),
            ((D, span_one), LOW),
            ((count, 3 * width), LOW),
            ((count, width), LOW),
            ((count, D), LOW),
            ((count, width), F32),
            ((count, LANES), F32),
            ((count, D), LOW),
            ((D, span_two), LOW),
            ((halves, NK, QD), LOW),
            ((count, depth), LOW),
            ((count, width), F32),
            ((count, width), F32),
            ((count, width), LOW),
            ((halves * PICKS, count), jnp.int32),
            ((count, MH * PICKS), jnp.int16),
            ((MH * PICKS, count), F32),
        ],
        [((2 * MH * PICKS, count), F32), ((count, D), LOW), ((8, D), F32), *swap, *swap, moving, moving, *sums]
        + [((MH * PICKS, count), F32)],
        halves,
    )
    memory, grad_pick, grad_table = memory_call(
        rows, cols, 1, pick_weights, low_picks, grad_memory, value_table
    )
    block = ((count, width), F32)
    scattered = [
        [((half,) + shape, F32), ((half - 1,) + shape, LOW), ((half - 1,) + shape, LOW)]
        for shape in (
            (shard_rows, depth + width),
            sub_keys.shape,
            (shard_rows, span_one),
            (shard_rows, width),
        )
    ]
    output, grad_tokens, own_qkv, own_attn, own_query, own_gate, own_mem, own_keys, gains = remote_call(
        back_kernel,
        rows,
        cols,
        2,
        6 * (cols - 1) + 3 * (rows - 1) + 4 * (half + half - 1),
        [
            pick_weights,
            grad_pick,
            index,
            memory,
            gate,
            grad_mixed,
            queries,
            hidden_two,
            full_cot,
            weights_two,
            keys,
            resid,
            factor_two,
            gain_two,
            recv_row,
            send_col,
            qkv,
            mixed,
            seq_lengths,
            hidden_one,
            weights_one,
            dealt,
            factor_one,
            gain_one,
        ],
        [
            block,
            block,
            (w_qkv.shape, F32),
            (w_attn_out.shape, F32),
            (w_query.shape, F32),
            (w_gate.shape, F32),
            (w_mem_out.shape, F32),
            (sub_keys.shape, F32),
            ((8, width), F32),
        ],
        [
            ((count, halves * NK), LOW),
            ((count, depth + width), LOW),
            ((count, width), LOW),
            ((D, width), F32),
            ((D, depth + width), F32),
            ((halves, NK, QD), F32),
            ((count, D), LOW),
            block,
            ((count, 3 * width), LOW),
            ((D, span_one), F32),
            *[moving] * 6,
            *sums,
            *sums,
            *swap,
            *swap,
            *scattered[0],
            *scattered[1],
            *scattered[2],
            *scattered[3],
            ((8, width), F32),
            ((rows, 8, width), F32),
        ],
        halves,
    )
    gain_span = width // rows
    gain_one_grad = lax.dynamic_slice_in_dim(gains[0], row_index * gain_span, gain_span)
    gain_two_grad = lax.dynamic_slice_in_dim(gains[1], row_index * gain_span, gain_span)
    return (
        output,
        grad_tokens,
        gain_one_grad,
        own_qkv,
        own_attn,
        gain_two_grad,
        own_query,
        own_keys,
        turn_call(grad_table),
        own_gate,
        own_mem,
    )


def solution(mesh):
    return jax.shard_map(
        per_device,
        mesh=mesh,
        in_specs=(
            P("row", "col"),
            P("row", "col"),
            P(),
            P("row", None),
            P("row", None, None),
            P("col"),
            P("row", "col"),
            P("col", "row"),
            P("col"),
            P("row", "col"),
            P("col", "row", None),
            P("row", "col"),
            P("row", "col"),
            P("col", "row"),
        ),
        out_specs=(
            P("row", "col"),
            P("row", "col"),
            P(("col", "row")),
            P("row", "col"),
            P("col", "row"),
            P(("col", "row")),
            P("row", "col"),
            P("col", "row", None),
            P("row", "col"),
            P("row", "col"),
            P("col", "row"),
        ),
        check_vma=False,
    )
```

```python
import functools

import jax
import jax.numpy as jnp
from jax import lax
from jax.experimental import pallas as pl
from jax.experimental.pallas import tpu as pltpu
from jax.sharding import PartitionSpec as P

D = 1024
HD = 64
MH = 4
QD = 512
NK = 256
PICKS = 32
LANES = 128
LANE_BITS = LANES.bit_length() - 1
KEY_BITS = NK.bit_length() - 1
EPS = 1e-05
MASKED = -1e30
F32 = jnp.float32
LOW = jnp.bfloat16
MESH = pl.DeviceIdType.MESH
NT_DIMS = (((1,), (1,)), ((), ()))
VMEM_SPEC = pl.BlockSpec(memory_space=pltpu.VMEM)
VMEM_BYTES = 60 * 2**20


def flip(index, mask):
    bit = 1
    while bit <= mask:
        if mask & bit:
            index = index + bit - 2 * bit * (index // bit % 2)
        bit *= 2
    return index


def cross(index, mask, size):
    total, bit = 0, 1
    while bit < size:
        a, b = index // bit % 2, mask // bit % 2
        total = total + bit * (a + b - 2 * a * b)
        bit *= 2
    return total


class Net:
    def __init__(self, rows, cols, sends, recvs):
        self.rows, self.cols = rows, cols
        self.row, self.col = lax.axis_index("row"), lax.axis_index("col")
        self.sends, self.recvs, self.used = sends, recvs, 0
        self.pending = []

    def place(self, row_k, col_k):
        return (flip(self.row, row_k), flip(self.col, col_k))

    def greet(self, row_ks, col_ks):
        barrier = pltpu.get_barrier_semaphore()
        places = [self.place(k, 0) for k in row_ks] + [self.place(0, k) for k in col_ks]
        for place in places:
            pl.semaphore_signal(barrier, inc=1, device_id=place, device_id_type=MESH)
        return len(places)

    def meet(self, greeted):
        pl.semaphore_wait(pltpu.get_barrier_semaphore(), greeted)

    def copy(self, src, dst, number, row_k=0, col_k=0):
        assert number < self.sends.shape[0]
        return pltpu.make_async_remote_copy(
            src_ref=src,
            dst_ref=dst,
            send_sem=self.sends.at[number],
            recv_sem=self.recvs.at[number],
            device_id=self.place(row_k, col_k),
            device_id_type=MESH,
        )

    def send(self, src, dst, row_k=0, col_k=0):
        copy = self.copy(src, dst, self.used, row_k, col_k)
        copy.start()
        self.used += 1
        self.pending.append(copy)
        return copy

    def drain(self):
        for copy in self.pending:
            copy.wait_send()

    def gather_start(self, src, view):
        sent = {b: self.send(src, view(self.row), row_k=2 * b) for b in reversed(self.bits())}
        return sent, self.send(src, view(self.row), row_k=1)

    def gather_pass(self, view, started, near):
        sent, sibling = started
        passed = [sibling] if near else []
        masks = [m for m in range(1, self.rows // 2) if (m % 2 == 1) == near]
        for m in sorted(masks, key=lambda m: (-(m & -m), m.bit_count())):
            sent[m].wait_recv()
            block = view(flip(self.row, 2 * m))
            for b in self.bits():
                if b < (m & -m):
                    sent[m ^ b] = self.send(block, block, row_k=2 * b)
            passed.append(self.send(block, block, row_k=1))
        return passed

    def bits(self):
        return [1 << i for i in range((self.rows // 2 - 1).bit_length())]

    def scatter_start(self, view, across):
        twin = flip(self.row, 1)
        return [
            self.send(view(flip(twin, 2 * j)), across.at[j], row_k=1)
            for j in range(self.rows // 2)
        ]

    def scatter_pass(self, view, across, started, outgoing, incoming, moved, near):
        masks = [m for m in range(1, self.rows // 2) if (m % 2 == 1) == near]
        for m in sorted(masks, key=lambda m: ((m & -m), -m.bit_count())):
            started[m].wait_recv()
            block = view(flip(self.row, 2 * m))[...] + across[m]
            for b in self.bits():
                if b < (m & -m):
                    moved[m ^ b].wait_recv()
                    block = block + incoming[(m ^ b) - 1].astype(F32)
            outgoing[m - 1] = block.astype(outgoing.dtype)
            moved[m] = self.send(outgoing.at[m - 1], incoming.at[m - 1], row_k=2 * (m & -m))
        return moved

    def scatter_end(self, view, across, started, incoming, moved):
        started[0].wait_recv()
        total = view(self.row)[...] + across[0]
        for b in self.bits():
            moved[b].wait_recv()
            total = total + incoming[b - 1].astype(F32)
        return total

    def columns_start(self, view):
        return [self.send(view(self.col), view(self.col), col_k=k) for k in range(1, self.cols)]


def wait_all(copies):
    for copy in copies:
        copy.wait_recv()


def rows_of(ref, count):
    return lambda index: ref.at[pl.ds(pl.multiple_of(index * count, count), count), :]


def columns_of(ref, count):
    return lambda index: ref.at[:, pl.ds(pl.multiple_of(index * count, count), count)]


def one_hot_rows(positions, slots):
    places = lax.broadcasted_iota(jnp.int32, (positions.shape[0], slots), 1)
    return jnp.where(positions == places, 1.0, 0.0).astype(LOW)


def one_hot_columns(positions, slots):
    places = lax.broadcasted_iota(jnp.int32, (slots, positions.shape[1]), 0)
    return jnp.where(positions == places, 1.0, 0.0).astype(LOW)


def pack_for_rows(net, packed, values, positions):
    slots = packed.shape[0]
    packed[...] = jnp.dot(
        one_hot_columns(positions, slots), values, preferred_element_type=F32
    ).astype(LOW)


def exchange_start(net, packed, got, capacity):
    mine = rows_of(got, capacity)
    theirs = rows_of(packed, capacity)
    copies = [
        net.send(theirs(flip(net.row, k)), mine(net.row), row_k=k) for k in range(1, net.rows)
    ]
    mine(net.row)[...] = theirs(net.row)[...]
    return copies


def unpack(got, positions):
    return jnp.dot(
        one_hot_rows(positions, got.shape[0]), got[...], preferred_element_type=F32
    )


def share_sums(net, sums, mine, theirs):
    tokens = sums.shape[0]
    mine[...] = jnp.broadcast_to(sums, (tokens, LANES)).T[:8]
    copies = [net.send(mine, theirs.at[k], col_k=k) for k in range(1, net.cols)]
    wait_all(copies)
    total = mine[...]
    for k in range(1, net.cols):
        total = total + theirs[k]
    return jnp.broadcast_to(total[:1], (LANES, tokens)).T


def widen(lanes, width):
    return jnp.concatenate([lanes] * (width // LANES), axis=1)


def first_of(size, mask):
    earlier = lax.broadcasted_iota(jnp.int32, (size, size), 0)
    later = lax.broadcasted_iota(jnp.int32, (size, size), 1)
    triangle = jnp.where(earlier < later, 1.0, 0.0).astype(LOW)
    return jnp.dot(mask.astype(LOW), triangle, preferred_element_type=F32)


def find_places(rows, row, order, send_row, send_col, recv_row, recv_col):
    count = order.shape[1]
    capacity = 2 * count // rows
    owner = order[...] // count
    owned = jnp.where(owner == row, 1.0, 0.0)
    rank = first_of(count, owned)
    low_order = order[...].astype(F32).T
    tokens = lax.broadcasted_iota(jnp.int32, (count, count), 1).astype(F32)
    first = (row * count).astype(F32)
    sent = jnp.zeros((1, count), F32)
    pick = lax.broadcasted_iota(jnp.int32, (8, count), 0)
    for d in range(rows):
        match = jnp.where(low_order[:, d : d + 1] - first == tokens, 1.0, 0.0).astype(LOW)
        pair = jnp.where(pick == 0, rank[d : d + 1] * owned[d : d + 1], owned[d : d + 1])
        found = jnp.dot(pair.astype(LOW), match, preferred_element_type=F32)
        sent = sent + found[:1] + found[1:2] * (d * capacity)
    send_row[...] = sent.astype(jnp.int32)
    send_col[...] = jnp.broadcast_to(sent, (LANES, count)).T[:, :1].astype(jnp.int32)
    blocks = lax.broadcasted_iota(jnp.int32, (rows, count), 0)
    mine = jnp.sum(jnp.where(blocks == row, order[...], 0), axis=0, keepdims=True)
    source = mine // count
    came = jnp.where(source == lax.broadcasted_iota(jnp.int32, (LANES, count), 0), 1.0, 0.0)
    place = jnp.sum(first_of(count, came) * came, axis=0, keepdims=True)
    place = place + source.astype(F32) * capacity
    recv_row[...] = place.astype(jnp.int32)
    recv_col[...] = jnp.broadcast_to(place, (LANES, count)).T[:, :1].astype(jnp.int32)


def sequence_ids(lengths, count, axis):
    places = lax.broadcasted_iota(jnp.int32, (1, count) if axis else (count, 1), axis)
    end = jnp.zeros((1, 1), jnp.int32)
    ids = jnp.zeros(places.shape, jnp.int32)
    for j in range(lengths.shape[1]):
        end = end + lengths[:, j : j + 1]
        ids = ids + jnp.where(places >= end, 1, 0)
    return ids


def front_kernel(
    rows,
    cols,
    halves,
    need,
    flush,
    order,
    picks,
    lengths,
    tokens_ref,
    cot,
    w_qkv,
    w_attn,
    w_query,
    w_gate,
    w_mem,
    sub_keys,
    norm_one,
    norm_two,
    send_row,
    send_col,
    recv_row,
    recv_col,
    hidden_one,
    dealt,
    factor_one,
    weights_one,
    qkv,
    mixed,
    hidden_two,
    resid,
    factor_two,
    full_cot,
    weights_two,
    keys,
    queries,
    gate,
    grad_mixed,
    grad_memory,
    index,
    low_picks,
    weights,
    scores_of,
    full,
    gains,
    packed,
    got,
    packed_cot,
    got_cot,
    outgoing,
    incoming,
    mine,
    theirs,
    turned,
    sends,
    recvs,
):
    net = Net(rows, cols, sends, recvs)
    greeted = net.greet(range(1, rows), range(1, cols))
    count, width = tokens_ref.shape
    capacity = packed.shape[0] // rows
    depth = halves * QD
    need(w_qkv, w_attn)
    place_one = rows_of(weights_one, w_qkv.shape[0])
    place_one(net.row)[:, : 3 * width] = w_qkv[...].astype(LOW)
    place_one(net.row)[:, 3 * width :] = w_attn[...].T.astype(LOW)
    net.meet(greeted)
    gather_one = net.gather_start(place_one(net.row), place_one)
    need(order, tokens_ref)
    find_places(rows, net.row, order, send_row, send_col, recv_row, recv_col)
    pack_for_rows(net, packed, tokens_ref[...], send_row[...])
    copies = exchange_start(net, packed, got, capacity)
    need(norm_one, norm_two, cot, w_query, w_gate, w_mem, sub_keys, picks, lengths)
    own_gain = columns_of(gains, width)
    own_gain(net.col)[...] = jnp.broadcast_to(
        norm_one[...].astype(LOW).astype(F32), (8, width)
    )
    gain_spread = net.columns_start(own_gain)
    pack_for_rows(net, packed_cot, cot[...], send_row[...])
    cot_copies = exchange_start(net, packed_cot, got_cot, capacity)
    place_two = rows_of(weights_two, w_query.shape[0])
    place_two(net.row)[:, :depth] = w_query[...].astype(LOW)
    place_two(net.row)[:, depth : depth + width] = w_gate[...].astype(LOW)
    place_two(net.row)[:, depth + width :] = w_mem[...].T.astype(LOW)
    span = sub_keys.shape[1]
    place_keys = lambda at: keys.at[:, pl.ds(pl.multiple_of(at * span, span), span), :]
    place_keys(net.row)[...] = sub_keys[...].astype(LOW)
    wait_all(copies)
    own = columns_of(full, width)
    values = unpack(got, recv_col[...])
    own(net.col)[...] = values.astype(LOW)
    spread = net.columns_start(own)
    dealt[...] = values
    left_one = net.gather_pass(place_one, gather_one, False)
    gather_two = net.gather_start(place_two(net.row), place_two)
    gather_keys = net.gather_start(place_keys(net.row), place_keys)
    low_picks[...] = (picks[...] - 32768).astype(jnp.int16)
    head = net.col * halves // 2
    head_rows = pl.ds(pl.multiple_of(head * PICKS, PICKS), PICKS)
    halves_of = []
    for h in range(halves):
        even = (net.col * halves + h) % 2 == 0
        halves_of.append(jnp.where(even, picks[...] >> KEY_BITS, picks[...] & (NK - 1)))
        turned[...] = halves_of[h].astype(F32).T
        index[h * PICKS : (h + 1) * PICKS] = turned[head_rows, :].astype(jnp.int32)
    ids_col = sequence_ids(lengths[...], count, 0)
    ids_row = sequence_ids(lengths[...], count, 1)
    wait_all(spread)
    wait_all(gain_spread)
    values = full[...].astype(F32)
    scale = lax.rsqrt(jnp.mean(values * values, axis=1, keepdims=True) + EPS)
    hidden_one[...] = (values * scale * gains[:1]).astype(LOW)
    factor_one[...] = jnp.broadcast_to(scale, (count, LANES))
    flush(hidden_one, factor_one, dealt, index, low_picks, send_row, send_col, recv_row, recv_col)
    wait_all(left_one + net.gather_pass(place_one, gather_one, True))
    flush(weights_one)
    qkv[...] = jnp.dot(
        hidden_one[...], weights_one[:, : 3 * width], preferred_element_type=F32
    ).astype(LOW)
    for h in range(width // HD):
        (_, _, value), probs = attention_scores(qkv, h, ids_col, ids_row)
        mixed[:, h * HD : (h + 1) * HD] = jnp.dot(
            probs.astype(LOW), value, preferred_element_type=F32
        ).astype(LOW)
    flush(qkv, mixed)
    own_part, reduce = project_start(
        net, mixed[...], weights_one.at[:, 3 * width :], outgoing, incoming
    )
    values = dealt[...] + project_end(own_part, incoming, reduce)
    resid[...] = values
    left = net.gather_pass(place_two, gather_two, False)
    left += net.gather_pass(place_keys, gather_keys, False)
    square = share_sums(net, jnp.sum(values * values, axis=1, keepdims=True), mine, theirs)
    scale = lax.rsqrt(square / D + EPS)
    factor_two[...] = scale
    flush(resid, factor_two)
    own = columns_of(hidden_two, width)
    gain_two = norm_two[...].astype(LOW).astype(F32)
    own(net.col)[...] = (resid[...] * widen(scale, width) * gain_two).astype(LOW)
    spread = net.columns_start(own)
    wait_all(cot_copies)
    own_cot = columns_of(full_cot, width)
    own_cot(net.col)[...] = unpack(got_cot, recv_col[...]).astype(LOW)
    cot_spread = net.columns_start(own_cot)
    left += net.gather_pass(place_two, gather_two, True)
    left += net.gather_pass(place_keys, gather_keys, True)
    wait_all(spread)
    wait_all(left)
    flush(hidden_two, weights_two, keys)
    for h in range(halves):
        columns = slice(h * QD, (h + 1) * QD)
        queries[:, columns] = jnp.dot(
            hidden_two[...], weights_two[:, columns], preferred_element_type=F32
        ).astype(LOW)
        scores = lax.dot_general(
            queries[:, columns], keys[h], NT_DIMS, preferred_element_type=F32
        )
        low_index = halves_of[h] & (LANES - 1)
        first = jnp.take_along_axis(scores[:, :LANES], low_index, axis=1)
        second = jnp.take_along_axis(scores[:, LANES:], low_index, axis=1)
        turned[...] = jnp.where(halves_of[h] >= LANES, second, first).T
        first_row = (net.col * halves + h) * PICKS
        scores_of[pl.ds(pl.multiple_of(first_row, PICKS), PICKS), :] = turned[head_rows, :]
    own_scores = rows_of(scores_of, halves * PICKS)
    score_spread = net.columns_start(own_scores)
    open_gate = jnp.dot(
        hidden_two[...], weights_two[:, depth : depth + width], preferred_element_type=F32
    )
    gate[...] = open_gate
    wait_all(cot_spread)
    flush(full_cot, queries, gate)
    back = jnp.dot(full_cot[...], weights_two[:, depth + width :], preferred_element_type=F32)
    grad_mixed[...] = back
    grad_memory[...] = (back * (open_gate * jax.nn.sigmoid(open_gate))).astype(LOW)
    wait_all(score_spread)
    for m in range(MH):
        score = (
            scores_of[2 * m * PICKS : (2 * m + 1) * PICKS]
            + scores_of[(2 * m + 1) * PICKS : (2 * m + 2) * PICKS]
        )
        shifted = jnp.exp(score - jnp.max(score, axis=0, keepdims=True))
        weights[m * PICKS : (m + 1) * PICKS] = shifted / jnp.sum(shifted, axis=0, keepdims=True)
    net.drain()


def norm_grad(net, grad_hidden, values, scale, gain, mine, theirs):
    width = values.shape[1]
    scaled = grad_hidden * gain
    inner = share_sums(net, jnp.sum(scaled * values, axis=1, keepdims=True), mine, theirs)
    wide = widen(scale, width)
    grads = wide * scaled - values * (wide * wide * wide) * widen(inner, width) / D
    grad_gain = jnp.sum(grad_hidden * values * wide, axis=0, keepdims=True)
    return grads, grad_gain


def project_start(net, left, weights, outgoing, incoming):
    width = outgoing.shape[2]

    def block(col):
        rows = rows_of(weights, width)(col)[...]
        return lax.dot_general(left, rows, NT_DIMS, preferred_element_type=F32)

    copies = []
    for k in range(1, net.cols):
        outgoing[k - 1] = block(flip(net.col, k)).astype(LOW)
        copies.append(net.send(outgoing.at[k - 1], incoming.at[k - 1], col_k=k))
    return block(net.col), copies


def project_end(total, incoming, copies):
    for k, copy in enumerate(copies):
        copy.wait_recv()
        total = total + incoming[k].astype(F32)
    return total


def attention_scores(qkv, head, ids_col, ids_row):
    parts = [qkv[:, (3 * head + j) * HD : (3 * head + j + 1) * HD] for j in range(3)]
    scores = lax.dot_general(parts[0], parts[1], NT_DIMS, preferred_element_type=F32) * HD ** (
        -0.5
    )
    asks = lax.broadcasted_iota(jnp.int32, scores.shape, 0)
    offers = lax.broadcasted_iota(jnp.int32, scores.shape, 1)
    allowed = (ids_col == ids_row) & (asks >= offers)
    scores = jnp.where(allowed, scores, MASKED)
    shifted = jnp.exp(scores - jnp.max(scores, axis=1, keepdims=True))
    return parts, shifted / jnp.sum(shifted, axis=1, keepdims=True)


def spread_picks(halves, weights, dw, index, out):
    tokens = weights.shape[1]
    grad = weights * (dw - jnp.sum(weights * dw, axis=0, keepdims=True))
    block = 128
    places = lax.broadcasted_iota(jnp.int32, (NK, block), 0)
    for h in range(halves):
        for b in range(tokens // block):
            columns = slice(b * block, (b + 1) * block)
            total = jnp.zeros((NK, block), F32)
            for k in range(PICKS):
                row = index[h * PICKS + k : h * PICKS + k + 1, columns]
                total = total + jnp.where(places == row, grad[k : k + 1, columns], 0.0)
            out[columns, h * NK : (h + 1) * NK] = total.T.astype(LOW)


def back_kernel(
    rows,
    cols,
    halves,
    need,
    flush,
    share,
    dw,
    index,
    memory,
    gate,
    grad_mixed,
    queries,
    hidden_two,
    cot,
    weights_two,
    keys,
    resid,
    factor_two,
    gain_two,
    recv_row,
    send_col,
    qkv,
    mixed,
    lengths,
    hidden_one,
    weights_one,
    dealt,
    factor_one,
    gain_one,
    output,
    grad_tokens,
    own_qkv,
    own_attn,
    own_query,
    own_gate,
    own_mem,
    own_keys,
    gains,
    grad_sub,
    both,
    mixed_two,
    grad_mem,
    grad_two,
    grad_keys,
    grad_low,
    grad_resid,
    grad_qkv,
    grad_one,
    one_outgoing,
    one_incoming,
    res_outgoing,
    res_incoming,
    two_outgoing,
    two_incoming,
    mine,
    theirs,
    mine_one,
    theirs_one,
    packed,
    got,
    packed_one,
    got_one,
    across_two,
    two_out,
    two_in,
    across_keys,
    keys_out,
    keys_in,
    across_one,
    one_out,
    one_in,
    across_mem,
    mem_out,
    mem_in,
    my_gains,
    their_gains,
    sends,
    recvs,
):
    net = Net(rows, cols, sends, recvs)
    capacity = packed.shape[0] // rows
    width = resid.shape[1]
    depth = halves * QD
    greeted = net.greet(range(1, rows), range(1, cols))
    need(gate, grad_mixed, memory)
    open_gate, back, read = gate[...], grad_mixed[...], memory[...]
    sigmoid = jax.nn.sigmoid(open_gate)
    both[:, depth:] = (back * read * sigmoid * (1.0 + open_gate * (1.0 - sigmoid))).astype(LOW)
    mixed_two[...] = (read * open_gate * sigmoid).astype(LOW)
    need(weights_two)
    net.meet(greeted)
    own_res, reduce_res = project_start(
        net, mixed_two[...], weights_two.at[:, depth + width :], res_outgoing, res_incoming
    )
    need(cot)
    grad_mem[...] = jnp.dot(cot[...].T, mixed_two[...], preferred_element_type=F32)
    moved_mem, moved_two, moved_keys, moved_one = {}, {}, {}, {}
    view_mem = rows_of(grad_mem, own_query.shape[0])
    started_mem = net.scatter_start(view_mem, across_mem)
    pass_mem = (view_mem, across_mem, started_mem, mem_out, mem_in, moved_mem)
    need(share, dw, index, keys)
    head = net.col * halves // 2
    own_share = share[pl.ds(pl.multiple_of(head * PICKS, PICKS), PICKS), :]
    spread_picks(halves, own_share, dw[...], index, grad_sub)
    net.scatter_pass(*pass_mem, True)
    for h in range(halves):
        both[:, h * QD : (h + 1) * QD] = jnp.dot(
            grad_sub[:, h * NK : (h + 1) * NK], keys[h], preferred_element_type=F32
        ).astype(LOW)
    own_part, reduce_two = project_start(
        net, both[...], weights_two.at[:, : depth + width], two_outgoing, two_incoming
    )
    need(resid, recv_row)
    block = resid[...] + project_end(own_res, res_incoming, reduce_res)
    pack_for_rows(net, packed, block.astype(LOW), recv_row[...])
    copies = exchange_start(net, packed, got, capacity)
    need(hidden_two, queries)
    grad_two[...] = jnp.dot(hidden_two[...].T, both[...], preferred_element_type=F32)
    for h in range(halves):
        grad_keys[h] = jnp.dot(
            grad_sub[:, h * NK : (h + 1) * NK].T,
            queries[:, h * QD : (h + 1) * QD],
            preferred_element_type=F32,
        )
    view_two = rows_of(grad_two, own_query.shape[0])
    span = own_keys.shape[1]
    view_keys = lambda at: grad_keys.at[:, pl.ds(pl.multiple_of(at * span, span), span), :]
    started_two = net.scatter_start(view_two, across_two)
    started_keys = net.scatter_start(view_keys, across_keys)
    pass_two = (view_two, across_two, started_two, two_out, two_in, moved_two)
    pass_keys = (view_keys, across_keys, started_keys, keys_out, keys_in, moved_keys)
    net.scatter_pass(*pass_two, True)
    net.scatter_pass(*pass_keys, True)
    net.scatter_pass(*pass_mem, False)
    need(lengths)
    ids_col = sequence_ids(lengths[...], memory.shape[0], 0)
    ids_row = sequence_ids(lengths[...], memory.shape[0], 1)
    need(factor_two, gain_two)
    grad_hidden = project_end(own_part, two_incoming, reduce_two)
    grads, gain_two_sum = norm_grad(
        net, grad_hidden, resid[...], factor_two[...], gain_two[...].astype(LOW).astype(F32), mine, theirs
    )
    own_cot = columns_of(cot, width)(net.col)[...]
    grads = grads + own_cot.astype(F32)
    grad_resid[...] = grads
    own = columns_of(grad_low, width)
    own(net.col)[...] = grads.astype(LOW)
    spread = net.columns_start(own)
    wait_all(spread)
    net.scatter_pass(*pass_two, False)
    net.scatter_pass(*pass_keys, False)
    need(weights_one, qkv, hidden_one, mixed, send_col, dealt, factor_one, gain_one)
    grad_heads = jnp.dot(
        grad_low[...], weights_one[:, 3 * width :], preferred_element_type=F32
    ).astype(LOW)
    for head in range(width // HD):
        (query, key, value), probs = attention_scores(qkv, head, ids_col, ids_row)
        grad_out = grad_heads[:, head * HD : (head + 1) * HD]
        grad_prob = lax.dot_general(grad_out, value, NT_DIMS, preferred_element_type=F32)
        inner = jnp.sum(probs * grad_prob, axis=1, keepdims=True)
        grad_score = (probs * (grad_prob - inner)).astype(LOW)
        pieces = (
            jnp.dot(grad_score, key, preferred_element_type=F32) * HD ** (-0.5),
            jnp.dot(grad_score.T, query, preferred_element_type=F32) * HD ** (-0.5),
            jnp.dot(probs.astype(LOW).T, grad_out, preferred_element_type=F32),
        )
        for j in range(3):
            grad_qkv[:, (3 * head + j) * HD : (3 * head + j + 1) * HD] = pieces[j].astype(LOW)
    own_part, reduce_one = project_start(
        net, grad_qkv[...], weights_one.at[:, : 3 * width], one_outgoing, one_incoming
    )
    grad_one[:, : 3 * width] = jnp.dot(
        hidden_one[...].T, grad_qkv[...], preferred_element_type=F32
    )
    grad_one[:, 3 * width :] = jnp.dot(grad_low[...].T, mixed[...], preferred_element_type=F32)
    view_one = rows_of(grad_one, own_qkv.shape[0])
    started_one = net.scatter_start(view_one, across_one)
    pass_one = (view_one, across_one, started_one, one_out, one_in, moved_one)
    net.scatter_pass(*pass_one, True)
    grad_hidden = project_end(own_part, one_incoming, reduce_one)
    grads, gain_one_sum = norm_grad(
        net,
        grad_hidden,
        dealt[...],
        factor_one[...],
        gain_one[...].astype(LOW).astype(F32),
        mine_one,
        theirs_one,
    )
    grads = grads + grad_resid[...]
    pack_for_rows(net, packed_one, grads.astype(LOW), recv_row[...])
    last = exchange_start(net, packed_one, got_one, capacity)
    net.scatter_pass(*pass_one, False)
    places = lax.broadcasted_iota(jnp.int32, my_gains.shape, 0)
    my_gains[...] = jnp.where(places == 0, gain_one_sum, gain_two_sum)
    gain_copies = [net.send(my_gains, their_gains.at[k], row_k=k) for k in range(1, rows)]
    total = net.scatter_end(view_two, across_two, started_two, two_in, moved_two)
    own_query[...] = total[:, :depth]
    own_gate[...] = total[:, depth:]
    own_mem[...] = net.scatter_end(view_mem, across_mem, started_mem, mem_in, moved_mem).T
    own_keys[...] = net.scatter_end(view_keys, across_keys, started_keys, keys_in, moved_keys)
    wait_all(copies)
    output[...] = unpack(got, send_col[...])
    flush(output)
    total = net.scatter_end(view_one, across_one, started_one, one_in, moved_one)
    own_qkv[...] = total[:, : 3 * width]
    own_attn[...] = total[:, 3 * width :].T
    total = my_gains[...]
    for k, copy in enumerate(gain_copies):
        copy.wait_recv()
        total = total + their_gains[k + 1]
    gains[...] = total
    wait_all(last)
    grad_tokens[...] = unpack(got_one, send_col[...])
    net.drain()


def staged(kernel, rows, cols, sizes, ins, outs, *refs):
    given, results = refs[:ins], refs[ins : ins + outs]
    rest = refs[ins + outs :]
    twins, rest = rest[: ins + outs], rest[ins + outs :]
    sems, rest = rest[0], rest[1:]
    sources, targets = twins[:ins], twins[ins:]
    waited, left = set(), []

    def moving(i):
        return pltpu.make_async_copy(given[i], sources[i], sems.at[i])

    def need(*wanted):
        for ref in wanted:
            i = [j for j in range(ins) if sources[j] is ref][0]
            if i not in waited:
                moving(i).wait()
                waited.add(i)

    def flush(*done):
        for ref in done:
            i = [j for j in range(outs) if targets[j] is ref][0]
            copy = pltpu.make_async_copy(targets[i], results[i], sems.at[ins + i])
            copy.start()
            left.append((i, copy))

    for i in range(ins):
        moving(i).start()
    kernel(rows, cols, *sizes, need, flush, *sources, *targets, *rest)
    assert len(waited) == ins
    flush(*[targets[i] for i in range(outs) if i not in [j for j, _ in left]])
    for _, copy in left:
        copy.wait()


def remote_call(kernel, rows, cols, number, copies, ins, outs, scratch, *sizes):
    twins = [(x.shape, x.dtype) for x in ins] + outs
    anywhere = pl.BlockSpec(memory_space=pl.ANY)
    return pl.pallas_call(
        functools.partial(staged, kernel, rows, cols, sizes, len(ins), len(outs)),
        out_shape=[jax.ShapeDtypeStruct(shape, dtype) for shape, dtype in outs],
        in_specs=[anywhere] * len(ins),
        out_specs=[anywhere] * len(outs),
        scratch_shapes=[pltpu.VMEM(shape, dtype) for shape, dtype in twins]
        + [pltpu.SemaphoreType.DMA((len(twins),))]
        + [pltpu.VMEM(shape, dtype) for shape, dtype in scratch]
        + [pltpu.SemaphoreType.DMA((copies,)), pltpu.SemaphoreType.DMA((copies,))],
        compiler_params=pltpu.CompilerParams(
            collective_id=number, has_side_effects=True, vmem_limit_bytes=VMEM_BYTES
        ),
    )(*ins)


def memory_kernel(
    rows,
    cols,
    own_weights,
    own_picks,
    own_grads,
    table_f32,
    memory,
    dw,
    gacc_out,
    gacc,
    table,
    stage,
    picks_of,
    grads_of,
    low_of,
    dense,
    hi_ref,
    lo_ref,
    wide_ref,
    found_ref,
    mem_all,
    mem_twin,
    mem_out,
    mem_in,
    dw_all,
    dw_twin,
    dw_out,
    dw_in,
    dw_cols,
    stage_sems,
    sends,
    recvs,
):
    net = Net(rows, cols, sends, recvs)
    half = rows // 2
    tok_block = own_picks.shape[0]
    span_rows, width = table.shape
    spans = span_rows // LANES
    pitch = spans + 8
    iters = 4
    per_tok = tok_block // iters
    per_span = spans // iters

    grads_at = rows_of(grads_of, tok_block)
    picks_at = rows_of(picks_of, tok_block)
    low_at = lambda index: low_of.at[index]
    views = (grads_at, picks_at, low_at)
    first_pass = 3 * half
    first_twin = first_pass + 3 * half
    first_out = first_twin + 2 * half
    first_col = first_out + 2 * half

    def gather(a, j):
        mine = views[a](net.row)
        return net.copy(mine, mine, 3 * j + a, row_k=2 * j if j else 1)

    def passing(a, j):
        there = views[a](flip(net.row, 2 * j))
        return net.copy(there, there, first_pass + 3 * j + a, row_k=1)

    def twin(a, j):
        src, dst = ((mem_all, mem_twin), (dw_all, dw_twin))[a]
        return net.copy(src.at[2 * j + 1], dst.at[j], first_twin + 2 * j + a, row_k=1)

    def outward(a, j):
        src, dst = ((mem_out, mem_in), (dw_out, dw_in))[a]
        return net.copy(src.at[j - 1], dst.at[j - 1], first_out + 2 * j + a, row_k=2 * j)

    head = lambda col: pl.ds(pl.multiple_of(col * MH // cols * PICKS, PICKS), PICKS)

    def dw_copy(k):
        return net.copy(
            dw_all.at[0, head(flip(net.col, k)), :],
            dw_cols.at[k - 1],
            first_col + k,
            col_k=k,
        )

    stage_rows = stage.shape[1]

    def stage_copy(i):
        source = table_f32.at[pl.ds(i * stage_rows, stage_rows), :]
        return pltpu.make_async_copy(source, stage.at[i % 2], stage_sems.at[i % 2])

    stage_copy(0).start()
    greeted = net.greet([1] + [2 * j for j in range(1, half)], range(1, cols))
    for i in range(span_rows // stage_rows):
        if (i + 1) * stage_rows < span_rows:
            stage_copy(i + 1).start()
        stage_copy(i).wait()
        table[i * stage_rows : (i + 1) * stage_rows, :] = stage[i % 2].astype(LOW)
    net.meet(greeted)
    grads_at(net.row)[...] = own_grads[...]
    picks_at(net.row)[...] = own_picks[...]
    low_at(net.row)[...] = own_weights[...].astype(LOW)
    for j in range(2):
        for a in range(3):
            gather(a, j).start()
    gacc[...] = jnp.zeros_like(gacc)
    mem_all[...] = jnp.zeros_like(mem_all)

    def one_block(step, _):
        k = jnp.where(step == 0, 0, jnp.where(step == rows - 1, 1, step + 1))
        there = cross(net.row, k, rows)
        for j in range(1, half):

            @pl.when(step == 2 * j - 1)
            def _():
                for a in range(3):
                    gather(a, j).wait_recv()
                    passing(a, j).start()
                if j + 1 < half:
                    for a in range(3):
                        gather(a, j + 1).start()

            @pl.when(step == 2 * j)
            def _():
                for a in range(3):
                    passing(a, j).wait_recv()

        @pl.when(step == rows - 1)
        def _():
            for a in range(3):
                gather(a, 0).wait_recv()

        picks = picks_at(there)[...].astype(jnp.int32) + 32768
        lo_int = picks & (LANES - 1)
        hi_ref[...] = ((picks >> LANE_BITS) - net.row * spans).astype(F32)
        lo_ref[...] = lo_int.astype(F32)
        wide_ref[...] = low_of[there].astype(F32).T
        places_lo = lax.broadcasted_iota(jnp.int32, (LANES, LANES), 0).astype(F32).astype(LOW)
        places_hi = lax.broadcasted_iota(jnp.int32, (spans, LANES), 0).astype(F32).astype(LOW)
        ones = jnp.ones((LANES, LANES), LOW)
        zeros = jnp.zeros((LANES, LANES), LOW)
        blank = jnp.zeros((spans, LANES), LOW)
        grads = grads_at(there)[...]
        grads_t = grads.T
        found_ref[...] = jnp.zeros_like(found_ref)
        hi_all = hi_ref[...]

        def token_pair(first):
            rights, lefts = [], []
            for token in (first, first + 1):
                lo_row = jnp.broadcast_to(lo_ref[pl.ds(token, 1), :], (LANES, LANES)).astype(LOW)
                hi_row = jnp.broadcast_to(hi_ref[pl.ds(token, 1), :], (spans, LANES)).astype(LOW)
                w_row = jnp.broadcast_to(wide_ref[pl.ds(token, 1), :], (spans, LANES)).astype(LOW)
                rights.append(jnp.where(lo_row == places_lo, ones, zeros))
                lefts.append(jnp.where(hi_row == places_hi, w_row, blank))
            right = jnp.concatenate(rights, axis=1)
            left = jnp.concatenate(
                [
                    jnp.concatenate([lefts[0], blank], axis=1),
                    jnp.concatenate([blank, lefts[1]], axis=1),
                ],
                axis=0,
            )
            both = lax.dot_general(left, right, NT_DIMS, preferred_element_type=F32)
            for j in range(2):
                dense[pl.ds(pl.multiple_of((first + j) * pitch, 8), spans), :] = both[
                    j * spans : (j + 1) * spans
                ]

        def look(found, first, number, between=None):
            span = pl.ds(pl.multiple_of(first * LANES, LANES), number * LANES)
            products = lax.dot_general(
                grads, table[span, :], NT_DIMS, preferred_element_type=F32
            )
            for j in range(number):
                picked = jnp.take_along_axis(
                    products[:, LANES * j : LANES * (j + 1)], lo_int, axis=1
                )
                found = jnp.where(hi_all == (first + j).astype(F32), picked, found)
                if between:
                    between(j)
            return found

        early = per_span // 2
        late = per_span - early

        def build(it, _):
            for j in range(1, half):

                @pl.when((it == 1) & (step == 2 * j + 1))
                def _():
                    twin(0, j).wait_recv()
                    twin(1, j).wait_recv()
                    mem_out[j - 1] = (mem_all[2 * j] + mem_twin[j]).astype(LOW)
                    outward(0, j).start()
                    dw_out[j - 1] = (dw_all[2 * j] + dw_twin[j]).astype(LOW)
                    outward(1, j).start()

            pairs = per_tok // 2 // early

            def some_pairs(j):
                for u in range(pairs):
                    token_pair(it * per_tok + (j * pairs + u) * 2)

            found_ref[...] = look(found_ref[...], it * early, early, some_pairs)
            return 0

        lax.fori_loop(0, iters, build, 0)
        parts = min(4, late)

        def multiply(it, _):
            found, total = found_ref[...], None
            for c in range(parts):
                low, high = c * late // parts, (c + 1) * late // parts
                found = look(found, early * iters + it * late + low, high - low)
                low, high = c * per_span // parts, (c + 1) * per_span // parts
                first = it * per_span + low
                chosen = jnp.concatenate(
                    [
                        dense[pl.ds(first + j, tok_block, stride=pitch), :].astype(LOW)
                        for j in range(high - low)
                    ],
                    axis=1,
                )
                span = pl.ds(pl.multiple_of(first * LANES, LANES), (high - low) * LANES)
                gacc[:, span] += jnp.dot(grads_t, chosen, preferred_element_type=F32)
                read = jnp.dot(chosen, table[span, :], preferred_element_type=F32)
                total = read if total is None else total + read
            mem_all[k] += total
            found_ref[...] = found
            return 0

        lax.fori_loop(0, iters, multiply, 0)
        dw_all[k] = found_ref[...].T
        for j in range(half):

            @pl.when(step == (2 * j if j else rows - 1))
            def _():
                twin(0, j).start()
                twin(1, j).start()

        return 0

    lax.fori_loop(0, rows, one_block, 0)
    leaving = pltpu.make_async_copy(gacc, gacc_out, stage_sems.at[2])
    leaving.start()
    twin(1, 0).wait_recv()
    total = dw_all[0] + dw_twin[0]
    for j in range(1, half):
        outward(1, j).wait_recv()
        total = total + dw_in[j - 1].astype(F32)
    dw_all[0] = total
    for k in range(1, cols):
        dw_copy(k).start()
    twin(0, 0).wait_recv()
    total = mem_all[0] + mem_twin[0]
    for j in range(1, half):
        outward(0, j).wait_recv()
        total = total + mem_in[j - 1].astype(F32)
    memory[...] = total
    total = dw_all[0, head(net.col), :]
    for k in range(1, cols):
        dw_copy(k).wait_recv()
        total = total + dw_cols[k - 1]
    dw[...] = total
    for k in range(1, cols):
        dw_copy(k).wait_send()
    for j in range(half):
        for a in range(3):
            gather(a, j).wait_send()
            if j:
                passing(a, j).wait_send()
        for a in range(2):
            twin(a, j).wait_send()
            if j:
                outward(a, j).wait_send()
    leaving.wait()


def finish_kernel(others, source, *refs):
    given, out, results = refs[:others], refs[others], refs[others + 1 :]

    @pl.when(pl.program_id(0) == 0)
    def _():
        for i in range(others):
            results[i][...] = given[i][...]

    out[...] = source[...].T


def finish_call(table, others):
    width, span_rows = table.shape
    block = min(4096, span_rows)
    whole = [
        pl.BlockSpec(x.shape, lambda i, rank=x.ndim: (0,) * rank, pipeline_mode=pl.Buffered(1))
        for x in others
    ]
    return pl.pallas_call(
        functools.partial(finish_kernel, len(others)),
        grid=(span_rows // block,),
        in_specs=[pl.BlockSpec((width, block), lambda i: (0, i))] + whole,
        out_specs=[pl.BlockSpec((block, width), lambda i: (i, 0))] + whole,
        out_shape=[jax.ShapeDtypeStruct((span_rows, width), F32)]
        + [jax.ShapeDtypeStruct(x.shape, x.dtype) for x in others],
        compiler_params=pltpu.CompilerParams(vmem_limit_bytes=VMEM_BYTES),
    )(table, *others)


def memory_call(rows, cols, number, weights, picks, grads, table):
    tokens, count = picks.shape
    span_rows, width = table.shape
    half = rows // 2
    copies = 10 * half + cols
    vmem = pltpu.VMEM
    return pl.pallas_call(
        functools.partial(memory_kernel, rows, cols),
        in_specs=[VMEM_SPEC, VMEM_SPEC, VMEM_SPEC, pl.BlockSpec(memory_space=pl.ANY)],
        out_specs=[VMEM_SPEC, VMEM_SPEC, pl.BlockSpec(memory_space=pl.ANY)],
        out_shape=[
            jax.ShapeDtypeStruct((tokens, width), F32),
            jax.ShapeDtypeStruct((PICKS, tokens), F32),
            jax.ShapeDtypeStruct((width, span_rows), F32),
        ],
        scratch_shapes=[
            vmem((width, span_rows), F32),
            vmem((span_rows, width), LOW),
            vmem((2, 1024, width), F32),
            vmem((rows * tokens, count), jnp.int16),
            vmem((rows * tokens, width), LOW),
            vmem((rows, count, tokens), LOW),
            vmem((tokens * (span_rows // LANES + 8), LANES), F32),
            vmem((tokens, count), F32),
            vmem((tokens, count), F32),
            vmem((tokens, count), F32),
            vmem((tokens, count), F32),
            vmem((rows, tokens, width), F32),
            vmem((half, tokens, width), F32),
            vmem((half - 1, tokens, width), LOW),
            vmem((half - 1, tokens, width), LOW),
            vmem((rows, count, tokens), F32),
            vmem((half, count, tokens), F32),
            vmem((half - 1, count, tokens), LOW),
            vmem((half - 1, count, tokens), LOW),
            vmem((cols - 1, PICKS, tokens), F32),
            pltpu.SemaphoreType.DMA((3,)),
            pltpu.SemaphoreType.DMA((copies,)),
            pltpu.SemaphoreType.DMA((copies,)),
        ],
        compiler_params=pltpu.CompilerParams(
            collective_id=number, has_side_effects=True, vmem_limit_bytes=63 * 2**20
        ),
    )(weights, picks, grads, table)


def per_device(
    tokens,
    cotangent,
    deal_order,
    seq_lengths,
    value_picks,
    norm1_gain,
    w_qkv,
    w_attn_out,
    norm2_gain,
    w_query,
    sub_keys,
    value_table,
    w_gate,
    w_mem_out,
):
    rows, cols = lax.axis_size("row"), lax.axis_size("col")
    row_index = lax.axis_index("row")
    count, width = tokens.shape
    slots = 2 * count
    half = rows // 2
    halves = sub_keys.shape[0]
    depth = halves * QD
    span_one, span_two = 4 * width, depth + 2 * width
    shard_rows = w_qkv.shape[0]
    flat_picks = value_picks.reshape(count, MH * PICKS)
    gain_one, gain_two = norm1_gain[None, :], norm2_gain[None, :]
    swap = [((slots, width), LOW), ((slots, width), LOW)]
    sums = [((8, count), F32), ((cols, 8, count), F32)]
    moving = ((cols - 1, count, width), LOW)
    (
        send_row,
        send_col,
        recv_row,
        recv_col,
        hidden_one,
        dealt,
        factor_one,
        weights_one,
        qkv,
        mixed,
        hidden_two,
        resid,
        factor_two,
        full_cot,
        weights_two,
        keys,
        queries,
        gate,
        grad_mixed,
        grad_memory,
        index,
        low_picks,
        pick_weights,
    ) = remote_call(
        front_kernel,
        rows,
        cols,
        0,
        7 * (cols - 1) + 5 * (rows - 1),
        [
            deal_order.reshape(rows, count),
            flat_picks,
            seq_lengths,
            tokens,
            cotangent,
            w_qkv,
            w_attn_out,
            w_query,
            w_gate,
            w_mem_out,
            sub_keys,
            gain_one,
            gain_two,
        ],
        [
            ((1, count), jnp.int32),
            ((count, 1), jnp.int32),
            ((1, count), jnp.int32),
            ((count, 1), jnp.int32),
            ((count, D), LOW),
            ((count, width), F32),
            ((count, LANES), F32),
            ((D, span_one), LOW),
            ((count, 3 * width), LOW),
            ((count, width), LOW),
            ((count, D), LOW),
            ((count, width), F32),
            ((count, LANES), F32),
            ((count, D), LOW),
            ((D, span_two), LOW),
            ((halves, NK, QD), LOW),
            ((count, depth), LOW),
            ((count, width), F32),
            ((count, width), F32),
            ((count, width), LOW),
            ((halves * PICKS, count), jnp.int32),
            ((count, MH * PICKS), jnp.int16),
            ((MH * PICKS, count), F32),
        ],
        [((2 * MH * PICKS, count), F32), ((count, D), LOW), ((8, D), F32), *swap, *swap, moving, moving, *sums]
        + [((MH * PICKS, count), F32)],
        halves,
    )
    memory, grad_pick, grad_table = memory_call(
        rows, cols, 1, pick_weights, low_picks, grad_memory, value_table
    )
    block = ((count, width), F32)
    scattered = [
        [((half,) + shape, F32), ((half - 1,) + shape, LOW), ((half - 1,) + shape, LOW)]
        for shape in (
            (shard_rows, depth + width),
            sub_keys.shape,
            (shard_rows, span_one),
            (shard_rows, width),
        )
    ]
    output, grad_tokens, own_qkv, own_attn, own_query, own_gate, own_mem, own_keys, gains = remote_call(
        back_kernel,
        rows,
        cols,
        2,
        6 * (cols - 1) + 3 * (rows - 1) + 4 * (half + half - 1),
        [
            pick_weights,
            grad_pick,
            index,
            memory,
            gate,
            grad_mixed,
            queries,
            hidden_two,
            full_cot,
            weights_two,
            keys,
            resid,
            factor_two,
            gain_two,
            recv_row,
            send_col,
            qkv,
            mixed,
            seq_lengths,
            hidden_one,
            weights_one,
            dealt,
            factor_one,
            gain_one,
        ],
        [
            block,
            block,
            (w_qkv.shape, F32),
            (w_attn_out.shape, F32),
            (w_query.shape, F32),
            (w_gate.shape, F32),
            (w_mem_out.shape, F32),
            (sub_keys.shape, F32),
            ((8, width), F32),
        ],
        [
            ((count, halves * NK), LOW),
            ((count, depth + width), LOW),
            ((count, width), LOW),
            ((D, width), F32),
            ((D, depth + width), F32),
            ((halves, NK, QD), F32),
            ((count, D), LOW),
            block,
            ((count, 3 * width), LOW),
            ((D, span_one), F32),
            *[moving] * 6,
            *sums,
            *sums,
            *swap,
            *swap,
            *scattered[0],
            *scattered[1],
            *scattered[2],
            *scattered[3],
            ((8, width), F32),
            ((rows, 8, width), F32),
        ],
        halves,
    )
    gain_span = width // rows
    gain_one_grad = lax.dynamic_slice_in_dim(gains[0], row_index * gain_span, gain_span)
    gain_two_grad = lax.dynamic_slice_in_dim(gains[1], row_index * gain_span, gain_span)
    others = (
        output,
        grad_tokens,
        own_qkv,
        own_attn,
        own_query,
        own_keys,
        own_gate,
        own_mem,
    )
    turned, *others = finish_call(grad_table, others)
    output, grad_tokens, own_qkv, own_attn, own_query, own_keys, own_gate, own_mem = others
    return (
        output,
        grad_tokens,
        gain_one_grad,
        own_qkv,
        own_attn,
        gain_two_grad,
        own_query,
        own_keys,
        turned,
        own_gate,
        own_mem,
    )


def solution(mesh):
    return jax.shard_map(
        per_device,
        mesh=mesh,
        in_specs=(
            P("row", "col"),
            P("row", "col"),
            P(),
            P("row", None),
            P("row", None, None),
            P("col"),
            P("row", "col"),
            P("col", "row"),
            P("col"),
            P("row", "col"),
            P("col", "row", None),
            P("row", "col"),
            P("row", "col"),
            P("col", "row"),
        ),
        out_specs=(
            P("row", "col"),
            P("row", "col"),
            P(("col", "row")),
            P("row", "col"),
            P("col", "row"),
            P(("col", "row")),
            P("row", "col"),
            P("col", "row", None),
            P("row", "col"),
            P("row", "col"),
            P("col", "row"),
        ),
        check_vma=False,
    )
```

```python
import functools

import jax
import jax.numpy as jnp
from jax import lax
from jax.experimental import pallas as pl
from jax.experimental.pallas import tpu as pltpu
from jax.sharding import PartitionSpec as P

D = 1024
HD = 64
MH = 4
QD = 512
NK = 256
PICKS = 32
LANES = 128
LANE_BITS = LANES.bit_length() - 1
KEY_BITS = NK.bit_length() - 1
EPS = 1e-05
MASKED = -1e30
F32 = jnp.float32
LOW = jnp.bfloat16
MESH = pl.DeviceIdType.MESH
NT_DIMS = (((1,), (1,)), ((), ()))
VMEM_SPEC = pl.BlockSpec(memory_space=pltpu.VMEM)
VMEM_BYTES = 60 * 2**20


def flip(index, mask):
    bit = 1
    while bit <= mask:
        if mask & bit:
            index = index + bit - 2 * bit * (index // bit % 2)
        bit *= 2
    return index


def cross(index, mask, size):
    total, bit = 0, 1
    while bit < size:
        a, b = index // bit % 2, mask // bit % 2
        total = total + bit * (a + b - 2 * a * b)
        bit *= 2
    return total


class Net:
    def __init__(self, rows, cols, sends, recvs):
        self.rows, self.cols = rows, cols
        self.row, self.col = lax.axis_index("row"), lax.axis_index("col")
        self.sends, self.recvs, self.used = sends, recvs, 0
        self.pending = []

    def place(self, row_k, col_k):
        return (flip(self.row, row_k), flip(self.col, col_k))

    def greet(self, row_ks, col_ks):
        barrier = pltpu.get_barrier_semaphore()
        places = [self.place(k, 0) for k in row_ks] + [self.place(0, k) for k in col_ks]
        for place in places:
            pl.semaphore_signal(barrier, inc=1, device_id=place, device_id_type=MESH)
        return len(places)

    def meet(self, greeted):
        pl.semaphore_wait(pltpu.get_barrier_semaphore(), greeted)

    def copy(self, src, dst, number, row_k=0, col_k=0):
        assert number < self.sends.shape[0]
        return pltpu.make_async_remote_copy(
            src_ref=src,
            dst_ref=dst,
            send_sem=self.sends.at[number],
            recv_sem=self.recvs.at[number],
            device_id=self.place(row_k, col_k),
            device_id_type=MESH,
        )

    def send(self, src, dst, row_k=0, col_k=0):
        copy = self.copy(src, dst, self.used, row_k, col_k)
        copy.start()
        self.used += 1
        self.pending.append(copy)
        return copy

    def drain(self):
        for copy in self.pending:
            copy.wait_send()

    def gather_start(self, src, view):
        sent = {b: self.send(src, view(self.row), row_k=2 * b) for b in reversed(self.bits())}
        return sent, self.send(src, view(self.row), row_k=1)

    def gather_pass(self, view, started, near):
        sent, sibling = started
        passed = [sibling] if near else []
        masks = [m for m in range(1, self.rows // 2) if (m % 2 == 1) == near]
        for m in sorted(masks, key=lambda m: (-(m & -m), m.bit_count())):
            sent[m].wait_recv()
            block = view(flip(self.row, 2 * m))
            for b in self.bits():
                if b < (m & -m):
                    sent[m ^ b] = self.send(block, block, row_k=2 * b)
            passed.append(self.send(block, block, row_k=1))
        return passed

    def bits(self):
        return [1 << i for i in range((self.rows // 2 - 1).bit_length())]

    def scatter_start(self, view, across):
        twin = flip(self.row, 1)
        return [
            self.send(view(flip(twin, 2 * j)), across.at[j], row_k=1)
            for j in range(self.rows // 2)
        ]

    def scatter_pass(self, view, across, started, outgoing, incoming, moved, near):
        masks = [m for m in range(1, self.rows // 2) if (m % 2 == 1) == near]
        for m in sorted(masks, key=lambda m: ((m & -m), -m.bit_count())):
            started[m].wait_recv()
            block = view(flip(self.row, 2 * m))[...] + across[m]
            for b in self.bits():
                if b < (m & -m):
                    moved[m ^ b].wait_recv()
                    block = block + incoming[(m ^ b) - 1].astype(F32)
            outgoing[m - 1] = block.astype(outgoing.dtype)
            moved[m] = self.send(outgoing.at[m - 1], incoming.at[m - 1], row_k=2 * (m & -m))
        return moved

    def scatter_end(self, view, across, started, incoming, moved):
        started[0].wait_recv()
        total = view(self.row)[...] + across[0]
        for b in self.bits():
            moved[b].wait_recv()
            total = total + incoming[b - 1].astype(F32)
        return total

    def columns_start(self, view):
        return [self.send(view(self.col), view(self.col), col_k=k) for k in range(1, self.cols)]


def wait_all(copies):
    for copy in copies:
        copy.wait_recv()


def rows_of(ref, count):
    return lambda index: ref.at[pl.ds(pl.multiple_of(index * count, count), count), :]


def columns_of(ref, count):
    return lambda index: ref.at[:, pl.ds(pl.multiple_of(index * count, count), count)]


def one_hot_rows(positions, slots):
    places = lax.broadcasted_iota(jnp.int32, (positions.shape[0], slots), 1)
    return jnp.where(positions == places, 1.0, 0.0).astype(LOW)


def one_hot_columns(positions, slots):
    places = lax.broadcasted_iota(jnp.int32, (slots, positions.shape[1]), 0)
    return jnp.where(positions == places, 1.0, 0.0).astype(LOW)


def pack_for_rows(net, packed, values, positions):
    slots = packed.shape[0]
    packed[...] = jnp.dot(
        one_hot_columns(positions, slots), values, preferred_element_type=F32
    ).astype(LOW)


def exchange_start(net, packed, got, capacity):
    mine = rows_of(got, capacity)
    theirs = rows_of(packed, capacity)
    copies = [
        net.send(theirs(flip(net.row, k)), mine(net.row), row_k=k) for k in range(1, net.rows)
    ]
    mine(net.row)[...] = theirs(net.row)[...]
    return copies


def unpack(got, positions):
    return jnp.dot(
        one_hot_rows(positions, got.shape[0]), got[...], preferred_element_type=F32
    )


def share_sums(net, sums, mine, theirs):
    tokens = sums.shape[0]
    mine[...] = jnp.broadcast_to(sums, (tokens, LANES)).T[:8]
    copies = [net.send(mine, theirs.at[k], col_k=k) for k in range(1, net.cols)]
    wait_all(copies)
    total = mine[...]
    for k in range(1, net.cols):
        total = total + theirs[k]
    return jnp.broadcast_to(total[:1], (LANES, tokens)).T


def widen(lanes, width):
    return jnp.concatenate([lanes] * (width // LANES), axis=1)


def first_of(size, mask):
    earlier = lax.broadcasted_iota(jnp.int32, (size, size), 0)
    later = lax.broadcasted_iota(jnp.int32, (size, size), 1)
    triangle = jnp.where(earlier < later, 1.0, 0.0).astype(LOW)
    return jnp.dot(mask.astype(LOW), triangle, preferred_element_type=F32)


def find_places(rows, row, order, send_row, send_col, recv_row, recv_col):
    count = order.shape[1]
    capacity = 2 * count // rows
    owner = order // count
    owned = jnp.where(owner == row, 1.0, 0.0)
    rank = first_of(count, owned)
    low_order = order.astype(F32).T
    tokens = lax.broadcasted_iota(jnp.int32, (count, count), 1).astype(F32)
    first = (row * count).astype(F32)
    sent = jnp.zeros((1, count), F32)
    pick = lax.broadcasted_iota(jnp.int32, (8, count), 0)
    for d in range(rows):
        match = jnp.where(low_order[:, d : d + 1] - first == tokens, 1.0, 0.0).astype(LOW)
        pair = jnp.where(pick == 0, rank[d : d + 1] * owned[d : d + 1], owned[d : d + 1])
        found = jnp.dot(pair.astype(LOW), match, preferred_element_type=F32)
        sent = sent + found[:1] + found[1:2] * (d * capacity)
    send_row[...] = sent.astype(jnp.int32)
    send_col[...] = jnp.broadcast_to(sent, (LANES, count)).T[:, :1].astype(jnp.int32)
    blocks = lax.broadcasted_iota(jnp.int32, (rows, count), 0)
    mine = jnp.sum(jnp.where(blocks == row, order, 0), axis=0, keepdims=True)
    source = mine // count
    came = jnp.where(source == lax.broadcasted_iota(jnp.int32, (LANES, count), 0), 1.0, 0.0)
    place = jnp.sum(first_of(count, came) * came, axis=0, keepdims=True)
    place = place + source.astype(F32) * capacity
    recv_row[...] = place.astype(jnp.int32)
    recv_col[...] = jnp.broadcast_to(place, (LANES, count)).T[:, :1].astype(jnp.int32)


def sequence_ids(lengths, count, axis):
    places = lax.broadcasted_iota(jnp.int32, (1, count) if axis else (count, 1), axis)
    end = jnp.zeros((1, 1), jnp.int32)
    ids = jnp.zeros(places.shape, jnp.int32)
    for j in range(lengths.shape[1]):
        end = end + lengths[:, j : j + 1]
        ids = ids + jnp.where(places >= end, 1, 0)
    return ids


def front_kernel(
    rows,
    cols,
    halves,
    need,
    flush,
    order,
    picks,
    lengths,
    tokens_ref,
    cot,
    w_qkv,
    w_attn,
    w_query,
    w_gate,
    w_mem,
    sub_keys,
    norm_one,
    norm_two,
    send_row,
    send_col,
    recv_row,
    recv_col,
    hidden_one,
    dealt,
    factor_one,
    weights_one,
    qkv,
    mixed,
    hidden_two,
    resid,
    factor_two,
    full_cot,
    weights_two,
    keys,
    queries,
    gate,
    grad_mixed,
    grad_memory,
    index,
    low_picks,
    weights,
    scores_of,
    full,
    gains,
    packed,
    got,
    packed_cot,
    got_cot,
    outgoing,
    incoming,
    mine,
    theirs,
    turned,
    sends,
    recvs,
):
    net = Net(rows, cols, sends, recvs)
    greeted = net.greet(range(1, rows), range(1, cols))
    count, width = tokens_ref.shape
    capacity = packed.shape[0] // rows
    depth = halves * QD
    need(w_qkv, w_attn)
    place_one = rows_of(weights_one, w_qkv.shape[0])
    place_one(net.row)[:, : 3 * width] = w_qkv[...].astype(LOW)
    place_one(net.row)[:, 3 * width :] = w_attn[...].T.astype(LOW)
    net.meet(greeted)
    gather_one = net.gather_start(place_one(net.row), place_one)
    need(order, tokens_ref)
    by_block = jnp.concatenate([order[:, d * count : (d + 1) * count] for d in range(rows)], axis=0)
    find_places(rows, net.row, by_block, send_row, send_col, recv_row, recv_col)
    pack_for_rows(net, packed, tokens_ref[...], send_row[...])
    copies = exchange_start(net, packed, got, capacity)
    need(norm_one, norm_two, cot, w_query, w_gate, w_mem, sub_keys, picks, lengths)
    own_gain = columns_of(gains, width)
    own_gain(net.col)[...] = jnp.broadcast_to(
        norm_one[...].astype(LOW).astype(F32), (8, width)
    )
    gain_spread = net.columns_start(own_gain)
    pack_for_rows(net, packed_cot, cot[...], send_row[...])
    cot_copies = exchange_start(net, packed_cot, got_cot, capacity)
    place_two = rows_of(weights_two, w_query.shape[0])
    place_two(net.row)[:, :depth] = w_query[...].astype(LOW)
    place_two(net.row)[:, depth : depth + width] = w_gate[...].astype(LOW)
    place_two(net.row)[:, depth + width :] = w_mem[...].T.astype(LOW)
    span = sub_keys.shape[1]
    place_keys = lambda at: keys.at[:, pl.ds(pl.multiple_of(at * span, span), span), :]
    place_keys(net.row)[...] = sub_keys[...].astype(LOW)
    wait_all(copies)
    own = columns_of(full, width)
    values = unpack(got, recv_col[...])
    own(net.col)[...] = values.astype(LOW)
    spread = net.columns_start(own)
    dealt[...] = values
    left_one = net.gather_pass(place_one, gather_one, False)
    gather_two = net.gather_start(place_two(net.row), place_two)
    gather_keys = net.gather_start(place_keys(net.row), place_keys)
    low_picks[...] = (picks[...] - 32768).astype(jnp.int16)
    head = net.col * halves // 2
    head_rows = pl.ds(pl.multiple_of(head * PICKS, PICKS), PICKS)
    halves_of = []
    for h in range(halves):
        even = (net.col * halves + h) % 2 == 0
        halves_of.append(jnp.where(even, picks[...] >> KEY_BITS, picks[...] & (NK - 1)))
        turned[...] = halves_of[h].astype(F32).T
        index[h * PICKS : (h + 1) * PICKS] = turned[head_rows, :].astype(jnp.int32)
    ids_col = sequence_ids(lengths[...], count, 0)
    ids_row = sequence_ids(lengths[...], count, 1)
    wait_all(spread)
    wait_all(gain_spread)
    values = full[...].astype(F32)
    scale = lax.rsqrt(jnp.mean(values * values, axis=1, keepdims=True) + EPS)
    hidden_one[...] = (values * scale * gains[:1]).astype(LOW)
    factor_one[...] = jnp.broadcast_to(scale, (count, LANES))
    flush(hidden_one, factor_one, dealt, index, low_picks, send_row, send_col, recv_row, recv_col)
    wait_all(left_one + net.gather_pass(place_one, gather_one, True))
    flush(weights_one)
    qkv[...] = jnp.dot(
        hidden_one[...], weights_one[:, : 3 * width], preferred_element_type=F32
    ).astype(LOW)
    parts, sent = two_parts(count), []
    for tokens in parts:
        for h in range(width // HD):
            (_, _, value), probs = attention_scores(
                qkv, h, ids_col, ids_row, tokens.start, tokens.stop
            )
            mixed[tokens, h * HD : (h + 1) * HD] = jnp.dot(
                probs.astype(LOW), value, preferred_element_type=F32
            ).astype(LOW)
        sent.append(
            project_start(
                net, mixed[tokens, :], weights_one.at[:, 3 * width :], outgoing, incoming, tokens
            )
        )
    flush(qkv, mixed)
    left = net.gather_pass(place_two, gather_two, False)
    left += net.gather_pass(place_keys, gather_keys, False)
    gain_two = norm_two[...].astype(LOW).astype(F32)
    spread = []
    for i, tokens in enumerate(parts):
        own_part, reduce = sent[i]
        values = dealt[tokens, :] + project_end(own_part, incoming, reduce, tokens)
        resid[tokens, :] = values
        square = share_sums(
            net, jnp.sum(values * values, axis=1, keepdims=True), mine.at[i], theirs.at[i]
        )
        scale = lax.rsqrt(square / D + EPS)
        factor_two[tokens, :] = scale
        own = lambda col: columns_of(hidden_two, width)(col).at[tokens, :]
        own(net.col)[...] = (values * widen(scale, width) * gain_two).astype(LOW)
        spread += net.columns_start(own)
    flush(resid, factor_two)
    wait_all(cot_copies)
    own_cot = columns_of(full_cot, width)
    own_cot(net.col)[...] = unpack(got_cot, recv_col[...]).astype(LOW)
    cot_spread = net.columns_start(own_cot)
    left += net.gather_pass(place_two, gather_two, True)
    left += net.gather_pass(place_keys, gather_keys, True)
    wait_all(spread)
    wait_all(left)
    flush(hidden_two, weights_two, keys)
    for h in range(halves):
        columns = slice(h * QD, (h + 1) * QD)
        queries[:, columns] = jnp.dot(
            hidden_two[...], weights_two[:, columns], preferred_element_type=F32
        ).astype(LOW)
        scores = lax.dot_general(
            queries[:, columns], keys[h], NT_DIMS, preferred_element_type=F32
        )
        low_index = halves_of[h] & (LANES - 1)
        first = jnp.take_along_axis(scores[:, :LANES], low_index, axis=1)
        second = jnp.take_along_axis(scores[:, LANES:], low_index, axis=1)
        turned[...] = jnp.where(halves_of[h] >= LANES, second, first).T
        first_row = (net.col * halves + h) * PICKS
        scores_of[pl.ds(pl.multiple_of(first_row, PICKS), PICKS), :] = turned[head_rows, :]
    own_scores = rows_of(scores_of, halves * PICKS)
    score_spread = net.columns_start(own_scores)
    open_gate = jnp.dot(
        hidden_two[...], weights_two[:, depth : depth + width], preferred_element_type=F32
    )
    gate[...] = open_gate
    wait_all(cot_spread)
    flush(full_cot, queries, gate)
    back = jnp.dot(full_cot[...], weights_two[:, depth + width :], preferred_element_type=F32)
    grad_mixed[...] = back
    grad_memory[...] = (back * (open_gate * jax.nn.sigmoid(open_gate))).astype(LOW)
    wait_all(score_spread)
    for m in range(MH):
        score = (
            scores_of[2 * m * PICKS : (2 * m + 1) * PICKS]
            + scores_of[(2 * m + 1) * PICKS : (2 * m + 2) * PICKS]
        )
        shifted = jnp.exp(score - jnp.max(score, axis=0, keepdims=True))
        weights[m * PICKS : (m + 1) * PICKS] = shifted / jnp.sum(shifted, axis=0, keepdims=True)
    net.drain()


def norm_grad(net, grad_hidden, values, scale, gain, mine, theirs):
    width = values.shape[1]
    scaled = grad_hidden * gain
    inner = share_sums(net, jnp.sum(scaled * values, axis=1, keepdims=True), mine, theirs)
    wide = widen(scale, width)
    grads = wide * scaled - values * (wide * wide * wide) * widen(inner, width) / D
    grad_gain = jnp.sum(grad_hidden * values * wide, axis=0, keepdims=True)
    return grads, grad_gain


def project_start(net, left, weights, outgoing, incoming, tokens=slice(None)):
    width = outgoing.shape[2]

    def block(col):
        rows = rows_of(weights, width)(col)[...]
        return lax.dot_general(left, rows, NT_DIMS, preferred_element_type=F32)

    copies = []
    for k in range(1, net.cols):
        outgoing[k - 1, tokens] = block(flip(net.col, k)).astype(LOW)
        copies.append(
            net.send(outgoing.at[k - 1, tokens], incoming.at[k - 1, tokens], col_k=k)
        )
    return block(net.col), copies


def project_end(total, incoming, copies, tokens=slice(None)):
    for k, copy in enumerate(copies):
        copy.wait_recv()
        total = total + incoming[k, tokens].astype(F32)
    return total


def two_parts(count):
    return (slice(0, count // 2), slice(count // 2, count))


def attention_scores(qkv, head, ids_col, ids_row, first, last):
    parts = [
        qkv[first if j == 0 else 0 : last, (3 * head + j) * HD : (3 * head + j + 1) * HD]
        for j in range(3)
    ]
    ids_col, ids_row = ids_col[first:last], ids_row[:, :last]
    scores = lax.dot_general(parts[0], parts[1], NT_DIMS, preferred_element_type=F32) * HD ** (
        -0.5
    )
    asks = lax.broadcasted_iota(jnp.int32, scores.shape, 0) + first
    offers = lax.broadcasted_iota(jnp.int32, scores.shape, 1)
    allowed = (ids_col == ids_row) & (asks >= offers)
    scores = jnp.where(allowed, scores, MASKED)
    shifted = jnp.exp(scores - jnp.max(scores, axis=1, keepdims=True))
    return parts, shifted / jnp.sum(shifted, axis=1, keepdims=True)


def spread_picks(halves, weights, dw, index, out):
    tokens = weights.shape[1]
    grad = weights * (dw - jnp.sum(weights * dw, axis=0, keepdims=True))
    block = 128
    places = lax.broadcasted_iota(jnp.int32, (NK, block), 0)
    for h in range(halves):
        for b in range(tokens // block):
            columns = slice(b * block, (b + 1) * block)
            total = jnp.zeros((NK, block), F32)
            for k in range(PICKS):
                row = index[h * PICKS + k : h * PICKS + k + 1, columns]
                total = total + jnp.where(places == row, grad[k : k + 1, columns], 0.0)
            out[columns, h * NK : (h + 1) * NK] = total.T.astype(LOW)


def back_kernel(
    rows,
    cols,
    halves,
    need,
    flush,
    share,
    dw,
    index,
    memory,
    gate,
    grad_mixed,
    queries,
    hidden_two,
    cot,
    weights_two,
    keys,
    resid,
    factor_two,
    gain_two,
    recv_row,
    send_col,
    qkv,
    mixed,
    lengths,
    hidden_one,
    weights_one,
    dealt,
    factor_one,
    gain_one,
    output,
    grad_tokens,
    own_qkv,
    own_attn,
    own_query,
    own_gate,
    own_mem,
    own_keys,
    gains,
    grad_sub,
    both,
    mixed_two,
    grad_mem,
    grad_two,
    grad_keys,
    grad_low,
    grad_resid,
    grad_qkv,
    grad_one,
    one_outgoing,
    one_incoming,
    res_outgoing,
    res_incoming,
    two_outgoing,
    two_incoming,
    mine,
    theirs,
    mine_one,
    theirs_one,
    packed,
    got,
    packed_one,
    got_one,
    across_two,
    two_out,
    two_in,
    across_keys,
    keys_out,
    keys_in,
    across_one,
    one_out,
    one_in,
    across_mem,
    mem_out,
    mem_in,
    my_gains,
    their_gains,
    sends,
    recvs,
):
    net = Net(rows, cols, sends, recvs)
    capacity = packed.shape[0] // rows
    width = resid.shape[1]
    depth = halves * QD
    greeted = net.greet(range(1, rows), range(1, cols))
    need(gate, grad_mixed, memory)
    open_gate, back, read = gate[...], grad_mixed[...], memory[...]
    sigmoid = jax.nn.sigmoid(open_gate)
    both[:, depth:] = (back * read * sigmoid * (1.0 + open_gate * (1.0 - sigmoid))).astype(LOW)
    mixed_two[...] = (read * open_gate * sigmoid).astype(LOW)
    need(weights_two)
    net.meet(greeted)
    own_res, reduce_res = project_start(
        net, mixed_two[...], weights_two.at[:, depth + width :], res_outgoing, res_incoming
    )
    need(cot)
    grad_mem[...] = jnp.dot(cot[...].T, mixed_two[...], preferred_element_type=F32)
    moved_mem, moved_two, moved_keys, moved_one = {}, {}, {}, {}
    view_mem = rows_of(grad_mem, own_query.shape[0])
    started_mem = net.scatter_start(view_mem, across_mem)
    pass_mem = (view_mem, across_mem, started_mem, mem_out, mem_in, moved_mem)
    need(share, dw, index, keys)
    head = net.col * halves // 2
    own_share = share[pl.ds(pl.multiple_of(head * PICKS, PICKS), PICKS), :]
    spread_picks(halves, own_share, dw[...], index, grad_sub)
    net.scatter_pass(*pass_mem, True)
    for h in range(halves):
        both[:, h * QD : (h + 1) * QD] = jnp.dot(
            grad_sub[:, h * NK : (h + 1) * NK], keys[h], preferred_element_type=F32
        ).astype(LOW)
    own_part, reduce_two = project_start(
        net, both[...], weights_two.at[:, : depth + width], two_outgoing, two_incoming
    )
    need(resid, recv_row)
    block = resid[...] + project_end(own_res, res_incoming, reduce_res)
    pack_for_rows(net, packed, block.astype(LOW), recv_row[...])
    copies = exchange_start(net, packed, got, capacity)
    need(hidden_two, queries)
    grad_two[...] = jnp.dot(hidden_two[...].T, both[...], preferred_element_type=F32)
    for h in range(halves):
        grad_keys[h] = jnp.dot(
            grad_sub[:, h * NK : (h + 1) * NK].T,
            queries[:, h * QD : (h + 1) * QD],
            preferred_element_type=F32,
        )
    view_two = rows_of(grad_two, own_query.shape[0])
    span = own_keys.shape[1]
    view_keys = lambda at: grad_keys.at[:, pl.ds(pl.multiple_of(at * span, span), span), :]
    started_two = net.scatter_start(view_two, across_two)
    started_keys = net.scatter_start(view_keys, across_keys)
    pass_two = (view_two, across_two, started_two, two_out, two_in, moved_two)
    pass_keys = (view_keys, across_keys, started_keys, keys_out, keys_in, moved_keys)
    net.scatter_pass(*pass_two, True)
    net.scatter_pass(*pass_keys, True)
    net.scatter_pass(*pass_mem, False)
    need(lengths)
    ids_col = sequence_ids(lengths[...], memory.shape[0], 0)
    ids_row = sequence_ids(lengths[...], memory.shape[0], 1)
    need(factor_two, gain_two)
    grad_hidden = project_end(own_part, two_incoming, reduce_two)
    grads, gain_two_sum = norm_grad(
        net, grad_hidden, resid[...], factor_two[...], gain_two[...].astype(LOW).astype(F32), mine, theirs
    )
    own_cot = columns_of(cot, width)(net.col)[...]
    grads = grads + own_cot.astype(F32)
    grad_resid[...] = grads
    own = columns_of(grad_low, width)
    own(net.col)[...] = grads.astype(LOW)
    spread = net.columns_start(own)
    wait_all(spread)
    net.scatter_pass(*pass_two, False)
    net.scatter_pass(*pass_keys, False)
    need(weights_one, qkv, hidden_one, mixed, send_col, dealt, factor_one, gain_one)
    grad_heads = jnp.dot(
        grad_low[...], weights_one[:, 3 * width :], preferred_element_type=F32
    ).astype(LOW)
    for head in range(width // HD):
        (query, key, value), probs = attention_scores(
            qkv, head, ids_col, ids_row, 0, memory.shape[0]
        )
        grad_out = grad_heads[:, head * HD : (head + 1) * HD]
        grad_prob = lax.dot_general(grad_out, value, NT_DIMS, preferred_element_type=F32)
        inner = jnp.sum(probs * grad_prob, axis=1, keepdims=True)
        grad_score = (probs * (grad_prob - inner)).astype(LOW)
        pieces = (
            jnp.dot(grad_score, key, preferred_element_type=F32) * HD ** (-0.5),
            jnp.dot(grad_score.T, query, preferred_element_type=F32) * HD ** (-0.5),
            jnp.dot(probs.astype(LOW).T, grad_out, preferred_element_type=F32),
        )
        for j in range(3):
            grad_qkv[:, (3 * head + j) * HD : (3 * head + j + 1) * HD] = pieces[j].astype(LOW)
    own_part, reduce_one = project_start(
        net, grad_qkv[...], weights_one.at[:, : 3 * width], one_outgoing, one_incoming
    )
    grad_one[:, : 3 * width] = jnp.dot(
        hidden_one[...].T, grad_qkv[...], preferred_element_type=F32
    )
    grad_one[:, 3 * width :] = jnp.dot(grad_low[...].T, mixed[...], preferred_element_type=F32)
    view_one = rows_of(grad_one, own_qkv.shape[0])
    started_one = net.scatter_start(view_one, across_one)
    pass_one = (view_one, across_one, started_one, one_out, one_in, moved_one)
    net.scatter_pass(*pass_one, True)
    grad_hidden = project_end(own_part, one_incoming, reduce_one)
    grads, gain_one_sum = norm_grad(
        net,
        grad_hidden,
        dealt[...],
        factor_one[...],
        gain_one[...].astype(LOW).astype(F32),
        mine_one,
        theirs_one,
    )
    grads = grads + grad_resid[...]
    pack_for_rows(net, packed_one, grads.astype(LOW), recv_row[...])
    last = exchange_start(net, packed_one, got_one, capacity)
    net.scatter_pass(*pass_one, False)
    places = lax.broadcasted_iota(jnp.int32, my_gains.shape, 0)
    my_gains[...] = jnp.where(places == 0, gain_one_sum, gain_two_sum)
    gain_copies = [net.send(my_gains, their_gains.at[k], row_k=k) for k in range(1, rows)]
    total = net.scatter_end(view_two, across_two, started_two, two_in, moved_two)
    own_query[...] = total[:, :depth]
    own_gate[...] = total[:, depth:]
    own_mem[...] = net.scatter_end(view_mem, across_mem, started_mem, mem_in, moved_mem).T
    own_keys[...] = net.scatter_end(view_keys, across_keys, started_keys, keys_in, moved_keys)
    wait_all(copies)
    output[...] = unpack(got, send_col[...])
    flush(output)
    total = net.scatter_end(view_one, across_one, started_one, one_in, moved_one)
    own_qkv[...] = total[:, : 3 * width]
    own_attn[...] = total[:, 3 * width :].T
    total = my_gains[...]
    for k, copy in enumerate(gain_copies):
        copy.wait_recv()
        total = total + their_gains[k + 1]
    gains[...] = total
    wait_all(last)
    grad_tokens[...] = unpack(got_one, send_col[...])
    net.drain()


def staged(kernel, rows, cols, sizes, ins, outs, *refs):
    given, results = refs[:ins], refs[ins : ins + outs]
    rest = refs[ins + outs :]
    twins, rest = rest[: ins + outs], rest[ins + outs :]
    sems, rest = rest[0], rest[1:]
    sources, targets = twins[:ins], twins[ins:]
    waited, left = set(), []

    def moving(i):
        return pltpu.make_async_copy(given[i], sources[i], sems.at[i])

    def need(*wanted):
        for ref in wanted:
            i = [j for j in range(ins) if sources[j] is ref][0]
            if i not in waited:
                moving(i).wait()
                waited.add(i)

    def flush(*done):
        for ref in done:
            i = [j for j in range(outs) if targets[j] is ref][0]
            copy = pltpu.make_async_copy(targets[i], results[i], sems.at[ins + i])
            copy.start()
            left.append((i, copy))

    for i in range(ins):
        moving(i).start()
    kernel(rows, cols, *sizes, need, flush, *sources, *targets, *rest)
    assert len(waited) == ins
    flush(*[targets[i] for i in range(outs) if i not in [j for j, _ in left]])
    for _, copy in left:
        copy.wait()


def remote_call(kernel, rows, cols, number, copies, ins, outs, scratch, *sizes):
    twins = [(x.shape, x.dtype) for x in ins] + outs
    anywhere = pl.BlockSpec(memory_space=pl.ANY)
    return pl.pallas_call(
        functools.partial(staged, kernel, rows, cols, sizes, len(ins), len(outs)),
        out_shape=[jax.ShapeDtypeStruct(shape, dtype) for shape, dtype in outs],
        in_specs=[anywhere] * len(ins),
        out_specs=[anywhere] * len(outs),
        scratch_shapes=[pltpu.VMEM(shape, dtype) for shape, dtype in twins]
        + [pltpu.SemaphoreType.DMA((len(twins),))]
        + [pltpu.VMEM(shape, dtype) for shape, dtype in scratch]
        + [pltpu.SemaphoreType.DMA((copies,)), pltpu.SemaphoreType.DMA((copies,))],
        compiler_params=pltpu.CompilerParams(
            collective_id=number, has_side_effects=True, vmem_limit_bytes=VMEM_BYTES
        ),
    )(*ins)


def memory_kernel(
    rows,
    cols,
    own_weights,
    own_picks,
    own_grads,
    table_f32,
    memory,
    dw,
    gacc_out,
    gacc,
    table,
    stage,
    picks_of,
    grads_of,
    low_of,
    dense,
    hi_ref,
    lo_ref,
    wide_ref,
    found_ref,
    mem_all,
    mem_twin,
    mem_out,
    mem_in,
    dw_all,
    dw_twin,
    dw_out,
    dw_in,
    dw_cols,
    stage_sems,
    sends,
    recvs,
):
    net = Net(rows, cols, sends, recvs)
    half = rows // 2
    tok_block = own_picks.shape[0]
    span_rows, width = table.shape
    spans = span_rows // LANES
    pitch = spans + 8
    iters = 4
    per_tok = tok_block // iters
    per_span = spans // iters

    grads_at = rows_of(grads_of, tok_block)
    picks_at = rows_of(picks_of, tok_block)
    low_at = lambda index: low_of.at[index]
    views = (grads_at, picks_at, low_at)
    first_pass = 3 * half
    first_twin = first_pass + 3 * half
    first_out = first_twin + 2 * half
    first_col = first_out + 2 * half

    def gather(a, j):
        mine = views[a](net.row)
        return net.copy(mine, mine, 3 * j + a, row_k=2 * j if j else 1)

    def passing(a, j):
        there = views[a](flip(net.row, 2 * j))
        return net.copy(there, there, first_pass + 3 * j + a, row_k=1)

    def twin(a, j):
        src, dst = ((mem_all, mem_twin), (dw_all, dw_twin))[a]
        return net.copy(src.at[2 * j + 1], dst.at[j], first_twin + 2 * j + a, row_k=1)

    def outward(a, j):
        src, dst = ((mem_out, mem_in), (dw_out, dw_in))[a]
        return net.copy(src.at[j - 1], dst.at[j - 1], first_out + 2 * j + a, row_k=2 * j)

    head = lambda col: pl.ds(pl.multiple_of(col * MH // cols * PICKS, PICKS), PICKS)

    def dw_copy(k):
        return net.copy(
            dw_all.at[0, head(flip(net.col, k)), :],
            dw_cols.at[k - 1],
            first_col + k,
            col_k=k,
        )

    stage_rows = stage.shape[1]

    def stage_copy(i):
        source = table_f32.at[pl.ds(i * stage_rows, stage_rows), :]
        return pltpu.make_async_copy(source, stage.at[i % 2], stage_sems.at[i % 2])

    stage_copy(0).start()
    greeted = net.greet([1] + [2 * j for j in range(1, half)], range(1, cols))
    for i in range(span_rows // stage_rows):
        if (i + 1) * stage_rows < span_rows:
            stage_copy(i + 1).start()
        stage_copy(i).wait()
        table[i * stage_rows : (i + 1) * stage_rows, :] = stage[i % 2].astype(LOW)
    net.meet(greeted)
    grads_at(net.row)[...] = own_grads[...]
    picks_at(net.row)[...] = own_picks[...]
    low_at(net.row)[...] = own_weights[...].astype(LOW)
    for j in range(2):
        for a in range(3):
            gather(a, j).start()
    gacc[...] = jnp.zeros_like(gacc)
    mem_all[...] = jnp.zeros_like(mem_all)

    def one_block(step, _):
        k = jnp.where(step == 0, 0, jnp.where(step == rows - 1, 1, step + 1))
        there = cross(net.row, k, rows)
        for j in range(1, half):

            @pl.when(step == 2 * j - 1)
            def _():
                for a in range(3):
                    gather(a, j).wait_recv()
                    passing(a, j).start()
                if j + 1 < half:
                    for a in range(3):
                        gather(a, j + 1).start()

            @pl.when(step == 2 * j)
            def _():
                for a in range(3):
                    passing(a, j).wait_recv()

        @pl.when(step == rows - 1)
        def _():
            for a in range(3):
                gather(a, 0).wait_recv()

        picks = picks_at(there)[...].astype(jnp.int32) + 32768
        lo_int = picks & (LANES - 1)
        hi_ref[...] = ((picks >> LANE_BITS) - net.row * spans).astype(F32)
        lo_ref[...] = lo_int.astype(F32)
        wide_ref[...] = low_of[there].astype(F32).T
        places_lo = lax.broadcasted_iota(jnp.int32, (LANES, LANES), 0).astype(F32).astype(LOW)
        places_hi = lax.broadcasted_iota(jnp.int32, (spans, LANES), 0).astype(F32).astype(LOW)
        ones = jnp.ones((LANES, LANES), LOW)
        zeros = jnp.zeros((LANES, LANES), LOW)
        blank = jnp.zeros((spans, LANES), LOW)
        grads = grads_at(there)[...]
        grads_t = grads.T
        found_ref[...] = jnp.zeros_like(found_ref)
        hi_all = hi_ref[...]

        def token_pair(first):
            rights, lefts = [], []
            for token in (first, first + 1):
                lo_row = jnp.broadcast_to(lo_ref[pl.ds(token, 1), :], (LANES, LANES)).astype(LOW)
                hi_row = jnp.broadcast_to(hi_ref[pl.ds(token, 1), :], (spans, LANES)).astype(LOW)
                w_row = jnp.broadcast_to(wide_ref[pl.ds(token, 1), :], (spans, LANES)).astype(LOW)
                rights.append(jnp.where(lo_row == places_lo, ones, zeros))
                lefts.append(jnp.where(hi_row == places_hi, w_row, blank))
            right = jnp.concatenate(rights, axis=1)
            left = jnp.concatenate(
                [
                    jnp.concatenate([lefts[0], blank], axis=1),
                    jnp.concatenate([blank, lefts[1]], axis=1),
                ],
                axis=0,
            )
            both = lax.dot_general(left, right, NT_DIMS, preferred_element_type=F32)
            for j in range(2):
                dense[pl.ds(pl.multiple_of((first + j) * pitch, 8), spans), :] = both[
                    j * spans : (j + 1) * spans
                ]

        def look(found, first, number, between=None):
            span = pl.ds(pl.multiple_of(first * LANES, LANES), number * LANES)
            products = lax.dot_general(
                grads, table[span, :], NT_DIMS, preferred_element_type=F32
            )
            for j in range(number):
                picked = jnp.take_along_axis(
                    products[:, LANES * j : LANES * (j + 1)], lo_int, axis=1
                )
                found = jnp.where(hi_all == (first + j).astype(F32), picked, found)
                if between:
                    between(j)
            return found

        early = per_span // 2
        late = per_span - early

        def build(it, _):
            for j in range(1, half):

                @pl.when((it == 1) & (step == 2 * j + 1))
                def _():
                    twin(0, j).wait_recv()
                    twin(1, j).wait_recv()
                    mem_out[j - 1] = (mem_all[2 * j] + mem_twin[j]).astype(LOW)
                    outward(0, j).start()
                    dw_out[j - 1] = (dw_all[2 * j] + dw_twin[j]).astype(LOW)
                    outward(1, j).start()

            pairs = per_tok // 2 // early

            def some_pairs(j):
                for u in range(pairs):
                    token_pair(it * per_tok + (j * pairs + u) * 2)

            found_ref[...] = look(found_ref[...], it * early, early, some_pairs)
            return 0

        lax.fori_loop(0, iters, build, 0)
        parts = min(4, late)

        def multiply(it, _):
            found, total = found_ref[...], None
            for c in range(parts):
                low, high = c * late // parts, (c + 1) * late // parts
                found = look(found, early * iters + it * late + low, high - low)
                low, high = c * per_span // parts, (c + 1) * per_span // parts
                first = it * per_span + low
                chosen = jnp.concatenate(
                    [
                        dense[pl.ds(first + j, tok_block, stride=pitch), :].astype(LOW)
                        for j in range(high - low)
                    ],
                    axis=1,
                )
                span = pl.ds(pl.multiple_of(first * LANES, LANES), (high - low) * LANES)
                gacc[:, span] += jnp.dot(grads_t, chosen, preferred_element_type=F32)
                read = jnp.dot(chosen, table[span, :], preferred_element_type=F32)
                total = read if total is None else total + read
            mem_all[k] += total
            found_ref[...] = found
            return 0

        lax.fori_loop(0, iters, multiply, 0)
        dw_all[k] = found_ref[...].T
        for j in range(half):

            @pl.when(step == (2 * j if j else rows - 1))
            def _():
                twin(0, j).start()
                twin(1, j).start()

        return 0

    lax.fori_loop(0, rows, one_block, 0)
    leaving = pltpu.make_async_copy(gacc, gacc_out, stage_sems.at[2])
    leaving.start()
    twin(1, 0).wait_recv()
    total = dw_all[0] + dw_twin[0]
    for j in range(1, half):
        outward(1, j).wait_recv()
        total = total + dw_in[j - 1].astype(F32)
    dw_all[0] = total
    for k in range(1, cols):
        dw_copy(k).start()
    twin(0, 0).wait_recv()
    total = mem_all[0] + mem_twin[0]
    for j in range(1, half):
        outward(0, j).wait_recv()
        total = total + mem_in[j - 1].astype(F32)
    memory[...] = total
    total = dw_all[0, head(net.col), :]
    for k in range(1, cols):
        dw_copy(k).wait_recv()
        total = total + dw_cols[k - 1]
    dw[...] = total
    for k in range(1, cols):
        dw_copy(k).wait_send()
    for j in range(half):
        for a in range(3):
            gather(a, j).wait_send()
            if j:
                passing(a, j).wait_send()
        for a in range(2):
            twin(a, j).wait_send()
            if j:
                outward(a, j).wait_send()
    leaving.wait()


def finish_kernel(others, source, *refs):
    given, out, results = refs[:others], refs[others], refs[others + 1 :]

    @pl.when(pl.program_id(0) == 0)
    def _():
        for i in range(others):
            results[i][...] = given[i][...]

    out[...] = source[...].T


def finish_call(table, others):
    width, span_rows = table.shape
    block = min(4096, span_rows)
    whole = [
        pl.BlockSpec(x.shape, lambda i, rank=x.ndim: (0,) * rank, pipeline_mode=pl.Buffered(1))
        for x in others
    ]
    return pl.pallas_call(
        functools.partial(finish_kernel, len(others)),
        grid=(span_rows // block,),
        in_specs=[pl.BlockSpec((width, block), lambda i: (0, i))] + whole,
        out_specs=[pl.BlockSpec((block, width), lambda i: (i, 0))] + whole,
        out_shape=[jax.ShapeDtypeStruct((span_rows, width), F32)]
        + [jax.ShapeDtypeStruct(x.shape, x.dtype) for x in others],
        compiler_params=pltpu.CompilerParams(vmem_limit_bytes=VMEM_BYTES),
    )(table, *others)


def memory_call(rows, cols, number, weights, picks, grads, table):
    tokens, count = picks.shape
    span_rows, width = table.shape
    half = rows // 2
    copies = 10 * half + cols
    vmem = pltpu.VMEM
    return pl.pallas_call(
        functools.partial(memory_kernel, rows, cols),
        in_specs=[VMEM_SPEC, VMEM_SPEC, VMEM_SPEC, pl.BlockSpec(memory_space=pl.ANY)],
        out_specs=[VMEM_SPEC, VMEM_SPEC, pl.BlockSpec(memory_space=pl.ANY)],
        out_shape=[
            jax.ShapeDtypeStruct((tokens, width), F32),
            jax.ShapeDtypeStruct((PICKS, tokens), F32),
            jax.ShapeDtypeStruct((width, span_rows), F32),
        ],
        scratch_shapes=[
            vmem((width, span_rows), F32),
            vmem((span_rows, width), LOW),
            vmem((2, 1024, width), F32),
            vmem((rows * tokens, count), jnp.int16),
            vmem((rows * tokens, width), LOW),
            vmem((rows, count, tokens), LOW),
            vmem((tokens * (span_rows // LANES + 8), LANES), F32),
            vmem((tokens, count), F32),
            vmem((tokens, count), F32),
            vmem((tokens, count), F32),
            vmem((tokens, count), F32),
            vmem((rows, tokens, width), F32),
            vmem((half, tokens, width), F32),
            vmem((half - 1, tokens, width), LOW),
            vmem((half - 1, tokens, width), LOW),
            vmem((rows, count, tokens), F32),
            vmem((half, count, tokens), F32),
            vmem((half - 1, count, tokens), LOW),
            vmem((half - 1, count, tokens), LOW),
            vmem((cols - 1, PICKS, tokens), F32),
            pltpu.SemaphoreType.DMA((3,)),
            pltpu.SemaphoreType.DMA((copies,)),
            pltpu.SemaphoreType.DMA((copies,)),
        ],
        compiler_params=pltpu.CompilerParams(
            collective_id=number, has_side_effects=True, vmem_limit_bytes=63 * 2**20
        ),
    )(weights, picks, grads, table)


def per_device(
    tokens,
    cotangent,
    deal_order,
    seq_lengths,
    value_picks,
    norm1_gain,
    w_qkv,
    w_attn_out,
    norm2_gain,
    w_query,
    sub_keys,
    value_table,
    w_gate,
    w_mem_out,
):
    rows, cols = lax.axis_size("row"), lax.axis_size("col")
    row_index = lax.axis_index("row")
    count, width = tokens.shape
    slots = 2 * count
    half = rows // 2
    halves = sub_keys.shape[0]
    depth = halves * QD
    span_one, span_two = 4 * width, depth + 2 * width
    shard_rows = w_qkv.shape[0]
    flat_picks = value_picks.reshape(count, MH * PICKS)
    gain_one, gain_two = norm1_gain[None, :], norm2_gain[None, :]
    swap = [((slots, width), LOW), ((slots, width), LOW)]
    sums = [((8, count), F32), ((cols, 8, count), F32)]
    part_sums = [((2, 8, count // 2), F32), ((2, cols, 8, count // 2), F32)]
    moving = ((cols - 1, count, width), LOW)
    (
        send_row,
        send_col,
        recv_row,
        recv_col,
        hidden_one,
        dealt,
        factor_one,
        weights_one,
        qkv,
        mixed,
        hidden_two,
        resid,
        factor_two,
        full_cot,
        weights_two,
        keys,
        queries,
        gate,
        grad_mixed,
        grad_memory,
        index,
        low_picks,
        pick_weights,
    ) = remote_call(
        front_kernel,
        rows,
        cols,
        0,
        10 * (cols - 1) + 5 * (rows - 1),
        [
            deal_order[None, :],
            flat_picks,
            seq_lengths,
            tokens,
            cotangent,
            w_qkv,
            w_attn_out,
            w_query,
            w_gate,
            w_mem_out,
            sub_keys,
            gain_one,
            gain_two,
        ],
        [
            ((1, count), jnp.int32),
            ((count, 1), jnp.int32),
            ((1, count), jnp.int32),
            ((count, 1), jnp.int32),
            ((count, D), LOW),
            ((count, width), F32),
            ((count, LANES), F32),
            ((D, span_one), LOW),
            ((count, 3 * width), LOW),
            ((count, width), LOW),
            ((count, D), LOW),
            ((count, width), F32),
            ((count, LANES), F32),
            ((count, D), LOW),
            ((D, span_two), LOW),
            ((halves, NK, QD), LOW),
            ((count, depth), LOW),
            ((count, width), F32),
            ((count, width), F32),
            ((count, width), LOW),
            ((halves * PICKS, count), jnp.int32),
            ((count, MH * PICKS), jnp.int16),
            ((MH * PICKS, count), F32),
        ],
        [((2 * MH * PICKS, count), F32), ((count, D), LOW), ((8, D), F32), *swap, *swap, moving, moving, *part_sums]
        + [((MH * PICKS, count), F32)],
        halves,
    )
    memory, grad_pick, grad_table = memory_call(
        rows, cols, 1, pick_weights, low_picks, grad_memory, value_table
    )
    block = ((count, width), F32)
    scattered = [
        [((half,) + shape, F32), ((half - 1,) + shape, LOW), ((half - 1,) + shape, LOW)]
        for shape in (
            (shard_rows, depth + width),
            sub_keys.shape,
            (shard_rows, span_one),
            (shard_rows, width),
        )
    ]
    output, grad_tokens, own_qkv, own_attn, own_query, own_gate, own_mem, own_keys, gains = remote_call(
        back_kernel,
        rows,
        cols,
        2,
        6 * (cols - 1) + 3 * (rows - 1) + 4 * (half + half - 1),
        [
            pick_weights,
            grad_pick,
            index,
            memory,
            gate,
            grad_mixed,
            queries,
            hidden_two,
            full_cot,
            weights_two,
            keys,
            resid,
            factor_two,
            gain_two,
            recv_row,
            send_col,
            qkv,
            mixed,
            seq_lengths,
            hidden_one,
            weights_one,
            dealt,
            factor_one,
            gain_one,
        ],
        [
            block,
            block,
            (w_qkv.shape, F32),
            (w_attn_out.shape, F32),
            (w_query.shape, F32),
            (w_gate.shape, F32),
            (w_mem_out.shape, F32),
            (sub_keys.shape, F32),
            ((8, width), F32),
        ],
        [
            ((count, halves * NK), LOW),
            ((count, depth + width), LOW),
            ((count, width), LOW),
            ((D, width), F32),
            ((D, depth + width), F32),
            ((halves, NK, QD), F32),
            ((count, D), LOW),
            block,
            ((count, 3 * width), LOW),
            ((D, span_one), F32),
            *[moving] * 6,
            *sums,
            *sums,
            *swap,
            *swap,
            *scattered[0],
            *scattered[1],
            *scattered[2],
            *scattered[3],
            ((8, width), F32),
            ((rows, 8, width), F32),
        ],
        halves,
    )
    gain_span = width // rows
    gain_one_grad = lax.dynamic_slice_in_dim(gains[0], row_index * gain_span, gain_span)
    gain_two_grad = lax.dynamic_slice_in_dim(gains[1], row_index * gain_span, gain_span)
    others = (
        output,
        grad_tokens,
        own_qkv,
        own_attn,
        own_query,
        own_keys,
        own_gate,
        own_mem,
    )
    turned, *others = finish_call(grad_table, others)
    output, grad_tokens, own_qkv, own_attn, own_query, own_keys, own_gate, own_mem = others
    return (
        output,
        grad_tokens,
        gain_one_grad,
        own_qkv,
        own_attn,
        gain_two_grad,
        own_query,
        own_keys,
        turned,
        own_gate,
        own_mem,
    )


def solution(mesh):
    return jax.shard_map(
        per_device,
        mesh=mesh,
        in_specs=(
            P("row", "col"),
            P("row", "col"),
            P(),
            P("row", None),
            P("row", None, None),
            P("col"),
            P("row", "col"),
            P("col", "row"),
            P("col"),
            P("row", "col"),
            P("col", "row", None),
            P("row", "col"),
            P("row", "col"),
            P("col", "row"),
        ),
        out_specs=(
            P("row", "col"),
            P("row", "col"),
            P(("col", "row")),
            P("row", "col"),
            P("col", "row"),
            P(("col", "row")),
            P("row", "col"),
            P("col", "row", None),
            P("row", "col"),
            P("row", "col"),
            P("col", "row"),
        ),
        check_vma=False,
    )
```

```python
import functools

import jax
import jax.numpy as jnp
from jax import lax
from jax.experimental import pallas as pl
from jax.experimental.pallas import tpu as pltpu
from jax.sharding import PartitionSpec as P

D = 1024
HD = 64
MH = 4
QD = 512
NK = 256
PICKS = 32
LANES = 128
LANE_BITS = LANES.bit_length() - 1
KEY_BITS = NK.bit_length() - 1
EPS = 1e-05
MASKED = -1e30
F32 = jnp.float32
LOW = jnp.bfloat16
MESH = pl.DeviceIdType.MESH
NT_DIMS = (((1,), (1,)), ((), ()))
VMEM_SPEC = pl.BlockSpec(memory_space=pltpu.VMEM)
VMEM_BYTES = 60 * 2**20


def flip(index, mask):
    bit = 1
    while bit <= mask:
        if mask & bit:
            index = index + bit - 2 * bit * (index // bit % 2)
        bit *= 2
    return index


def cross(index, mask, size):
    total, bit = 0, 1
    while bit < size:
        a, b = index // bit % 2, mask // bit % 2
        total = total + bit * (a + b - 2 * a * b)
        bit *= 2
    return total


class Net:
    def __init__(self, rows, cols, sends, recvs):
        self.rows, self.cols = rows, cols
        self.row, self.col = lax.axis_index("row"), lax.axis_index("col")
        self.sends, self.recvs, self.used = sends, recvs, 0
        self.pending = []

    def place(self, row_k, col_k):
        return (flip(self.row, row_k), flip(self.col, col_k))

    def greet(self, row_ks, col_ks):
        barrier = pltpu.get_barrier_semaphore()
        places = [self.place(k, 0) for k in row_ks] + [self.place(0, k) for k in col_ks]
        for place in places:
            pl.semaphore_signal(barrier, inc=1, device_id=place, device_id_type=MESH)
        return len(places)

    def meet(self, greeted):
        pl.semaphore_wait(pltpu.get_barrier_semaphore(), greeted)

    def copy(self, src, dst, number, row_k=0, col_k=0):
        assert number < self.sends.shape[0]
        return pltpu.make_async_remote_copy(
            src_ref=src,
            dst_ref=dst,
            send_sem=self.sends.at[number],
            recv_sem=self.recvs.at[number],
            device_id=self.place(row_k, col_k),
            device_id_type=MESH,
        )

    def send(self, src, dst, row_k=0, col_k=0):
        copy = self.copy(src, dst, self.used, row_k, col_k)
        copy.start()
        self.used += 1
        self.pending.append(copy)
        return copy

    def drain(self):
        for copy in self.pending:
            copy.wait_send()

    def gather_start(self, src, view):
        sent = {b: self.send(src, view(self.row), row_k=2 * b) for b in reversed(self.bits())}
        return sent, self.send(src, view(self.row), row_k=1)

    def gather_pass(self, view, started, near):
        sent, sibling = started
        passed = [sibling] if near else []
        masks = [m for m in range(1, self.rows // 2) if (m % 2 == 1) == near]
        for m in sorted(masks, key=lambda m: (-(m & -m), m.bit_count())):
            sent[m].wait_recv()
            block = view(flip(self.row, 2 * m))
            for b in self.bits():
                if b < (m & -m):
                    sent[m ^ b] = self.send(block, block, row_k=2 * b)
            passed.append(self.send(block, block, row_k=1))
        return passed

    def bits(self):
        return [1 << i for i in range((self.rows // 2 - 1).bit_length())]

    def scatter_start(self, view, across):
        twin = flip(self.row, 1)
        return [
            self.send(view(flip(twin, 2 * j)), across.at[j], row_k=1)
            for j in range(self.rows // 2)
        ]

    def scatter_pass(self, view, across, started, outgoing, incoming, moved, near):
        masks = [m for m in range(1, self.rows // 2) if (m % 2 == 1) == near]
        for m in sorted(masks, key=lambda m: ((m & -m), -m.bit_count())):
            started[m].wait_recv()
            block = view(flip(self.row, 2 * m))[...] + across[m]
            for b in self.bits():
                if b < (m & -m):
                    moved[m ^ b].wait_recv()
                    block = block + incoming[(m ^ b) - 1].astype(F32)
            outgoing[m - 1] = block.astype(outgoing.dtype)
            moved[m] = self.send(outgoing.at[m - 1], incoming.at[m - 1], row_k=2 * (m & -m))
        return moved

    def scatter_end(self, view, across, started, incoming, moved):
        started[0].wait_recv()
        total = view(self.row)[...] + across[0]
        for b in self.bits():
            moved[b].wait_recv()
            total = total + incoming[b - 1].astype(F32)
        return total

    def columns_start(self, view):
        return [self.send(view(self.col), view(self.col), col_k=k) for k in range(1, self.cols)]


def wait_all(copies):
    for copy in copies:
        copy.wait_recv()


def rows_of(ref, count):
    return lambda index: ref.at[pl.ds(pl.multiple_of(index * count, count), count), :]


def columns_of(ref, count):
    return lambda index: ref.at[:, pl.ds(pl.multiple_of(index * count, count), count)]


def one_hot_rows(positions, slots):
    places = lax.broadcasted_iota(jnp.int32, (positions.shape[0], slots), 1)
    return jnp.where(positions == places, 1.0, 0.0).astype(LOW)


def one_hot_columns(positions, slots):
    places = lax.broadcasted_iota(jnp.int32, (slots, positions.shape[1]), 0)
    return jnp.where(positions == places, 1.0, 0.0).astype(LOW)


def pack_for_rows(net, packed, values, positions):
    slots = packed.shape[0]
    packed[...] = jnp.dot(
        one_hot_columns(positions, slots), values, preferred_element_type=F32
    ).astype(LOW)


def exchange_start(net, packed, got, capacity):
    mine = rows_of(got, capacity)
    theirs = rows_of(packed, capacity)
    copies = [
        net.send(theirs(flip(net.row, k)), mine(net.row), row_k=k) for k in range(1, net.rows)
    ]
    mine(net.row)[...] = theirs(net.row)[...]
    return copies


def unpack(got, positions):
    return jnp.dot(
        one_hot_rows(positions, got.shape[0]), got[...], preferred_element_type=F32
    )


def share_sums(net, sums, mine, theirs):
    tokens = sums.shape[0]
    mine[...] = jnp.broadcast_to(sums, (tokens, LANES)).T[:8]
    copies = [net.send(mine, theirs.at[k], col_k=k) for k in range(1, net.cols)]
    wait_all(copies)
    total = mine[...]
    for k in range(1, net.cols):
        total = total + theirs[k]
    return jnp.broadcast_to(total[:1], (LANES, tokens)).T


def widen(lanes, width):
    return jnp.concatenate([lanes] * (width // LANES), axis=1)


def first_of(size, mask):
    earlier = lax.broadcasted_iota(jnp.int32, (size, size), 0)
    later = lax.broadcasted_iota(jnp.int32, (size, size), 1)
    triangle = jnp.where(earlier < later, 1.0, 0.0).astype(LOW)
    return jnp.dot(mask.astype(LOW), triangle, preferred_element_type=F32)


def find_places(rows, row, order, send_row, send_col, recv_row, recv_col):
    count = order.shape[1]
    capacity = 2 * count // rows
    owner = order // count
    owned = jnp.where(owner == row, 1.0, 0.0)
    rank = first_of(count, owned)
    low_order = order.astype(F32).T
    tokens = lax.broadcasted_iota(jnp.int32, (count, count), 1).astype(F32)
    first = (row * count).astype(F32)
    sent = jnp.zeros((1, count), F32)
    pick = lax.broadcasted_iota(jnp.int32, (8, count), 0)
    for d in range(rows):
        match = jnp.where(low_order[:, d : d + 1] - first == tokens, 1.0, 0.0).astype(LOW)
        pair = jnp.where(pick == 0, rank[d : d + 1] * owned[d : d + 1], owned[d : d + 1])
        found = jnp.dot(pair.astype(LOW), match, preferred_element_type=F32)
        sent = sent + found[:1] + found[1:2] * (d * capacity)
    send_row[...] = sent.astype(jnp.int32)
    send_col[...] = jnp.broadcast_to(sent, (LANES, count)).T[:, :1].astype(jnp.int32)
    blocks = lax.broadcasted_iota(jnp.int32, (rows, count), 0)
    mine = jnp.sum(jnp.where(blocks == row, order, 0), axis=0, keepdims=True)
    source = mine // count
    came = jnp.where(source == lax.broadcasted_iota(jnp.int32, (LANES, count), 0), 1.0, 0.0)
    place = jnp.sum(first_of(count, came) * came, axis=0, keepdims=True)
    place = place + source.astype(F32) * capacity
    recv_row[...] = place.astype(jnp.int32)
    recv_col[...] = jnp.broadcast_to(place, (LANES, count)).T[:, :1].astype(jnp.int32)


def sequence_ids(lengths, count, axis):
    places = lax.broadcasted_iota(jnp.int32, (1, count) if axis else (count, 1), axis)
    end = jnp.zeros((1, 1), jnp.int32)
    ids = jnp.zeros(places.shape, jnp.int32)
    for j in range(lengths.shape[1]):
        end = end + lengths[:, j : j + 1]
        ids = ids + jnp.where(places >= end, 1, 0)
    return ids


def front_kernel(
    rows,
    cols,
    halves,
    need,
    flush,
    order,
    picks,
    lengths,
    tokens_ref,
    cot,
    w_qkv,
    w_attn,
    w_query,
    w_gate,
    w_mem,
    sub_keys,
    norm_one,
    norm_two,
    send_row,
    send_col,
    recv_row,
    recv_col,
    hidden_one,
    dealt,
    factor_one,
    weights_one,
    qkv,
    mixed,
    hidden_two,
    resid,
    factor_two,
    full_cot,
    weights_two,
    keys,
    queries,
    gate,
    grad_mixed,
    grad_memory,
    index,
    low_picks,
    weights,
    scores_of,
    flat_picks,
    full,
    gains,
    packed,
    got,
    packed_cot,
    got_cot,
    outgoing,
    incoming,
    mine,
    theirs,
    turned,
    sends,
    recvs,
):
    net = Net(rows, cols, sends, recvs)
    greeted = net.greet(range(1, rows), range(1, cols))
    count, width = tokens_ref.shape
    capacity = packed.shape[0] // rows
    depth = halves * QD
    need(w_qkv, w_attn)
    place_one = rows_of(weights_one, w_qkv.shape[0])
    place_one(net.row)[:, : 3 * width] = w_qkv[...].astype(LOW)
    place_one(net.row)[:, 3 * width :] = w_attn[...].T.astype(LOW)
    net.meet(greeted)
    gather_one = net.gather_start(place_one(net.row), place_one)
    need(order, tokens_ref)
    by_block = jnp.concatenate([order[:, d * count : (d + 1) * count] for d in range(rows)], axis=0)
    find_places(rows, net.row, by_block, send_row, send_col, recv_row, recv_col)
    pack_for_rows(net, packed, tokens_ref[...], send_row[...])
    copies = exchange_start(net, packed, got, capacity)
    need(norm_one, norm_two, cot, w_query, w_gate, w_mem, sub_keys, picks, lengths)
    own_gain = columns_of(gains, width)
    own_gain(net.col)[...] = jnp.broadcast_to(
        norm_one[...].astype(LOW).astype(F32), (8, width)
    )
    gain_spread = net.columns_start(own_gain)
    pack_for_rows(net, packed_cot, cot[...], send_row[...])
    cot_copies = exchange_start(net, packed_cot, got_cot, capacity)
    place_two = rows_of(weights_two, w_query.shape[0])
    place_two(net.row)[:, :depth] = w_query[...].astype(LOW)
    place_two(net.row)[:, depth : depth + width] = w_gate[...].astype(LOW)
    place_two(net.row)[:, depth + width :] = w_mem[...].T.astype(LOW)
    span = sub_keys.shape[1]
    place_keys = lambda at: keys.at[:, pl.ds(pl.multiple_of(at * span, span), span), :]
    place_keys(net.row)[...] = sub_keys[...].astype(LOW)
    wait_all(copies)
    own = columns_of(full, width)
    values = unpack(got, recv_col[...])
    own(net.col)[...] = values.astype(LOW)
    spread = net.columns_start(own)
    dealt[...] = values
    left_one = net.gather_pass(place_one, gather_one, False)
    gather_two = net.gather_start(place_two(net.row), place_two)
    gather_keys = net.gather_start(place_keys(net.row), place_keys)
    for m in range(MH):
        flat_picks[:, m * PICKS : (m + 1) * PICKS] = picks[:, m, :]
    low_picks[...] = (flat_picks[...] - 32768).astype(jnp.int16)
    head = net.col * halves // 2
    head_rows = pl.ds(pl.multiple_of(head * PICKS, PICKS), PICKS)
    halves_of = []
    for h in range(halves):
        even = (net.col * halves + h) % 2 == 0
        halves_of.append(jnp.where(even, flat_picks[...] >> KEY_BITS, flat_picks[...] & (NK - 1)))
        turned[...] = halves_of[h].astype(F32).T
        index[h * PICKS : (h + 1) * PICKS] = turned[head_rows, :].astype(jnp.int32)
    ids_col = sequence_ids(lengths[...], count, 0)
    ids_row = sequence_ids(lengths[...], count, 1)
    wait_all(spread)
    wait_all(gain_spread)
    values = full[...].astype(F32)
    scale = lax.rsqrt(jnp.mean(values * values, axis=1, keepdims=True) + EPS)
    hidden_one[...] = (values * scale * gains[:1]).astype(LOW)
    factor_one[...] = jnp.broadcast_to(scale, (count, LANES))
    flush(hidden_one, factor_one, dealt, index, low_picks, send_row, send_col, recv_row, recv_col)
    wait_all(left_one + net.gather_pass(place_one, gather_one, True))
    flush(weights_one)
    qkv[...] = jnp.dot(
        hidden_one[...], weights_one[:, : 3 * width], preferred_element_type=F32
    ).astype(LOW)
    parts, sent = two_parts(count), []
    for tokens in parts:
        for h in range(width // HD):
            (_, _, value), probs = attention_scores(
                qkv, h, ids_col, ids_row, tokens.start, tokens.stop
            )
            mixed[tokens, h * HD : (h + 1) * HD] = jnp.dot(
                probs.astype(LOW), value, preferred_element_type=F32
            ).astype(LOW)
        sent.append(
            project_start(
                net, mixed[tokens, :], weights_one.at[:, 3 * width :], outgoing, incoming, tokens
            )
        )
    flush(qkv, mixed)
    left = net.gather_pass(place_two, gather_two, False)
    left += net.gather_pass(place_keys, gather_keys, False)
    gain_two = norm_two[...].astype(LOW).astype(F32)
    spread = []
    for i, tokens in enumerate(parts):
        own_part, reduce = sent[i]
        values = dealt[tokens, :] + project_end(own_part, incoming, reduce, tokens)
        resid[tokens, :] = values
        square = share_sums(
            net, jnp.sum(values * values, axis=1, keepdims=True), mine.at[i], theirs.at[i]
        )
        scale = lax.rsqrt(square / D + EPS)
        factor_two[tokens, :] = scale
        own = lambda col: columns_of(hidden_two, width)(col).at[tokens, :]
        own(net.col)[...] = (values * widen(scale, width) * gain_two).astype(LOW)
        spread += net.columns_start(own)
    flush(resid, factor_two)
    wait_all(cot_copies)
    own_cot = columns_of(full_cot, width)
    own_cot(net.col)[...] = unpack(got_cot, recv_col[...]).astype(LOW)
    cot_spread = net.columns_start(own_cot)
    left += net.gather_pass(place_two, gather_two, True)
    left += net.gather_pass(place_keys, gather_keys, True)
    wait_all(spread)
    wait_all(left)
    flush(hidden_two, weights_two, keys)
    for h in range(halves):
        columns = slice(h * QD, (h + 1) * QD)
        queries[:, columns] = jnp.dot(
            hidden_two[...], weights_two[:, columns], preferred_element_type=F32
        ).astype(LOW)
        scores = lax.dot_general(
            queries[:, columns], keys[h], NT_DIMS, preferred_element_type=F32
        )
        low_index = halves_of[h] & (LANES - 1)
        first = jnp.take_along_axis(scores[:, :LANES], low_index, axis=1)
        second = jnp.take_along_axis(scores[:, LANES:], low_index, axis=1)
        turned[...] = jnp.where(halves_of[h] >= LANES, second, first).T
        first_row = (net.col * halves + h) * PICKS
        scores_of[pl.ds(pl.multiple_of(first_row, PICKS), PICKS), :] = turned[head_rows, :]
    own_scores = rows_of(scores_of, halves * PICKS)
    score_spread = net.columns_start(own_scores)
    open_gate = jnp.dot(
        hidden_two[...], weights_two[:, depth : depth + width], preferred_element_type=F32
    )
    gate[...] = open_gate
    wait_all(cot_spread)
    flush(full_cot, queries, gate)
    back = jnp.dot(full_cot[...], weights_two[:, depth + width :], preferred_element_type=F32)
    grad_mixed[...] = back
    grad_memory[...] = (back * (open_gate * jax.nn.sigmoid(open_gate))).astype(LOW)
    wait_all(score_spread)
    for m in range(MH):
        score = (
            scores_of[2 * m * PICKS : (2 * m + 1) * PICKS]
            + scores_of[(2 * m + 1) * PICKS : (2 * m + 2) * PICKS]
        )
        shifted = jnp.exp(score - jnp.max(score, axis=0, keepdims=True))
        weights[m * PICKS : (m + 1) * PICKS] = shifted / jnp.sum(shifted, axis=0, keepdims=True)
    net.drain()


def norm_grad(net, grad_hidden, values, scale, gain, mine, theirs):
    width = values.shape[1]
    scaled = grad_hidden * gain
    inner = share_sums(net, jnp.sum(scaled * values, axis=1, keepdims=True), mine, theirs)
    wide = widen(scale, width)
    grads = wide * scaled - values * (wide * wide * wide) * widen(inner, width) / D
    grad_gain = jnp.sum(grad_hidden * values * wide, axis=0, keepdims=True)
    return grads, grad_gain


def project_start(net, left, weights, outgoing, incoming, tokens=slice(None)):
    width = outgoing.shape[2]

    def block(col):
        rows = rows_of(weights, width)(col)[...]
        return lax.dot_general(left, rows, NT_DIMS, preferred_element_type=F32)

    copies = []
    for k in range(1, net.cols):
        outgoing[k - 1, tokens] = block(flip(net.col, k)).astype(LOW)
        copies.append(
            net.send(outgoing.at[k - 1, tokens], incoming.at[k - 1, tokens], col_k=k)
        )
    return block(net.col), copies


def project_end(total, incoming, copies, tokens=slice(None)):
    for k, copy in enumerate(copies):
        copy.wait_recv()
        total = total + incoming[k, tokens].astype(F32)
    return total


def two_parts(count):
    return (slice(0, count // 2), slice(count // 2, count))


def attention_scores(qkv, head, ids_col, ids_row, first, last):
    parts = [
        qkv[first if j == 0 else 0 : last, (3 * head + j) * HD : (3 * head + j + 1) * HD]
        for j in range(3)
    ]
    ids_col, ids_row = ids_col[first:last], ids_row[:, :last]
    scores = lax.dot_general(parts[0], parts[1], NT_DIMS, preferred_element_type=F32) * HD ** (
        -0.5
    )
    asks = lax.broadcasted_iota(jnp.int32, scores.shape, 0) + first
    offers = lax.broadcasted_iota(jnp.int32, scores.shape, 1)
    allowed = (ids_col == ids_row) & (asks >= offers)
    scores = jnp.where(allowed, scores, MASKED)
    shifted = jnp.exp(scores - jnp.max(scores, axis=1, keepdims=True))
    return parts, shifted / jnp.sum(shifted, axis=1, keepdims=True)


def spread_picks(halves, weights, dw, index, out):
    tokens = weights.shape[1]
    grad = weights * (dw - jnp.sum(weights * dw, axis=0, keepdims=True))
    block = 128
    places = lax.broadcasted_iota(jnp.int32, (NK, block), 0)
    for h in range(halves):
        for b in range(tokens // block):
            columns = slice(b * block, (b + 1) * block)
            total = jnp.zeros((NK, block), F32)
            for k in range(PICKS):
                row = index[h * PICKS + k : h * PICKS + k + 1, columns]
                total = total + jnp.where(places == row, grad[k : k + 1, columns], 0.0)
            out[columns, h * NK : (h + 1) * NK] = total.T.astype(LOW)


def back_kernel(
    rows,
    cols,
    halves,
    need,
    flush,
    share,
    dw,
    index,
    memory,
    gate,
    grad_mixed,
    queries,
    hidden_two,
    cot,
    weights_two,
    keys,
    resid,
    factor_two,
    gain_two,
    recv_row,
    send_col,
    qkv,
    mixed,
    lengths,
    hidden_one,
    weights_one,
    dealt,
    factor_one,
    gain_one,
    output,
    grad_tokens,
    own_qkv,
    own_attn,
    own_query,
    own_gate,
    own_mem,
    own_keys,
    gains,
    grad_sub,
    both,
    mixed_two,
    grad_mem,
    grad_two,
    grad_keys,
    grad_low,
    grad_resid,
    grad_qkv,
    grad_one,
    one_outgoing,
    one_incoming,
    res_outgoing,
    res_incoming,
    two_outgoing,
    two_incoming,
    mine,
    theirs,
    mine_one,
    theirs_one,
    packed,
    got,
    packed_one,
    got_one,
    across_two,
    two_out,
    two_in,
    across_keys,
    keys_out,
    keys_in,
    across_one,
    one_out,
    one_in,
    across_mem,
    mem_out,
    mem_in,
    my_gains,
    their_gains,
    sends,
    recvs,
):
    net = Net(rows, cols, sends, recvs)
    capacity = packed.shape[0] // rows
    width = resid.shape[1]
    depth = halves * QD
    greeted = net.greet(range(1, rows), range(1, cols))
    need(gate, grad_mixed, memory)
    open_gate, back, read = gate[...], grad_mixed[...], memory[...]
    sigmoid = jax.nn.sigmoid(open_gate)
    both[:, depth:] = (back * read * sigmoid * (1.0 + open_gate * (1.0 - sigmoid))).astype(LOW)
    mixed_two[...] = (read * open_gate * sigmoid).astype(LOW)
    need(weights_two)
    net.meet(greeted)
    own_res, reduce_res = project_start(
        net, mixed_two[...], weights_two.at[:, depth + width :], res_outgoing, res_incoming
    )
    need(cot)
    grad_mem[...] = jnp.dot(cot[...].T, mixed_two[...], preferred_element_type=F32)
    moved_mem, moved_two, moved_keys, moved_one = {}, {}, {}, {}
    view_mem = rows_of(grad_mem, own_query.shape[0])
    started_mem = net.scatter_start(view_mem, across_mem)
    pass_mem = (view_mem, across_mem, started_mem, mem_out, mem_in, moved_mem)
    need(share, dw, index, keys)
    head = net.col * halves // 2
    own_share = share[pl.ds(pl.multiple_of(head * PICKS, PICKS), PICKS), :]
    spread_picks(halves, own_share, dw[...], index, grad_sub)
    net.scatter_pass(*pass_mem, True)
    for h in range(halves):
        both[:, h * QD : (h + 1) * QD] = jnp.dot(
            grad_sub[:, h * NK : (h + 1) * NK], keys[h], preferred_element_type=F32
        ).astype(LOW)
    own_part, reduce_two = project_start(
        net, both[...], weights_two.at[:, : depth + width], two_outgoing, two_incoming
    )
    need(resid, recv_row)
    block = resid[...] + project_end(own_res, res_incoming, reduce_res)
    pack_for_rows(net, packed, block.astype(LOW), recv_row[...])
    copies = exchange_start(net, packed, got, capacity)
    need(hidden_two, queries)
    grad_two[...] = jnp.dot(hidden_two[...].T, both[...], preferred_element_type=F32)
    for h in range(halves):
        grad_keys[h] = jnp.dot(
            grad_sub[:, h * NK : (h + 1) * NK].T,
            queries[:, h * QD : (h + 1) * QD],
            preferred_element_type=F32,
        )
    view_two = rows_of(grad_two, own_query.shape[0])
    span = own_keys.shape[1]
    view_keys = lambda at: grad_keys.at[:, pl.ds(pl.multiple_of(at * span, span), span), :]
    started_two = net.scatter_start(view_two, across_two)
    started_keys = net.scatter_start(view_keys, across_keys)
    pass_two = (view_two, across_two, started_two, two_out, two_in, moved_two)
    pass_keys = (view_keys, across_keys, started_keys, keys_out, keys_in, moved_keys)
    net.scatter_pass(*pass_two, True)
    net.scatter_pass(*pass_keys, True)
    net.scatter_pass(*pass_mem, False)
    need(lengths)
    ids_col = sequence_ids(lengths[...], memory.shape[0], 0)
    ids_row = sequence_ids(lengths[...], memory.shape[0], 1)
    need(factor_two, gain_two)
    grad_hidden = project_end(own_part, two_incoming, reduce_two)
    grads, gain_two_sum = norm_grad(
        net, grad_hidden, resid[...], factor_two[...], gain_two[...].astype(LOW).astype(F32), mine, theirs
    )
    own_cot = columns_of(cot, width)(net.col)[...]
    grads = grads + own_cot.astype(F32)
    grad_resid[...] = grads
    own = columns_of(grad_low, width)
    own(net.col)[...] = grads.astype(LOW)
    spread = net.columns_start(own)
    wait_all(spread)
    net.scatter_pass(*pass_two, False)
    net.scatter_pass(*pass_keys, False)
    need(weights_one, qkv, hidden_one, mixed, send_col, dealt, factor_one, gain_one)
    grad_heads = jnp.dot(
        grad_low[...], weights_one[:, 3 * width :], preferred_element_type=F32
    ).astype(LOW)
    for head in range(width // HD):
        (query, key, value), probs = attention_scores(
            qkv, head, ids_col, ids_row, 0, memory.shape[0]
        )
        grad_out = grad_heads[:, head * HD : (head + 1) * HD]
        grad_prob = lax.dot_general(grad_out, value, NT_DIMS, preferred_element_type=F32)
        inner = jnp.sum(probs * grad_prob, axis=1, keepdims=True)
        grad_score = (probs * (grad_prob - inner)).astype(LOW)
        pieces = (
            jnp.dot(grad_score, key, preferred_element_type=F32) * HD ** (-0.5),
            jnp.dot(grad_score.T, query, preferred_element_type=F32) * HD ** (-0.5),
            jnp.dot(probs.astype(LOW).T, grad_out, preferred_element_type=F32),
        )
        for j in range(3):
            grad_qkv[:, (3 * head + j) * HD : (3 * head + j + 1) * HD] = pieces[j].astype(LOW)
    own_part, reduce_one = project_start(
        net, grad_qkv[...], weights_one.at[:, : 3 * width], one_outgoing, one_incoming
    )
    grad_one[:, : 3 * width] = jnp.dot(
        hidden_one[...].T, grad_qkv[...], preferred_element_type=F32
    )
    grad_one[:, 3 * width :] = jnp.dot(grad_low[...].T, mixed[...], preferred_element_type=F32)
    view_one = rows_of(grad_one, own_qkv.shape[0])
    started_one = net.scatter_start(view_one, across_one)
    pass_one = (view_one, across_one, started_one, one_out, one_in, moved_one)
    net.scatter_pass(*pass_one, True)
    grad_hidden = project_end(own_part, one_incoming, reduce_one)
    grads, gain_one_sum = norm_grad(
        net,
        grad_hidden,
        dealt[...],
        factor_one[...],
        gain_one[...].astype(LOW).astype(F32),
        mine_one,
        theirs_one,
    )
    grads = grads + grad_resid[...]
    pack_for_rows(net, packed_one, grads.astype(LOW), recv_row[...])
    last = exchange_start(net, packed_one, got_one, capacity)
    net.scatter_pass(*pass_one, False)
    places = lax.broadcasted_iota(jnp.int32, my_gains.shape, 0)
    my_gains[...] = jnp.where(places == 0, gain_one_sum, gain_two_sum)
    gain_copies = [net.send(my_gains, their_gains.at[k], row_k=k) for k in range(1, rows)]
    total = net.scatter_end(view_two, across_two, started_two, two_in, moved_two)
    own_query[...] = total[:, :depth]
    own_gate[...] = total[:, depth:]
    own_mem[...] = net.scatter_end(view_mem, across_mem, started_mem, mem_in, moved_mem).T
    own_keys[...] = net.scatter_end(view_keys, across_keys, started_keys, keys_in, moved_keys)
    wait_all(copies)
    output[...] = unpack(got, send_col[...])
    flush(output)
    total = net.scatter_end(view_one, across_one, started_one, one_in, moved_one)
    own_qkv[...] = total[:, : 3 * width]
    own_attn[...] = total[:, 3 * width :].T
    total = my_gains[...]
    for k, copy in enumerate(gain_copies):
        copy.wait_recv()
        total = total + their_gains[k + 1]
    gains[...] = total
    wait_all(last)
    grad_tokens[...] = unpack(got_one, send_col[...])
    net.drain()


def staged(kernel, rows, cols, sizes, ins, outs, *refs):
    given, results = refs[:ins], refs[ins : ins + outs]
    rest = refs[ins + outs :]
    twins, rest = rest[: ins + outs], rest[ins + outs :]
    sems, rest = rest[0], rest[1:]
    sources, targets = twins[:ins], twins[ins:]
    waited, left = set(), []

    def moving(i):
        return pltpu.make_async_copy(given[i], sources[i], sems.at[i])

    def need(*wanted):
        for ref in wanted:
            i = [j for j in range(ins) if sources[j] is ref][0]
            if i not in waited:
                moving(i).wait()
                waited.add(i)

    def flush(*done):
        for ref in done:
            i = [j for j in range(outs) if targets[j] is ref][0]
            copy = pltpu.make_async_copy(targets[i], results[i], sems.at[ins + i])
            copy.start()
            left.append((i, copy))

    for i in range(ins):
        moving(i).start()
    kernel(rows, cols, *sizes, need, flush, *sources, *targets, *rest)
    assert len(waited) == ins
    flush(*[targets[i] for i in range(outs) if i not in [j for j, _ in left]])
    for _, copy in left:
        copy.wait()


def remote_call(kernel, rows, cols, number, copies, ins, outs, scratch, *sizes):
    twins = [(x.shape, x.dtype) for x in ins] + outs
    anywhere = pl.BlockSpec(memory_space=pl.ANY)
    return pl.pallas_call(
        functools.partial(staged, kernel, rows, cols, sizes, len(ins), len(outs)),
        out_shape=[jax.ShapeDtypeStruct(shape, dtype) for shape, dtype in outs],
        in_specs=[anywhere] * len(ins),
        out_specs=[anywhere] * len(outs),
        scratch_shapes=[pltpu.VMEM(shape, dtype) for shape, dtype in twins]
        + [pltpu.SemaphoreType.DMA((len(twins),))]
        + [pltpu.VMEM(shape, dtype) for shape, dtype in scratch]
        + [pltpu.SemaphoreType.DMA((copies,)), pltpu.SemaphoreType.DMA((copies,))],
        compiler_params=pltpu.CompilerParams(
            collective_id=number, has_side_effects=True, vmem_limit_bytes=VMEM_BYTES
        ),
    )(*ins)


def memory_kernel(
    rows,
    cols,
    own_weights,
    own_picks,
    own_grads,
    table_f32,
    memory,
    dw,
    gacc_out,
    gacc,
    table,
    stage,
    picks_of,
    grads_of,
    low_of,
    dense,
    hi_ref,
    lo_ref,
    wide_ref,
    found_ref,
    mem_all,
    mem_twin,
    mem_out,
    mem_in,
    dw_all,
    dw_twin,
    dw_out,
    dw_in,
    dw_cols,
    stage_sems,
    sends,
    recvs,
):
    net = Net(rows, cols, sends, recvs)
    half = rows // 2
    tok_block = own_picks.shape[0]
    span_rows, width = table.shape
    spans = span_rows // LANES
    pitch = spans + 8
    iters = 4
    per_tok = tok_block // iters
    per_span = spans // iters

    grads_at = rows_of(grads_of, tok_block)
    picks_at = rows_of(picks_of, tok_block)
    low_at = lambda index: low_of.at[index]
    views = (grads_at, picks_at, low_at)
    first_pass = 3 * half
    first_twin = first_pass + 3 * half
    first_out = first_twin + 2 * half
    first_col = first_out + 2 * half

    def gather(a, j):
        mine = views[a](net.row)
        return net.copy(mine, mine, 3 * j + a, row_k=2 * j if j else 1)

    def passing(a, j):
        there = views[a](flip(net.row, 2 * j))
        return net.copy(there, there, first_pass + 3 * j + a, row_k=1)

    def twin(a, j):
        src, dst = ((mem_all, mem_twin), (dw_all, dw_twin))[a]
        return net.copy(src.at[2 * j + 1], dst.at[j], first_twin + 2 * j + a, row_k=1)

    def outward(a, j):
        src, dst = ((mem_out, mem_in), (dw_out, dw_in))[a]
        return net.copy(src.at[j - 1], dst.at[j - 1], first_out + 2 * j + a, row_k=2 * j)

    head = lambda col: pl.ds(pl.multiple_of(col * MH // cols * PICKS, PICKS), PICKS)

    def dw_copy(k):
        return net.copy(
            dw_all.at[0, head(flip(net.col, k)), :],
            dw_cols.at[k - 1],
            first_col + k,
            col_k=k,
        )

    stage_rows = stage.shape[1]

    def stage_copy(i):
        source = table_f32.at[pl.ds(i * stage_rows, stage_rows), :]
        return pltpu.make_async_copy(source, stage.at[i % 2], stage_sems.at[i % 2])

    stage_copy(0).start()
    greeted = net.greet([1] + [2 * j for j in range(1, half)], range(1, cols))
    for i in range(span_rows // stage_rows):
        if (i + 1) * stage_rows < span_rows:
            stage_copy(i + 1).start()
        stage_copy(i).wait()
        table[i * stage_rows : (i + 1) * stage_rows, :] = stage[i % 2].astype(LOW)
    net.meet(greeted)
    grads_at(net.row)[...] = own_grads[...]
    picks_at(net.row)[...] = own_picks[...]
    low_at(net.row)[...] = own_weights[...].astype(LOW)
    for j in range(2):
        for a in range(3):
            gather(a, j).start()
    gacc[...] = jnp.zeros_like(gacc)
    mem_all[...] = jnp.zeros_like(mem_all)

    def one_block(step, _):
        k = jnp.where(step == 0, 0, jnp.where(step == rows - 1, 1, step + 1))
        there = cross(net.row, k, rows)
        for j in range(1, half):

            @pl.when(step == 2 * j - 1)
            def _():
                for a in range(3):
                    gather(a, j).wait_recv()
                    passing(a, j).start()
                if j + 1 < half:
                    for a in range(3):
                        gather(a, j + 1).start()

            @pl.when(step == 2 * j)
            def _():
                for a in range(3):
                    passing(a, j).wait_recv()

        @pl.when(step == rows - 1)
        def _():
            for a in range(3):
                gather(a, 0).wait_recv()

        picks = picks_at(there)[...].astype(jnp.int32) + 32768
        lo_int = picks & (LANES - 1)
        hi_ref[...] = ((picks >> LANE_BITS) - net.row * spans).astype(F32)
        lo_ref[...] = lo_int.astype(F32)
        wide_ref[...] = low_of[there].astype(F32).T
        places_lo = lax.broadcasted_iota(jnp.int32, (LANES, LANES), 0).astype(F32).astype(LOW)
        places_hi = lax.broadcasted_iota(jnp.int32, (spans, LANES), 0).astype(F32).astype(LOW)
        ones = jnp.ones((LANES, LANES), LOW)
        zeros = jnp.zeros((LANES, LANES), LOW)
        blank = jnp.zeros((spans, LANES), LOW)
        grads = grads_at(there)[...]
        grads_t = grads.T
        found_ref[...] = jnp.zeros_like(found_ref)
        hi_all = hi_ref[...]

        def token_pair(first):
            rights, lefts = [], []
            for token in (first, first + 1):
                lo_row = jnp.broadcast_to(lo_ref[pl.ds(token, 1), :], (LANES, LANES)).astype(LOW)
                hi_row = jnp.broadcast_to(hi_ref[pl.ds(token, 1), :], (spans, LANES)).astype(LOW)
                w_row = jnp.broadcast_to(wide_ref[pl.ds(token, 1), :], (spans, LANES)).astype(LOW)
                rights.append(jnp.where(lo_row == places_lo, ones, zeros))
                lefts.append(jnp.where(hi_row == places_hi, w_row, blank))
            right = jnp.concatenate(rights, axis=1)
            left = jnp.concatenate(
                [
                    jnp.concatenate([lefts[0], blank], axis=1),
                    jnp.concatenate([blank, lefts[1]], axis=1),
                ],
                axis=0,
            )
            both = lax.dot_general(left, right, NT_DIMS, preferred_element_type=F32)
            for j in range(2):
                dense[pl.ds(pl.multiple_of((first + j) * pitch, 8), spans), :] = both[
                    j * spans : (j + 1) * spans
                ]

        def look(found, first, number, between=None):
            span = pl.ds(pl.multiple_of(first * LANES, LANES), number * LANES)
            products = lax.dot_general(
                grads, table[span, :], NT_DIMS, preferred_element_type=F32
            )
            for j in range(number):
                picked = jnp.take_along_axis(
                    products[:, LANES * j : LANES * (j + 1)], lo_int, axis=1
                )
                found = jnp.where(hi_all == (first + j).astype(F32), picked, found)
                if between:
                    between(j)
            return found

        early = per_span // 2
        late = per_span - early

        def build(it, _):
            for j in range(1, half):

                @pl.when((it == 1) & (step == 2 * j + 1))
                def _():
                    twin(0, j).wait_recv()
                    twin(1, j).wait_recv()
                    mem_out[j - 1] = (mem_all[2 * j] + mem_twin[j]).astype(LOW)
                    outward(0, j).start()
                    dw_out[j - 1] = (dw_all[2 * j] + dw_twin[j]).astype(LOW)
                    outward(1, j).start()

            pairs = per_tok // 2 // early

            def some_pairs(j):
                for u in range(pairs):
                    token_pair(it * per_tok + (j * pairs + u) * 2)

            found_ref[...] = look(found_ref[...], it * early, early, some_pairs)
            return 0

        lax.fori_loop(0, iters, build, 0)
        parts = min(4, late)

        def multiply(it, _):
            found, total = found_ref[...], None
            for c in range(parts):
                low, high = c * late // parts, (c + 1) * late // parts
                found = look(found, early * iters + it * late + low, high - low)
                low, high = c * per_span // parts, (c + 1) * per_span // parts
                first = it * per_span + low
                chosen = jnp.concatenate(
                    [
                        dense[pl.ds(first + j, tok_block, stride=pitch), :].astype(LOW)
                        for j in range(high - low)
                    ],
                    axis=1,
                )
                span = pl.ds(pl.multiple_of(first * LANES, LANES), (high - low) * LANES)
                gacc[:, span] += jnp.dot(grads_t, chosen, preferred_element_type=F32)
                read = jnp.dot(chosen, table[span, :], preferred_element_type=F32)
                total = read if total is None else total + read
            mem_all[k] += total
            found_ref[...] = found
            return 0

        lax.fori_loop(0, iters, multiply, 0)
        dw_all[k] = found_ref[...].T
        for j in range(half):

            @pl.when(step == (2 * j if j else rows - 1))
            def _():
                twin(0, j).start()
                twin(1, j).start()

        return 0

    lax.fori_loop(0, rows, one_block, 0)
    leaving = pltpu.make_async_copy(gacc, gacc_out, stage_sems.at[2])
    leaving.start()
    twin(1, 0).wait_recv()
    total = dw_all[0] + dw_twin[0]
    for j in range(1, half):
        outward(1, j).wait_recv()
        total = total + dw_in[j - 1].astype(F32)
    dw_all[0] = total
    for k in range(1, cols):
        dw_copy(k).start()
    twin(0, 0).wait_recv()
    total = mem_all[0] + mem_twin[0]
    for j in range(1, half):
        outward(0, j).wait_recv()
        total = total + mem_in[j - 1].astype(F32)
    memory[...] = total
    total = dw_all[0, head(net.col), :]
    for k in range(1, cols):
        dw_copy(k).wait_recv()
        total = total + dw_cols[k - 1]
    dw[...] = total
    for k in range(1, cols):
        dw_copy(k).wait_send()
    for j in range(half):
        for a in range(3):
            gather(a, j).wait_send()
            if j:
                passing(a, j).wait_send()
        for a in range(2):
            twin(a, j).wait_send()
            if j:
                outward(a, j).wait_send()
    leaving.wait()


def finish_kernel(others, source, *refs):
    given, out, results = refs[:others], refs[others], refs[others + 1 :]

    @pl.when(pl.program_id(0) == 0)
    def _():
        for i in range(others):
            results[i][...] = given[i][...]

    out[...] = source[...].T


def finish_call(table, others):
    width, span_rows = table.shape
    block = min(4096, span_rows)
    whole = [
        pl.BlockSpec(x.shape, lambda i, rank=x.ndim: (0,) * rank, pipeline_mode=pl.Buffered(1))
        for x in others
    ]
    return pl.pallas_call(
        functools.partial(finish_kernel, len(others)),
        grid=(span_rows // block,),
        in_specs=[pl.BlockSpec((width, block), lambda i: (0, i))] + whole,
        out_specs=[pl.BlockSpec((block, width), lambda i: (i, 0))] + whole,
        out_shape=[jax.ShapeDtypeStruct((span_rows, width), F32)]
        + [jax.ShapeDtypeStruct(x.shape, x.dtype) for x in others],
        compiler_params=pltpu.CompilerParams(vmem_limit_bytes=VMEM_BYTES),
    )(table, *others)


def memory_call(rows, cols, number, weights, picks, grads, table):
    tokens, count = picks.shape
    span_rows, width = table.shape
    half = rows // 2
    copies = 10 * half + cols
    vmem = pltpu.VMEM
    return pl.pallas_call(
        functools.partial(memory_kernel, rows, cols),
        in_specs=[VMEM_SPEC, VMEM_SPEC, VMEM_SPEC, pl.BlockSpec(memory_space=pl.ANY)],
        out_specs=[VMEM_SPEC, VMEM_SPEC, pl.BlockSpec(memory_space=pl.ANY)],
        out_shape=[
            jax.ShapeDtypeStruct((tokens, width), F32),
            jax.ShapeDtypeStruct((PICKS, tokens), F32),
            jax.ShapeDtypeStruct((width, span_rows), F32),
        ],
        scratch_shapes=[
            vmem((width, span_rows), F32),
            vmem((span_rows, width), LOW),
            vmem((2, 1024, width), F32),
            vmem((rows * tokens, count), jnp.int16),
            vmem((rows * tokens, width), LOW),
            vmem((rows, count, tokens), LOW),
            vmem((tokens * (span_rows // LANES + 8), LANES), F32),
            vmem((tokens, count), F32),
            vmem((tokens, count), F32),
            vmem((tokens, count), F32),
            vmem((tokens, count), F32),
            vmem((rows, tokens, width), F32),
            vmem((half, tokens, width), F32),
            vmem((half - 1, tokens, width), LOW),
            vmem((half - 1, tokens, width), LOW),
            vmem((rows, count, tokens), F32),
            vmem((half, count, tokens), F32),
            vmem((half - 1, count, tokens), LOW),
            vmem((half - 1, count, tokens), LOW),
            vmem((cols - 1, PICKS, tokens), F32),
            pltpu.SemaphoreType.DMA((3,)),
            pltpu.SemaphoreType.DMA((copies,)),
            pltpu.SemaphoreType.DMA((copies,)),
        ],
        compiler_params=pltpu.CompilerParams(
            collective_id=number, has_side_effects=True, vmem_limit_bytes=63 * 2**20
        ),
    )(weights, picks, grads, table)


def per_device(
    tokens,
    cotangent,
    deal_order,
    seq_lengths,
    value_picks,
    norm1_gain,
    w_qkv,
    w_attn_out,
    norm2_gain,
    w_query,
    sub_keys,
    value_table,
    w_gate,
    w_mem_out,
):
    rows, cols = lax.axis_size("row"), lax.axis_size("col")
    row_index = lax.axis_index("row")
    count, width = tokens.shape
    slots = 2 * count
    half = rows // 2
    halves = sub_keys.shape[0]
    depth = halves * QD
    span_one, span_two = 4 * width, depth + 2 * width
    shard_rows = w_qkv.shape[0]
    gain_one, gain_two = norm1_gain[None, :], norm2_gain[None, :]
    swap = [((slots, width), LOW), ((slots, width), LOW)]
    sums = [((8, count), F32), ((cols, 8, count), F32)]
    part_sums = [((2, 8, count // 2), F32), ((2, cols, 8, count // 2), F32)]
    moving = ((cols - 1, count, width), LOW)
    (
        send_row,
        send_col,
        recv_row,
        recv_col,
        hidden_one,
        dealt,
        factor_one,
        weights_one,
        qkv,
        mixed,
        hidden_two,
        resid,
        factor_two,
        full_cot,
        weights_two,
        keys,
        queries,
        gate,
        grad_mixed,
        grad_memory,
        index,
        low_picks,
        pick_weights,
    ) = remote_call(
        front_kernel,
        rows,
        cols,
        0,
        10 * (cols - 1) + 5 * (rows - 1),
        [
            deal_order[None, :],
            value_picks,
            seq_lengths,
            tokens,
            cotangent,
            w_qkv,
            w_attn_out,
            w_query,
            w_gate,
            w_mem_out,
            sub_keys,
            gain_one,
            gain_two,
        ],
        [
            ((1, count), jnp.int32),
            ((count, 1), jnp.int32),
            ((1, count), jnp.int32),
            ((count, 1), jnp.int32),
            ((count, D), LOW),
            ((count, width), F32),
            ((count, LANES), F32),
            ((D, span_one), LOW),
            ((count, 3 * width), LOW),
            ((count, width), LOW),
            ((count, D), LOW),
            ((count, width), F32),
            ((count, LANES), F32),
            ((count, D), LOW),
            ((D, span_two), LOW),
            ((halves, NK, QD), LOW),
            ((count, depth), LOW),
            ((count, width), F32),
            ((count, width), F32),
            ((count, width), LOW),
            ((halves * PICKS, count), jnp.int32),
            ((count, MH * PICKS), jnp.int16),
            ((MH * PICKS, count), F32),
        ],
        [((2 * MH * PICKS, count), F32), ((count, MH * PICKS), jnp.int32), ((count, D), LOW), ((8, D), F32), *swap, *swap, moving, moving, *part_sums]
        + [((MH * PICKS, count), F32)],
        halves,
    )
    memory, grad_pick, grad_table = memory_call(
        rows, cols, 1, pick_weights, low_picks, grad_memory, value_table
    )
    block = ((count, width), F32)
    scattered = [
        [((half,) + shape, F32), ((half - 1,) + shape, LOW), ((half - 1,) + shape, LOW)]
        for shape in (
            (shard_rows, depth + width),
            sub_keys.shape,
            (shard_rows, span_one),
            (shard_rows, width),
        )
    ]
    output, grad_tokens, own_qkv, own_attn, own_query, own_gate, own_mem, own_keys, gains = remote_call(
        back_kernel,
        rows,
        cols,
        2,
        6 * (cols - 1) + 3 * (rows - 1) + 4 * (half + half - 1),
        [
            pick_weights,
            grad_pick,
            index,
            memory,
            gate,
            grad_mixed,
            queries,
            hidden_two,
            full_cot,
            weights_two,
            keys,
            resid,
            factor_two,
            gain_two,
            recv_row,
            send_col,
            qkv,
            mixed,
            seq_lengths,
            hidden_one,
            weights_one,
            dealt,
            factor_one,
            gain_one,
        ],
        [
            block,
            block,
            (w_qkv.shape, F32),
            (w_attn_out.shape, F32),
            (w_query.shape, F32),
            (w_gate.shape, F32),
            (w_mem_out.shape, F32),
            (sub_keys.shape, F32),
            ((8, width), F32),
        ],
        [
            ((count, halves * NK), LOW),
            ((count, depth + width), LOW),
            ((count, width), LOW),
            ((D, width), F32),
            ((D, depth + width), F32),
            ((halves, NK, QD), F32),
            ((count, D), LOW),
            block,
            ((count, 3 * width), LOW),
            ((D, span_one), F32),
            *[moving] * 6,
            *sums,
            *sums,
            *swap,
            *swap,
            *scattered[0],
            *scattered[1],
            *scattered[2],
            *scattered[3],
            ((8, width), F32),
            ((rows, 8, width), F32),
        ],
        halves,
    )
    gain_span = width // rows
    gain_one_grad = lax.dynamic_slice_in_dim(gains[0], row_index * gain_span, gain_span)
    gain_two_grad = lax.dynamic_slice_in_dim(gains[1], row_index * gain_span, gain_span)
    others = (
        output,
        grad_tokens,
        own_qkv,
        own_attn,
        own_query,
        own_keys,
        own_gate,
        own_mem,
    )
    turned, *others = finish_call(grad_table, others)
    output, grad_tokens, own_qkv, own_attn, own_query, own_keys, own_gate, own_mem = others
    return (
        output,
        grad_tokens,
        gain_one_grad,
        own_qkv,
        own_attn,
        gain_two_grad,
        own_query,
        own_keys,
        turned,
        own_gate,
        own_mem,
    )


def solution(mesh):
    return jax.shard_map(
        per_device,
        mesh=mesh,
        in_specs=(
            P("row", "col"),
            P("row", "col"),
            P(),
            P("row", None),
            P("row", None, None),
            P("col"),
            P("row", "col"),
            P("col", "row"),
            P("col"),
            P("row", "col"),
            P("col", "row", None),
            P("row", "col"),
            P("row", "col"),
            P("col", "row"),
        ),
        out_specs=(
            P("row", "col"),
            P("row", "col"),
            P(("col", "row")),
            P("row", "col"),
            P("col", "row"),
            P(("col", "row")),
            P("row", "col"),
            P("col", "row", None),
            P("row", "col"),
            P("row", "col"),
            P("col", "row"),
        ),
        check_vma=False,
    )
```
